32 devices in a mesh: ray: 8 (over y, x, core), tile: 4 (over z).
Axes of the slice: x: 2, y: 2, z: 4, core: 2. Of those that a mesh axis runs over, the one named last changes fastest.
Arguments:
- volume: bfloat16 [32, 16, 16, 256], P('tile'), may hold values from -8 to 8
- sample_cells: int32 [512, 128], P(('ray', 'tile')), may hold values from 0 to 8191, as said below
- sample_fracs: float32 [3, 512, 128], P(None, ('ray', 'tile')), may hold values from 0 to 1
- view_mask: int32 [512, 128], P(('ray', 'tile')), may hold values 0 or 1
- pixel_of_ray: int32 [32, 16], P(('ray', 'tile')), may hold values from 0 to 15, each once within a row
- conv_weight: bfloat16 [2, 27, 256, 256], replicated, may hold values from -0.078125 to 0.078125
- norm_gain: float32 [2, 256], replicated, may hold values from 0.5 to 1.5
- norm_shift: float32 [2, 256], replicated, may hold values from -3 to 3
- hidden_weight: bfloat16 [2, 256, 256], replicated, may hold values from -0.375 to 0.375
- hidden_bias: float32 [2, 256], replicated, may hold values from -3 to 3
- density_weight: bfloat16 [2, 256], replicated, may hold values from -0.375 to 0.375
- density_bias: float32 [2], replicated, may hold values from -2 to 2
- semantic_weight: bfloat16 [2, 256, 18], replicated, may hold values from -0.375 to 0.375
- semantic_bias: float32 [2, 18], replicated, may hold values from -4 to 4
- render_cotangent: bfloat16 [2, 512, 19], P(None, ('ray', 'tile')), may hold values from -6 to 6
- volume_cotangent: bfloat16 [32, 16, 16, 256], P('tile'), may hold values from -6 to 6
Outputs:
- rendered: float32 [2, 512, 19], P(None, ('ray', 'tile'))
- volume_out: bfloat16 [32, 16, 16, 256], P('tile')
- volume_grad: float32 [32, 16, 16, 256], P('tile')
- conv_grad: float32 [2, 27, 256, 256], replicated
- gain_grad: float32 [2, 256], replicated
- shift_grad: float32 [2, 256], replicated
- hidden_weight_grad: float32 [2, 256, 256], replicated
- hidden_bias_grad: float32 [2, 256], replicated
- density_weight_grad: float32 [2, 256], replicated
- density_bias_grad: float32 [2], replicated
- semantic_weight_grad: float32 [2, 256, 18], replicated
- semantic_bias_grad: float32 [2, 18], replicated
The draws below stay inside these ranges and needn't reach their ends.
Inputs may be any that keep to these rules, and one draw needn't show every extreme that they name: `sample_cells`: on the rays of one device exactly 768 samples lie in one tile of 8 x-planes, the same tile for all devices with the same index along ray; the remaining samples are spread over the other tiles as evenly as their number allows. A sample's cell is never on the last plane of its tile along x, nor on the last plane along y or z.
All inputs are finite; a program needn't handle non-finite values. No bound on the sum of `view_mask` on one device may be relied on, other than what follows from the above.
Results may differ from the reference program's by a relative error of at most 0.0052.
Values may be sent and summed in bfloat16 or wider, within the bound.
No kernel may reach another device: no remote copies, remote signals or barrier semaphores. Data moves between devices by JAX's collectives and lax.ppermute only.
A program may use at most 256 MiB of HBM per device.

```python
import jax
import jax.numpy as jnp
from jax import lax

C = 256
CLASSES = 18
NS = 128
LAYERS = 2
VX = 8
VY = 16
VZ = 16
RAYS_DEV = 16
CAP = 768
NX = 32
RAYS = 512
N_TILE = 4
DEVICES = 32


def draw_volume(key, part):
    key = jax.random.fold_in(key, 5)
    position = jnp.arange(NX, dtype=jnp.float32) / (NX - 1)
    noise = jax.random.truncated_normal(key, -4.0, 4.0, (NX, VY, VZ, C), jnp.float32)
    scale = 0.6 + 1.2 * position
    return (noise * scale[:, None, None, None]).astype(jnp.bfloat16)


def draw_sample_cells(key, part):
    key = jax.random.fold_in(key, 7)
    keys = jax.random.split(key, 5)
    blocks = RAYS // RAYS_DEV
    count = RAYS_DEV * NS
    row_hot = jax.random.randint(keys[0], (blocks // N_TILE,), 0, N_TILE)
    hot = jnp.repeat(row_hot, N_TILE)
    order = jax.vmap(lambda single: jax.random.permutation(single, count))(jax.random.split(keys[1], blocks))
    rest = jnp.maximum(order - CAP, 0) % (N_TILE - 1)
    other = rest + (rest >= hot[:, None]).astype(jnp.int32)
    owner = jnp.where(order < CAP, hot[:, None], other)
    base_x = jax.random.randint(keys[2], (blocks, count), 0, VX - 1)
    base_y = jax.random.randint(keys[3], (blocks, count), 0, VY - 1)
    base_z = jax.random.randint(keys[4], (blocks, count), 0, VZ - 1)
    cell = ((owner * VX + base_x) * VY + base_y) * VZ + base_z
    return cell.reshape(RAYS, NS).astype(jnp.int32)


def set_ends(values, key, least, top_value):
    index_at = [jax.random.randint(jax.random.fold_in(key, axis), (), 0, length) for axis, length in enumerate(values.shape)]
    widest = values.shape.index(max(values.shape))
    neighbour = index_at[:widest] + [(index_at[widest] + 1) % values.shape[widest]] + index_at[widest + 1:]
    return values.at[tuple(index_at)].set(least).at[tuple(neighbour)].set(top_value)


def level_of(key, extent, pieces, least, high):
    level, own = 1.0, jax.random.fold_in(key, 6)
    for dim, parts in pieces:
        heights = jnp.exp(jax.random.uniform(jax.random.fold_in(own, dim), (parts,), jnp.float32, least / len(pieces), high / len(pieces)))
        level = level * jnp.repeat(heights, extent[dim] // parts).reshape([-1 if axis == dim else 1 for axis in range(len(extent))])
    return level


def gaussian(key, dims, deviation, limit, pieces=(), kind=jnp.bfloat16):
    values = deviation * jax.random.normal(key, dims, jnp.float32)
    if pieces:
        values = values * level_of(key, dims, pieces, -0.22, 0.18)
    return jnp.clip(values, -limit, limit).astype(kind)


def setup_inputs(seed: int = 0) -> dict:
    key_of = jax.random.split(jax.random.key(seed), 17)
    volume = draw_volume(jax.random.fold_in(key_of[16], 71), 0)
    sample_cells = draw_sample_cells(jax.random.fold_in(key_of[16], 71), 0)
    sample_fracs = jnp.clip(1.0 * jax.random.uniform(key_of[2], (3, RAYS, NS), jnp.float32) ** level_of(key_of[2], (3, RAYS, NS), ((1, 32),), -0.2, 0.2), 0.0, 1.0)
    view_mask = set_ends((jax.random.randint(key_of[3], (RAYS, NS), 0, 6) < 5).astype(jnp.int32), jax.random.fold_in(key_of[3], 1), 0, 1)
    pixel_of_ray = jax.vmap(lambda own: jax.random.permutation(own, RAYS_DEV))(jax.random.split(key_of[4], DEVICES)).reshape((DEVICES, RAYS_DEV)).astype(jnp.int32)
    conv_weight = gaussian(key_of[5], (LAYERS, 27, C, C), (27 * C) ** -0.5, 0.078125)
    norm_gain = jnp.clip(1.0 + 0.1 * jax.random.normal(key_of[6], (LAYERS, C), jnp.float32), 0.5, 1.5)
    norm_shift = gaussian(key_of[7], (LAYERS, C), 0.5, 3.0, (), jnp.float32)
    hidden_weight = gaussian(key_of[8], (LAYERS, C, C), C ** -0.5, 0.375)
    hidden_bias = gaussian(key_of[9], (LAYERS, C), 0.5, 3.0, (), jnp.float32)
    density_weight = gaussian(key_of[10], (LAYERS, C), C ** -0.5, 0.375)
    density_bias = gaussian(key_of[11], (LAYERS,), 0.5, 2.0, (), jnp.float32)
    semantic_weight = gaussian(key_of[12], (LAYERS, C, CLASSES), C ** -0.5, 0.375)
    semantic_bias = gaussian(key_of[13], (LAYERS, CLASSES), 1.0, 4.0, (), jnp.float32)
    render_cotangent = gaussian(key_of[14], (LAYERS, RAYS, CLASSES + 1), 1.0, 6.0, ((1, 32),))
    volume_cotangent = gaussian(key_of[15], (NX, VY, VZ, C), 1.0, 6.0, ((0, 4),))
    return {"volume": volume, "sample_cells": sample_cells, "sample_fracs": sample_fracs, "view_mask": view_mask, "pixel_of_ray": pixel_of_ray, "conv_weight": conv_weight, "norm_gain": norm_gain, "norm_shift": norm_shift, "hidden_weight": hidden_weight, "hidden_bias": hidden_bias, "density_weight": density_weight, "density_bias": density_bias, "semantic_weight": semantic_weight, "semantic_bias": semantic_bias, "render_cotangent": render_cotangent, "volume_cotangent": volume_cotangent}


@jax.custom_vjp
def low(v):
    return lax.optimization_barrier(v.astype(jnp.bfloat16)).astype(jnp.float32)

@jax.custom_vjp
def low_back(v):
    return v

def low_keep(v):
    return (low(v), None)

def low_pass(kept, grad):
    return (grad,)

def back_keep(v):
    return (v, None)

def back_low(kept, grad):
    return (low(grad),)
low.defvjp(low_keep, low_pass)
low_back.defvjp(back_keep, back_low)
epsilon = 1e-05

def matmul(left, right):
    return jnp.dot(left, right, precision=lax.Precision.HIGHEST, preferred_element_type=jnp.float32)

def convolve(rounded, weight):
    padded = jnp.pad(rounded, ((1, 1), (1, 1), (1, 1), (0, 0)))
    total = jnp.zeros((NX * VY * VZ, C), jnp.float32)
    number = 0
    for a in range(3):
        for b in range(3):
            for c in range(3):
                piece = padded[a:a + NX, b:b + VY, c:c + VZ].reshape(NX * VY * VZ, C)
                total = total + matmul(piece, weight[number])
                number += 1
    return total

def render_block(table, hidden_matrix, hidden_offset, head_matrix, head_offset, block):
    cells, fracs, visible, pixels = block
    flat = cells.reshape(-1)
    along_x = fracs[0].reshape(-1)
    along_y = fracs[1].reshape(-1)
    along_z = fracs[2].reshape(-1)
    feature = jnp.zeros((flat.shape[0], C), jnp.float32)
    for a in range(2):
        weight_x = along_x if a else 1.0 - along_x
        for b in range(2):
            weight_y = along_y if b else 1.0 - along_y
            for c in range(2):
                weight_z = along_z if c else 1.0 - along_z
                corner = low(weight_x * weight_y * weight_z)
                feature = feature + corner[:, None] * table[flat + a * VY * VZ + b * VZ + c]
    feature = low_back(low(feature))
    inner = low_back(matmul(feature, hidden_matrix) + hidden_offset)
    hidden = low(jax.nn.softplus(inner))
    heads = low_back(matmul(hidden, head_matrix) + head_offset)
    semantic = heads[:, :CLASSES].reshape(RAYS_DEV, NS, CLASSES)
    density = jax.nn.softplus(heads[:, CLASSES]).reshape(RAYS_DEV, NS)
    optical = visible * density * (4.0 / NS)
    passing = jnp.exp(-(jnp.cumsum(optical, axis=1) - optical))
    weights = passing * (1.0 - jnp.exp(-optical))
    colour = lax.optimization_barrier(jnp.sum(weights[:, :, None] * semantic, axis=1))
    opacity = lax.optimization_barrier(jnp.sum(weights, axis=1))
    result = jnp.concatenate([colour, opacity[:, None]], axis=1)
    return jnp.zeros_like(result).at[pixels].set(result)

def reference(volume, sample_cells, sample_fracs, view_mask, pixel_of_ray, conv_weight, norm_gain, norm_shift, hidden_weight, hidden_bias, density_weight, density_bias, semantic_weight, semantic_bias, render_cotangent, volume_cotangent):
    blocks = (sample_cells.reshape(DEVICES, RAYS_DEV, NS), jnp.transpose(sample_fracs.reshape(3, DEVICES, RAYS_DEV, NS), (1, 0, 2, 3)), view_mask.astype(jnp.float32).reshape(DEVICES, RAYS_DEV, NS), pixel_of_ray)

    def forward(volume_input, conv_matrix, gains, shifts, hidden_matrix, hidden_offset, density_vector, density_offset, semantic_matrix, semantic_offset):
        current = volume_input
        rounded = low(volume_input)
        pictures = []
        for layer in range(LAYERS):
            conv_out = low_back(convolve(rounded, conv_matrix[layer]))
            mean = lax.optimization_barrier(jnp.mean(conv_out, axis=0))
            spread = lax.optimization_barrier(jnp.mean(conv_out * conv_out, axis=0)) - mean * mean
            normal = (conv_out - mean) * lax.rsqrt(spread + epsilon) * gains[layer] + shifts[layer]
            current = current + jax.nn.silu(normal).reshape(current.shape)
            rounded = low(current)
            table = rounded.reshape(NX * VY * VZ, C)
            head_matrix = jnp.concatenate([semantic_matrix[layer], density_vector[layer][:, None]], axis=1)
            head_offset = jnp.concatenate([semantic_offset[layer], density_offset[layer:layer + 1]])
            layer_matrix = hidden_matrix[layer]
            layer_offset = hidden_offset[layer]

            def one_block(block):
                return render_block(table, layer_matrix, layer_offset, head_matrix, head_offset, block)
            images = lax.map(jax.checkpoint(one_block), blocks)
            pictures.append(images.reshape(RAYS, CLASSES + 1))
        return (jnp.stack(pictures), current)
    outputs, backward = jax.vjp(forward, volume.astype(jnp.float32), conv_weight.astype(jnp.float32), norm_gain, norm_shift, hidden_weight.astype(jnp.float32), hidden_bias, density_weight.astype(jnp.float32), density_bias, semantic_weight.astype(jnp.float32), semantic_bias)
    grads = backward((render_cotangent.astype(jnp.float32), volume_cotangent.astype(jnp.float32)))
    return (outputs[0], outputs[1].astype(jnp.bfloat16), grads[0], grads[1], grads[2], grads[3], grads[4], grads[5], grads[6], grads[7], grads[8], grads[9])
```

```python
import functools

import jax
import jax.numpy as jnp
from jax import lax
from jax.experimental import pallas as pl
from jax.experimental.pallas import tpu as pltpu
from jax.sharding import PartitionSpec as P

CAP = 768
WINDOW = 256
LANES = 128
PROWS = 24
DROWS = 32
COORDS = 8
BLOCKS = 8
PACK = 320
epsilon = 1e-05
MIB = 1024 * 1024

BF = jnp.bfloat16
F32 = jnp.float32
VMEM = pltpu.VMEM
SMEM = pltpu.SMEM


def nn(left, right):
    return jnp.dot(left, right, preferred_element_type=F32)


def nt(left, right):
    return lax.dot_general(left, right, (((1,), (1,)), ((), ())), preferred_element_type=F32)


def iota(shape, dim):
    return lax.broadcasted_iota(jnp.int32, shape, dim)


def whole(shape):
    return pl.BlockSpec(shape, lambda *_: (0,) * len(shape))


def planes_of(step, shape, first=0):
    return pl.BlockSpec((step,) + shape[1:], lambda i: (i + first // step,) + (0,) * (len(shape) - 1))


def sspec():
    return pl.BlockSpec(memory_space=SMEM)


def aspec():
    return pl.BlockSpec(memory_space=pl.ANY)


def hspec():
    return pl.BlockSpec(memory_space=pltpu.HBM)


def ordered(kernel, operands, in_specs, follow, **options):
    count, skip = len(operands), len(follow)

    def body(*refs):
        kernel(*refs[:count], *refs[count + skip :])

    return pl.pallas_call(body, in_specs=list(in_specs) + [aspec()] * skip, **options)(
        *operands, *follow
    )


def params(mib):
    return pltpu.CompilerParams(vmem_limit_bytes=int(mib * MIB))


def cost(flops, moved):
    return pl.CostEstimate(flops=int(flops), bytes_accessed=int(moved), transcendentals=0)


def lane_cumsum(x):
    lane = iota(x.shape, 1)
    shift = 1
    while shift < x.shape[1]:
        x = x + jnp.where(lane >= shift, pltpu.roll(x, shift, 1), 0.0)
        shift *= 2
    return x


def window_onehots(starts, owner_row, rank_row, ray, rays, tiles):
    rows = iota((WINDOW, rank_row.shape[1]), 0)
    hots, bases = [], []
    for t in range(tiles):
        start = starts[t * rays + ray]
        base = (start // LANES) * LANES
        place = jnp.where(owner_row == t, rank_row + (start - base), -1)
        hots.append((rows == place).astype(F32).astype(BF))
        bases.append(pl.multiple_of(base, LANES))
    return jnp.concatenate(hots, axis=0), bases


def prep_kernel(extent, starts, cells_ref, fracs_ref, out_ref, owner_ref, rank_ref, vals, acc):
    depth, height, width = extent
    tiles = out_ref.shape[0]
    rays, samples = cells_ref.shape
    cells = cells_ref[...]
    voxels = depth * height * width
    owner = lax.div(cells, voxels)
    local = cells - owner * voxels
    base_x = lax.div(local, height * width)
    inner = local - base_x * (height * width)
    base_y = lax.div(inner, width)
    base_z = inner - base_y * width
    rank = jnp.zeros(cells.shape, F32)
    for t in range(tiles):
        mine = owner == t
        rank = jnp.where(mine, lane_cumsum(jnp.where(mine, 1.0, 0.0)) - 1.0, rank)
    owner_ref[...] = owner
    rank_ref[...] = rank.astype(jnp.int32)
    vals[...] = jnp.zeros_like(vals)
    rows = [(base_x + 1).astype(F32), base_y.astype(F32), base_z.astype(F32)]
    low = []
    for d in range(3):
        frac = fracs_ref[d]
        high = frac.astype(BF).astype(F32)
        rows.append(high)
        low.append(frac - high)
    rows += low
    for number, row in enumerate(rows):
        for k in range(rays):
            vals[number : number + 1, k * samples : (k + 1) * samples] = row[k : k + 1]
    acc[...] = jnp.zeros_like(acc)
    for k in range(rays):
        hot, bases = window_onehots(
            starts, owner_ref[k : k + 1, :], rank_ref[k : k + 1, :], k, rays, tiles
        )
        moved = nt(vals[:, k * samples : (k + 1) * samples].astype(BF), hot)
        for t in range(tiles):
            acc[t, :, pl.ds(bases[t], WINDOW)] += moved[:, t * WINDOW : (t + 1) * WINDOW]
    out_ref[...] = jnp.zeros_like(out_ref)
    wide = out_ref.shape[2]
    lines = CAP // wide
    for n in range(lines):
        part = slice(n * wide, (n + 1) * wide)
        for r in range(6):
            value = acc[:, r : r + 1, part]
            if r >= 3:
                value = value + acc[:, r + 3 : r + 4, part]
            out_ref[:, r * lines + n : r * lines + n + 1, :] = value


def prepare(extent, starts, cells, fracs, tiles, wide, follow=()):
    rays, samples = cells.shape
    outs = ((tiles, COORDS * CAP // wide, wide), (rays, samples), (rays, samples))
    return ordered(
        functools.partial(prep_kernel, extent),
        (starts, cells, fracs,),
        [sspec(), whole(cells.shape), whole(fracs.shape)],
        follow,
        grid=(1,),
        out_shape=(
            jax.ShapeDtypeStruct(outs[0], F32),
            jax.ShapeDtypeStruct(outs[1], jnp.int32),
            jax.ShapeDtypeStruct(outs[2], jnp.int32),
        ),
        out_specs=tuple(whole(s) for s in outs),
        scratch_shapes=[VMEM((16, rays * samples), F32), VMEM((tiles, 16, CAP + WINDOW), F32)],
        compiler_params=params(60),
        cost_estimate=cost(4e8, 1e6),
        name="prep",
    )


def started(source, target, sem):
    copy = pltpu.make_async_copy(source, target, sem)
    copy.start()
    return copy


def put_plane(xs, p, value, width):
    rows, channels = value.shape
    along = lax.rem(iota(value.shape, 0), width)
    left = jnp.where(along == 0, 0.0, pltpu.roll(value, 1, 0))
    right = jnp.where(along == width - 1, 0.0, pltpu.roll(value, rows - 1, 0))
    xs[p, width : width + rows, 0:channels] = left.astype(BF)
    xs[p, width : width + rows, channels : 2 * channels] = value.astype(BF)
    xs[p, width : width + rows, 2 * channels : 3 * channels] = right.astype(BF)


def clear_edges(xs, width, rows):
    planes, _, wide = xs.shape
    for p in range(planes):
        xs[p, 0:width, :] = jnp.zeros((width, wide), BF)
        xs[p, width + rows : 2 * width + rows, :] = jnp.zeros((width, wide), BF)


def taps(xs, p, width, rows):
    return jnp.concatenate(
        [xs[p + a, b * width : b * width + rows, :] for a in range(3) for b in range(3)], axis=1
    )


def tap_pair(xs, first, width, rows):
    return jnp.concatenate(
        [taps(xs, first, width, rows), taps(xs, first + 1, width, rows)], axis=0
    )


def add_stats(sums, one, two):
    sums[0:1, :] += jnp.sum(one, axis=0, keepdims=True)
    sums[1:2, :] += jnp.sum(two, axis=0, keepdims=True)


def conv_scratch(planes, rows, width, channels, turned):
    shape = (channels, 27 * channels) if turned else (27 * channels, channels)
    return [VMEM((planes, rows + 2 * width, 3 * channels), BF), VMEM(shape, BF)]


def sems(*counts):
    return [pltpu.SemaphoreType.DMA((n,)) for n in counts]


def any_outs(*shapes):
    return tuple(jax.ShapeDtypeStruct(shape, dtype) for shape, dtype in shapes)


def conv_first_kernel(
    width, layer, before, own, after, coords, w_hbm, y_ref, v_ref, mix_ref,
    raw, xs, weight, y_buf, mix, in_sem, out_sem,
):
    planes, rows, channels = own.shape
    pairs = planes // 2 + 1
    body = [
        started(own.at[pl.ds(2 * i, 2)], raw.at[pl.ds(2 * i + 2, 2)], in_sem.at[i])
        for i in range(planes // 2)
    ]
    ends = [
        started(before, raw.at[pl.ds(0, 2)], in_sem.at[pairs]),
        started(after, raw.at[pl.ds(planes + 2, 2)], in_sem.at[pairs + 1]),
    ]
    heavy = started(w_hbm.at[layer], weight, in_sem.at[pairs + 2])
    light = started(coords, mix.at[:, pl.ds(8, coords.shape[1]), :], in_sem.at[pairs + 3])
    clear_edges(xs, width, rows)
    mix[:, 0:8, :] = jnp.zeros((mix.shape[0], 8, channels), F32)
    for copy in body + ends:
        copy.wait()

    @pl.loop(0, planes + 4)
    def _(p):
        put_plane(xs, p, raw[p].astype(F32), width)

    done = [started(raw.at[pl.ds(1, planes + 2)], v_ref, out_sem.at[pairs])]
    light.wait()
    heavy.wait()

    def out_copy(i):
        two = pl.ds(2 * i, 2)
        return pltpu.make_async_copy(y_buf.at[two], y_ref.at[two], out_sem.at[i])

    @pl.loop(0, pairs)
    def _(i):
        p = 2 * i
        part = nn(tap_pair(xs, p, width, rows), weight[...])
        y_buf[p] = part[:rows]
        y_buf[p + 1] = part[rows:]
        out_copy(i).start()
        for side, outer in ((0, 0), (1, pairs - 1)):

            @pl.when(i != outer)
            def _():
                kept = part[side * rows : (side + 1) * rows]
                add_stats(mix.at[0], kept, kept * kept)

    for t in range(1, mix.shape[0]):
        mix[t, 0:8, :] = mix[0, 0:8, :]
    done.append(started(mix, mix_ref, out_sem.at[pairs + 1]))
    for copy in done:
        copy.wait()
    for i in range(pairs):
        out_copy(i).wait()


def conv_first(before, own, after, coords, weights, layer, width):
    planes, rows, channels = own.shape
    ext = (planes + 2, rows, channels)
    tiles, lines, _ = coords.shape
    pairs = planes // 2 + 1
    return ordered(
        functools.partial(conv_first_kernel, width, layer),
        (before, own, after, coords, weights),
        [aspec()] * 5,
        (),
        out_shape=any_outs((ext, F32), (ext, BF), ((tiles, 8 + lines, channels), F32)),
        out_specs=(aspec(),) * 3,
        scratch_shapes=[VMEM((planes + 4, rows, channels), BF)]
        + conv_scratch(planes + 4, rows, width, channels, False)
        + [VMEM(ext, F32), VMEM((tiles, 8 + lines, channels), F32)]
        + sems(pairs + 4, pairs + 2),
        compiler_params=params(60),
        cost_estimate=cost(2 * 27 * channels * channels * rows * (planes + 2), 8e6),
        name="conv_first",
    )


def moments(total, count):
    both = jnp.sum(total, axis=0)
    mean = both[0:1, :] / count
    return mean, lax.rsqrt(both[1:2, :] / count - mean * mean + epsilon)


def row_of(ref, layer):
    return ref[layer : layer + 1, :]


def silu(value):
    return value * (1.0 / (1.0 + jnp.exp(-value)))


def conv_next_kernel(
    width, layer, count, flags, y_ext, v_ext, total_hbm, gain_hbm, shift_hbm, w_hbm,
    v_ref, r_ref, y_ref, stat_ref, first_ref, last_ref,
    y_in, v_in, total, gain, shift, xs, weight, v_buf, r_buf, y_buf, edges, stat, in_sem, out_sem,
):
    ext_planes, rows, channels = y_ext.shape
    pairs = ext_planes // 2
    small = [
        started(total_hbm.at[:, pl.ds(0, 8), :], total, in_sem.at[2 * pairs]),
        started(gain_hbm, gain, in_sem.at[2 * pairs + 1]),
        started(shift_hbm, shift, in_sem.at[2 * pairs + 2]),
    ]
    def in_copies(i):
        two = pl.ds(2 * i, 2)
        return (
            pltpu.make_async_copy(y_ext.at[two], y_in.at[two], in_sem.at[2 * i]),
            pltpu.make_async_copy(v_ext.at[two], v_in.at[two], in_sem.at[2 * i + 1]),
        )

    def mid_copies(i):
        two = pl.ds(2 * i, 2)
        return (
            pltpu.make_async_copy(v_buf.at[two], v_ref.at[two], out_sem.at[3 * i]),
            pltpu.make_async_copy(r_buf.at[two], r_ref.at[two], out_sem.at[3 * i + 1]),
        )

    def out_copy(i):
        two = pl.ds(2 * i - 2, 2)
        return pltpu.make_async_copy(y_buf.at[two], y_ref.at[two], out_sem.at[3 * i + 2])

    for i in range(pairs):
        for copy in in_copies(i):
            copy.start()
    heavy = started(w_hbm.at[layer + 1], weight, in_sem.at[2 * pairs + 3])
    clear_edges(xs, width, rows)
    stat[...] = jnp.zeros_like(stat)
    for copy in small:
        copy.wait()
    mean, inverse = moments(total[...], count)
    gains, shifts = row_of(gain, layer), row_of(shift, layer)

    @pl.loop(0, pairs)
    def _(i):
        for copy in in_copies(i):
            copy.wait()
        for side in range(2):
            p = 2 * i + side
            fresh = v_in[p].astype(F32) + silu((y_in[p] - mean) * inverse * gains + shifts)
            v_buf[p] = fresh
            outside = (p == side * (ext_planes - 1)) & (flags[side] == 0)
            rounded = jnp.where(outside, 0.0, fresh).astype(BF)
            r_buf[p] = rounded
            put_plane(xs, p, rounded.astype(F32), width)
        for copy in mid_copies(i):
            copy.start()

        @pl.when(i == 1)
        def _():
            heavy.wait()

        @pl.when(i > 0)
        def _():
            p = 2 * i - 2
            part = nn(tap_pair(xs, p, width, rows), weight[...])
            y_buf[p] = part[:rows]
            y_buf[p + 1] = part[rows:]
            add_stats(stat.at[0], part, part * part)
            out_copy(i).start()

    edges[0] = y_buf[0].astype(BF)
    edges[1] = y_buf[ext_planes - 3].astype(BF)
    for t in range(1, stat.shape[0]):
        stat[t] = stat[0]
    done = [
        started(stat, stat_ref, out_sem.at[2]),
        started(edges.at[pl.ds(0, 1)], first_ref, out_sem.at[3 * pairs]),
        started(edges.at[pl.ds(1, 1)], last_ref, out_sem.at[3 * pairs + 1]),
    ]
    for i in range(pairs):
        done += list(mid_copies(i)) + ([out_copy(i)] if i else [])
    for copy in done:
        copy.wait()


def conv_next(flags, y_ext, v_ext, total, gain, shift, weights, layer, width, count, follow=()):
    ext_planes, rows, channels = y_ext.shape
    ext = y_ext.shape
    inner = (ext_planes - 2, rows, channels)
    stat = (total.shape[0], 8, channels)
    pairs = ext_planes // 2
    edge = (1, rows, channels)
    return ordered(
        functools.partial(conv_next_kernel, width, layer, count),
        (flags, y_ext, v_ext, total, gain, shift, weights),
        [sspec()] + [aspec()] * 6,
        follow,
        out_shape=any_outs((ext, F32), (ext, BF), (inner, F32), (stat, F32), (edge, BF), (edge, BF)),
        out_specs=(aspec(),) * 6,
        scratch_shapes=[VMEM(ext, F32), VMEM(ext, BF), VMEM(stat, F32)]
        + [VMEM(gain.shape, F32)] * 2
        + conv_scratch(ext_planes, rows, width, channels, False)
        + [VMEM(ext, F32), VMEM(ext, BF), VMEM(inner, F32)]
        + [VMEM((2, rows, channels), BF), VMEM(stat, F32)]
        + sems(2 * pairs + 4, 3 * pairs + 2),
        compiler_params=params(60),
        cost_estimate=cost(2 * 27 * channels * channels * rows * (ext_planes - 2), 16e6),
        name="conv_next",
    )


def fill_weights(table, coords, extent):
    depth, height, width = extent
    samples = coords[0].shape[1]

    def along(base, frac, size):
        grid = iota((size, samples), 0).astype(F32)
        lower = jnp.where(grid == base, 1.0 - frac, 0.0)
        return lower + jnp.where(grid == base + 1.0, frac, 0.0)

    on_x = along(coords[0] - 1.0, coords[3], depth)
    on_y = along(coords[1], coords[4], height)
    on_z = along(coords[2], coords[5], width)
    for x in range(depth):
        on_xy = on_x[x : x + 1] * on_y
        for y in range(height):
            row = (x * height + y) * width
            table[row : row + width, :] = (on_xy[y : y + 1] * on_z).astype(BF)


def diagonal(rows, columns):
    return iota((rows, columns), 0) == iota((rows, columns), 1)


def identity(rows, columns):
    return diagonal(rows, columns).astype(F32).astype(BF)


def head_rows(semantic, density, rows):
    channels, classes = semantic.shape
    turned = nt(identity(rows, classes), semantic)
    return jnp.where(iota((rows, channels), 0) == classes, density.astype(F32), turned).astype(BF)


def column(row, rows):
    return jnp.sum(jnp.where(diagonal(rows, row.shape[1]), row, 0.0), axis=1, keepdims=True)


def coord_rows(block, slots):
    lines = slots // block.shape[1]
    return [
        jnp.concatenate(
            [block[8 + r * lines + n : 9 + r * lines + n, :] for n in range(lines)], axis=1
        )
        for r in range(6)
    ]


def sample_kernel(
    extent, layer, first, count, coords, *refs
):
    if count is None:
        r_hbm, refs = refs[0], refs[1:]
    else:
        y_hbm, v_hbm, total_hbm, gain, shift, refs = refs[0], refs[1], refs[2], refs[3], refs[4], refs[5:]
    hidden, hidden_b, semantic, density, semantic_b, density_b, refs = *refs[:6], refs[6:]
    p_ref, f_ref, g_ref, s_ref, refs = *refs[:4], refs[4:]
    if count is not None:
        r_out, refs = refs[0], refs[1:]
    turned, table, rounded, hidden_t, bias, head_t, head_b, sem, refs = *refs[:8], refs[8:]
    channels = turned.shape[0]
    depth = extent[0]
    classes = semantic.shape[2]
    slots = table.shape[1]
    rows = rounded.shape[1]
    step = pl.program_id(0)

    if count is not None:
        y_in, v_in, total, load_sem = refs

    def in_copies(p):
        return (
            pltpu.make_async_copy(y_hbm.at[p], y_in.at[p], load_sem.at[2 * p]),
            pltpu.make_async_copy(v_hbm.at[p + 1], v_in.at[p], load_sem.at[2 * p + 1]),
        )

    def out_copy(p):
        return pltpu.make_async_copy(rounded.at[p], r_out.at[p], sem.at[p])

    @pl.when(step == 0)
    def _():
        if count is None:
            copy = started(r_hbm.at[pl.ds(first, depth)], rounded, sem.at[0])
        else:
            light = started(total_hbm, total, load_sem.at[2 * depth])
            for p in range(depth):
                for copy in in_copies(p):
                    copy.start()
        same = identity(channels, channels)
        hidden_t[...] = nt(same, hidden[layer]).astype(BF)
        bias[...] = column(hidden_b[layer : layer + 1, :], channels)
        head_t[...] = head_rows(semantic[layer], density[layer : layer + 1, :], PROWS)
        last = jnp.sum(
            jnp.where(iota((1, density_b.shape[1]), 1) == layer, density_b[...], 0.0),
            axis=1,
            keepdims=True,
        )
        place = iota((PROWS, 1), 0) == classes
        head_b[...] = jnp.where(place, last, column(semantic_b[layer : layer + 1, :], PROWS))
        if count is None:
            copy.wait()
        else:
            light.wait()
            mean, inverse = moments(total[...], count)
            gains, shifts = row_of(gain, layer), row_of(shift, layer)

        @pl.loop(0, depth)
        def _(p):
            if count is not None:
                for copy in in_copies(p):
                    copy.wait()
                fresh = v_in[p] + silu((y_in[p] - mean) * inverse * gains + shifts)
                rounded[p] = fresh.astype(BF)
                out_copy(p).start()
            turned[:, pl.ds(pl.multiple_of(p * rows, rows), rows)] = nt(same, rounded[p]).astype(BF)

    fill_weights(table, coord_rows(coords[0], slots), extent)
    feature = nn(turned[...], table[...]).astype(BF)
    f_ref[0] = feature
    inner = nn(hidden_t[...], feature) + bias[...]
    small = jnp.exp(-jnp.abs(inner))
    act = (jnp.maximum(inner, 0.0) + jnp.log1p(small)).astype(BF)
    g_ref[0] = act
    s_ref[0] = jnp.where(inner >= 0.0, 1.0, small) / (1.0 + small)
    p_ref[0] = nn(head_t[...], act) + head_b[...]
    if count is not None:

        @pl.when(step == pl.num_programs(0) - 1)
        def _():
            for p in range(depth):
                out_copy(p).wait()


def per_tile(rows, lanes):
    return pl.BlockSpec((1, rows, lanes), lambda t: (t, 0, 0))


def sample(extent, received, source, layer, mlp, count=None, follow=()):
    tiles, lines, wide = received.shape
    slots = CAP
    rows, channels = extent[1] * extent[2], mlp[0].shape[1]
    depth = extent[0]
    voxels = depth * rows
    outs = [((tiles, PROWS, slots), F32)] + [((tiles, channels, slots), d) for d in (BF, BF, F32)]
    out_specs = [per_tile(n, slots) for n in (PROWS, channels, channels, channels)]
    scratch = [
        VMEM((channels, voxels), BF),
        VMEM((voxels, slots), BF),
        VMEM((depth, rows, channels), BF),
        VMEM((channels, channels), BF),
        VMEM((channels, 1), F32),
        VMEM((PROWS, channels), BF),
        VMEM((PROWS, 1), F32),
    ] + sems(depth)
    if count is None:
        first, given, specs = source[1], source[:1], [aspec()]
    else:
        first, given = 0, source
        specs = [aspec()] * 3 + [whole(x.shape) for x in source[3:]]
        outs.append(((depth, rows, channels), BF))
        out_specs.append(aspec())
        scratch += [VMEM((depth, rows, channels), F32)] * 2 + [VMEM(source[2].shape, F32)]
        scratch += sems(2 * depth + 1)
    return ordered(
        functools.partial(sample_kernel, extent, layer, first, count),
        (received,) + tuple(given) + mlp,
        [per_tile(lines, wide)] + specs + [whole(x.shape) for x in mlp],
        follow,
        grid=(tiles,),
        out_shape=any_outs(*outs),
        out_specs=tuple(out_specs),
        scratch_shapes=scratch,
        compiler_params=params(60),
        cost_estimate=cost(2 * voxels * channels * tiles * slots, 8e6),
        name="sample",
    )


def sample_back_kernel(
    extent, layer, coords, dp_ref, f_ref, g_ref, s_ref, hidden, semantic, density, *refs
):
    du_ref, pack_ref, total, table, head = refs[-5:]
    step = pl.program_id(0)
    channels = hidden.shape[1]
    slots = table.shape[1]

    @pl.when(step == 0)
    def _():
        total[...] = jnp.zeros_like(total)
        pack_ref[0:PACK, :] = jnp.zeros((PACK, channels), F32)
        if len(refs) > 5:
            pack_ref[PACK : 2 * PACK, :] = refs[0][...]
        rows = head_rows(semantic[layer], density[layer : layer + 1, :], DROWS)
        head[...] = nt(identity(channels, channels), rows).astype(BF)

    fill_weights(table, coord_rows(coords[0], slots), extent)
    grad_heads = dp_ref[0]
    grad_inner = (nn(head[...], grad_heads) * s_ref[0]).astype(BF)
    ones = jnp.ones((16, slots), BF)
    pack_ref[0:channels, :] += nt(f_ref[0], grad_inner)
    pack_ref[channels : channels + 16, :] += nt(ones, grad_inner)
    at = channels + 16
    pack_ref[at : at + DROWS, :] += nt(grad_heads, g_ref[0])
    at += DROWS
    pack_ref[at : at + 16, 0:DROWS] += nt(ones, grad_heads)
    grad_features = nn(hidden[layer], grad_inner).astype(BF)
    total[...] += nt(table[...], grad_features)

    @pl.when(step == pl.num_programs(0) - 1)
    def _():
        du_ref[...] = total[...].astype(BF)


def sample_back(extent, layer, received, grad_heads, feature, act, slope, mlp, packs, follow=()):
    tiles, lines, wide = received.shape
    _, channels, slots = feature.shape
    voxels = extent[0] * extent[1] * extent[2]
    hidden, _, semantic, density = mlp[:4]
    outs = ((voxels, channels), (PACK * (1 + len(packs)), channels))
    return ordered(
        functools.partial(sample_back_kernel, extent, layer),
        (received, grad_heads, feature, act, slope, hidden, semantic, density) + packs,
        [per_tile(lines, wide)]
        + [per_tile(n, slots) for n in (DROWS, channels, channels, channels)]
        + [whole(x.shape) for x in (hidden, semantic, density) + packs],
        follow,
        grid=(tiles,),
        out_shape=any_outs((outs[0], BF), (outs[1], F32)),
        out_specs=tuple(whole(shape) for shape in outs),
        scratch_shapes=[
            VMEM((voxels, channels), F32),
            VMEM((voxels, slots), BF),
            VMEM((channels, DROWS), BF),
        ],
        compiler_params=params(60),
        cost_estimate=cost(2 * voxels * channels * tiles * slots, 10e6),
        name="sample_back",
    )


def composite_kernel(
    classes, layer, starts, pixels, owner_ref, rank_ref, view, heads, cot,
    pic_ref, dp_ref, split, by_ray, grads, density, weights, grad_w, acc,
):
    tiles = heads.shape[0]
    rays, samples = owner_ref.shape
    step = 4.0 / samples
    split[...] = jnp.zeros_like(split)
    for t in range(tiles):
        value = heads[t]
        high = value.astype(BF)
        split[t, 0:PROWS, 0:CAP] = high.astype(F32)
        split[t, PROWS : 2 * PROWS, 0:CAP] = value - high.astype(F32)

    def hots(k):
        return window_onehots(
            starts, owner_ref[k : k + 1, :], rank_ref[k : k + 1, :], k, rays, tiles
        )

    for k in range(rays):
        hot, bases = hots(k)
        windows = jnp.concatenate(
            [split[t, :, pl.ds(bases[t], WINDOW)].astype(BF) for t in range(tiles)], axis=1
        )
        both = nn(windows, hot)
        one = both[:PROWS] + both[PROWS:]
        by_ray[k] = one
        density[k : k + 1, :] = one[classes : classes + 1]

    pre = density[...]
    visible = view[...].astype(F32)
    small = jnp.exp(-jnp.abs(pre))
    optical = visible * (jnp.maximum(pre, 0.0) + jnp.log1p(small)) * step
    passing = jnp.exp(-(lane_cumsum(optical) - optical))
    fading = jnp.exp(-optical)
    weight = passing * (1.0 - fading)
    weights[...] = weight
    row = iota((PROWS, samples), 0)
    lane = iota((PROWS, rays), 1)
    cotangent = nt(identity(PROWS, classes + 1), cot[layer])
    picture = jnp.zeros((PROWS, rays), F32)
    for k in range(rays):
        there = lane == pixels[k]
        dpic = jnp.sum(jnp.where(there, cotangent, 0.0), axis=1, keepdims=True)
        value = jnp.where(row < classes, by_ray[k], jnp.where(row == classes, 1.0, 0.0))
        one = weights[k : k + 1, :]
        colour = jnp.sum(value * one, axis=1, keepdims=True)
        picture = jnp.where(there, colour, picture)
        grad_w[k : k + 1, :] = jnp.sum(value * dpic, axis=0, keepdims=True)
        grads[k] = dpic * one
    pic_ref[...] = picture
    grad_weight = grad_w[...]
    carried = grad_weight * weight
    later = jnp.sum(carried, axis=1, keepdims=True) - lane_cumsum(carried)
    grad_optical = grad_weight * passing * fading - later
    slope = jnp.where(pre >= 0.0, 1.0, small) / (1.0 + small)
    density[...] = grad_optical * visible * step * slope
    acc[...] = jnp.zeros_like(acc)
    zero = jnp.zeros((DROWS - PROWS, samples), F32)
    for k in range(rays):
        hot, bases = hots(k)
        grad = jnp.where(row == classes, density[k : k + 1, :], grads[k])
        moved = nt(jnp.concatenate([grad, zero], axis=0).astype(BF), hot)
        for t in range(tiles):
            acc[t, :, pl.ds(bases[t], WINDOW)] += moved[:, t * WINDOW : (t + 1) * WINDOW]
    for t in range(tiles):
        dp_ref[t] = acc[t, :, 0:CAP].astype(BF)


def composite(starts, pixels, owner, rank, view, heads, cot, layer, classes, follow=()):
    tiles, _, slots = heads.shape
    rays, samples = owner.shape
    outs = ((PROWS, rays), (tiles, DROWS, slots))
    return ordered(
        functools.partial(composite_kernel, classes, layer),
        (starts, pixels, owner, rank, view, heads, cot,),
        [sspec(), sspec()] + [whole(x.shape) for x in (owner, rank, view, heads, cot)],
        follow,
        grid=(1,),
        out_shape=(jax.ShapeDtypeStruct(outs[0], F32), jax.ShapeDtypeStruct(outs[1], BF)),
        out_specs=tuple(whole(s) for s in outs),
        scratch_shapes=[
            VMEM((tiles, 2 * PROWS, CAP + WINDOW), F32),
            VMEM((rays, PROWS, samples), F32),
            VMEM((rays, PROWS, samples), F32),
            VMEM((rays, samples), F32),
            VMEM((rays, samples), F32),
            VMEM((rays, samples), F32),
            VMEM((tiles, DROWS, CAP + WINDOW), F32),
        ],
        compiler_params=params(60),
        cost_estimate=cost(1e9, 1e6),
        name="composite",
    )


def add_kernel(parts, out_ref):
    total = parts[0].astype(F32)
    for n in range(1, parts.shape[0]):
        total = total + parts[n].astype(F32)
    total = total.astype(out_ref.dtype)
    for n in range(out_ref.shape[0]):
        out_ref[n] = total


def add_parts(parts, copies, follow=()):
    shape = (copies,) + parts.shape[1:]
    return ordered(
        add_kernel,
        (parts,),
        [whole(parts.shape)],
        follow,
        grid=(1,),
        out_shape=jax.ShapeDtypeStruct(shape, parts.dtype),
        out_specs=whole(shape),
        compiler_params=params(60),
        cost_estimate=cost(1e6, 2e6),
        name="add_parts",
    )


def hold_kernel(*refs):
    del refs


def hold(values, follow):
    return ordered(
        hold_kernel,
        values,
        [aspec()] * len(values),
        follow,
        out_shape=any_outs(*((x.shape, x.dtype) for x in values)),
        out_specs=(aspec(),) * len(values),
        input_output_aliases={n: n for n in range(len(values))},
        compiler_params=params(60),
        name="hold",
    )


def halve_kernel(value, left_ref, right_ref):
    half = left_ref.shape[-1]
    for t in range(value.shape[0]):
        left_ref[t] = value[t, :, :half]
        right_ref[t] = value[t, :, half:]


def halve(value, follow):
    shape = value.shape[:-1] + (value.shape[-1] // 2,)
    return ordered(
        halve_kernel,
        (value,),
        [whole(value.shape)],
        follow,
        grid=(1,),
        out_shape=(jax.ShapeDtypeStruct(shape, value.dtype),) * 2,
        out_specs=(whole(shape),) * 2,
        compiler_params=params(60),
        cost_estimate=cost(1e6, 1e6),
        name="halve",
    )


def all_to_all(value, axis):
    return lax.all_to_all(value, axis, split_axis=0, concat_axis=0, tiled=True)


def exchange(first, last):
    devices = lax.axis_size("tile")
    up = [(i, i + 1) for i in range(devices - 1)]
    down = [(i + 1, i) for i in range(devices - 1)]
    return lax.ppermute(last, "tile", up), lax.ppermute(first, "tile", down)


def ray_grid():
    chips = lax.axis_size("ray") // 2
    across = max(n for n in range(1, chips + 1) if chips % n == 0 and n * n <= chips)
    return chips // across, across


def from_ray(value, down, right, core):
    tall, wide = ray_grid()
    pairs = []
    for y in range(tall):
        for x in range(wide):
            for c in range(2):
                source = ((y + down) % tall * wide + (x + right) % wide) * 2 + (c + core) % 2
                pairs.append((source, (y * wide + x) * 2 + c))
    return lax.ppermute(value, "ray", pairs)


def stack_kernel(groups, *refs):
    count = sum(groups)
    outs = refs[count:]
    at = 0
    for out_ref, size in zip(outs, groups):
        for n in range(size):
            out_ref[n] = refs[at][...]
            at += 1


def stacks(groups, follow=()):
    flat = [x for group in groups for x in group]
    shapes = [(len(group),) + group[0].shape for group in groups]
    return ordered(
        functools.partial(stack_kernel, [len(group) for group in groups]),
        tuple(flat),
        [whole(x.shape) for x in flat],
        follow,
        grid=(1,),
        out_shape=any_outs(*((shape, flat[0].dtype) for shape in shapes)),
        out_specs=tuple(whole(shape) for shape in shapes),
        compiler_params=params(60),
        cost_estimate=cost(1e6, 1e6),
        name="stacks",
    )


def gather_ray(left, right, placed):
    tall, wide = ray_grid()
    a = [left] + [from_ray(left, 0, x, 0) for x in range(1, wide)]
    b = [right] + [from_ray(right, y, 0, 0) for y in range(1, tall)]
    a, b = stacks((a, b))
    a = [a] + [from_ray(a, y, 0, 0) for y in range(1, tall)]
    b = [b] + [from_ray(b, 0, x, 0) for x in range(1, wide)]
    (both,) = stacks((a + b,), follow=(placed,))
    both = both.reshape((2, tall * wide) + left.shape)
    return both, from_ray(both, 0, 0, 1)


def norm_grads(y, grad, mean, inverse, gains, shifts):
    centred = (y - mean) * inverse
    normal = centred * gains + shifts
    sigma = 1.0 / (1.0 + jnp.exp(-normal))
    return grad * sigma * (1.0 + normal * (1.0 - sigma)), centred


def finish_back(sums, edges, ups, spare, out_sem):
    rows = edges.shape[1] - 16
    value = sums[...]
    high = value.astype(BF).astype(F32)
    middle = (value - high).astype(BF).astype(F32)
    low = value - high - middle
    tail = jnp.concatenate([high[0:2], middle[0:2], low[0:2], jnp.zeros((10,) + high.shape[1:], F32)], axis=0)
    tail = tail.astype(BF)
    edges[0, rows:, :] = tail
    edges[1, rows:, :] = tail
    spare[...] = tail
    first_ref, last_ref, far_ref = ups
    copies = [
        started(edges.at[0], first_ref, out_sem.at[0]),
        started(edges.at[1], last_ref, out_sem.at[1]),
        started(spare, far_ref, out_sem.at[2]),
    ]
    for copy in copies:
        copy.wait()


def norm_back_kernel(
    layer, count, cot, local, y, total_hbm, gain_hbm, shift_hbm, first_ref, last_ref, far_ref,
    cot_in, local_in, y_in, total, gain, shift, edges, sums, spare, in_sem, out_sem,
):
    planes, rows, _ = cot.shape
    small = [
        started(total_hbm, total, in_sem.at[3 * planes]),
        started(gain_hbm, gain, in_sem.at[3 * planes + 1]),
        started(shift_hbm, shift, in_sem.at[3 * planes + 2]),
    ]

    def in_copies(p):
        return [
            pltpu.make_async_copy(source.at[p], target.at[p], in_sem.at[3 * p + n])
            for n, (source, target) in enumerate(((cot, cot_in), (local, local_in), (y, y_in)))
        ]

    for p in range(planes):
        for copy in in_copies(p):
            copy.start()
    sums[...] = jnp.zeros_like(sums)
    for copy in small:
        copy.wait()
    mean, inverse = moments(total[...], count)
    gains, shifts = row_of(gain, layer), row_of(shift, layer)

    @pl.loop(0, planes)
    def _(p):
        for copy in in_copies(p):
            copy.wait()
        grad = cot_in[p].astype(F32) + local_in[p].astype(F32)
        inner, centred = norm_grads(y_in[p], grad, mean, inverse, gains, shifts)
        add_stats(sums, inner, inner * centred)
        for side, edge in ((0, 0), (1, planes - 1)):

            @pl.when(p == edge)
            def _():
                edges[side, 0:rows, :] = inner.astype(BF)

    finish_back(sums, edges, (first_ref, last_ref, far_ref), spare, out_sem)


def back_shapes(rows, channels):
    return ((rows + 16, channels), BF), ((rows + 16, channels), BF), ((16, channels), BF)


def back_scratch(rows, channels):
    return [VMEM((2, rows + 16, channels), BF), VMEM((8, channels), F32), VMEM((16, channels), BF)]


def norm_back(cot, local, y, total, gain, shift, layer, count, follow=()):
    planes, rows, channels = local.shape
    return ordered(
        functools.partial(norm_back_kernel, layer, count),
        (cot, local, y, total, gain, shift),
        [aspec()] * 6,
        follow,
        out_shape=any_outs(*back_shapes(rows, channels)),
        out_specs=(aspec(),) * 3,
        scratch_shapes=[VMEM(x.shape, x.dtype) for x in (cot, local, y, total, gain, shift)]
        + back_scratch(rows, channels)
        + sems(3 * planes + 3, 3),
        compiler_params=params(60),
        cost_estimate=cost(1e7, 8e6),
        name="norm_back",
    )


def share_back(sent):
    first, last, far = sent
    tiles = lax.axis_size("tile")

    def move(value, by):
        return lax.ppermute(value, "tile", [(i, (i + by) % tiles) for i in range(tiles)])

    return (move(last, 1), move(first, tiles - 1)) + tuple(move(far, n) for n in range(2, tiles - 1))


def turn_kernel(width, block, r_ref, out_ref, turned):
    planes, rows, channels = r_ref.shape
    chosen = out_ref.shape[1]
    pick = iota((chosen, channels), 1) == iota((chosen, channels), 0) + block[0] * chosen
    pick = pick.astype(F32).astype(BF)
    place = iota((chosen, rows), 1)
    on_y, on_z = lax.div(place, width), lax.rem(place, width)
    height = rows // width
    for p in range(planes):
        turned[...] = nt(pick, r_ref[p])
        for b in range(3):
            for c in range(3):
                shift = (b - 1) * width + (c - 1)
                value = turned[...]
                if shift:
                    value = pltpu.roll(value, (-shift) % rows, 1)
                y, z = on_y + (b - 1), on_z + (c - 1)
                inside = (y >= 0) & (y < height) & (z >= 0) & (z < width)
                value = jnp.where(inside, value, 0.0).astype(BF)
                for a in range(3):
                    target = p - a
                    if 0 <= target < planes - 2:
                        out_ref[9 * a + 3 * b + c, :, target * rows : (target + 1) * rows] = value


def turn(block, rounded, width, blocks, follow=()):
    planes, rows, channels = rounded.shape
    chosen = channels // blocks
    shape = (27, chosen, (planes - 2) * rows)
    return ordered(
        functools.partial(turn_kernel, width),
        (block, rounded,),
        [sspec(), whole(rounded.shape)],
        follow,
        grid=(1,),
        out_shape=jax.ShapeDtypeStruct(shape, BF),
        out_specs=whole(shape),
        scratch_shapes=[VMEM((chosen, rows), F32)],
        compiler_params=params(60),
        cost_estimate=cost(1e8, 5e6),
        name="turn",
    )


def weight_grad_kernel(layer, count, first, parts, tiles, spots, taps_hbm, *refs):
    grads, refs = refs[:parts], refs[parts:]
    if first:
        y, refs = refs[0], refs[1:]
        y_before, y_after = y.at[pl.ds(0, 1)], y.at[pl.ds(y.shape[0] - 1, 1)]
    else:
        y, y_before, y_after, refs = refs[0], refs[1], refs[2], refs[3:]
    own_far, others, refs = refs[0], refs[1:tiles], refs[tiles:]
    total_hbm, gain_hbm, shift_hbm, refs = *refs[:3], refs[3:]
    dy_ref, wg_ref, back_ref, refs = *refs[:3], refs[3:]
    grads_in, refs = refs[:parts], refs[parts:]
    (taps_in, y_in, y_halo, dn_halo, rest, back, total, gain, shift, dy_buf, dy_rows, wg_buf, in_sem,
     out_sem) = refs
    planes, rows, channels = grads[0].shape
    spare = (parts + 1) * planes
    lists = [
        (total_hbm.at[:, pl.ds(0, 8), :], total),
        (gain_hbm, gain),
        (shift_hbm, shift),
        (y_before, y_halo.at[pl.ds(0, 1)]),
        (y_after, y_halo.at[pl.ds(1, 1)]),
        (others[0], dn_halo.at[0]),
        (others[1], dn_halo.at[1]),
        (own_far, rest.at[0]),
    ] + [(other, rest.at[n + 1]) for n, other in enumerate(others[2:])]
    small = [
        started(source, target, in_sem.at[spare + n]) for n, (source, target) in enumerate(lists)
    ]

    def in_copies(p):
        copies = [pltpu.make_async_copy(y.at[p + first], y_in.at[p], in_sem.at[(parts + 1) * p])]
        for n in range(parts):
            copies.append(
                pltpu.make_async_copy(
                    grads[n].at[p], grads_in[n].at[p], in_sem.at[(parts + 1) * p + 1 + n]
                )
            )
        return copies

    for p in range(planes):
        for copy in in_copies(p):
            copy.start()
    heavy = started(taps_hbm, taps_in, in_sem.at[spare + len(lists)])
    for copy in small:
        copy.wait()
    tile = spots[2]
    tails = [rest[0], dn_halo[0, rows:, :], dn_halo[1, rows:, :]]
    tails += [rest[n] for n in range(1, rest.shape[0])]
    for by, tail in zip([0, 1, tiles - 1] + list(range(2, tiles - 1)), tails):
        value = tail.astype(F32)
        value = value[0:2] + value[2:4] + value[4:6]
        back[lax.rem(tile + tiles - by, tiles), 0:2, :] = value
    mean, inverse = moments(total[...], count)
    gains, shifts = row_of(gain, layer), row_of(shift, layer)
    scale = inverse * gains
    both = back[0, 0:2, :]
    for t in range(1, tiles):
        both = both + back[t, 0:2, :]
    back[0, 0:2, :] = both
    sums = both / count

    def finish(inner, centred):
        return scale * (inner - sums[0:1, :] - centred * sums[1:2, :])

    for side, place in ((0, 0), (1, planes + 1)):
        centred = (y_halo[side].astype(F32) - mean) * inverse
        value = finish(dn_halo[side, 0:rows, :].astype(F32), centred)
        dy_buf[place] = jnp.where(spots[side] > 0, value, 0.0).astype(BF)

    @pl.loop(0, planes)
    def _(p):
        for copy in in_copies(p):
            copy.wait()
        grad = grads_in[0][p].astype(F32)
        for n in range(1, parts):
            grad = grad + grads_in[n][p].astype(F32)
        value = finish(*norm_grads(y_in[p], grad, mean, inverse, gains, shifts)).astype(BF)
        dy_buf[p + 1] = value
        dy_rows[pl.ds(pl.multiple_of(p * rows, rows), rows), :] = value

    done = [
        started(dy_buf, dy_ref, out_sem.at[0]),
        started(back.at[0, pl.ds(0, 2), :], back_ref, out_sem.at[2]),
    ]
    heavy.wait()
    wg_buf[...] = nn(taps_in[...], dy_rows[...]).astype(BF)
    done.append(started(wg_buf, wg_ref, out_sem.at[1]))
    for copy in done:
        copy.wait()


def weight_grad(
    spots, taps_t, grads, y, y_halo, far, others, total, gain, shift, layer, count
):
    planes, rows, channels = grads[0].shape
    wide = taps_t.shape[0]
    tiles = len(others) + 1
    ext = (planes + 2, rows, channels)
    own = (planes, rows, channels)
    operands = (taps_t,) + tuple(grads) + (y,) + tuple(y_halo) + (far,) + tuple(others)
    operands += (total, gain, shift)
    return ordered(
        functools.partial(weight_grad_kernel, layer, count, 0 if y_halo else 1, len(grads), tiles),
        (spots,) + operands,
        [sspec()] + [aspec()] * len(operands),
        (),
        out_shape=any_outs((ext, BF), ((wide, channels), BF), ((2, channels), F32)),
        out_specs=(aspec(),) * 3,
        scratch_shapes=[VMEM(x.shape, x.dtype) for x in grads]
        + [
            VMEM(taps_t.shape, BF),
            VMEM(own, F32),
            VMEM((2, rows, channels), BF if y_halo else F32),
            VMEM((2, rows + 16, channels), BF),
            VMEM((tiles - 2, 16, channels), BF),
            VMEM((tiles, 8, channels), F32),
            VMEM((tiles, 8, channels), F32),
            VMEM(gain.shape, F32),
            VMEM(gain.shape, F32),
            VMEM(ext, BF),
            VMEM((planes * rows, channels), BF),
            VMEM((wide, channels), BF),
        ]
        + sems((len(grads) + 1) * planes + 8 + tiles, 3),
        compiler_params=params(60),
        cost_estimate=cost(2 * wide * planes * rows * channels, 12e6),
        name="weight_grad",
    )


def conv_back_kernel(width, layer, count, parts, dy, w_hbm, *refs):
    more = count is not None
    grads, refs = refs[:parts], refs[parts:]
    if more:
        y, total_hbm, gain_hbm, shift_hbm, refs = *refs[:4], refs[4:]
    out_ref, refs = refs[0], refs[1:]
    if more:
        sent, refs = refs[:3], refs[3:]
    grads_in, refs = refs[:parts], refs[parts:]
    raw, xs, weight, out_buf, in_sem, w_sem, out_sem, refs = *refs[:7], refs[7:]
    ext_planes, rows, channels = dy.shape
    planes = ext_planes - 2
    pairs = planes // 2
    each = parts + 1
    body = started(dy, raw, in_sem.at[each * pairs])
    heavy = [
        started(
            w_hbm.at[layer, pl.ds((26 - o) * channels, channels), :],
            weight.at[:, pl.ds(o * channels, channels)],
            w_sem.at[o],
        )
        for o in range(27)
    ]
    small = []
    if more:
        y_in, total, gain, shift, edges, sums, spare, back_sem = refs
        small = [
            started(source, target, in_sem.at[each * pairs + 1 + n])
            for n, (source, target) in enumerate(
                ((total_hbm.at[:, pl.ds(0, 8), :], total), (gain_hbm, gain), (shift_hbm, shift))
            )
        ]
        sums[...] = jnp.zeros_like(sums)

    def in_copies(i):
        two = pl.ds(2 * i, 2)
        copies = [
            pltpu.make_async_copy(grads[n].at[two], grads_in[n].at[two], in_sem.at[each * i + n])
            for n in range(parts)
        ]
        if more:
            copies.append(
                pltpu.make_async_copy(
                    y.at[pl.ds(2 * i + 1, 2)], y_in.at[two], in_sem.at[each * i + parts]
                )
            )
        return copies

    def out_copy(i):
        two = pl.ds(2 * i, 2)
        return pltpu.make_async_copy(out_buf.at[two], out_ref.at[two], out_sem.at[i])

    for i in range(pairs):
        for copy in in_copies(i):
            copy.start()
    clear_edges(xs, width, rows)
    body.wait()

    @pl.loop(0, ext_planes)
    def _(p):
        put_plane(xs, p, raw[p].astype(F32), width)

    for copy in small + heavy:
        copy.wait()
    if more:
        mean, inverse = moments(total[...], count)
        gains, shifts = row_of(gain, layer - 1), row_of(shift, layer - 1)

    @pl.loop(0, pairs)
    def _(i):
        part = nt(tap_pair(xs, 2 * i, width, rows), weight[...])
        for copy in in_copies(i):
            copy.wait()
        for side in range(2):
            p = 2 * i + side
            value = part[side * rows : (side + 1) * rows]
            for n in range(parts):
                value = value + grads_in[n][p].astype(F32)
            out_buf[p] = value
            if more:
                inner, centred = norm_grads(y_in[p], value, mean, inverse, gains, shifts)
                add_stats(sums, inner, inner * centred)

                @pl.when(p == side * (planes - 1))
                def _():
                    edges[side, 0:rows, :] = inner.astype(BF)

        out_copy(i).start()

    if more:
        finish_back(sums, edges, sent, spare, back_sem)
    for i in range(pairs):
        out_copy(i).wait()


def conv_back(dy, grads, weights, layer, width, norm=None, follow=()):
    ext_planes, rows, channels = dy.shape
    own = (ext_planes - 2, rows, channels)
    pairs = own[0] // 2
    outs, extra, scratch = [(own, F32)], (), []
    if norm is not None:
        y, total, gain, shift, count = norm
        extra = (y, total, gain, shift)
        outs += list(back_shapes(rows, channels))
        scratch = [VMEM(own, F32), VMEM((total.shape[0], 8, channels), F32)]
        scratch += [VMEM(gain.shape, F32), VMEM(gain.shape, F32)]
        scratch += back_scratch(rows, channels) + sems(3)
    else:
        count = None
    return ordered(
        functools.partial(conv_back_kernel, width, layer, count, len(grads)),
        (dy, weights) + tuple(grads) + extra,
        [aspec()] * (2 + len(grads) + len(extra)),
        follow,
        out_shape=any_outs(*outs),
        out_specs=(aspec(),) * len(outs),
        scratch_shapes=[VMEM(x.shape, x.dtype) for x in grads]
        + [VMEM(dy.shape, BF)]
        + conv_scratch(ext_planes, rows, width, channels, True)
        + [VMEM(own, F32)]
        + sems(pairs * (len(grads) + 1) + 4, 27, pairs)
        + scratch,
        compiler_params=params(60),
        cost_estimate=cost(2 * 27 * channels * channels * rows * own[0], 10e6),
        name="conv_back",
    )


GROUP = 9


def place_kernel(part, out_ref):
    blocks, offsets, chosen, _ = part.shape
    for o in range(offsets):
        for b in range(blocks):
            out_ref[0, o, b * chosen : (b + 1) * chosen, :] = part[b, o].astype(F32)


def place(parts, layer, layers, follow=()):
    blocks, offsets, chosen, channels = parts.shape
    shape = (layers, offsets, blocks * chosen, channels)
    return ordered(
        place_kernel,
        (parts,),
        [pl.BlockSpec((blocks, GROUP, chosen, channels), lambda o: (0, o, 0, 0))],
        follow,
        grid=(offsets // GROUP,),
        out_shape=jax.ShapeDtypeStruct(shape, F32),
        out_specs=pl.BlockSpec((1, GROUP) + shape[2:], lambda o: (layer, o, 0, 0)),
        compiler_params=params(60),
        cost_estimate=cost(1e6, 11e6),
        name="place",
    )


def place_near_kernel(tall, wide, blocks, spot, own, other, kept, out_ref):
    _, _, offsets, chosen, half = own.shape
    y, x, core = spot[0], spot[1], spot[2]
    for source, cross in ((own, 0), (other, 1)):
        for side in range(2):
            for n in range(tall * wide):
                down, right = (n // wide, n % wide) if side == 0 else (n % tall, n // tall)
                ray = lax.rem(y + down, tall) * wide + lax.rem(x + right, wide)
                ray = ray * 2 + lax.rem(core + cross, 2)
                row = pl.multiple_of(lax.rem(ray, blocks) * chosen, chosen)
                for o in range(offsets):
                    out_ref[0, o, pl.ds(row, chosen), side * half : (side + 1) * half] = source[
                        side, n, o
                    ].astype(F32)


def place_near(spot, own, other, kept, layer, blocks):
    _, rays, offsets, chosen, half = own.shape
    tall, wide = ray_grid()
    spec = pl.BlockSpec((2, rays, GROUP, chosen, half), lambda o: (0, 0, o, 0, 0))
    return pl.pallas_call(
        functools.partial(place_near_kernel, tall, wide, blocks),
        grid=(offsets // GROUP,),
        out_shape=jax.ShapeDtypeStruct(kept.shape, F32),
        in_specs=[sspec(), spec, spec, aspec()],
        out_specs=pl.BlockSpec((1, GROUP) + kept.shape[2:], lambda o: (layer, o, 0, 0)),
        input_output_aliases={3: 0},
        compiler_params=params(60),
        cost_estimate=cost(1e6, 11e6),
        name="place_near",
    )(spot, own, other, kept)


def per_device(
    volume,
    sample_cells,
    sample_fracs,
    view_mask,
    pixel_of_ray,
    conv_weight,
    norm_gain,
    norm_shift,
    hidden_weight,
    hidden_bias,
    density_weight,
    density_bias,
    semantic_weight,
    semantic_bias,
    render_cotangent,
    volume_cotangent,
):
    extent = volume.shape[:3]
    depth, height, width, channels = volume.shape
    rows = height * width
    voxels = depth * rows
    tiles = lax.axis_size("tile")
    ray_devices = lax.axis_size("ray")
    count = float(voxels * tiles)
    rays, samples = sample_cells.shape
    classes = semantic_weight.shape[2]
    layers = conv_weight.shape[0]
    blocks = min(BLOCKS, ray_devices)
    chosen = channels // blocks
    tile, ray = lax.axis_index("tile"), lax.axis_index("ray")
    block = lax.rem(ray, blocks).astype(jnp.int32).reshape(1)
    tall, wide = ray_grid()
    spot = jnp.stack([ray // (2 * wide), ray // 2 % wide, ray % 2]).astype(jnp.int32)

    own = volume.reshape(depth, rows, channels)
    before, after = exchange(own[:2], own[-2:])
    flags = jnp.stack([tile > 0, tile < tiles - 1]).astype(jnp.int32)

    owner_of = lax.div(sample_cells, voxels)
    held = owner_of[None] == jnp.arange(tiles, dtype=jnp.int32)[:, None, None]
    earlier = jnp.arange(rays)[None, :] < jnp.arange(rays)[:, None]
    starts = jnp.sum(
        (held[:, None, :, :] & earlier[None, :, :, None]).astype(jnp.int32), axis=(2, 3)
    ).reshape(tiles * rays)
    pixels = pixel_of_ray[0]
    buffer, owner, rank = prepare(extent, starts, sample_cells, sample_fracs, tiles, channels)

    weights = conv_weight.reshape(layers, 27 * channels, channels)
    mlp = (
        hidden_weight,
        hidden_bias,
        semantic_weight,
        density_weight,
        semantic_bias,
        density_bias[None],
    )
    y_ext, v_ext, mixed = conv_first(before, own, after, buffer, weights, 0, width)
    total = received = all_to_all(mixed, "tile")
    taps_first = turn(block, v_ext, width, blocks)
    v_next, r_ext, y_next, stat, y_first, y_last = conv_next(
        flags, y_ext, v_ext, total, norm_gain, norm_shift, weights, 0, width, count,
        follow=(taps_first,),
    )
    total_next = all_to_all(stat, "tile")
    heads, feature, act, slope = sample(extent, received, (r_ext, 1), 0, mlp)
    heads_last, feature_last, act_last, slope_last, r_last = sample(
        extent, received, (y_next, v_next, total_next, norm_gain, norm_shift), 1, mlp, count,
        follow=(heads,),
    )

    def draw(heads, layer, follow):
        return composite(
            starts, pixels, owner, rank, view_mask, all_to_all(heads, "tile"), render_cotangent,
            layer, classes, follow=follow,
        )

    picture, grad_heads = draw(heads, 0, (heads_last,))
    picture_last, grad_heads_last = draw(heads_last, 1, (grad_heads,))
    shares = (ray_devices, voxels // ray_devices, channels)
    planes = (depth, rows, channels)
    local, pack = sample_back(
        extent, 0, received, all_to_all(grad_heads, "tile"), feature, act, slope, mlp, (),
        follow=(grad_heads_last,),
    )
    parts = all_to_all(local.reshape(shares), "ray")
    local_last, packed = sample_back(
        extent, 1, received, all_to_all(grad_heads_last, "tile"), feature_last, act_last,
        slope_last, mlp, (pack,), follow=(local,),
    )
    parts_last = all_to_all(local_last.reshape(shares), "ray")
    copies = add_parts(parts, ray_devices, follow=(local_last,))
    (packed,) = hold((packed,), (copies,))
    packed = all_to_all(packed.reshape(ray_devices, -1, channels), "ray")
    copies_last = add_parts(parts_last, ray_devices, follow=(copies, local_last))
    sums_last = all_to_all(copies_last, "ray").reshape(planes)
    y_edges = exchange(*hold((y_first, y_last), (copies_last,)))
    packed = add_parts(packed, tiles, follow=(copies_last,))
    taps_next = turn(block, r_ext, width, blocks, follow=(packed,))

    cot = volume_cotangent.reshape(planes)
    wide_taps = (27 * chosen, voxels)
    spots = jnp.stack([tile > 0, tile < tiles - 1, tile]).astype(jnp.int32)
    sent = norm_back(
        cot, sums_last, y_next, total_next, norm_gain, norm_shift, 1, count,
        follow=(taps_next,) + y_edges,
    )
    (copies,) = hold((copies,), (sent[2],))
    sums = all_to_all(copies, "ray").reshape(planes)
    dy, part, back_last = weight_grad(
        spots, taps_next.reshape(wide_taps), (cot, sums_last), y_next, y_edges, sent[2],
        share_back(sent), total_next, norm_gain, norm_shift, 1, count,
    )
    shard = lax.psum_scatter(part, "tile", scatter_dimension=0, tiled=True)
    grad, *sent = conv_back(
        dy, (cot, sums_last, sums), weights, 1, width,
        (y_ext, total, norm_gain, norm_shift, count),
    )
    (shard,) = hold((shard,), (sent[2],))
    gathered = lax.all_gather(shard, ("ray", "tile"), axis=0, tiled=True)

    dy, part, back = weight_grad(
        spots, taps_first.reshape(wide_taps), (grad,), y_ext, (), sent[2], share_back(sent), total,
        norm_gain, norm_shift, 0, count,
    )
    parts = all_to_all(part.reshape(tiles, 27 * chosen // tiles, channels), "tile")
    packed = add_parts(all_to_all(packed, "tile"), ray_devices, follow=(part,))
    copies = add_parts(parts, tiles, follow=(packed,))
    slices = all_to_all(copies, "tile")
    (grad,) = conv_back(dy, (grad,), weights, 0, width, follow=(copies,))
    packed = all_to_all(packed, "ray").reshape(layers, PACK, channels)[::-1]
    left, right = halve(slices, (grad,))
    half = (27, chosen, channels // 2)
    gathered = gathered[: blocks * 27 * chosen].reshape(blocks, 27, chosen, channels)
    conv_grad = place(gathered, 1, layers, follow=(left,))
    near, far = gather_ray(left.reshape(half), right.reshape(half), conv_grad)
    conv_grad = place_near(spot, near, far, conv_grad, 0, blocks)

    at = channels + 16
    heads = packed[:, at : at + DROWS]
    head_bias = packed[:, at + DROWS, :DROWS]
    return (
        jnp.swapaxes(jnp.stack([picture, picture_last])[:, : classes + 1], 1, 2),
        r_last.reshape(volume.shape),
        grad.reshape(volume.shape),
        conv_grad,
        jnp.stack([back, back_last])[:, 1],
        jnp.stack([back, back_last])[:, 0],
        packed[:, :channels],
        packed[:, channels],
        heads[:, classes],
        head_bias[:, classes],
        jnp.swapaxes(heads[:, :classes], 1, 2),
        head_bias[:, :classes],
    )


def solution(mesh):
    in_specs = (
        P("tile", None, None, None),
        P(("ray", "tile"), None),
        P(None, ("ray", "tile"), None),
        P(("ray", "tile"), None),
        P(("ray", "tile"), None),
        P(),
        P(),
        P(),
        P(),
        P(),
        P(),
        P(),
        P(),
        P(),
        P(None, ("ray", "tile"), None),
        P("tile", None, None, None),
    )
    out_specs = (
        P(None, ("ray", "tile"), None),
        P("tile", None, None, None),
        P("tile", None, None, None),
        P(),
        P(),
        P(),
        P(),
        P(),
        P(),
        P(),
        P(),
        P(),
    )
    return jax.shard_map(
        per_device, mesh=mesh, in_specs=in_specs, out_specs=out_specs, check_vma=False
    )
```

```python
import functools

import jax
import jax.numpy as jnp
from jax import lax
from jax.experimental import pallas as pl
from jax.experimental.pallas import tpu as pltpu
from jax.sharding import PartitionSpec as P

CAP = 768
WINDOW = 256
LANES = 128
PROWS = 24
DROWS = 32
COORDS = 8
BLOCKS = 8
PACK = 320
epsilon = 1e-05
MIB = 1024 * 1024

BF = jnp.bfloat16
F32 = jnp.float32
VMEM = pltpu.VMEM
SMEM = pltpu.SMEM


def nn(left, right):
    return jnp.dot(left, right, preferred_element_type=F32)


def nt(left, right):
    return lax.dot_general(left, right, (((1,), (1,)), ((), ())), preferred_element_type=F32)


def iota(shape, dim):
    return lax.broadcasted_iota(jnp.int32, shape, dim)


def whole(shape):
    return pl.BlockSpec(shape, lambda *_: (0,) * len(shape))


def planes_of(step, shape, first=0):
    return pl.BlockSpec((step,) + shape[1:], lambda i: (i + first // step,) + (0,) * (len(shape) - 1))


def sspec():
    return pl.BlockSpec(memory_space=SMEM)


def aspec():
    return pl.BlockSpec(memory_space=pl.ANY)


def hspec():
    return pl.BlockSpec(memory_space=pltpu.HBM)


def ordered(kernel, operands, in_specs, follow, **options):
    count, skip = len(operands), len(follow)

    def body(*refs):
        kernel(*refs[:count], *refs[count + skip :])

    return pl.pallas_call(body, in_specs=list(in_specs) + [aspec()] * skip, **options)(
        *operands, *follow
    )


def params(mib):
    return pltpu.CompilerParams(vmem_limit_bytes=int(mib * MIB))


def cost():
    return pl.CostEstimate(flops=1, bytes_accessed=1, transcendentals=0)


def lane_cumsum(x):
    lane = iota(x.shape, 1)
    shift = 1
    while shift < x.shape[1]:
        x = x + jnp.where(lane >= shift, pltpu.roll(x, shift, 1), 0.0)
        shift *= 2
    return x


def window_onehots(starts, owner_row, rank_row, ray, rays, tiles):
    rows = iota((WINDOW, rank_row.shape[1]), 0)
    hots, bases = [], []
    for t in range(tiles):
        start = starts[t * rays + ray]
        base = (start // LANES) * LANES
        place = jnp.where(owner_row == t, rank_row + (start - base), -1)
        hots.append((rows == place).astype(F32).astype(BF))
        bases.append(pl.multiple_of(base, LANES))
    return jnp.concatenate(hots, axis=0), bases


def prep_kernel(extent, starts, cells_ref, fracs_ref, out_ref, owner_ref, rank_ref, vals, acc):
    depth, height, width = extent
    tiles = out_ref.shape[0]
    rays, samples = cells_ref.shape
    cells = cells_ref[...]
    voxels = depth * height * width
    owner = lax.div(cells, voxels)
    local = cells - owner * voxels
    base_x = lax.div(local, height * width)
    inner = local - base_x * (height * width)
    base_y = lax.div(inner, width)
    base_z = inner - base_y * width
    rank = jnp.zeros(cells.shape, F32)
    for t in range(tiles):
        mine = owner == t
        rank = jnp.where(mine, lane_cumsum(jnp.where(mine, 1.0, 0.0)) - 1.0, rank)
    owner_ref[...] = owner
    rank_ref[...] = rank.astype(jnp.int32)
    vals[...] = jnp.zeros_like(vals)
    rows = [(base_x + 1).astype(F32), base_y.astype(F32), base_z.astype(F32)]
    low = []
    for d in range(3):
        frac = fracs_ref[d]
        high = frac.astype(BF).astype(F32)
        rows.append(high)
        low.append(frac - high)
    rows += low
    for number, row in enumerate(rows):
        for k in range(rays):
            vals[number : number + 1, k * samples : (k + 1) * samples] = row[k : k + 1]
    acc[...] = jnp.zeros_like(acc)
    for k in range(rays):
        hot, bases = window_onehots(
            starts, owner_ref[k : k + 1, :], rank_ref[k : k + 1, :], k, rays, tiles
        )
        moved = nt(vals[:, k * samples : (k + 1) * samples].astype(BF), hot)
        for t in range(tiles):
            acc[t, :, pl.ds(bases[t], WINDOW)] += moved[:, t * WINDOW : (t + 1) * WINDOW]
    out_ref[...] = jnp.zeros_like(out_ref)
    wide = out_ref.shape[2]
    lines = CAP // wide
    for n in range(lines):
        part = slice(n * wide, (n + 1) * wide)
        for r in range(6):
            value = acc[:, r : r + 1, part]
            if r >= 3:
                value = value + acc[:, r + 3 : r + 4, part]
            out_ref[:, r * lines + n : r * lines + n + 1, :] = value


def prepare(extent, starts, cells, fracs, tiles, wide, follow=()):
    rays, samples = cells.shape
    outs = ((tiles, COORDS * CAP // wide, wide), (rays, samples), (rays, samples))
    return ordered(
        functools.partial(prep_kernel, extent),
        (starts, cells, fracs,),
        [sspec(), whole(cells.shape), whole(fracs.shape)],
        follow,
        grid=(1,),
        out_shape=(
            jax.ShapeDtypeStruct(outs[0], F32),
            jax.ShapeDtypeStruct(outs[1], jnp.int32),
            jax.ShapeDtypeStruct(outs[2], jnp.int32),
        ),
        out_specs=tuple(whole(s) for s in outs),
        scratch_shapes=[VMEM((16, rays * samples), F32), VMEM((tiles, 16, CAP + WINDOW), F32)],
        compiler_params=params(62.5),
        cost_estimate=cost(),
        name="prep",
    )


def started(source, target, sem):
    copy = pltpu.make_async_copy(source, target, sem)
    copy.start()
    return copy


def put_plane(xs, p, value, width):
    rows, channels = value.shape
    along = lax.rem(iota(value.shape, 0), width)
    left = jnp.where(along == 0, 0.0, pltpu.roll(value, 1, 0))
    right = jnp.where(along == width - 1, 0.0, pltpu.roll(value, rows - 1, 0))
    xs[p, width : width + rows, 0:channels] = left.astype(BF)
    xs[p, width : width + rows, channels : 2 * channels] = value.astype(BF)
    xs[p, width : width + rows, 2 * channels : 3 * channels] = right.astype(BF)


def clear_edges(xs, width, rows):
    planes, _, wide = xs.shape
    for p in range(planes):
        xs[p, 0:width, :] = jnp.zeros((width, wide), BF)
        xs[p, width + rows : 2 * width + rows, :] = jnp.zeros((width, wide), BF)


def taps(xs, p, width, rows):
    return jnp.concatenate(
        [xs[p + a, b * width : b * width + rows, :] for a in range(3) for b in range(3)], axis=1
    )


def tap_group(xs, first, count, width, rows):
    return jnp.concatenate([taps(xs, first + n, width, rows) for n in range(count)], axis=0)


def add_stats(sums, one, two):
    sums[0:1, :] += jnp.sum(one, axis=0, keepdims=True)
    sums[1:2, :] += jnp.sum(two, axis=0, keepdims=True)


def conv_scratch(planes, rows, width, channels, turned):
    shape = (channels, 27 * channels) if turned else (27 * channels, channels)
    return [VMEM((planes, rows + 2 * width, 3 * channels), BF), VMEM(shape, BF)]


def sems(*counts):
    return [pltpu.SemaphoreType.DMA((n,)) for n in counts]


def any_outs(*shapes):
    return tuple(jax.ShapeDtypeStruct(shape, dtype) for shape, dtype in shapes)


def conv_first_kernel(
    width, layer, before, own, after, coords, w_hbm, y_ref, v_ref, mix_ref,
    raw, xs, weight, y_buf, mix, in_sem, out_sem,
):
    planes, rows, channels = own.shape
    pairs = planes // 2 + 1
    body = [
        started(own.at[pl.ds(2 * i, 2)], raw.at[pl.ds(2 * i + 2, 2)], in_sem.at[i])
        for i in range(planes // 2)
    ]
    ends = [
        started(before, raw.at[pl.ds(0, 2)], in_sem.at[pairs]),
        started(after, raw.at[pl.ds(planes + 2, 2)], in_sem.at[pairs + 1]),
    ]
    heavy = started(w_hbm.at[layer], weight, in_sem.at[pairs + 2])
    light = started(coords, mix.at[:, pl.ds(8, coords.shape[1]), :], in_sem.at[pairs + 3])
    clear_edges(xs, width, rows)
    mix[:, 0:8, :] = jnp.zeros((mix.shape[0], 8, channels), F32)
    for copy in body + ends:
        copy.wait()

    @pl.loop(0, planes + 4)
    def _(p):
        put_plane(xs, p, raw[p].astype(F32), width)

    done = [started(raw.at[pl.ds(1, planes + 2)], v_ref, out_sem.at[pairs])]
    light.wait()
    heavy.wait()

    group = (planes + 2) // 2

    def out_copy(i):
        some = pl.ds(group * i, group)
        return pltpu.make_async_copy(y_buf.at[some], y_ref.at[some], out_sem.at[i])

    @pl.loop(0, 2)
    def _(i):
        p = group * i
        part = nn(tap_group(xs, p, group, width, rows), weight[...])
        for n in range(group):
            y_buf[p + n] = part[n * rows : (n + 1) * rows]
        out_copy(i).start()
        inner = part[rows : (group - 1) * rows]
        add_stats(mix.at[0], inner, inner * inner)
        edge = jnp.where(i == 0, part[(group - 1) * rows :], part[:rows])
        add_stats(mix.at[0], edge, edge * edge)

    for t in range(1, mix.shape[0]):
        mix[t, 0:8, :] = mix[0, 0:8, :]
    done.append(started(mix, mix_ref, out_sem.at[pairs + 1]))
    for copy in done:
        copy.wait()
    for i in range(2):
        out_copy(i).wait()


def conv_first(before, own, after, coords, weights, layer, width):
    planes, rows, channels = own.shape
    ext = (planes + 2, rows, channels)
    tiles, lines, _ = coords.shape
    pairs = planes // 2 + 1
    return ordered(
        functools.partial(conv_first_kernel, width, layer),
        (before, own, after, coords, weights),
        [aspec()] * 5,
        (),
        out_shape=any_outs((ext, F32), (ext, BF), ((tiles, 8 + lines, channels), F32)),
        out_specs=(aspec(),) * 3,
        scratch_shapes=[VMEM((planes + 4, rows, channels), BF)]
        + conv_scratch(planes + 4, rows, width, channels, False)
        + [VMEM(ext, F32), VMEM((tiles, 8 + lines, channels), F32)]
        + sems(pairs + 4, pairs + 2),
        compiler_params=params(62.5),
        cost_estimate=cost(),
        name="conv_first",
    )


def moments(total, count):
    both = jnp.sum(total, axis=0)
    mean = both[0:1, :] / count
    return mean, lax.rsqrt(both[1:2, :] / count - mean * mean + epsilon)


def row_of(ref, layer):
    return ref[layer : layer + 1, :]


def silu(value):
    return value * (1.0 / (1.0 + jnp.exp(-value)))


def conv_next_kernel(
    width, layer, count, flags, y_ext, v_ext, total_hbm, gain_hbm, shift_hbm, w_hbm,
    v_ref, r_ref, y_ref, stat_ref, first_ref, last_ref,
    y_in, v_in, total, gain, shift, xs, weight, v_buf, r_buf, y_buf, edges, stat, in_sem, out_sem,
):
    ext_planes, rows, channels = y_ext.shape
    pairs = ext_planes // 2
    small = [
        started(total_hbm.at[:, pl.ds(0, 8), :], total, in_sem.at[2 * pairs]),
        started(gain_hbm, gain, in_sem.at[2 * pairs + 1]),
        started(shift_hbm, shift, in_sem.at[2 * pairs + 2]),
    ]
    def in_copies(i):
        two = pl.ds(2 * i, 2)
        return (
            pltpu.make_async_copy(y_ext.at[two], y_in.at[two], in_sem.at[2 * i]),
            pltpu.make_async_copy(v_ext.at[two], v_in.at[two], in_sem.at[2 * i + 1]),
        )

    def mid_copies(i):
        two = pl.ds(2 * i, 2)
        return (
            pltpu.make_async_copy(v_buf.at[two], v_ref.at[two], out_sem.at[3 * i]),
            pltpu.make_async_copy(r_buf.at[two], r_ref.at[two], out_sem.at[3 * i + 1]),
        )

    def out_copy(i):
        two = pl.ds(2 * i - 2, 2)
        return pltpu.make_async_copy(y_buf.at[two], y_ref.at[two], out_sem.at[3 * i + 2])

    for i in range(pairs):
        for copy in in_copies(i):
            copy.start()
    heavy = started(w_hbm.at[layer + 1], weight, in_sem.at[2 * pairs + 3])
    clear_edges(xs, width, rows)
    stat[...] = jnp.zeros_like(stat)
    for copy in small:
        copy.wait()
    mean, inverse = moments(total[...], count)
    gains, shifts = row_of(gain, layer), row_of(shift, layer)

    @pl.loop(0, pairs)
    def _(i):
        for copy in in_copies(i):
            copy.wait()
        for side in range(2):
            p = 2 * i + side
            fresh = v_in[p].astype(F32) + silu((y_in[p] - mean) * inverse * gains + shifts)
            v_buf[p] = fresh
            outside = (p == side * (ext_planes - 1)) & (flags[side] == 0)
            rounded = jnp.where(outside, 0.0, fresh).astype(BF)
            r_buf[p] = rounded
            put_plane(xs, p, rounded.astype(F32), width)
        for copy in mid_copies(i):
            copy.start()

        @pl.when(i == 1)
        def _():
            heavy.wait()

        @pl.when(i > 0)
        def _():
            p = 2 * i - 2
            part = nn(tap_group(xs, p, 2, width, rows), weight[...])
            y_buf[p] = part[:rows]
            y_buf[p + 1] = part[rows:]
            add_stats(stat.at[0], part, part * part)
            out_copy(i).start()

    edges[0] = y_buf[0].astype(BF)
    edges[1] = y_buf[ext_planes - 3].astype(BF)
    for t in range(1, stat.shape[0]):
        stat[t] = stat[0]
    done = [
        started(stat, stat_ref, out_sem.at[2]),
        started(edges.at[pl.ds(0, 1)], first_ref, out_sem.at[3 * pairs]),
        started(edges.at[pl.ds(1, 1)], last_ref, out_sem.at[3 * pairs + 1]),
    ]
    for i in range(pairs):
        done += list(mid_copies(i)) + ([out_copy(i)] if i else [])
    for copy in done:
        copy.wait()


def conv_next(flags, y_ext, v_ext, total, gain, shift, weights, layer, width, count, follow=()):
    ext_planes, rows, channels = y_ext.shape
    ext = y_ext.shape
    inner = (ext_planes - 2, rows, channels)
    stat = (total.shape[0], 8, channels)
    pairs = ext_planes // 2
    edge = (1, rows, channels)
    return ordered(
        functools.partial(conv_next_kernel, width, layer, count),
        (flags, y_ext, v_ext, total, gain, shift, weights),
        [sspec()] + [aspec()] * 6,
        follow,
        out_shape=any_outs((ext, F32), (ext, BF), (inner, F32), (stat, F32), (edge, BF), (edge, BF)),
        out_specs=(aspec(),) * 6,
        scratch_shapes=[VMEM(ext, F32), VMEM(ext, BF), VMEM(stat, F32)]
        + [VMEM(gain.shape, F32)] * 2
        + conv_scratch(ext_planes, rows, width, channels, False)
        + [VMEM(ext, F32), VMEM(ext, BF), VMEM(inner, F32)]
        + [VMEM((2, rows, channels), BF), VMEM(stat, F32)]
        + sems(2 * pairs + 4, 3 * pairs + 2),
        compiler_params=params(62.5),
        cost_estimate=cost(),
        name="conv_next",
    )


def fill_weights(table, coords, extent):
    depth, height, width = extent
    samples = coords[0].shape[1]

    def along(base, frac, size):
        grid = iota((size, samples), 0).astype(F32)
        lower = jnp.where(grid == base, 1.0 - frac, 0.0)
        return lower + jnp.where(grid == base + 1.0, frac, 0.0)

    on_x = along(coords[0] - 1.0, coords[3], depth)
    on_y = along(coords[1], coords[4], height)
    on_z = along(coords[2], coords[5], width)
    for x in range(depth):
        on_xy = on_x[x : x + 1] * on_y
        for y in range(height):
            row = (x * height + y) * width
            table[row : row + width, :] = (on_xy[y : y + 1] * on_z).astype(BF)


def diagonal(rows, columns):
    return iota((rows, columns), 0) == iota((rows, columns), 1)


def identity(rows, columns):
    return diagonal(rows, columns).astype(F32).astype(BF)


def head_rows(semantic, density, rows):
    channels, classes = semantic.shape
    turned = nt(identity(rows, classes), semantic)
    return jnp.where(iota((rows, channels), 0) == classes, density.astype(F32), turned).astype(BF)


def column(row, rows):
    return jnp.sum(jnp.where(diagonal(rows, row.shape[1]), row, 0.0), axis=1, keepdims=True)


def coord_rows(block, slots):
    lines = slots // block.shape[1]
    return [
        jnp.concatenate(
            [block[8 + r * lines + n : 9 + r * lines + n, :] for n in range(lines)], axis=1
        )
        for r in range(6)
    ]


def sample_kernel(
    extent, layer, first, count, coords, *refs
):
    if count is None:
        r_hbm, refs = refs[0], refs[1:]
    else:
        y_hbm, v_hbm, total_hbm, gain, shift, refs = refs[0], refs[1], refs[2], refs[3], refs[4], refs[5:]
    hidden, hidden_b, semantic, density, semantic_b, density_b, refs = *refs[:6], refs[6:]
    p_ref, f_ref, g_ref, s_ref, refs = *refs[:4], refs[4:]
    if count is not None:
        r_out, refs = refs[0], refs[1:]
    turned, table, rounded, hidden_t, bias, head_t, head_b, sem, refs = *refs[:8], refs[8:]
    channels = turned.shape[0]
    depth = extent[0]
    classes = semantic.shape[2]
    slots = table.shape[1]
    rows = rounded.shape[1]
    step = pl.program_id(0)

    if count is not None:
        y_in, v_in, total, load_sem = refs

    def in_copies(p):
        return (
            pltpu.make_async_copy(y_hbm.at[p], y_in.at[p], load_sem.at[2 * p]),
            pltpu.make_async_copy(v_hbm.at[p + 1], v_in.at[p], load_sem.at[2 * p + 1]),
        )

    def out_copy(p):
        return pltpu.make_async_copy(rounded.at[p], r_out.at[p], sem.at[p])

    @pl.when(step == 0)
    def _():
        if count is None:
            copy = started(r_hbm.at[pl.ds(first, depth)], rounded, sem.at[0])
        else:
            light = started(total_hbm, total, load_sem.at[2 * depth])
            for p in range(depth):
                for copy in in_copies(p):
                    copy.start()
        same = identity(channels, channels)
        hidden_t[...] = nt(same, hidden[layer]).astype(BF)
        bias[...] = column(hidden_b[layer : layer + 1, :], channels)
        head_t[...] = head_rows(semantic[layer], density[layer : layer + 1, :], PROWS)
        last = jnp.sum(
            jnp.where(iota((1, density_b.shape[1]), 1) == layer, density_b[...], 0.0),
            axis=1,
            keepdims=True,
        )
        place = iota((PROWS, 1), 0) == classes
        head_b[...] = jnp.where(place, last, column(semantic_b[layer : layer + 1, :], PROWS))
        if count is None:
            copy.wait()
        else:
            light.wait()
            mean, inverse = moments(total[...], count)
            gains, shifts = row_of(gain, layer), row_of(shift, layer)

        @pl.loop(0, depth)
        def _(p):
            if count is not None:
                for copy in in_copies(p):
                    copy.wait()
                fresh = v_in[p] + silu((y_in[p] - mean) * inverse * gains + shifts)
                rounded[p] = fresh.astype(BF)
                out_copy(p).start()
            turned[:, pl.ds(pl.multiple_of(p * rows, rows), rows)] = nt(same, rounded[p]).astype(BF)

    fill_weights(table, coord_rows(coords[0], slots), extent)
    feature = nn(turned[...], table[...]).astype(BF)
    f_ref[0] = feature
    inner = nn(hidden_t[...], feature) + bias[...]
    small = jnp.exp(-jnp.abs(inner))
    act = (jnp.maximum(inner, 0.0) + jnp.log1p(small)).astype(BF)
    g_ref[0] = act
    s_ref[0] = jnp.where(inner >= 0.0, 1.0, small) / (1.0 + small)
    p_ref[0] = nn(head_t[...], act) + head_b[...]
    if count is not None:

        @pl.when(step == pl.num_programs(0) - 1)
        def _():
            for p in range(depth):
                out_copy(p).wait()


def per_tile(rows, lanes):
    return pl.BlockSpec((1, rows, lanes), lambda t: (t, 0, 0))


def sample(extent, received, source, layer, mlp, count=None, follow=()):
    tiles, lines, wide = received.shape
    slots = CAP
    rows, channels = extent[1] * extent[2], mlp[0].shape[1]
    depth = extent[0]
    voxels = depth * rows
    outs = [((tiles, PROWS, slots), F32)] + [((tiles, channels, slots), d) for d in (BF, BF, F32)]
    out_specs = [per_tile(n, slots) for n in (PROWS, channels, channels, channels)]
    scratch = [
        VMEM((channels, voxels), BF),
        VMEM((voxels, slots), BF),
        VMEM((depth, rows, channels), BF),
        VMEM((channels, channels), BF),
        VMEM((channels, 1), F32),
        VMEM((PROWS, channels), BF),
        VMEM((PROWS, 1), F32),
    ] + sems(depth)
    if count is None:
        first, given, specs = source[1], source[:1], [aspec()]
    else:
        first, given = 0, source
        specs = [aspec()] * 3 + [whole(x.shape) for x in source[3:]]
        outs.append(((depth, rows, channels), BF))
        out_specs.append(aspec())
        scratch += [VMEM((depth, rows, channels), F32)] * 2 + [VMEM(source[2].shape, F32)]
        scratch += sems(2 * depth + 1)
    return ordered(
        functools.partial(sample_kernel, extent, layer, first, count),
        (received,) + tuple(given) + mlp,
        [per_tile(lines, wide)] + specs + [whole(x.shape) for x in mlp],
        follow,
        grid=(tiles,),
        out_shape=any_outs(*outs),
        out_specs=tuple(out_specs),
        scratch_shapes=scratch,
        compiler_params=params(62.5),
        cost_estimate=cost(),
        name="sample",
    )


def sample_back_kernel(
    extent, layer, coords, dp_ref, f_ref, g_ref, s_ref, hidden, semantic, density, *refs
):
    du_ref, pack_ref, total, table, head = refs[-5:]
    step = pl.program_id(0)
    channels = hidden.shape[1]
    slots = table.shape[1]

    @pl.when(step == 0)
    def _():
        total[...] = jnp.zeros_like(total)
        pack_ref[0:PACK, :] = jnp.zeros((PACK, channels), F32)
        if len(refs) > 5:
            pack_ref[PACK : 2 * PACK, :] = refs[0][...]
        rows = head_rows(semantic[layer], density[layer : layer + 1, :], DROWS)
        head[...] = nt(identity(channels, channels), rows).astype(BF)

    fill_weights(table, coord_rows(coords[0], slots), extent)
    grad_heads = dp_ref[0]
    grad_inner = (nn(head[...], grad_heads) * s_ref[0]).astype(BF)
    ones = jnp.ones((16, slots), BF)
    pack_ref[0:channels, :] += nt(f_ref[0], grad_inner)
    pack_ref[channels : channels + 16, :] += nt(ones, grad_inner)
    at = channels + 16
    pack_ref[at : at + DROWS, :] += nt(grad_heads, g_ref[0])
    at += DROWS
    pack_ref[at : at + 16, 0:DROWS] += nt(ones, grad_heads)
    grad_features = nn(hidden[layer], grad_inner).astype(BF)
    total[...] += nt(table[...], grad_features)

    @pl.when(step == pl.num_programs(0) - 1)
    def _():
        du_ref[...] = total[...].astype(BF)


def sample_back(extent, layer, received, grad_heads, feature, act, slope, mlp, packs, follow=()):
    tiles, lines, wide = received.shape
    _, channels, slots = feature.shape
    voxels = extent[0] * extent[1] * extent[2]
    hidden, _, semantic, density = mlp[:4]
    outs = ((voxels, channels), (PACK * (1 + len(packs)), channels))
    return ordered(
        functools.partial(sample_back_kernel, extent, layer),
        (received, grad_heads, feature, act, slope, hidden, semantic, density) + packs,
        [per_tile(lines, wide)]
        + [per_tile(n, slots) for n in (DROWS, channels, channels, channels)]
        + [whole(x.shape) for x in (hidden, semantic, density) + packs],
        follow,
        grid=(tiles,),
        out_shape=any_outs((outs[0], BF), (outs[1], F32)),
        out_specs=tuple(whole(shape) for shape in outs),
        scratch_shapes=[
            VMEM((voxels, channels), F32),
            VMEM((voxels, slots), BF),
            VMEM((channels, DROWS), BF),
        ],
        compiler_params=params(62.5),
        cost_estimate=cost(),
        name="sample_back",
    )


def composite_kernel(
    classes, layer, starts, pixels, owner_ref, rank_ref, view, heads, cot,
    pic_ref, dp_ref, split, by_ray, grads, density, weights, grad_w, acc,
):
    tiles = heads.shape[0]
    rays, samples = owner_ref.shape
    step = 4.0 / samples
    split[...] = jnp.zeros_like(split)
    for t in range(tiles):
        value = heads[t]
        high = value.astype(BF)
        split[t, 0:PROWS, 0:CAP] = high.astype(F32)
        split[t, PROWS : 2 * PROWS, 0:CAP] = value - high.astype(F32)

    def hots(k):
        return window_onehots(
            starts, owner_ref[k : k + 1, :], rank_ref[k : k + 1, :], k, rays, tiles
        )

    for k in range(rays):
        hot, bases = hots(k)
        windows = jnp.concatenate(
            [split[t, :, pl.ds(bases[t], WINDOW)].astype(BF) for t in range(tiles)], axis=1
        )
        both = nn(windows, hot)
        one = both[:PROWS] + both[PROWS:]
        by_ray[k] = one
        density[k : k + 1, :] = one[classes : classes + 1]

    pre = density[...]
    visible = view[...].astype(F32)
    small = jnp.exp(-jnp.abs(pre))
    optical = visible * (jnp.maximum(pre, 0.0) + jnp.log1p(small)) * step
    passing = jnp.exp(-(lane_cumsum(optical) - optical))
    fading = jnp.exp(-optical)
    weight = passing * (1.0 - fading)
    weights[...] = weight
    row = iota((PROWS, samples), 0)
    lane = iota((PROWS, rays), 1)
    cotangent = nt(identity(PROWS, classes + 1), cot[layer])
    picture = jnp.zeros((PROWS, rays), F32)
    for k in range(rays):
        there = lane == pixels[k]
        dpic = jnp.sum(jnp.where(there, cotangent, 0.0), axis=1, keepdims=True)
        value = jnp.where(row < classes, by_ray[k], jnp.where(row == classes, 1.0, 0.0))
        one = weights[k : k + 1, :]
        colour = jnp.sum(value * one, axis=1, keepdims=True)
        picture = jnp.where(there, colour, picture)
        grad_w[k : k + 1, :] = jnp.sum(value * dpic, axis=0, keepdims=True)
        grads[k] = dpic * one
    pic_ref[...] = picture
    grad_weight = grad_w[...]
    carried = grad_weight * weight
    later = jnp.sum(carried, axis=1, keepdims=True) - lane_cumsum(carried)
    grad_optical = grad_weight * passing * fading - later
    slope = jnp.where(pre >= 0.0, 1.0, small) / (1.0 + small)
    density[...] = grad_optical * visible * step * slope
    acc[...] = jnp.zeros_like(acc)
    zero = jnp.zeros((DROWS - PROWS, samples), F32)
    for k in range(rays):
        hot, bases = hots(k)
        grad = jnp.where(row == classes, density[k : k + 1, :], grads[k])
        moved = nt(jnp.concatenate([grad, zero], axis=0).astype(BF), hot)
        for t in range(tiles):
            acc[t, :, pl.ds(bases[t], WINDOW)] += moved[:, t * WINDOW : (t + 1) * WINDOW]
    for t in range(tiles):
        dp_ref[t] = acc[t, :, 0:CAP].astype(BF)


def composite(starts, pixels, owner, rank, view, heads, cot, layer, classes, follow=()):
    tiles, _, slots = heads.shape
    rays, samples = owner.shape
    outs = ((PROWS, rays), (tiles, DROWS, slots))
    return ordered(
        functools.partial(composite_kernel, classes, layer),
        (starts, pixels, owner, rank, view, heads, cot,),
        [sspec(), sspec()] + [whole(x.shape) for x in (owner, rank, view, heads, cot)],
        follow,
        grid=(1,),
        out_shape=(jax.ShapeDtypeStruct(outs[0], F32), jax.ShapeDtypeStruct(outs[1], BF)),
        out_specs=tuple(whole(s) for s in outs),
        scratch_shapes=[
            VMEM((tiles, 2 * PROWS, CAP + WINDOW), F32),
            VMEM((rays, PROWS, samples), F32),
            VMEM((rays, PROWS, samples), F32),
            VMEM((rays, samples), F32),
            VMEM((rays, samples), F32),
            VMEM((rays, samples), F32),
            VMEM((tiles, DROWS, CAP + WINDOW), F32),
        ],
        compiler_params=params(62.5),
        cost_estimate=cost(),
        name="composite",
    )


def add_kernel(parts, out_ref):
    total = parts[0].astype(F32)
    for n in range(1, parts.shape[0]):
        total = total + parts[n].astype(F32)
    total = total.astype(out_ref.dtype)
    for n in range(out_ref.shape[0]):
        out_ref[n] = total


def add_parts(parts, copies, follow=()):
    shape = (copies,) + parts.shape[1:]
    return ordered(
        add_kernel,
        (parts,),
        [whole(parts.shape)],
        follow,
        grid=(1,),
        out_shape=jax.ShapeDtypeStruct(shape, parts.dtype),
        out_specs=whole(shape),
        compiler_params=params(62.5),
        cost_estimate=cost(),
        name="add_parts",
    )


def hold_kernel(*refs):
    del refs


def hold(values, follow):
    return ordered(
        hold_kernel,
        values,
        [aspec()] * len(values),
        follow,
        out_shape=any_outs(*((x.shape, x.dtype) for x in values)),
        out_specs=(aspec(),) * len(values),
        input_output_aliases={n: n for n in range(len(values))},
        compiler_params=params(62.5),
        cost_estimate=cost(),
        name="hold",
    )


def all_to_all(value, axis):
    return lax.all_to_all(value, axis, split_axis=0, concat_axis=0, tiled=True)


def exchange(first, last):
    devices = lax.axis_size("tile")
    up = [(i, i + 1) for i in range(devices - 1)]
    down = [(i + 1, i) for i in range(devices - 1)]
    return lax.ppermute(last, "tile", up), lax.ppermute(first, "tile", down)


def norm_grads(y, grad, mean, inverse, gains, shifts):
    centred = (y - mean) * inverse
    normal = centred * gains + shifts
    sigma = 1.0 / (1.0 + jnp.exp(-normal))
    return grad * sigma * (1.0 + normal * (1.0 - sigma)), centred


def finish_back(sums, edges, ups, spare, out_sem):
    rows = edges.shape[1] - 16
    value = sums[...]
    high = value.astype(BF).astype(F32)
    middle = (value - high).astype(BF).astype(F32)
    low = value - high - middle
    tail = jnp.concatenate([high[0:2], middle[0:2], low[0:2], jnp.zeros((10,) + high.shape[1:], F32)], axis=0)
    tail = tail.astype(BF)
    edges[0, rows:, :] = tail
    edges[1, rows:, :] = tail
    spare[...] = tail
    first_ref, last_ref, far_ref = ups
    copies = [
        started(edges.at[0], first_ref, out_sem.at[0]),
        started(edges.at[1], last_ref, out_sem.at[1]),
        started(spare, far_ref, out_sem.at[2]),
    ]
    for copy in copies:
        copy.wait()


def norm_back_kernel(
    layer, count, cot, local, y, total_hbm, gain_hbm, shift_hbm, first_ref, last_ref, far_ref,
    cot_in, local_in, y_in, total, gain, shift, edges, sums, spare, in_sem, out_sem,
):
    planes, rows, _ = cot.shape
    small = [
        started(total_hbm, total, in_sem.at[3 * planes]),
        started(gain_hbm, gain, in_sem.at[3 * planes + 1]),
        started(shift_hbm, shift, in_sem.at[3 * planes + 2]),
    ]

    def in_copies(p):
        return [
            pltpu.make_async_copy(source.at[p], target.at[p], in_sem.at[3 * p + n])
            for n, (source, target) in enumerate(((cot, cot_in), (local, local_in), (y, y_in)))
        ]

    for p in range(planes):
        for copy in in_copies(p):
            copy.start()
    sums[...] = jnp.zeros_like(sums)
    for copy in small:
        copy.wait()
    mean, inverse = moments(total[...], count)
    gains, shifts = row_of(gain, layer), row_of(shift, layer)

    @pl.loop(0, planes)
    def _(p):
        for copy in in_copies(p):
            copy.wait()
        grad = cot_in[p].astype(F32) + local_in[p].astype(F32)
        inner, centred = norm_grads(y_in[p], grad, mean, inverse, gains, shifts)
        add_stats(sums, inner, inner * centred)
        for side, edge in ((0, 0), (1, planes - 1)):

            @pl.when(p == edge)
            def _():
                edges[side, 0:rows, :] = inner.astype(BF)

    finish_back(sums, edges, (first_ref, last_ref, far_ref), spare, out_sem)


def back_shapes(rows, channels):
    return ((rows + 16, channels), BF), ((rows + 16, channels), BF), ((16, channels), BF)


def back_scratch(rows, channels):
    return [VMEM((2, rows + 16, channels), BF), VMEM((8, channels), F32), VMEM((16, channels), BF)]


def norm_back(cot, local, y, total, gain, shift, layer, count, follow=()):
    planes, rows, channels = local.shape
    return ordered(
        functools.partial(norm_back_kernel, layer, count),
        (cot, local, y, total, gain, shift),
        [aspec()] * 6,
        follow,
        out_shape=any_outs(*back_shapes(rows, channels)),
        out_specs=(aspec(),) * 3,
        scratch_shapes=[VMEM(x.shape, x.dtype) for x in (cot, local, y, total, gain, shift)]
        + back_scratch(rows, channels)
        + sems(3 * planes + 3, 3),
        compiler_params=params(62.5),
        cost_estimate=cost(),
        name="norm_back",
    )


def share_back(sent):
    first, last, far = sent
    tiles = lax.axis_size("tile")

    def move(value, by):
        return lax.ppermute(value, "tile", [(i, (i + by) % tiles) for i in range(tiles)])

    return (move(last, 1), move(first, tiles - 1)) + tuple(move(far, n) for n in range(2, tiles - 1))


def turn_kernel(width, block, r_ref, out_ref, turned):
    planes, rows, channels = r_ref.shape
    chosen = out_ref.shape[1]
    pick = iota((chosen, channels), 1) == iota((chosen, channels), 0) + block[0] * chosen
    pick = pick.astype(F32).astype(BF)
    place = iota((chosen, rows), 1)
    on_y, on_z = lax.div(place, width), lax.rem(place, width)
    height = rows // width
    for p in range(planes):
        turned[...] = nt(pick, r_ref[p])
        for b in range(3):
            for c in range(3):
                shift = (b - 1) * width + (c - 1)
                value = turned[...]
                if shift:
                    value = pltpu.roll(value, (-shift) % rows, 1)
                y, z = on_y + (b - 1), on_z + (c - 1)
                inside = (y >= 0) & (y < height) & (z >= 0) & (z < width)
                value = jnp.where(inside, value, 0.0).astype(BF)
                for a in range(3):
                    target = p - a
                    if 0 <= target < planes - 2:
                        out_ref[9 * a + 3 * b + c, :, target * rows : (target + 1) * rows] = value


def turn(block, rounded, width, blocks, follow=()):
    planes, rows, channels = rounded.shape
    chosen = channels // blocks
    shape = (27, chosen, (planes - 2) * rows)
    return ordered(
        functools.partial(turn_kernel, width),
        (block, rounded,),
        [sspec(), whole(rounded.shape)],
        follow,
        grid=(1,),
        out_shape=jax.ShapeDtypeStruct(shape, BF),
        out_specs=whole(shape),
        scratch_shapes=[VMEM((chosen, rows), F32)],
        compiler_params=params(62.5),
        cost_estimate=cost(),
        name="turn",
    )


def weight_grad_kernel(layer, count, first, parts, tiles, spots, taps_hbm, *refs):
    grads, refs = refs[:parts], refs[parts:]
    if first:
        y, refs = refs[0], refs[1:]
        y_before, y_after = y.at[pl.ds(0, 1)], y.at[pl.ds(y.shape[0] - 1, 1)]
    else:
        y, y_before, y_after, refs = refs[0], refs[1], refs[2], refs[3:]
    own_far, others, refs = refs[0], refs[1:tiles], refs[tiles:]
    total_hbm, gain_hbm, shift_hbm, refs = *refs[:3], refs[3:]
    dy_ref, wg_ref, back_ref, refs = *refs[:3], refs[3:]
    grads_in, refs = refs[:parts], refs[parts:]
    (taps_in, y_in, y_halo, dn_halo, rest, back, total, gain, shift, dy_buf, dy_rows, wg_buf, in_sem,
     out_sem) = refs
    planes, rows, channels = grads[0].shape
    spare = (parts + 1) * planes
    lists = [
        (total_hbm.at[:, pl.ds(0, 8), :], total),
        (gain_hbm, gain),
        (shift_hbm, shift),
        (y_before, y_halo.at[pl.ds(0, 1)]),
        (y_after, y_halo.at[pl.ds(1, 1)]),
        (others[0], dn_halo.at[0]),
        (others[1], dn_halo.at[1]),
        (own_far, rest.at[0]),
    ] + [(other, rest.at[n + 1]) for n, other in enumerate(others[2:])]
    small = [
        started(source, target, in_sem.at[spare + n]) for n, (source, target) in enumerate(lists)
    ]

    def in_copies(p):
        copies = [pltpu.make_async_copy(y.at[p + first], y_in.at[p], in_sem.at[(parts + 1) * p])]
        for n in range(parts):
            copies.append(
                pltpu.make_async_copy(
                    grads[n].at[p], grads_in[n].at[p], in_sem.at[(parts + 1) * p + 1 + n]
                )
            )
        return copies

    for p in range(planes):
        for copy in in_copies(p):
            copy.start()
    heavy = started(taps_hbm, taps_in, in_sem.at[spare + len(lists)])
    for copy in small:
        copy.wait()
    tile = spots[2]
    tails = [rest[0], dn_halo[0, rows:, :], dn_halo[1, rows:, :]]
    tails += [rest[n] for n in range(1, rest.shape[0])]
    for by, tail in zip([0, 1, tiles - 1] + list(range(2, tiles - 1)), tails):
        value = tail.astype(F32)
        value = value[0:2] + value[2:4] + value[4:6]
        back[lax.rem(tile + tiles - by, tiles), 0:2, :] = value
    mean, inverse = moments(total[...], count)
    gains, shifts = row_of(gain, layer), row_of(shift, layer)
    scale = inverse * gains
    both = back[0, 0:2, :]
    for t in range(1, tiles):
        both = both + back[t, 0:2, :]
    back[0, 0:2, :] = both
    sums = both / count

    def finish(inner, centred):
        return scale * (inner - sums[0:1, :] - centred * sums[1:2, :])

    for side, place in ((0, 0), (1, planes + 1)):
        centred = (y_halo[side].astype(F32) - mean) * inverse
        value = finish(dn_halo[side, 0:rows, :].astype(F32), centred)
        dy_buf[place] = jnp.where(spots[side] > 0, value, 0.0).astype(BF)

    @pl.loop(0, planes)
    def _(p):
        for copy in in_copies(p):
            copy.wait()
        grad = grads_in[0][p].astype(F32)
        for n in range(1, parts):
            grad = grad + grads_in[n][p].astype(F32)
        value = finish(*norm_grads(y_in[p], grad, mean, inverse, gains, shifts)).astype(BF)
        dy_buf[p + 1] = value
        dy_rows[pl.ds(pl.multiple_of(p * rows, rows), rows), :] = value

    done = [
        started(dy_buf, dy_ref, out_sem.at[0]),
        started(back.at[0, pl.ds(0, 2), :], back_ref, out_sem.at[2]),
    ]
    heavy.wait()
    wg_buf[...] = nn(taps_in[...], dy_rows[...]).astype(BF)
    done.append(started(wg_buf, wg_ref, out_sem.at[1]))
    for copy in done:
        copy.wait()


def weight_grad(
    spots, taps_t, grads, y, y_halo, far, others, total, gain, shift, layer, count, follow=()
):
    planes, rows, channels = grads[0].shape
    wide = taps_t.shape[0]
    tiles = len(others) + 1
    ext = (planes + 2, rows, channels)
    own = (planes, rows, channels)
    operands = (taps_t,) + tuple(grads) + (y,) + tuple(y_halo) + (far,) + tuple(others)
    operands += (total, gain, shift)
    return ordered(
        functools.partial(weight_grad_kernel, layer, count, 0 if y_halo else 1, len(grads), tiles),
        (spots,) + operands,
        [sspec()] + [aspec()] * len(operands),
        follow,
        out_shape=any_outs((ext, BF), ((wide, channels), BF), ((2, channels), F32)),
        out_specs=(aspec(),) * 3,
        scratch_shapes=[VMEM(x.shape, x.dtype) for x in grads]
        + [
            VMEM(taps_t.shape, BF),
            VMEM(own, F32),
            VMEM((2, rows, channels), BF if y_halo else F32),
            VMEM((2, rows + 16, channels), BF),
            VMEM((tiles - 2, 16, channels), BF),
            VMEM((tiles, 8, channels), F32),
            VMEM((tiles, 8, channels), F32),
            VMEM(gain.shape, F32),
            VMEM(gain.shape, F32),
            VMEM(ext, BF),
            VMEM((planes * rows, channels), BF),
            VMEM((wide, channels), BF),
        ]
        + sems((len(grads) + 1) * planes + 8 + tiles, 3),
        compiler_params=params(62.5),
        cost_estimate=cost(),
        name="weight_grad",
    )


def conv_back_kernel(width, layer, count, parts, dy, w_hbm, *refs):
    more = count is not None
    grads, refs = refs[:parts], refs[parts:]
    if more:
        y, total_hbm, gain_hbm, shift_hbm, refs = *refs[:4], refs[4:]
    out_ref, refs = refs[0], refs[1:]
    if more:
        sent, refs = refs[:3], refs[3:]
    grads_in, refs = refs[:parts], refs[parts:]
    raw, xs, weight, out_buf, in_sem, w_sem, out_sem, refs = *refs[:7], refs[7:]
    ext_planes, rows, channels = dy.shape
    planes = ext_planes - 2
    group = planes // 2
    pairs = 2
    each = parts + 1
    body = started(dy, raw, in_sem.at[each * pairs])
    heavy = [
        started(
            w_hbm.at[layer, pl.ds((26 - o) * channels, channels), :],
            weight.at[:, pl.ds(o * channels, channels)],
            w_sem.at[o],
        )
        for o in range(27)
    ]
    small = []
    if more:
        y_in, total, gain, shift, edges, sums, spare, back_sem = refs
        small = [
            started(source, target, in_sem.at[each * pairs + 1 + n])
            for n, (source, target) in enumerate(
                ((total_hbm.at[:, pl.ds(0, 8), :], total), (gain_hbm, gain), (shift_hbm, shift))
            )
        ]
        sums[...] = jnp.zeros_like(sums)

    def in_copies(i):
        two = pl.ds(group * i, group)
        copies = [
            pltpu.make_async_copy(grads[n].at[two], grads_in[n].at[two], in_sem.at[each * i + n])
            for n in range(parts)
        ]
        if more:
            copies.append(
                pltpu.make_async_copy(
                    y.at[pl.ds(group * i + 1, group)], y_in.at[two], in_sem.at[each * i + parts]
                )
            )
        return copies

    def out_copy(i):
        two = pl.ds(group * i, group)
        return pltpu.make_async_copy(out_buf.at[two], out_ref.at[two], out_sem.at[i])

    for i in range(pairs):
        for copy in in_copies(i):
            copy.start()
    clear_edges(xs, width, rows)
    body.wait()

    @pl.loop(0, ext_planes)
    def _(p):
        put_plane(xs, p, raw[p].astype(F32), width)

    for copy in small + heavy:
        copy.wait()
    if more:
        mean, inverse = moments(total[...], count)
        gains, shifts = row_of(gain, layer - 1), row_of(shift, layer - 1)

    @pl.loop(0, pairs)
    def _(i):
        part = nt(tap_group(xs, group * i, group, width, rows), weight[...])
        for copy in in_copies(i):
            copy.wait()
        for n_plane in range(group):
            p = group * i + n_plane
            value = part[n_plane * rows : (n_plane + 1) * rows]
            for n in range(parts):
                value = value + grads_in[n][p].astype(F32)
            out_buf[p] = value
            if more:
                inner, centred = norm_grads(y_in[p], value, mean, inverse, gains, shifts)
                add_stats(sums, inner, inner * centred)

                for side, near in ((0, 0), (1, group - 1)):
                    if n_plane == near:

                        @pl.when(p == side * (planes - 1))
                        def _():
                            edges[side, 0:rows, :] = inner.astype(BF)

        out_copy(i).start()

    if more:
        finish_back(sums, edges, sent, spare, back_sem)
    for i in range(pairs):
        out_copy(i).wait()


def conv_back(dy, grads, weights, layer, width, norm=None, follow=()):
    ext_planes, rows, channels = dy.shape
    own = (ext_planes - 2, rows, channels)
    pairs = 2
    outs, extra, scratch = [(own, F32)], (), []
    if norm is not None:
        y, total, gain, shift, count = norm
        extra = (y, total, gain, shift)
        outs += list(back_shapes(rows, channels))
        scratch = [VMEM(own, F32), VMEM((total.shape[0], 8, channels), F32)]
        scratch += [VMEM(gain.shape, F32), VMEM(gain.shape, F32)]
        scratch += back_scratch(rows, channels) + sems(3)
    else:
        count = None
    return ordered(
        functools.partial(conv_back_kernel, width, layer, count, len(grads)),
        (dy, weights) + tuple(grads) + extra,
        [aspec()] * (2 + len(grads) + len(extra)),
        follow,
        out_shape=any_outs(*outs),
        out_specs=(aspec(),) * len(outs),
        scratch_shapes=[VMEM(x.shape, x.dtype) for x in grads]
        + [VMEM(dy.shape, BF)]
        + conv_scratch(ext_planes, rows, width, channels, True)
        + [VMEM(own, F32)]
        + sems(pairs * (len(grads) + 1) + 4, 27, pairs)
        + scratch,
        compiler_params=params(62.5),
        cost_estimate=cost(),
        name="conv_back",
    )


GROUP = 9


def place_kernel(part, *refs):
    out_ref = refs[-1]
    blocks, offsets, chosen, _ = part.shape
    for o in range(offsets):
        for b in range(blocks):
            out_ref[0, o, b * chosen : (b + 1) * chosen, :] = part[b, o].astype(F32)


def place(parts, layer, layers, kept, follow=()):
    blocks, offsets, chosen, channels = parts.shape
    shape = (layers, offsets, blocks * chosen, channels)
    return ordered(
        place_kernel,
        (parts,) + kept,
        [pl.BlockSpec((blocks, GROUP, chosen, channels), lambda o: (0, o, 0, 0))]
        + [aspec()] * len(kept),
        follow,
        grid=(offsets // GROUP,),
        out_shape=jax.ShapeDtypeStruct(shape, F32),
        out_specs=pl.BlockSpec((1, GROUP) + shape[2:], lambda o: (layer, o, 0, 0)),
        input_output_aliases={1: 0} if kept else {},
        compiler_params=params(62.5),
        cost_estimate=cost(),
        name="place",
    )


def per_device(
    volume,
    sample_cells,
    sample_fracs,
    view_mask,
    pixel_of_ray,
    conv_weight,
    norm_gain,
    norm_shift,
    hidden_weight,
    hidden_bias,
    density_weight,
    density_bias,
    semantic_weight,
    semantic_bias,
    render_cotangent,
    volume_cotangent,
):
    extent = volume.shape[:3]
    depth, height, width, channels = volume.shape
    rows = height * width
    voxels = depth * rows
    tiles = lax.axis_size("tile")
    ray_devices = lax.axis_size("ray")
    count = float(voxels * tiles)
    rays, samples = sample_cells.shape
    classes = semantic_weight.shape[2]
    layers = conv_weight.shape[0]
    blocks = min(BLOCKS, ray_devices)
    chosen = channels // blocks
    tile, ray = lax.axis_index("tile"), lax.axis_index("ray")
    block = lax.rem(ray, blocks).astype(jnp.int32).reshape(1)

    own = volume.reshape(depth, rows, channels)
    before, after = exchange(own[:2], own[-2:])
    flags = jnp.stack([tile > 0, tile < tiles - 1]).astype(jnp.int32)

    owner_of = lax.div(sample_cells, voxels)
    held = owner_of[None] == jnp.arange(tiles, dtype=jnp.int32)[:, None, None]
    earlier = jnp.arange(rays)[None, :] < jnp.arange(rays)[:, None]
    starts = jnp.sum(
        (held[:, None, :, :] & earlier[None, :, :, None]).astype(jnp.int32), axis=(2, 3)
    ).reshape(tiles * rays)
    pixels = pixel_of_ray[0]
    buffer, owner, rank = prepare(extent, starts, sample_cells, sample_fracs, tiles, channels)

    weights = conv_weight.reshape(layers, 27 * channels, channels)
    mlp = (
        hidden_weight,
        hidden_bias,
        semantic_weight,
        density_weight,
        semantic_bias,
        density_bias[None],
    )
    y_ext, v_ext, mixed = conv_first(before, own, after, buffer, weights, 0, width)
    total = received = all_to_all(mixed, "tile")
    taps_first = turn(block, v_ext, width, blocks)
    v_next, r_ext, y_next, stat, y_first, y_last = conv_next(
        flags, y_ext, v_ext, total, norm_gain, norm_shift, weights, 0, width, count,
        follow=(taps_first,),
    )
    total_next = all_to_all(stat, "tile")
    heads, feature, act, slope = sample(extent, received, (r_ext, 1), 0, mlp)
    heads_last, feature_last, act_last, slope_last, r_last = sample(
        extent, received, (y_next, v_next, total_next, norm_gain, norm_shift), 1, mlp, count,
        follow=(heads,),
    )

    def draw(heads, layer, follow):
        return composite(
            starts, pixels, owner, rank, view_mask, all_to_all(heads, "tile"), render_cotangent,
            layer, classes, follow=follow,
        )

    picture, grad_heads = draw(heads, 0, (heads_last,))
    picture_last, grad_heads_last = draw(heads_last, 1, (grad_heads,))
    shares = (ray_devices, voxels // ray_devices, channels)
    planes = (depth, rows, channels)
    local, pack = sample_back(
        extent, 0, received, all_to_all(grad_heads, "tile"), feature, act, slope, mlp, (),
        follow=(grad_heads_last,),
    )
    parts = all_to_all(local.reshape(shares), "ray")
    local_last, packed = sample_back(
        extent, 1, received, all_to_all(grad_heads_last, "tile"), feature_last, act_last,
        slope_last, mlp, (pack,), follow=(local,),
    )
    copies = add_parts(parts, ray_devices, follow=(local_last,))
    parts_last = all_to_all(local_last.reshape(shares), "ray")
    taps_next = turn(block, r_ext, width, blocks, follow=(copies,))
    copies_last = add_parts(parts_last, ray_devices, follow=(taps_next,))
    sums_last = all_to_all(copies_last, "ray").reshape(planes)
    y_edges = exchange(*hold((y_first, y_last), (copies_last,)))

    cot = volume_cotangent.reshape(planes)
    wide_taps = (27 * chosen, voxels)
    spots = jnp.stack([tile > 0, tile < tiles - 1, tile]).astype(jnp.int32)
    sent = norm_back(
        cot, sums_last, y_next, total_next, norm_gain, norm_shift, 1, count,
        follow=y_edges,
    )
    (copies,) = hold((copies,), (sent[2],))
    sums = all_to_all(copies, "ray").reshape(planes)
    (packed,) = hold((packed,), (sums,))
    packed = lax.psum_scatter(packed, "ray", scatter_dimension=0, tiled=True)
    dy, part, back_last = weight_grad(
        spots, taps_next.reshape(wide_taps), (cot, sums_last), y_next, y_edges, sent[2],
        share_back(sent), total_next, norm_gain, norm_shift, 1, count,
    )
    shard = lax.psum_scatter(part, "tile", scatter_dimension=0, tiled=True)
    grad, *sent = conv_back(
        dy, (cot, sums_last, sums), weights, 1, width,
        (y_ext, total, norm_gain, norm_shift, count),
    )
    others = share_back(sent)
    shards = add_parts(shard[None], tiles, follow=others)
    shard = all_to_all(shards, "tile")

    dy, part, back = weight_grad(
        spots, taps_first.reshape(wide_taps), (grad,), y_ext, (), sent[2], others, total,
        norm_gain, norm_shift, 0, count, follow=(shards,),
    )
    (part,) = hold((part,), (shard,))
    parts = all_to_all(part.reshape(tiles, 27 * chosen // tiles, channels), "tile")
    (shard,) = hold((shard,), (part,))
    copies = add_parts(parts, tiles, follow=(shard,))
    slices = all_to_all(copies, "tile")

    def gather(slices):
        whole_grad = lax.all_gather(slices, "ray", axis=0, tiled=True)
        return whole_grad.reshape(-1, 27, chosen, channels)[:blocks]

    conv_grad = place(gather(shard), 1, layers, (), follow=(slices,))
    packed = all_to_all(add_parts(packed[None], tiles, follow=(slices,)), "tile")
    (grad,) = conv_back(dy, (grad,), weights, 0, width, follow=(conv_grad,))
    packed = all_to_all(add_parts(packed, ray_devices, follow=(grad,)), "ray")
    packed = packed.reshape(layers, PACK, channels)[::-1]
    conv_grad = place(gather(slices), 0, layers, (conv_grad,), follow=(grad,))

    at = channels + 16
    heads = packed[:, at : at + DROWS]
    head_bias = packed[:, at + DROWS, :DROWS]
    return (
        jnp.swapaxes(jnp.stack([picture, picture_last])[:, : classes + 1], 1, 2),
        r_last.reshape(volume.shape),
        grad.reshape(volume.shape),
        conv_grad,
        jnp.stack([back, back_last])[:, 1],
        jnp.stack([back, back_last])[:, 0],
        packed[:, :channels],
        packed[:, channels],
        heads[:, classes],
        head_bias[:, classes],
        jnp.swapaxes(heads[:, :classes], 1, 2),
        head_bias[:, :classes],
    )


def solution(mesh):
    in_specs = (
        P("tile", None, None, None),
        P(("ray", "tile"), None),
        P(None, ("ray", "tile"), None),
        P(("ray", "tile"), None),
        P(("ray", "tile"), None),
        P(),
        P(),
        P(),
        P(),
        P(),
        P(),
        P(),
        P(),
        P(),
        P(None, ("ray", "tile"), None),
        P("tile", None, None, None),
    )
    out_specs = (
        P(None, ("ray", "tile"), None),
        P("tile", None, None, None),
        P("tile", None, None, None),
        P(),
        P(),
        P(),
        P(),
        P(),
        P(),
        P(),
        P(),
        P(),
    )
    return jax.shard_map(
        per_device, mesh=mesh, in_specs=in_specs, out_specs=out_specs, check_vma=False
    )
```

```python
import functools

import jax
import jax.numpy as jnp
from jax import lax
from jax.experimental import pallas as pl
from jax.experimental.pallas import tpu as pltpu
from jax.sharding import PartitionSpec as P

CAP = 768
WINDOW = 256
LANES = 128
PROWS = 24
DROWS = 32
COORDS = 8
BLOCKS = 8
PACK = 320
epsilon = 1e-05
MIB = 1024 * 1024

BF = jnp.bfloat16
F32 = jnp.float32
VMEM = pltpu.VMEM
SMEM = pltpu.SMEM


def nn(left, right):
    return jnp.dot(left, right, preferred_element_type=F32)


def nt(left, right):
    return lax.dot_general(left, right, (((1,), (1,)), ((), ())), preferred_element_type=F32)


def iota(shape, dim):
    return lax.broadcasted_iota(jnp.int32, shape, dim)


def whole(shape):
    return pl.BlockSpec(shape, lambda *_: (0,) * len(shape))


def planes_of(step, shape, first=0):
    return pl.BlockSpec((step,) + shape[1:], lambda i: (i + first // step,) + (0,) * (len(shape) - 1))


def sspec():
    return pl.BlockSpec(memory_space=SMEM)


def aspec():
    return pl.BlockSpec(memory_space=pl.ANY)


def hspec():
    return pl.BlockSpec(memory_space=pltpu.HBM)


def ordered(kernel, operands, in_specs, follow, **options):
    count, skip = len(operands), len(follow)

    def body(*refs):
        kernel(*refs[:count], *refs[count + skip :])

    return pl.pallas_call(body, in_specs=list(in_specs) + [aspec()] * skip, **options)(
        *operands, *follow
    )


def params(mib):
    return pltpu.CompilerParams(vmem_limit_bytes=int(mib * MIB))


def cost():
    return pl.CostEstimate(flops=1, bytes_accessed=1, transcendentals=0)


def lane_cumsum(x):
    lane = iota(x.shape, 1)
    shift = 1
    while shift < x.shape[1]:
        x = x + jnp.where(lane >= shift, pltpu.roll(x, shift, 1), 0.0)
        shift *= 2
    return x


def window_onehots(starts, owner_row, rank_row, ray, rays, tiles):
    rows = iota((WINDOW, rank_row.shape[1]), 0)
    hots, bases = [], []
    for t in range(tiles):
        start = starts[t * rays + ray]
        base = (start // LANES) * LANES
        place = jnp.where(owner_row == t, rank_row + (start - base), -1)
        hots.append((rows == place).astype(F32).astype(BF))
        bases.append(pl.multiple_of(base, LANES))
    return jnp.concatenate(hots, axis=0), bases


def prep_kernel(extent, starts, cells_ref, fracs_ref, out_ref, owner_ref, rank_ref, vals, acc):
    depth, height, width = extent
    tiles = out_ref.shape[0]
    rays, samples = cells_ref.shape
    cells = cells_ref[...]
    voxels = depth * height * width
    owner = lax.div(cells, voxels)
    local = cells - owner * voxels
    base_x = lax.div(local, height * width)
    inner = local - base_x * (height * width)
    base_y = lax.div(inner, width)
    base_z = inner - base_y * width
    rank = jnp.zeros(cells.shape, F32)
    for t in range(tiles):
        mine = owner == t
        rank = jnp.where(mine, lane_cumsum(jnp.where(mine, 1.0, 0.0)) - 1.0, rank)
    owner_ref[...] = owner
    rank_ref[...] = rank.astype(jnp.int32)
    vals[...] = jnp.zeros_like(vals)
    rows = [(base_x + 1).astype(F32), base_y.astype(F32), base_z.astype(F32)]
    low = []
    for d in range(3):
        frac = fracs_ref[d]
        high = frac.astype(BF).astype(F32)
        rows.append(high)
        low.append(frac - high)
    rows += low
    for number, row in enumerate(rows):
        for k in range(rays):
            vals[number : number + 1, k * samples : (k + 1) * samples] = row[k : k + 1]
    acc[...] = jnp.zeros_like(acc)
    for k in range(rays):
        hot, bases = window_onehots(
            starts, owner_ref[k : k + 1, :], rank_ref[k : k + 1, :], k, rays, tiles
        )
        moved = nt(vals[:, k * samples : (k + 1) * samples].astype(BF), hot)
        for t in range(tiles):
            acc[t, :, pl.ds(bases[t], WINDOW)] += moved[:, t * WINDOW : (t + 1) * WINDOW]
    out_ref[...] = jnp.zeros_like(out_ref)
    wide = out_ref.shape[2]
    lines = CAP // wide
    for n in range(lines):
        part = slice(n * wide, (n + 1) * wide)
        for r in range(6):
            value = acc[:, r : r + 1, part]
            if r >= 3:
                value = value + acc[:, r + 3 : r + 4, part]
            out_ref[:, r * lines + n : r * lines + n + 1, :] = value


def prepare(extent, starts, cells, fracs, tiles, wide, follow=()):
    rays, samples = cells.shape
    outs = ((tiles, COORDS * CAP // wide, wide), (rays, samples), (rays, samples))
    return ordered(
        functools.partial(prep_kernel, extent),
        (starts, cells, fracs,),
        [sspec(), whole(cells.shape), whole(fracs.shape)],
        follow,
        grid=(1,),
        out_shape=(
            jax.ShapeDtypeStruct(outs[0], F32),
            jax.ShapeDtypeStruct(outs[1], jnp.int32),
            jax.ShapeDtypeStruct(outs[2], jnp.int32),
        ),
        out_specs=tuple(whole(s) for s in outs),
        scratch_shapes=[VMEM((16, rays * samples), F32), VMEM((tiles, 16, CAP + WINDOW), F32)],
        compiler_params=params(62.5),
        cost_estimate=cost(),
        name="prep",
    )


def started(source, target, sem):
    copy = pltpu.make_async_copy(source, target, sem)
    copy.start()
    return copy


def put_plane(xs, p, value, width):
    rows, channels = value.shape
    along = lax.rem(iota(value.shape, 0), width)
    left = jnp.where(along == 0, 0.0, pltpu.roll(value, 1, 0))
    right = jnp.where(along == width - 1, 0.0, pltpu.roll(value, rows - 1, 0))
    xs[p, width : width + rows, 0:channels] = left.astype(BF)
    xs[p, width : width + rows, channels : 2 * channels] = value.astype(BF)
    xs[p, width : width + rows, 2 * channels : 3 * channels] = right.astype(BF)


def clear_edges(xs, width, rows):
    planes, _, wide = xs.shape
    for p in range(planes):
        xs[p, 0:width, :] = jnp.zeros((width, wide), BF)
        xs[p, width + rows : 2 * width + rows, :] = jnp.zeros((width, wide), BF)


def taps(xs, p, width, rows):
    return jnp.concatenate(
        [xs[p + a, b * width : b * width + rows, :] for a in range(3) for b in range(3)], axis=1
    )


def tap_group(xs, first, count, width, rows):
    return jnp.concatenate([taps(xs, first + n, width, rows) for n in range(count)], axis=0)


def add_stats(sums, one, two):
    sums[0:1, :] += jnp.sum(one, axis=0, keepdims=True)
    sums[1:2, :] += jnp.sum(two, axis=0, keepdims=True)


def conv_scratch(planes, rows, width, channels, turned):
    shape = (channels, 27 * channels) if turned else (27 * channels, channels)
    return [VMEM((planes, rows + 2 * width, 3 * channels), BF), VMEM(shape, BF)]


def sems(*counts):
    return [pltpu.SemaphoreType.DMA((n,)) for n in counts]


def any_outs(*shapes):
    return tuple(jax.ShapeDtypeStruct(shape, dtype) for shape, dtype in shapes)


def conv_first_kernel(
    width, layer, before, own, after, coords, w_hbm, y_ref, v_ref, mix_ref,
    raw, xs, weight, y_buf, mix, in_sem, out_sem,
):
    planes, rows, channels = own.shape
    pairs = planes // 2 + 1
    body = [
        started(own.at[pl.ds(2 * i, 2)], raw.at[pl.ds(2 * i + 2, 2)], in_sem.at[i])
        for i in range(planes // 2)
    ]
    ends = [
        started(before, raw.at[pl.ds(0, 2)], in_sem.at[pairs]),
        started(after, raw.at[pl.ds(planes + 2, 2)], in_sem.at[pairs + 1]),
    ]
    heavy = started(w_hbm.at[layer], weight, in_sem.at[pairs + 2])
    light = started(coords, mix.at[:, pl.ds(8, coords.shape[1]), :], in_sem.at[pairs + 3])
    clear_edges(xs, width, rows)
    mix[:, 0:8, :] = jnp.zeros((mix.shape[0], 8, channels), F32)
    for copy in body + ends:
        copy.wait()

    @pl.loop(0, planes + 4)
    def _(p):
        put_plane(xs, p, raw[p].astype(F32), width)

    done = [started(raw.at[pl.ds(1, planes + 2)], v_ref, out_sem.at[pairs])]
    light.wait()
    heavy.wait()

    group = (planes + 2) // 2

    def out_copy(i):
        some = pl.ds(group * i, group)
        return pltpu.make_async_copy(y_buf.at[some], y_ref.at[some], out_sem.at[i])

    @pl.loop(0, 2)
    def _(i):
        p = group * i
        part = nn(tap_group(xs, p, group, width, rows), weight[...])
        for n in range(group):
            y_buf[p + n] = part[n * rows : (n + 1) * rows]
        out_copy(i).start()
        inner = part[rows : (group - 1) * rows]
        add_stats(mix.at[0], inner, inner * inner)
        edge = jnp.where(i == 0, part[(group - 1) * rows :], part[:rows])
        add_stats(mix.at[0], edge, edge * edge)

    for t in range(1, mix.shape[0]):
        mix[t, 0:8, :] = mix[0, 0:8, :]
    done.append(started(mix, mix_ref, out_sem.at[pairs + 1]))
    for copy in done:
        copy.wait()
    for i in range(2):
        out_copy(i).wait()


def conv_first(before, own, after, coords, weights, layer, width):
    planes, rows, channels = own.shape
    ext = (planes + 2, rows, channels)
    tiles, lines, _ = coords.shape
    pairs = planes // 2 + 1
    return ordered(
        functools.partial(conv_first_kernel, width, layer),
        (before, own, after, coords, weights),
        [aspec()] * 5,
        (),
        out_shape=any_outs((ext, F32), (ext, BF), ((tiles, 8 + lines, channels), F32)),
        out_specs=(aspec(),) * 3,
        scratch_shapes=[VMEM((planes + 4, rows, channels), BF)]
        + conv_scratch(planes + 4, rows, width, channels, False)
        + [VMEM(ext, F32), VMEM((tiles, 8 + lines, channels), F32)]
        + sems(pairs + 4, pairs + 2),
        compiler_params=params(62.5),
        cost_estimate=cost(),
        name="conv_first",
    )


def moments(total, count):
    both = jnp.sum(total, axis=0)
    mean = both[0:1, :] / count
    return mean, lax.rsqrt(both[1:2, :] / count - mean * mean + epsilon)


def row_of(ref, layer):
    return ref[layer : layer + 1, :]


def inverse_of(value):
    guess = pl.reciprocal(value, approx=True)
    return guess * (2.0 - value * guess)


def sigmoid(value):
    return inverse_of(1.0 + jnp.exp(jnp.minimum(-value, 80.0)))


def silu(value):
    return value * sigmoid(value)


def affine(mean, inverse, gains, shifts):
    scale = inverse * gains
    return scale, shifts - mean * scale


def conv_next_kernel(
    width, layer, count, flags, y_ext, v_ext, total_hbm, gain_hbm, shift_hbm, w_hbm,
    v_ref, r_ref, y_ref, stat_ref, first_ref, last_ref,
    y_in, v_in, total, gain, shift, xs, weight, v_buf, r_buf, y_buf, edges, stat, in_sem, out_sem,
):
    ext_planes, rows, channels = y_ext.shape
    pairs = ext_planes // 2
    small = [
        started(total_hbm.at[:, pl.ds(0, 8), :], total, in_sem.at[2 * pairs]),
        started(gain_hbm, gain, in_sem.at[2 * pairs + 1]),
        started(shift_hbm, shift, in_sem.at[2 * pairs + 2]),
    ]
    def in_copies(i):
        two = pl.ds(2 * i, 2)
        return (
            pltpu.make_async_copy(y_ext.at[two], y_in.at[two], in_sem.at[2 * i]),
            pltpu.make_async_copy(v_ext.at[two], v_in.at[two], in_sem.at[2 * i + 1]),
        )

    def mid_copies(i):
        two = pl.ds(2 * i, 2)
        return (
            pltpu.make_async_copy(v_buf.at[two], v_ref.at[two], out_sem.at[3 * i]),
            pltpu.make_async_copy(r_buf.at[two], r_ref.at[two], out_sem.at[3 * i + 1]),
        )

    def out_copy(i):
        two = pl.ds(2 * i - 2, 2)
        return pltpu.make_async_copy(y_buf.at[two], y_ref.at[two], out_sem.at[3 * i + 2])

    for i in range(pairs):
        for copy in in_copies(i):
            copy.start()
    heavy = started(w_hbm.at[layer + 1], weight, in_sem.at[2 * pairs + 3])
    clear_edges(xs, width, rows)
    stat[...] = jnp.zeros_like(stat)
    for copy in small:
        copy.wait()
    mean, inverse = moments(total[...], count)
    scale, offset = affine(mean, inverse, row_of(gain, layer), row_of(shift, layer))

    @pl.loop(0, pairs)
    def _(i):
        for copy in in_copies(i):
            copy.wait()
        for side in range(2):
            p = 2 * i + side
            fresh = v_in[p].astype(F32) + silu(y_in[p] * scale + offset)
            v_buf[p] = fresh
            outside = (p == side * (ext_planes - 1)) & (flags[side] == 0)
            rounded = jnp.where(outside, 0.0, fresh).astype(BF)
            r_buf[p] = rounded
            put_plane(xs, p, rounded.astype(F32), width)
        for copy in mid_copies(i):
            copy.start()

        @pl.when(i == 1)
        def _():
            heavy.wait()

        @pl.when(i > 0)
        def _():
            p = 2 * i - 2
            part = nn(tap_group(xs, p, 2, width, rows), weight[...])
            y_buf[p] = part[:rows]
            y_buf[p + 1] = part[rows:]
            add_stats(stat.at[0], part, part * part)
            out_copy(i).start()

    edges[0] = y_buf[0].astype(BF)
    edges[1] = y_buf[ext_planes - 3].astype(BF)
    for t in range(1, stat.shape[0]):
        stat[t] = stat[0]
    done = [
        started(stat, stat_ref, out_sem.at[2]),
        started(edges.at[pl.ds(0, 1)], first_ref, out_sem.at[3 * pairs]),
        started(edges.at[pl.ds(1, 1)], last_ref, out_sem.at[3 * pairs + 1]),
    ]
    for i in range(pairs):
        done += list(mid_copies(i)) + ([out_copy(i)] if i else [])
    for copy in done:
        copy.wait()


def conv_next(flags, y_ext, v_ext, total, gain, shift, weights, layer, width, count, follow=()):
    ext_planes, rows, channels = y_ext.shape
    ext = y_ext.shape
    inner = (ext_planes - 2, rows, channels)
    stat = (total.shape[0], 8, channels)
    pairs = ext_planes // 2
    edge = (1, rows, channels)
    return ordered(
        functools.partial(conv_next_kernel, width, layer, count),
        (flags, y_ext, v_ext, total, gain, shift, weights),
        [sspec()] + [aspec()] * 6,
        follow,
        out_shape=any_outs((ext, F32), (ext, BF), (inner, F32), (stat, F32), (edge, BF), (edge, BF)),
        out_specs=(aspec(),) * 6,
        scratch_shapes=[VMEM(ext, F32), VMEM(ext, BF), VMEM(stat, F32)]
        + [VMEM(gain.shape, F32)] * 2
        + conv_scratch(ext_planes, rows, width, channels, False)
        + [VMEM(ext, F32), VMEM(ext, BF), VMEM(inner, F32)]
        + [VMEM((2, rows, channels), BF), VMEM(stat, F32)]
        + sems(2 * pairs + 4, 3 * pairs + 2),
        compiler_params=params(62.5),
        cost_estimate=cost(),
        name="conv_next",
    )


def fill_weights(table, coords, extent):
    depth, height, width = extent
    samples = coords[0].shape[1]

    def along(base, frac, size):
        grid = iota((size, samples), 0).astype(F32)
        lower = jnp.where(grid == base, 1.0 - frac, 0.0)
        return lower + jnp.where(grid == base + 1.0, frac, 0.0)

    on_x = along(coords[0] - 1.0, coords[3], depth)
    on_y = along(coords[1], coords[4], height)
    on_z = along(coords[2], coords[5], width)
    for x in range(depth):
        on_xy = on_x[x : x + 1] * on_y
        for y in range(height):
            row = (x * height + y) * width
            table[row : row + width, :] = (on_xy[y : y + 1] * on_z).astype(BF)


def diagonal(rows, columns):
    return iota((rows, columns), 0) == iota((rows, columns), 1)


def identity(rows, columns):
    return diagonal(rows, columns).astype(F32).astype(BF)


def head_rows(semantic, density, rows):
    channels, classes = semantic.shape
    turned = nt(identity(rows, classes), semantic)
    return jnp.where(iota((rows, channels), 0) == classes, density.astype(F32), turned).astype(BF)


def column(row, rows):
    return jnp.sum(jnp.where(diagonal(rows, row.shape[1]), row, 0.0), axis=1, keepdims=True)


def coord_rows(block, slots):
    lines = slots // block.shape[1]
    return [
        jnp.concatenate(
            [block[8 + r * lines + n : 9 + r * lines + n, :] for n in range(lines)], axis=1
        )
        for r in range(6)
    ]


def sample_kernel(
    extent, layer, first, count, coords, *refs
):
    if count is None:
        r_hbm, refs = refs[0], refs[1:]
    else:
        y_hbm, v_hbm, total_hbm, gain, shift, refs = refs[0], refs[1], refs[2], refs[3], refs[4], refs[5:]
    hidden, hidden_b, semantic, density, semantic_b, density_b, refs = *refs[:6], refs[6:]
    p_ref, f_ref, g_ref, s_ref, refs = *refs[:4], refs[4:]
    if count is not None:
        r_out, refs = refs[0], refs[1:]
    turned, table, rounded, hidden_t, bias, head_t, head_b, sem, refs = *refs[:8], refs[8:]
    channels = turned.shape[0]
    depth = extent[0]
    classes = semantic.shape[2]
    slots = table.shape[1]
    rows = rounded.shape[1]
    step = pl.program_id(0)

    if count is not None:
        y_in, v_in, total, load_sem = refs

    def in_copies(p):
        return (
            pltpu.make_async_copy(y_hbm.at[p], y_in.at[p], load_sem.at[2 * p]),
            pltpu.make_async_copy(v_hbm.at[p + 1], v_in.at[p], load_sem.at[2 * p + 1]),
        )

    def out_copy(p):
        return pltpu.make_async_copy(rounded.at[p], r_out.at[p], sem.at[p])

    @pl.when(step == 0)
    def _():
        if count is None:
            copy = started(r_hbm.at[pl.ds(first, depth)], rounded, sem.at[0])
        else:
            light = started(total_hbm, total, load_sem.at[2 * depth])
            for p in range(depth):
                for copy in in_copies(p):
                    copy.start()
        same = identity(channels, channels)
        hidden_t[...] = nt(same, hidden[layer]).astype(BF)
        bias[...] = column(hidden_b[layer : layer + 1, :], channels)
        head_t[...] = head_rows(semantic[layer], density[layer : layer + 1, :], PROWS)
        last = jnp.sum(
            jnp.where(iota((1, density_b.shape[1]), 1) == layer, density_b[...], 0.0),
            axis=1,
            keepdims=True,
        )
        place = iota((PROWS, 1), 0) == classes
        head_b[...] = jnp.where(place, last, column(semantic_b[layer : layer + 1, :], PROWS))
        if count is None:
            copy.wait()
        else:
            light.wait()
            mean, inverse = moments(total[...], count)
            scale, offset = affine(mean, inverse, row_of(gain, layer), row_of(shift, layer))

        @pl.loop(0, depth)
        def _(p):
            if count is not None:
                for copy in in_copies(p):
                    copy.wait()
                fresh = v_in[p] + silu(y_in[p] * scale + offset)
                rounded[p] = fresh.astype(BF)
                out_copy(p).start()
            turned[:, pl.ds(pl.multiple_of(p * rows, rows), rows)] = nt(same, rounded[p]).astype(BF)

    fill_weights(table, coord_rows(coords[0], slots), extent)
    feature = nn(turned[...], table[...]).astype(BF)
    f_ref[0] = feature
    inner = nn(hidden_t[...], feature) + bias[...]
    small = jnp.exp(-jnp.abs(inner))
    act = (jnp.maximum(inner, 0.0) + jnp.log1p(small)).astype(BF)
    g_ref[0] = act
    s_ref[0] = jnp.where(inner >= 0.0, 1.0, small) * inverse_of(1.0 + small)
    p_ref[0] = nn(head_t[...], act) + head_b[...]
    if count is not None:

        @pl.when(step == pl.num_programs(0) - 1)
        def _():
            for p in range(depth):
                out_copy(p).wait()


def per_tile(rows, lanes):
    return pl.BlockSpec((1, rows, lanes), lambda t: (t, 0, 0))


def sample(extent, received, source, layer, mlp, count=None, follow=()):
    tiles, lines, wide = received.shape
    slots = CAP
    rows, channels = extent[1] * extent[2], mlp[0].shape[1]
    depth = extent[0]
    voxels = depth * rows
    outs = [((tiles, PROWS, slots), F32)] + [((tiles, channels, slots), d) for d in (BF, BF, F32)]
    out_specs = [per_tile(n, slots) for n in (PROWS, channels, channels, channels)]
    scratch = [
        VMEM((channels, voxels), BF),
        VMEM((voxels, slots), BF),
        VMEM((depth, rows, channels), BF),
        VMEM((channels, channels), BF),
        VMEM((channels, 1), F32),
        VMEM((PROWS, channels), BF),
        VMEM((PROWS, 1), F32),
    ] + sems(depth)
    if count is None:
        first, given, specs = source[1], source[:1], [aspec()]
    else:
        first, given = 0, source
        specs = [aspec()] * 3 + [whole(x.shape) for x in source[3:]]
        outs.append(((depth, rows, channels), BF))
        out_specs.append(aspec())
        scratch += [VMEM((depth, rows, channels), F32)] * 2 + [VMEM(source[2].shape, F32)]
        scratch += sems(2 * depth + 1)
    return ordered(
        functools.partial(sample_kernel, extent, layer, first, count),
        (received,) + tuple(given) + mlp,
        [per_tile(lines, wide)] + specs + [whole(x.shape) for x in mlp],
        follow,
        grid=(tiles,),
        out_shape=any_outs(*outs),
        out_specs=tuple(out_specs),
        scratch_shapes=scratch,
        compiler_params=params(62.5),
        cost_estimate=cost(),
        name="sample",
    )


def sample_back_kernel(
    extent, layer, coords, dp_ref, f_ref, g_ref, s_ref, hidden, semantic, density, *refs
):
    du_ref, pack_ref, total, table, head = refs[-5:]
    step = pl.program_id(0)
    channels = hidden.shape[1]
    slots = table.shape[1]

    @pl.when(step == 0)
    def _():
        total[...] = jnp.zeros_like(total)
        pack_ref[0:PACK, :] = jnp.zeros((PACK, channels), F32)
        if len(refs) > 5:
            pack_ref[PACK : 2 * PACK, :] = refs[0][...]
        rows = head_rows(semantic[layer], density[layer : layer + 1, :], DROWS)
        head[...] = nt(identity(channels, channels), rows).astype(BF)

    fill_weights(table, coord_rows(coords[0], slots), extent)
    grad_heads = dp_ref[0]
    grad_inner = (nn(head[...], grad_heads) * s_ref[0]).astype(BF)
    ones = jnp.ones((16, slots), BF)
    pack_ref[0:channels, :] += nt(f_ref[0], grad_inner)
    pack_ref[channels : channels + 16, :] += nt(ones, grad_inner)
    at = channels + 16
    pack_ref[at : at + DROWS, :] += nt(grad_heads, g_ref[0])
    at += DROWS
    pack_ref[at : at + 16, 0:DROWS] += nt(ones, grad_heads)
    grad_features = nn(hidden[layer], grad_inner).astype(BF)
    total[...] += nt(table[...], grad_features)

    @pl.when(step == pl.num_programs(0) - 1)
    def _():
        du_ref[...] = total[...].astype(BF)


def sample_back(extent, layer, received, grad_heads, feature, act, slope, mlp, packs, follow=()):
    tiles, lines, wide = received.shape
    _, channels, slots = feature.shape
    voxels = extent[0] * extent[1] * extent[2]
    hidden, _, semantic, density = mlp[:4]
    outs = ((voxels, channels), (PACK * (1 + len(packs)), channels))
    return ordered(
        functools.partial(sample_back_kernel, extent, layer),
        (received, grad_heads, feature, act, slope, hidden, semantic, density) + packs,
        [per_tile(lines, wide)]
        + [per_tile(n, slots) for n in (DROWS, channels, channels, channels)]
        + [whole(x.shape) for x in (hidden, semantic, density) + packs],
        follow,
        grid=(tiles,),
        out_shape=any_outs((outs[0], BF), (outs[1], F32)),
        out_specs=tuple(whole(shape) for shape in outs),
        scratch_shapes=[
            VMEM((voxels, channels), F32),
            VMEM((voxels, slots), BF),
            VMEM((channels, DROWS), BF),
        ],
        compiler_params=params(62.5),
        cost_estimate=cost(),
        name="sample_back",
    )


def composite_kernel(
    classes, layer, starts, pixels, owner_ref, rank_ref, view, heads, cot,
    pic_ref, dp_ref, split, by_ray, grads, density, weights, grad_w, acc,
):
    tiles = heads.shape[0]
    rays, samples = owner_ref.shape
    step = 4.0 / samples
    split[...] = jnp.zeros_like(split)
    for t in range(tiles):
        value = heads[t]
        high = value.astype(BF)
        split[t, 0:PROWS, 0:CAP] = high.astype(F32)
        split[t, PROWS : 2 * PROWS, 0:CAP] = value - high.astype(F32)

    def hots(k):
        return window_onehots(
            starts, owner_ref[k : k + 1, :], rank_ref[k : k + 1, :], k, rays, tiles
        )

    for k in range(rays):
        hot, bases = hots(k)
        windows = jnp.concatenate(
            [split[t, :, pl.ds(bases[t], WINDOW)].astype(BF) for t in range(tiles)], axis=1
        )
        both = nn(windows, hot)
        one = both[:PROWS] + both[PROWS:]
        by_ray[k] = one
        density[k : k + 1, :] = one[classes : classes + 1]

    pre = density[...]
    visible = view[...].astype(F32)
    small = jnp.exp(-jnp.abs(pre))
    optical = visible * (jnp.maximum(pre, 0.0) + jnp.log1p(small)) * step
    passing = jnp.exp(-(lane_cumsum(optical) - optical))
    fading = jnp.exp(-optical)
    weight = passing * (1.0 - fading)
    weights[...] = weight
    row = iota((PROWS, samples), 0)
    lane = iota((PROWS, rays), 1)
    cotangent = nt(identity(PROWS, classes + 1), cot[layer])
    picture = jnp.zeros((PROWS, rays), F32)
    for k in range(rays):
        there = lane == pixels[k]
        dpic = jnp.sum(jnp.where(there, cotangent, 0.0), axis=1, keepdims=True)
        value = jnp.where(row < classes, by_ray[k], jnp.where(row == classes, 1.0, 0.0))
        one = weights[k : k + 1, :]
        colour = jnp.sum(value * one, axis=1, keepdims=True)
        picture = jnp.where(there, colour, picture)
        grad_w[k : k + 1, :] = jnp.sum(value * dpic, axis=0, keepdims=True)
        grads[k] = dpic * one
    pic_ref[...] = picture
    grad_weight = grad_w[...]
    carried = grad_weight * weight
    later = jnp.sum(carried, axis=1, keepdims=True) - lane_cumsum(carried)
    grad_optical = grad_weight * passing * fading - later
    slope = jnp.where(pre >= 0.0, 1.0, small) / (1.0 + small)
    density[...] = grad_optical * visible * step * slope
    acc[...] = jnp.zeros_like(acc)
    zero = jnp.zeros((DROWS - PROWS, samples), F32)
    for k in range(rays):
        hot, bases = hots(k)
        grad = jnp.where(row == classes, density[k : k + 1, :], grads[k])
        moved = nt(jnp.concatenate([grad, zero], axis=0).astype(BF), hot)
        for t in range(tiles):
            acc[t, :, pl.ds(bases[t], WINDOW)] += moved[:, t * WINDOW : (t + 1) * WINDOW]
    for t in range(tiles):
        dp_ref[t] = acc[t, :, 0:CAP].astype(BF)


def composite(starts, pixels, owner, rank, view, heads, cot, layer, classes, follow=()):
    tiles, _, slots = heads.shape
    rays, samples = owner.shape
    outs = ((PROWS, rays), (tiles, DROWS, slots))
    return ordered(
        functools.partial(composite_kernel, classes, layer),
        (starts, pixels, owner, rank, view, heads, cot,),
        [sspec(), sspec()] + [whole(x.shape) for x in (owner, rank, view, heads, cot)],
        follow,
        grid=(1,),
        out_shape=(jax.ShapeDtypeStruct(outs[0], F32), jax.ShapeDtypeStruct(outs[1], BF)),
        out_specs=tuple(whole(s) for s in outs),
        scratch_shapes=[
            VMEM((tiles, 2 * PROWS, CAP + WINDOW), F32),
            VMEM((rays, PROWS, samples), F32),
            VMEM((rays, PROWS, samples), F32),
            VMEM((rays, samples), F32),
            VMEM((rays, samples), F32),
            VMEM((rays, samples), F32),
            VMEM((tiles, DROWS, CAP + WINDOW), F32),
        ],
        compiler_params=params(62.5),
        cost_estimate=cost(),
        name="composite",
    )


def add_kernel(parts, out_ref):
    total = parts[0].astype(F32)
    for n in range(1, parts.shape[0]):
        total = total + parts[n].astype(F32)
    total = total.astype(out_ref.dtype)
    for n in range(out_ref.shape[0]):
        out_ref[n] = total


def add_parts(parts, copies, follow=()):
    shape = (copies,) + parts.shape[1:]
    return ordered(
        add_kernel,
        (parts,),
        [whole(parts.shape)],
        follow,
        grid=(1,),
        out_shape=jax.ShapeDtypeStruct(shape, parts.dtype),
        out_specs=whole(shape),
        compiler_params=params(8),
        cost_estimate=cost(),
        name="add_parts",
    )


def hold_kernel(*refs):
    del refs


def hold(values, follow):
    return ordered(
        hold_kernel,
        values,
        [aspec()] * len(values),
        follow,
        out_shape=any_outs(*((x.shape, x.dtype) for x in values)),
        out_specs=(aspec(),) * len(values),
        input_output_aliases={n: n for n in range(len(values))},
        compiler_params=params(62.5),
        cost_estimate=cost(),
        name="hold",
    )


def all_to_all(value, axis):
    return lax.all_to_all(value, axis, split_axis=0, concat_axis=0, tiled=True)


def exchange(first, last):
    devices = lax.axis_size("tile")
    up = [(i, i + 1) for i in range(devices - 1)]
    down = [(i + 1, i) for i in range(devices - 1)]
    return lax.ppermute(last, "tile", up), lax.ppermute(first, "tile", down)


def norm_grads(y, grad, mean, inverse, gains, shifts):
    centred = (y - mean) * inverse
    normal = centred * gains + shifts
    sigma = sigmoid(normal)
    return grad * sigma * (1.0 + normal * (1.0 - sigma)), centred


def finish_back(sums, edges, ups, spare, out_sem):
    rows = edges.shape[1] - 16
    value = sums[...]
    high = value.astype(BF).astype(F32)
    middle = (value - high).astype(BF).astype(F32)
    low = value - high - middle
    tail = jnp.concatenate([high[0:2], middle[0:2], low[0:2], jnp.zeros((10,) + high.shape[1:], F32)], axis=0)
    tail = tail.astype(BF)
    edges[0, rows:, :] = tail
    edges[1, rows:, :] = tail
    spare[...] = tail
    first_ref, last_ref, far_ref = ups
    copies = [
        started(edges.at[0], first_ref, out_sem.at[0]),
        started(edges.at[1], last_ref, out_sem.at[1]),
        started(spare, far_ref, out_sem.at[2]),
    ]
    for copy in copies:
        copy.wait()


def norm_back_kernel(
    layer, count, cot, local, y, total_hbm, gain_hbm, shift_hbm, first_ref, last_ref, far_ref,
    cot_in, local_in, y_in, total, gain, shift, edges, sums, spare, in_sem, out_sem,
):
    planes, rows, _ = cot.shape
    small = [
        started(total_hbm, total, in_sem.at[3 * planes]),
        started(gain_hbm, gain, in_sem.at[3 * planes + 1]),
        started(shift_hbm, shift, in_sem.at[3 * planes + 2]),
    ]

    def in_copies(p):
        return [
            pltpu.make_async_copy(source.at[p], target.at[p], in_sem.at[3 * p + n])
            for n, (source, target) in enumerate(((cot, cot_in), (local, local_in), (y, y_in)))
        ]

    for p in range(planes):
        for copy in in_copies(p):
            copy.start()
    sums[...] = jnp.zeros_like(sums)
    for copy in small:
        copy.wait()
    mean, inverse = moments(total[...], count)
    gains, shifts = row_of(gain, layer), row_of(shift, layer)

    @pl.loop(0, planes)
    def _(p):
        for copy in in_copies(p):
            copy.wait()
        grad = cot_in[p].astype(F32) + local_in[p].astype(F32)
        inner, centred = norm_grads(y_in[p], grad, mean, inverse, gains, shifts)
        add_stats(sums, inner, inner * centred)
        for side, edge in ((0, 0), (1, planes - 1)):

            @pl.when(p == edge)
            def _():
                edges[side, 0:rows, :] = inner.astype(BF)

    finish_back(sums, edges, (first_ref, last_ref, far_ref), spare, out_sem)


def back_shapes(rows, channels):
    return ((rows + 16, channels), BF), ((rows + 16, channels), BF), ((16, channels), BF)


def back_scratch(rows, channels):
    return [VMEM((2, rows + 16, channels), BF), VMEM((8, channels), F32), VMEM((16, channels), BF)]


def norm_back(cot, local, y, total, gain, shift, layer, count, follow=()):
    planes, rows, channels = local.shape
    return ordered(
        functools.partial(norm_back_kernel, layer, count),
        (cot, local, y, total, gain, shift),
        [aspec()] * 6,
        follow,
        out_shape=any_outs(*back_shapes(rows, channels)),
        out_specs=(aspec(),) * 3,
        scratch_shapes=[VMEM(x.shape, x.dtype) for x in (cot, local, y, total, gain, shift)]
        + back_scratch(rows, channels)
        + sems(3 * planes + 3, 3),
        compiler_params=params(62.5),
        cost_estimate=cost(),
        name="norm_back",
    )


def share_back(sent):
    first, last, far = sent
    tiles = lax.axis_size("tile")

    def move(value, by):
        return lax.ppermute(value, "tile", [(i, (i + by) % tiles) for i in range(tiles)])

    return (move(last, 1), move(first, tiles - 1)) + tuple(move(far, n) for n in range(2, tiles - 1))


def turn_kernel(width, block, r_ref, out_ref, turned):
    planes, rows, channels = r_ref.shape
    chosen = out_ref.shape[1]
    pick = iota((chosen, channels), 1) == iota((chosen, channels), 0) + block[0] * chosen
    pick = pick.astype(F32).astype(BF)
    place = iota((chosen, rows), 1)
    on_y, on_z = lax.div(place, width), lax.rem(place, width)
    height = rows // width
    for p in range(planes):
        turned[...] = nt(pick, r_ref[p])
        for b in range(3):
            for c in range(3):
                shift = (b - 1) * width + (c - 1)
                value = turned[...]
                if shift:
                    value = pltpu.roll(value, (-shift) % rows, 1)
                y, z = on_y + (b - 1), on_z + (c - 1)
                inside = (y >= 0) & (y < height) & (z >= 0) & (z < width)
                value = jnp.where(inside, value, 0.0).astype(BF)
                for a in range(3):
                    target = p - a
                    if 0 <= target < planes - 2:
                        out_ref[9 * a + 3 * b + c, :, target * rows : (target + 1) * rows] = value


def turn(block, rounded, width, blocks, follow=()):
    planes, rows, channels = rounded.shape
    chosen = channels // blocks
    shape = (27, chosen, (planes - 2) * rows)
    return ordered(
        functools.partial(turn_kernel, width),
        (block, rounded,),
        [sspec(), whole(rounded.shape)],
        follow,
        grid=(1,),
        out_shape=jax.ShapeDtypeStruct(shape, BF),
        out_specs=whole(shape),
        scratch_shapes=[VMEM((chosen, rows), F32)],
        compiler_params=params(62.5),
        cost_estimate=cost(),
        name="turn",
    )


def weight_grad_kernel(layer, count, first, parts, tiles, spots, taps_hbm, *refs):
    grads, refs = refs[:parts], refs[parts:]
    if first:
        y, refs = refs[0], refs[1:]
        y_before, y_after = y.at[pl.ds(0, 1)], y.at[pl.ds(y.shape[0] - 1, 1)]
    else:
        y, y_before, y_after, refs = refs[0], refs[1], refs[2], refs[3:]
    own_far, others, refs = refs[0], refs[1:tiles], refs[tiles:]
    total_hbm, gain_hbm, shift_hbm, refs = *refs[:3], refs[3:]
    dy_ref, wg_ref, back_ref, refs = *refs[:3], refs[3:]
    grads_in, refs = refs[:parts], refs[parts:]
    (taps_in, y_in, y_halo, dn_halo, rest, back, total, gain, shift, dy_buf, dy_rows, wg_buf, in_sem,
     out_sem) = refs
    planes, rows, channels = grads[0].shape
    spare = (parts + 1) * planes
    lists = [
        (total_hbm.at[:, pl.ds(0, 8), :], total),
        (gain_hbm, gain),
        (shift_hbm, shift),
        (y_before, y_halo.at[pl.ds(0, 1)]),
        (y_after, y_halo.at[pl.ds(1, 1)]),
        (others[0], dn_halo.at[0]),
        (others[1], dn_halo.at[1]),
        (own_far, rest.at[0]),
    ] + [(other, rest.at[n + 1]) for n, other in enumerate(others[2:])]
    small = [
        started(source, target, in_sem.at[spare + n]) for n, (source, target) in enumerate(lists)
    ]

    def in_copies(p):
        copies = [pltpu.make_async_copy(y.at[p + first], y_in.at[p], in_sem.at[(parts + 1) * p])]
        for n in range(parts):
            copies.append(
                pltpu.make_async_copy(
                    grads[n].at[p], grads_in[n].at[p], in_sem.at[(parts + 1) * p + 1 + n]
                )
            )
        return copies

    for p in range(planes):
        for copy in in_copies(p):
            copy.start()
    heavy = started(taps_hbm, taps_in, in_sem.at[spare + len(lists)])
    for copy in small:
        copy.wait()
    tile = spots[2]
    tails = [rest[0], dn_halo[0, rows:, :], dn_halo[1, rows:, :]]
    tails += [rest[n] for n in range(1, rest.shape[0])]
    for by, tail in zip([0, 1, tiles - 1] + list(range(2, tiles - 1)), tails):
        value = tail.astype(F32)
        value = value[0:2] + value[2:4] + value[4:6]
        back[lax.rem(tile + tiles - by, tiles), 0:2, :] = value
    mean, inverse = moments(total[...], count)
    gains, shifts = row_of(gain, layer), row_of(shift, layer)
    scale = inverse * gains
    both = back[0, 0:2, :]
    for t in range(1, tiles):
        both = both + back[t, 0:2, :]
    back[0, 0:2, :] = both
    sums = both / count

    def finish(inner, centred):
        return scale * (inner - sums[0:1, :] - centred * sums[1:2, :])

    for side, place in ((0, 0), (1, planes + 1)):
        centred = (y_halo[side].astype(F32) - mean) * inverse
        value = finish(dn_halo[side, 0:rows, :].astype(F32), centred)
        dy_buf[place] = jnp.where(spots[side] > 0, value, 0.0).astype(BF)

    @pl.loop(0, planes)
    def _(p):
        for copy in in_copies(p):
            copy.wait()
        grad = grads_in[0][p].astype(F32)
        for n in range(1, parts):
            grad = grad + grads_in[n][p].astype(F32)
        value = finish(*norm_grads(y_in[p], grad, mean, inverse, gains, shifts)).astype(BF)
        dy_buf[p + 1] = value
        dy_rows[pl.ds(pl.multiple_of(p * rows, rows), rows), :] = value

    done = [
        started(dy_buf, dy_ref, out_sem.at[0]),
        started(back.at[0, pl.ds(0, 2), :], back_ref, out_sem.at[2]),
    ]
    heavy.wait()
    wg_buf[...] = nn(taps_in[...], dy_rows[...]).astype(BF)
    done.append(started(wg_buf, wg_ref, out_sem.at[1]))
    for copy in done:
        copy.wait()


def weight_grad(
    spots, taps_t, grads, y, y_halo, far, others, total, gain, shift, layer, count, follow=()
):
    planes, rows, channels = grads[0].shape
    wide = taps_t.shape[0]
    tiles = len(others) + 1
    ext = (planes + 2, rows, channels)
    own = (planes, rows, channels)
    operands = (taps_t,) + tuple(grads) + (y,) + tuple(y_halo) + (far,) + tuple(others)
    operands += (total, gain, shift)
    return ordered(
        functools.partial(weight_grad_kernel, layer, count, 0 if y_halo else 1, len(grads), tiles),
        (spots,) + operands,
        [sspec()] + [aspec()] * len(operands),
        follow,
        out_shape=any_outs((ext, BF), ((wide, channels), BF), ((2, channels), F32)),
        out_specs=(aspec(),) * 3,
        scratch_shapes=[VMEM(x.shape, x.dtype) for x in grads]
        + [
            VMEM(taps_t.shape, BF),
            VMEM(own, F32),
            VMEM((2, rows, channels), BF if y_halo else F32),
            VMEM((2, rows + 16, channels), BF),
            VMEM((tiles - 2, 16, channels), BF),
            VMEM((tiles, 8, channels), F32),
            VMEM((tiles, 8, channels), F32),
            VMEM(gain.shape, F32),
            VMEM(gain.shape, F32),
            VMEM(ext, BF),
            VMEM((planes * rows, channels), BF),
            VMEM((wide, channels), BF),
        ]
        + sems((len(grads) + 1) * planes + 8 + tiles, 3),
        compiler_params=params(62.5),
        cost_estimate=cost(),
        name="weight_grad",
    )


def conv_back_kernel(width, layer, count, parts, dy, w_hbm, *refs):
    more = count is not None
    grads, refs = refs[:parts], refs[parts:]
    if more:
        y, total_hbm, gain_hbm, shift_hbm, refs = *refs[:4], refs[4:]
    out_ref, refs = refs[0], refs[1:]
    if more:
        sent, refs = refs[:3], refs[3:]
    grads_in, refs = refs[:parts], refs[parts:]
    raw, xs, weight, out_buf, in_sem, w_sem, out_sem, refs = *refs[:7], refs[7:]
    ext_planes, rows, channels = dy.shape
    planes = ext_planes - 2
    group = planes // 2
    pairs = 2
    each = parts + 1
    body = started(dy, raw, in_sem.at[each * pairs])
    heavy = [
        started(
            w_hbm.at[layer, pl.ds((26 - o) * channels, channels), :],
            weight.at[:, pl.ds(o * channels, channels)],
            w_sem.at[o],
        )
        for o in range(27)
    ]
    small = []
    if more:
        y_in, total, gain, shift, edges, sums, spare, back_sem = refs
        small = [
            started(source, target, in_sem.at[each * pairs + 1 + n])
            for n, (source, target) in enumerate(
                ((total_hbm.at[:, pl.ds(0, 8), :], total), (gain_hbm, gain), (shift_hbm, shift))
            )
        ]
        sums[...] = jnp.zeros_like(sums)

    def in_copies(i):
        two = pl.ds(group * i, group)
        copies = [
            pltpu.make_async_copy(grads[n].at[two], grads_in[n].at[two], in_sem.at[each * i + n])
            for n in range(parts)
        ]
        if more:
            copies.append(
                pltpu.make_async_copy(
                    y.at[pl.ds(group * i + 1, group)], y_in.at[two], in_sem.at[each * i + parts]
                )
            )
        return copies

    def out_copy(i):
        two = pl.ds(group * i, group)
        return pltpu.make_async_copy(out_buf.at[two], out_ref.at[two], out_sem.at[i])

    for i in range(pairs):
        for copy in in_copies(i):
            copy.start()
    clear_edges(xs, width, rows)
    body.wait()

    @pl.loop(0, ext_planes)
    def _(p):
        put_plane(xs, p, raw[p].astype(F32), width)

    for copy in small + heavy:
        copy.wait()
    if more:
        mean, inverse = moments(total[...], count)
        gains, shifts = row_of(gain, layer - 1), row_of(shift, layer - 1)

    @pl.loop(0, pairs)
    def _(i):
        part = nt(tap_group(xs, group * i, group, width, rows), weight[...])
        for copy in in_copies(i):
            copy.wait()
        for n_plane in range(group):
            p = group * i + n_plane
            value = part[n_plane * rows : (n_plane + 1) * rows]
            for n in range(parts):
                value = value + grads_in[n][p].astype(F32)
            out_buf[p] = value
            if more:
                inner, centred = norm_grads(y_in[p], value, mean, inverse, gains, shifts)
                add_stats(sums, inner, inner * centred)

                for side, near in ((0, 0), (1, group - 1)):
                    if n_plane == near:

                        @pl.when(p == side * (planes - 1))
                        def _():
                            edges[side, 0:rows, :] = inner.astype(BF)

        out_copy(i).start()

    if more:
        finish_back(sums, edges, sent, spare, back_sem)
    for i in range(pairs):
        out_copy(i).wait()


def conv_back(dy, grads, weights, layer, width, norm=None, follow=()):
    ext_planes, rows, channels = dy.shape
    own = (ext_planes - 2, rows, channels)
    pairs = 2
    outs, extra, scratch = [(own, F32)], (), []
    if norm is not None:
        y, total, gain, shift, count = norm
        extra = (y, total, gain, shift)
        outs += list(back_shapes(rows, channels))
        scratch = [VMEM(own, F32), VMEM((total.shape[0], 8, channels), F32)]
        scratch += [VMEM(gain.shape, F32), VMEM(gain.shape, F32)]
        scratch += back_scratch(rows, channels) + sems(3)
    else:
        count = None
    return ordered(
        functools.partial(conv_back_kernel, width, layer, count, len(grads)),
        (dy, weights) + tuple(grads) + extra,
        [aspec()] * (2 + len(grads) + len(extra)),
        follow,
        out_shape=any_outs(*outs),
        out_specs=(aspec(),) * len(outs),
        scratch_shapes=[VMEM(x.shape, x.dtype) for x in grads]
        + [VMEM(dy.shape, BF)]
        + conv_scratch(ext_planes, rows, width, channels, True)
        + [VMEM(own, F32)]
        + sems(pairs * (len(grads) + 1) + 4, 27, pairs)
        + scratch,
        compiler_params=params(62.5),
        cost_estimate=cost(),
        name="conv_back",
    )


GROUP = 9


def place_kernel(part, *refs):
    out_ref = refs[-1]
    blocks, offsets, chosen, _ = part.shape
    for o in range(offsets):
        for b in range(blocks):
            out_ref[0, o, b * chosen : (b + 1) * chosen, :] = part[b, o].astype(F32)


def place(parts, layer, layers, kept, follow=()):
    blocks, offsets, chosen, channels = parts.shape
    shape = (layers, offsets, blocks * chosen, channels)
    return ordered(
        place_kernel,
        (parts,) + kept,
        [pl.BlockSpec((blocks, GROUP, chosen, channels), lambda o: (0, o, 0, 0))]
        + [aspec()] * len(kept),
        follow,
        grid=(offsets // GROUP,),
        out_shape=jax.ShapeDtypeStruct(shape, F32),
        out_specs=pl.BlockSpec((1, GROUP) + shape[2:], lambda o: (layer, o, 0, 0)),
        input_output_aliases={1: 0} if kept else {},
        compiler_params=params(62.5),
        cost_estimate=cost(),
        name="place",
    )


def per_device(
    volume,
    sample_cells,
    sample_fracs,
    view_mask,
    pixel_of_ray,
    conv_weight,
    norm_gain,
    norm_shift,
    hidden_weight,
    hidden_bias,
    density_weight,
    density_bias,
    semantic_weight,
    semantic_bias,
    render_cotangent,
    volume_cotangent,
):
    extent = volume.shape[:3]
    depth, height, width, channels = volume.shape
    rows = height * width
    voxels = depth * rows
    tiles = lax.axis_size("tile")
    ray_devices = lax.axis_size("ray")
    count = float(voxels * tiles)
    rays, samples = sample_cells.shape
    classes = semantic_weight.shape[2]
    layers = conv_weight.shape[0]
    blocks = min(BLOCKS, ray_devices)
    chosen = channels // blocks
    tile, ray = lax.axis_index("tile"), lax.axis_index("ray")
    block = lax.rem(ray, blocks).astype(jnp.int32).reshape(1)

    own = volume.reshape(depth, rows, channels)
    before, after = exchange(own[:2], own[-2:])
    flags = jnp.stack([tile > 0, tile < tiles - 1]).astype(jnp.int32)

    owner_of = lax.div(sample_cells, voxels)
    held = owner_of[None] == jnp.arange(tiles, dtype=jnp.int32)[:, None, None]
    earlier = jnp.arange(rays)[None, :] < jnp.arange(rays)[:, None]
    starts = jnp.sum(
        (held[:, None, :, :] & earlier[None, :, :, None]).astype(jnp.int32), axis=(2, 3)
    ).reshape(tiles * rays)
    pixels = pixel_of_ray[0]
    buffer, owner, rank = prepare(extent, starts, sample_cells, sample_fracs, tiles, channels)

    weights = conv_weight.reshape(layers, 27 * channels, channels)
    mlp = (
        hidden_weight,
        hidden_bias,
        semantic_weight,
        density_weight,
        semantic_bias,
        density_bias[None],
    )
    y_ext, v_ext, mixed = conv_first(before, own, after, buffer, weights, 0, width)
    total = received = all_to_all(mixed, "tile")
    taps_first = turn(block, v_ext, width, blocks)
    v_next, r_ext, y_next, stat, y_first, y_last = conv_next(
        flags, y_ext, v_ext, total, norm_gain, norm_shift, weights, 0, width, count,
        follow=(taps_first,),
    )
    total_next = all_to_all(stat, "tile")
    heads, feature, act, slope = sample(extent, received, (r_ext, 1), 0, mlp)
    heads_last, feature_last, act_last, slope_last, r_last = sample(
        extent, received, (y_next, v_next, total_next, norm_gain, norm_shift), 1, mlp, count,
        follow=(heads,),
    )

    def draw(heads, layer, follow):
        return composite(
            starts, pixels, owner, rank, view_mask, all_to_all(heads, "tile"), render_cotangent,
            layer, classes, follow=follow,
        )

    picture, grad_heads = draw(heads, 0, (heads_last,))
    picture_last, grad_heads_last = draw(heads_last, 1, (grad_heads,))
    shares = (ray_devices, voxels // ray_devices, channels)
    planes = (depth, rows, channels)
    local, pack = sample_back(
        extent, 0, received, all_to_all(grad_heads, "tile"), feature, act, slope, mlp, (),
        follow=(grad_heads_last,),
    )
    sums = lax.psum(local, "ray").reshape(planes)
    local_last, packed = sample_back(
        extent, 1, received, all_to_all(grad_heads_last, "tile"), feature_last, act_last,
        slope_last, mlp, (pack,), follow=(local,),
    )
    parts_last = all_to_all(local_last.reshape(shares), "ray")
    taps_next = turn(block, r_ext, width, blocks, follow=(local_last,))
    copies_last = add_parts(parts_last, ray_devices, follow=(taps_next,))
    sums_last = all_to_all(copies_last, "ray").reshape(planes)
    y_edges = exchange(*hold((y_first, y_last), (copies_last,)))

    cot = volume_cotangent.reshape(planes)
    wide_taps = (27 * chosen, voxels)
    spots = jnp.stack([tile > 0, tile < tiles - 1, tile]).astype(jnp.int32)
    sent = norm_back(
        cot, sums_last, y_next, total_next, norm_gain, norm_shift, 1, count,
        follow=y_edges,
    )
    dy, part, back_last = weight_grad(
        spots, taps_next.reshape(wide_taps), (cot, sums_last), y_next, y_edges, sent[2],
        share_back(sent), total_next, norm_gain, norm_shift, 1, count,
    )
    shard = lax.psum_scatter(part, "tile", scatter_dimension=0, tiled=True)
    (held,) = hold((packed,), (sums,))
    packed = all_to_all(held.reshape(ray_devices, -1, channels), "ray")
    grad, *sent = conv_back(
        dy, (cot, sums_last, sums), weights, 1, width,
        (y_ext, total, norm_gain, norm_shift, count), follow=(held,),
    )
    packed = add_parts(packed, tiles, follow=(sent[2],))
    others = share_back(sent)
    shards = add_parts(shard[None], tiles, follow=others)
    shard = all_to_all(shards, "tile")

    dy, part, back = weight_grad(
        spots, taps_first.reshape(wide_taps), (grad,), y_ext, (), sent[2], others, total,
        norm_gain, norm_shift, 0, count, follow=(shards, packed),
    )
    (part,) = hold((part,), (shard,))
    parts = all_to_all(part.reshape(tiles, 27 * chosen // tiles, channels), "tile")
    (shard,) = hold((shard,), (part,))
    copies = add_parts(parts, tiles, follow=(shard,))
    slices = all_to_all(copies, "tile")

    def gather(slices):
        whole_grad = lax.all_gather(slices, "ray", axis=0, tiled=True)
        return whole_grad.reshape(-1, 27, chosen, channels)[:blocks]

    conv_grad = place(gather(shard), 1, layers, (), follow=(slices,))
    packed = all_to_all(*hold((packed,), (slices,)), "tile")
    (grad,) = conv_back(dy, (grad,), weights, 0, width, follow=(conv_grad,))
    packed = all_to_all(add_parts(packed, ray_devices, follow=(grad,)), "ray")
    packed = packed.reshape(layers, PACK, channels)[::-1]
    conv_grad = place(gather(slices), 0, layers, (conv_grad,), follow=(grad,))

    at = channels + 16
    heads = packed[:, at : at + DROWS]
    head_bias = packed[:, at + DROWS, :DROWS]
    return (
        jnp.swapaxes(jnp.stack([picture, picture_last])[:, : classes + 1], 1, 2),
        r_last.reshape(volume.shape),
        grad.reshape(volume.shape),
        conv_grad,
        jnp.stack([back, back_last])[:, 1],
        jnp.stack([back, back_last])[:, 0],
        packed[:, :channels],
        packed[:, channels],
        heads[:, classes],
        head_bias[:, classes],
        jnp.swapaxes(heads[:, :classes], 1, 2),
        head_bias[:, :classes],
    )


def solution(mesh):
    in_specs = (
        P("tile", None, None, None),
        P(("ray", "tile"), None),
        P(None, ("ray", "tile"), None),
        P(("ray", "tile"), None),
        P(("ray", "tile"), None),
        P(),
        P(),
        P(),
        P(),
        P(),
        P(),
        P(),
        P(),
        P(),
        P(None, ("ray", "tile"), None),
        P("tile", None, None, None),
    )
    out_specs = (
        P(None, ("ray", "tile"), None),
        P("tile", None, None, None),
        P("tile", None, None, None),
        P(),
        P(),
        P(),
        P(),
        P(),
        P(),
        P(),
        P(),
        P(),
    )
    return jax.shard_map(
        per_device, mesh=mesh, in_specs=in_specs, out_specs=out_specs, check_vma=False
    )
```

```python
import functools

import jax
import jax.numpy as jnp
from jax import lax
from jax.experimental import pallas as pl
from jax.experimental.pallas import tpu as pltpu
from jax.sharding import PartitionSpec as P

CAP = 768
WINDOW = 256
LANES = 128
PROWS = 24
DROWS = 32
COORDS = 8
BLOCKS = 8
PACK = 320
epsilon = 1e-05
MIB = 1024 * 1024

BF = jnp.bfloat16
F32 = jnp.float32
VMEM = pltpu.VMEM
SMEM = pltpu.SMEM


def nn(left, right):
    return jnp.dot(left, right, preferred_element_type=F32)


def nt(left, right):
    return lax.dot_general(left, right, (((1,), (1,)), ((), ())), preferred_element_type=F32)


def iota(shape, dim):
    return lax.broadcasted_iota(jnp.int32, shape, dim)


def whole(shape):
    return pl.BlockSpec(shape, lambda *_: (0,) * len(shape))


def planes_of(step, shape, first=0):
    return pl.BlockSpec((step,) + shape[1:], lambda i: (i + first // step,) + (0,) * (len(shape) - 1))


def sspec():
    return pl.BlockSpec(memory_space=SMEM)


def aspec():
    return pl.BlockSpec(memory_space=pl.ANY)


def hspec():
    return pl.BlockSpec(memory_space=pltpu.HBM)


def ordered(kernel, operands, in_specs, follow, **options):
    count, skip = len(operands), len(follow)

    def body(*refs):
        kernel(*refs[:count], *refs[count + skip :])

    return pl.pallas_call(body, in_specs=list(in_specs) + [aspec()] * skip, **options)(
        *operands, *follow
    )


def params(mib):
    return pltpu.CompilerParams(vmem_limit_bytes=int(mib * MIB))


def cost():
    return pl.CostEstimate(flops=1, bytes_accessed=1, transcendentals=0)


def lane_cumsum(x):
    lane = iota(x.shape, 1)
    shift = 1
    while shift < x.shape[1]:
        x = x + jnp.where(lane >= shift, pltpu.roll(x, shift, 1), 0.0)
        shift *= 2
    return x


def window_onehots(starts, owner_row, rank_row, ray, rays, tiles):
    rows = iota((WINDOW, rank_row.shape[1]), 0)
    hots, bases = [], []
    for t in range(tiles):
        start = starts[t * rays + ray]
        base = (start // LANES) * LANES
        place = jnp.where(owner_row == t, rank_row + (start - base), -1)
        hots.append((rows == place).astype(F32).astype(BF))
        bases.append(pl.multiple_of(base, LANES))
    return jnp.concatenate(hots, axis=0), bases


def prep_kernel(extent, starts, cells_ref, fracs_ref, out_ref, owner_ref, rank_ref, vals, acc):
    depth, height, width = extent
    tiles = out_ref.shape[0]
    rays, samples = cells_ref.shape
    cells = cells_ref[...]
    voxels = depth * height * width
    owner = lax.div(cells, voxels)
    local = cells - owner * voxels
    base_x = lax.div(local, height * width)
    inner = local - base_x * (height * width)
    base_y = lax.div(inner, width)
    base_z = inner - base_y * width
    rank = jnp.zeros(cells.shape, F32)
    for t in range(tiles):
        mine = owner == t
        rank = jnp.where(mine, lane_cumsum(jnp.where(mine, 1.0, 0.0)) - 1.0, rank)
    owner_ref[...] = owner
    rank_ref[...] = rank.astype(jnp.int32)
    vals[...] = jnp.zeros_like(vals)
    rows = [(base_x + 1).astype(F32), base_y.astype(F32), base_z.astype(F32)]
    low = []
    for d in range(3):
        frac = fracs_ref[d]
        high = frac.astype(BF).astype(F32)
        rows.append(high)
        low.append(frac - high)
    rows += low
    for number, row in enumerate(rows):
        for k in range(rays):
            vals[number : number + 1, k * samples : (k + 1) * samples] = row[k : k + 1]
    acc[...] = jnp.zeros_like(acc)
    for k in range(rays):
        hot, bases = window_onehots(
            starts, owner_ref[k : k + 1, :], rank_ref[k : k + 1, :], k, rays, tiles
        )
        moved = nt(vals[:, k * samples : (k + 1) * samples].astype(BF), hot)
        for t in range(tiles):
            acc[t, :, pl.ds(bases[t], WINDOW)] += moved[:, t * WINDOW : (t + 1) * WINDOW]
    out_ref[...] = jnp.zeros_like(out_ref)
    wide = out_ref.shape[2]
    lines = CAP // wide
    for n in range(lines):
        part = slice(n * wide, (n + 1) * wide)
        for r in range(6):
            value = acc[:, r : r + 1, part]
            if r >= 3:
                value = value + acc[:, r + 3 : r + 4, part]
            out_ref[:, r * lines + n : r * lines + n + 1, :] = value


def prepare(extent, starts, cells, fracs, tiles, wide, follow=()):
    rays, samples = cells.shape
    outs = ((tiles, COORDS * CAP // wide, wide), (rays, samples), (rays, samples))
    return ordered(
        functools.partial(prep_kernel, extent),
        (starts, cells, fracs,),
        [sspec(), whole(cells.shape), whole(fracs.shape)],
        follow,
        grid=(1,),
        out_shape=(
            jax.ShapeDtypeStruct(outs[0], F32),
            jax.ShapeDtypeStruct(outs[1], jnp.int32),
            jax.ShapeDtypeStruct(outs[2], jnp.int32),
        ),
        out_specs=tuple(whole(s) for s in outs),
        scratch_shapes=[VMEM((16, rays * samples), F32), VMEM((tiles, 16, CAP + WINDOW), F32)],
        compiler_params=params(62.5),
        cost_estimate=cost(),
        name="prep",
    )


def started(source, target, sem):
    copy = pltpu.make_async_copy(source, target, sem)
    copy.start()
    return copy


def put_plane(xs, p, value, width):
    rows, channels = value.shape
    along = lax.rem(iota(value.shape, 0), width)
    left = jnp.where(along == 0, 0.0, pltpu.roll(value, 1, 0))
    right = jnp.where(along == width - 1, 0.0, pltpu.roll(value, rows - 1, 0))
    xs[p, width : width + rows, 0:channels] = left.astype(BF)
    xs[p, width : width + rows, channels : 2 * channels] = value.astype(BF)
    xs[p, width : width + rows, 2 * channels : 3 * channels] = right.astype(BF)


def clear_edges(xs, width, rows):
    planes, _, wide = xs.shape
    for p in range(planes):
        xs[p, 0:width, :] = jnp.zeros((width, wide), BF)
        xs[p, width + rows : 2 * width + rows, :] = jnp.zeros((width, wide), BF)


def taps(xs, p, width, rows):
    return jnp.concatenate(
        [xs[p + a, b * width : b * width + rows, :] for a in range(3) for b in range(3)], axis=1
    )


def tap_group(xs, first, count, width, rows):
    return jnp.concatenate([taps(xs, first + n, width, rows) for n in range(count)], axis=0)


def add_stats(sums, one, two):
    sums[0:1, :] += jnp.sum(one, axis=0, keepdims=True)
    sums[1:2, :] += jnp.sum(two, axis=0, keepdims=True)


def conv_scratch(planes, rows, width, channels, turned):
    shape = (channels, 27 * channels) if turned else (27 * channels, channels)
    return [VMEM((planes, rows + 2 * width, 3 * channels), BF), VMEM(shape, BF)]


def sems(*counts):
    return [pltpu.SemaphoreType.DMA((n,)) for n in counts]


def any_outs(*shapes):
    return tuple(jax.ShapeDtypeStruct(shape, dtype) for shape, dtype in shapes)


def conv_first_kernel(
    width, layer, before, own, after, coords, w_hbm, y_ref, v_ref, mix_ref,
    raw, xs, weight, y_buf, mix, in_sem, out_sem,
):
    planes, rows, channels = own.shape
    pairs = planes // 2 + 1
    body = [
        started(own.at[pl.ds(2 * i, 2)], raw.at[pl.ds(2 * i + 2, 2)], in_sem.at[i])
        for i in range(planes // 2)
    ]
    ends = [
        started(before, raw.at[pl.ds(0, 2)], in_sem.at[pairs]),
        started(after, raw.at[pl.ds(planes + 2, 2)], in_sem.at[pairs + 1]),
    ]
    heavy = started(w_hbm.at[layer], weight, in_sem.at[pairs + 2])
    light = started(coords, mix.at[:, pl.ds(8, coords.shape[1]), :], in_sem.at[pairs + 3])
    clear_edges(xs, width, rows)
    mix[:, 0:8, :] = jnp.zeros((mix.shape[0], 8, channels), F32)
    for copy in body + ends:
        copy.wait()

    @pl.loop(0, planes + 4)
    def _(p):
        put_plane(xs, p, raw[p].astype(F32), width)

    done = [started(raw.at[pl.ds(1, planes + 2)], v_ref, out_sem.at[pairs])]
    light.wait()
    heavy.wait()

    group = (planes + 2) // 2

    def out_copy(i):
        some = pl.ds(group * i, group)
        return pltpu.make_async_copy(y_buf.at[some], y_ref.at[some], out_sem.at[i])

    @pl.loop(0, 2)
    def _(i):
        p = group * i
        part = nn(tap_group(xs, p, group, width, rows), weight[...])
        for n in range(group):
            y_buf[p + n] = part[n * rows : (n + 1) * rows]
        out_copy(i).start()
        inner = part[rows : (group - 1) * rows]
        add_stats(mix.at[0], inner, inner * inner)
        edge = jnp.where(i == 0, part[(group - 1) * rows :], part[:rows])
        add_stats(mix.at[0], edge, edge * edge)

    for t in range(1, mix.shape[0]):
        mix[t, 0:8, :] = mix[0, 0:8, :]
    done.append(started(mix, mix_ref, out_sem.at[pairs + 1]))
    for copy in done:
        copy.wait()
    for i in range(2):
        out_copy(i).wait()


def conv_first(before, own, after, coords, weights, layer, width):
    planes, rows, channels = own.shape
    ext = (planes + 2, rows, channels)
    tiles, lines, _ = coords.shape
    pairs = planes // 2 + 1
    return ordered(
        functools.partial(conv_first_kernel, width, layer),
        (before, own, after, coords, weights),
        [aspec()] * 5,
        (),
        out_shape=any_outs((ext, F32), (ext, BF), ((tiles, 8 + lines, channels), F32)),
        out_specs=(aspec(),) * 3,
        scratch_shapes=[VMEM((planes + 4, rows, channels), BF)]
        + conv_scratch(planes + 4, rows, width, channels, False)
        + [VMEM(ext, F32), VMEM((tiles, 8 + lines, channels), F32)]
        + sems(pairs + 4, pairs + 2),
        compiler_params=params(62.5),
        cost_estimate=cost(),
        name="conv_first",
    )


def moments(total, count):
    both = jnp.sum(total, axis=0)
    mean = both[0:1, :] / count
    return mean, lax.rsqrt(both[1:2, :] / count - mean * mean + epsilon)


def row_of(ref, layer):
    return ref[layer : layer + 1, :]


def silu(value):
    return value * (1.0 / (1.0 + jnp.exp(-value)))


def conv_next_kernel(
    width, layer, count, flags, y_ext, v_ext, total_hbm, gain_hbm, shift_hbm, w_hbm,
    v_ref, r_ref, y_ref, stat_ref, first_ref, last_ref,
    y_in, v_in, total, gain, shift, xs, weight, v_buf, r_buf, y_buf, edges, stat, in_sem, out_sem,
):
    ext_planes, rows, channels = y_ext.shape
    pairs = ext_planes // 2
    small = [
        started(total_hbm.at[:, pl.ds(0, 8), :], total, in_sem.at[2 * pairs]),
        started(gain_hbm, gain, in_sem.at[2 * pairs + 1]),
        started(shift_hbm, shift, in_sem.at[2 * pairs + 2]),
    ]
    def in_copies(i):
        two = pl.ds(2 * i, 2)
        return (
            pltpu.make_async_copy(y_ext.at[two], y_in.at[two], in_sem.at[2 * i]),
            pltpu.make_async_copy(v_ext.at[two], v_in.at[two], in_sem.at[2 * i + 1]),
        )

    def mid_copies(i):
        two = pl.ds(2 * i, 2)
        return (
            pltpu.make_async_copy(v_buf.at[two], v_ref.at[two], out_sem.at[3 * i]),
            pltpu.make_async_copy(r_buf.at[two], r_ref.at[two], out_sem.at[3 * i + 1]),
        )

    def out_copy(i):
        two = pl.ds(2 * i - 2, 2)
        return pltpu.make_async_copy(y_buf.at[two], y_ref.at[two], out_sem.at[3 * i + 2])

    for i in range(pairs):
        for copy in in_copies(i):
            copy.start()
    heavy = started(w_hbm.at[layer + 1], weight, in_sem.at[2 * pairs + 3])
    clear_edges(xs, width, rows)
    stat[...] = jnp.zeros_like(stat)
    for copy in small:
        copy.wait()
    mean, inverse = moments(total[...], count)
    gains, shifts = row_of(gain, layer), row_of(shift, layer)

    @pl.loop(0, pairs)
    def _(i):
        for copy in in_copies(i):
            copy.wait()
        for side in range(2):
            p = 2 * i + side
            fresh = v_in[p].astype(F32) + silu((y_in[p] - mean) * inverse * gains + shifts)
            v_buf[p] = fresh
            outside = (p == side * (ext_planes - 1)) & (flags[side] == 0)
            rounded = jnp.where(outside, 0.0, fresh).astype(BF)
            r_buf[p] = rounded
            put_plane(xs, p, rounded.astype(F32), width)
        for copy in mid_copies(i):
            copy.start()

        @pl.when(i == 1)
        def _():
            heavy.wait()

        @pl.when(i > 0)
        def _():
            p = 2 * i - 2
            part = nn(tap_group(xs, p, 2, width, rows), weight[...])
            y_buf[p] = part[:rows]
            y_buf[p + 1] = part[rows:]
            add_stats(stat.at[0], part, part * part)
            out_copy(i).start()

    edges[0] = y_buf[0].astype(BF)
    edges[1] = y_buf[ext_planes - 3].astype(BF)
    for t in range(1, stat.shape[0]):
        stat[t] = stat[0]
    done = [
        started(stat, stat_ref, out_sem.at[2]),
        started(edges.at[pl.ds(0, 1)], first_ref, out_sem.at[3 * pairs]),
        started(edges.at[pl.ds(1, 1)], last_ref, out_sem.at[3 * pairs + 1]),
    ]
    for i in range(pairs):
        done += list(mid_copies(i)) + ([out_copy(i)] if i else [])
    for copy in done:
        copy.wait()


def conv_next(flags, y_ext, v_ext, total, gain, shift, weights, layer, width, count, follow=()):
    ext_planes, rows, channels = y_ext.shape
    ext = y_ext.shape
    inner = (ext_planes - 2, rows, channels)
    stat = (total.shape[0], 8, channels)
    pairs = ext_planes // 2
    edge = (1, rows, channels)
    return ordered(
        functools.partial(conv_next_kernel, width, layer, count),
        (flags, y_ext, v_ext, total, gain, shift, weights),
        [sspec()] + [aspec()] * 6,
        follow,
        out_shape=any_outs((ext, F32), (ext, BF), (inner, F32), (stat, F32), (edge, BF), (edge, BF)),
        out_specs=(aspec(),) * 6,
        scratch_shapes=[VMEM(ext, F32), VMEM(ext, BF), VMEM(stat, F32)]
        + [VMEM(gain.shape, F32)] * 2
        + conv_scratch(ext_planes, rows, width, channels, False)
        + [VMEM(ext, F32), VMEM(ext, BF), VMEM(inner, F32)]
        + [VMEM((2, rows, channels), BF), VMEM(stat, F32)]
        + sems(2 * pairs + 4, 3 * pairs + 2),
        compiler_params=params(62.5),
        cost_estimate=cost(),
        name="conv_next",
    )


def fill_weights(table, coords, extent):
    depth, height, width = extent
    samples = coords[0].shape[1]

    def along(base, frac, size):
        grid = iota((size, samples), 0).astype(F32)
        lower = jnp.where(grid == base, 1.0 - frac, 0.0)
        return lower + jnp.where(grid == base + 1.0, frac, 0.0)

    on_x = along(coords[0] - 1.0, coords[3], depth)
    on_y = along(coords[1], coords[4], height)
    on_z = along(coords[2], coords[5], width)
    for x in range(depth):
        on_xy = on_x[x : x + 1] * on_y
        for y in range(height):
            row = (x * height + y) * width
            table[row : row + width, :] = (on_xy[y : y + 1] * on_z).astype(BF)


def diagonal(rows, columns):
    return iota((rows, columns), 0) == iota((rows, columns), 1)


def identity(rows, columns):
    return diagonal(rows, columns).astype(F32).astype(BF)


def head_rows(semantic, density, rows):
    channels, classes = semantic.shape
    turned = nt(identity(rows, classes), semantic)
    return jnp.where(iota((rows, channels), 0) == classes, density.astype(F32), turned).astype(BF)


def column(row, rows):
    return jnp.sum(jnp.where(diagonal(rows, row.shape[1]), row, 0.0), axis=1, keepdims=True)


def coord_rows(block, slots):
    lines = slots // block.shape[1]
    return [
        jnp.concatenate(
            [block[8 + r * lines + n : 9 + r * lines + n, :] for n in range(lines)], axis=1
        )
        for r in range(6)
    ]


def sample_kernel(
    extent, layer, first, count, coords, *refs
):
    if count is None:
        r_hbm, refs = refs[0], refs[1:]
    else:
        y_hbm, v_hbm, total_hbm, gain, shift, refs = refs[0], refs[1], refs[2], refs[3], refs[4], refs[5:]
    hidden, hidden_b, semantic, density, semantic_b, density_b, refs = *refs[:6], refs[6:]
    p_ref, f_ref, g_ref, s_ref, refs = *refs[:4], refs[4:]
    if count is not None:
        r_out, refs = refs[0], refs[1:]
    turned, table, rounded, hidden_t, bias, head_t, head_b, sem, refs = *refs[:8], refs[8:]
    channels = turned.shape[0]
    depth = extent[0]
    classes = semantic.shape[2]
    slots = table.shape[1]
    rows = rounded.shape[1]
    step = pl.program_id(0)

    if count is not None:
        y_in, v_in, total, load_sem = refs

    def in_copies(p):
        return (
            pltpu.make_async_copy(y_hbm.at[p], y_in.at[p], load_sem.at[2 * p]),
            pltpu.make_async_copy(v_hbm.at[p + 1], v_in.at[p], load_sem.at[2 * p + 1]),
        )

    def out_copy(p):
        return pltpu.make_async_copy(rounded.at[p], r_out.at[p], sem.at[p])

    @pl.when(step == 0)
    def _():
        if count is None:
            copy = started(r_hbm.at[pl.ds(first, depth)], rounded, sem.at[0])
        else:
            light = started(total_hbm, total, load_sem.at[2 * depth])
            for p in range(depth):
                for copy in in_copies(p):
                    copy.start()
        same = identity(channels, channels)
        hidden_t[...] = nt(same, hidden[layer]).astype(BF)
        bias[...] = column(hidden_b[layer : layer + 1, :], channels)
        head_t[...] = head_rows(semantic[layer], density[layer : layer + 1, :], PROWS)
        last = jnp.sum(
            jnp.where(iota((1, density_b.shape[1]), 1) == layer, density_b[...], 0.0),
            axis=1,
            keepdims=True,
        )
        place = iota((PROWS, 1), 0) == classes
        head_b[...] = jnp.where(place, last, column(semantic_b[layer : layer + 1, :], PROWS))
        if count is None:
            copy.wait()
        else:
            light.wait()
            mean, inverse = moments(total[...], count)
            gains, shifts = row_of(gain, layer), row_of(shift, layer)

        @pl.loop(0, depth)
        def _(p):
            if count is not None:
                for copy in in_copies(p):
                    copy.wait()
                fresh = v_in[p] + silu((y_in[p] - mean) * inverse * gains + shifts)
                rounded[p] = fresh.astype(BF)
                out_copy(p).start()
            turned[:, pl.ds(pl.multiple_of(p * rows, rows), rows)] = nt(same, rounded[p]).astype(BF)

    fill_weights(table, coord_rows(coords[0], slots), extent)
    feature = nn(turned[...], table[...]).astype(BF)
    f_ref[0] = feature
    inner = nn(hidden_t[...], feature) + bias[...]
    small = jnp.exp(-jnp.abs(inner))
    act = (jnp.maximum(inner, 0.0) + jnp.log1p(small)).astype(BF)
    g_ref[0] = act
    s_ref[0] = jnp.where(inner >= 0.0, 1.0, small) / (1.0 + small)
    p_ref[0] = nn(head_t[...], act) + head_b[...]
    if count is not None:

        @pl.when(step == pl.num_programs(0) - 1)
        def _():
            for p in range(depth):
                out_copy(p).wait()


def per_tile(rows, lanes):
    return pl.BlockSpec((1, rows, lanes), lambda t: (t, 0, 0))


def sample(extent, received, source, layer, mlp, count=None, follow=()):
    tiles, lines, wide = received.shape
    slots = CAP
    rows, channels = extent[1] * extent[2], mlp[0].shape[1]
    depth = extent[0]
    voxels = depth * rows
    outs = [((tiles, PROWS, slots), F32)] + [((tiles, channels, slots), d) for d in (BF, BF, F32)]
    out_specs = [per_tile(n, slots) for n in (PROWS, channels, channels, channels)]
    scratch = [
        VMEM((channels, voxels), BF),
        VMEM((voxels, slots), BF),
        VMEM((depth, rows, channels), BF),
        VMEM((channels, channels), BF),
        VMEM((channels, 1), F32),
        VMEM((PROWS, channels), BF),
        VMEM((PROWS, 1), F32),
    ] + sems(depth)
    if count is None:
        first, given, specs = source[1], source[:1], [aspec()]
    else:
        first, given = 0, source
        specs = [aspec()] * 3 + [whole(x.shape) for x in source[3:]]
        outs.append(((depth, rows, channels), BF))
        out_specs.append(aspec())
        scratch += [VMEM((depth, rows, channels), F32)] * 2 + [VMEM(source[2].shape, F32)]
        scratch += sems(2 * depth + 1)
    return ordered(
        functools.partial(sample_kernel, extent, layer, first, count),
        (received,) + tuple(given) + mlp,
        [per_tile(lines, wide)] + specs + [whole(x.shape) for x in mlp],
        follow,
        grid=(tiles,),
        out_shape=any_outs(*outs),
        out_specs=tuple(out_specs),
        scratch_shapes=scratch,
        compiler_params=params(62.5),
        cost_estimate=cost(),
        name="sample",
    )


def sample_back_kernel(
    extent, layer, coords, dp_ref, f_ref, g_ref, s_ref, hidden, semantic, density, *refs
):
    du_ref, pack_ref, total, table, head = refs[-5:]
    step = pl.program_id(0)
    channels = hidden.shape[1]
    slots = table.shape[1]

    @pl.when(step == 0)
    def _():
        total[...] = jnp.zeros_like(total)
        pack_ref[0:PACK, :] = jnp.zeros((PACK, channels), F32)
        if len(refs) > 5:
            pack_ref[PACK : 2 * PACK, :] = refs[0][...]
        rows = head_rows(semantic[layer], density[layer : layer + 1, :], DROWS)
        head[...] = nt(identity(channels, channels), rows).astype(BF)

    fill_weights(table, coord_rows(coords[0], slots), extent)
    grad_heads = dp_ref[0]
    grad_inner = (nn(head[...], grad_heads) * s_ref[0]).astype(BF)
    ones = jnp.ones((16, slots), BF)
    pack_ref[0:channels, :] += nt(f_ref[0], grad_inner)
    pack_ref[channels : channels + 16, :] += nt(ones, grad_inner)
    at = channels + 16
    pack_ref[at : at + DROWS, :] += nt(grad_heads, g_ref[0])
    at += DROWS
    pack_ref[at : at + 16, 0:DROWS] += nt(ones, grad_heads)
    grad_features = nn(hidden[layer], grad_inner).astype(BF)
    total[...] += nt(table[...], grad_features)

    @pl.when(step == pl.num_programs(0) - 1)
    def _():
        du_ref[...] = total[...].astype(BF)


def sample_back(extent, layer, received, grad_heads, feature, act, slope, mlp, packs, follow=()):
    tiles, lines, wide = received.shape
    _, channels, slots = feature.shape
    voxels = extent[0] * extent[1] * extent[2]
    hidden, _, semantic, density = mlp[:4]
    outs = ((voxels, channels), (PACK * (1 + len(packs)), channels))
    return ordered(
        functools.partial(sample_back_kernel, extent, layer),
        (received, grad_heads, feature, act, slope, hidden, semantic, density) + packs,
        [per_tile(lines, wide)]
        + [per_tile(n, slots) for n in (DROWS, channels, channels, channels)]
        + [whole(x.shape) for x in (hidden, semantic, density) + packs],
        follow,
        grid=(tiles,),
        out_shape=any_outs((outs[0], BF), (outs[1], F32)),
        out_specs=tuple(whole(shape) for shape in outs),
        scratch_shapes=[
            VMEM((voxels, channels), F32),
            VMEM((voxels, slots), BF),
            VMEM((channels, DROWS), BF),
        ],
        compiler_params=params(62.5),
        cost_estimate=cost(),
        name="sample_back",
    )


def composite_kernel(
    classes, layer, starts, pixels, owner_ref, rank_ref, view, heads, cot,
    pic_ref, dp_ref, split, by_ray, grads, density, weights, grad_w, acc,
):
    tiles = heads.shape[0]
    rays, samples = owner_ref.shape
    step = 4.0 / samples
    split[...] = jnp.zeros_like(split)
    for t in range(tiles):
        value = heads[t]
        high = value.astype(BF)
        split[t, 0:PROWS, 0:CAP] = high.astype(F32)
        split[t, PROWS : 2 * PROWS, 0:CAP] = value - high.astype(F32)

    def hots(k):
        return window_onehots(
            starts, owner_ref[k : k + 1, :], rank_ref[k : k + 1, :], k, rays, tiles
        )

    for k in range(rays):
        hot, bases = hots(k)
        windows = jnp.concatenate(
            [split[t, :, pl.ds(bases[t], WINDOW)].astype(BF) for t in range(tiles)], axis=1
        )
        both = nn(windows, hot)
        one = both[:PROWS] + both[PROWS:]
        by_ray[k] = one
        density[k : k + 1, :] = one[classes : classes + 1]

    pre = density[...]
    visible = view[...].astype(F32)
    small = jnp.exp(-jnp.abs(pre))
    optical = visible * (jnp.maximum(pre, 0.0) + jnp.log1p(small)) * step
    passing = jnp.exp(-(lane_cumsum(optical) - optical))
    fading = jnp.exp(-optical)
    weight = passing * (1.0 - fading)
    weights[...] = weight
    row = iota((PROWS, samples), 0)
    lane = iota((PROWS, rays), 1)
    cotangent = nt(identity(PROWS, classes + 1), cot[layer])
    picture = jnp.zeros((PROWS, rays), F32)
    for k in range(rays):
        there = lane == pixels[k]
        dpic = jnp.sum(jnp.where(there, cotangent, 0.0), axis=1, keepdims=True)
        value = jnp.where(row < classes, by_ray[k], jnp.where(row == classes, 1.0, 0.0))
        one = weights[k : k + 1, :]
        colour = jnp.sum(value * one, axis=1, keepdims=True)
        picture = jnp.where(there, colour, picture)
        grad_w[k : k + 1, :] = jnp.sum(value * dpic, axis=0, keepdims=True)
        grads[k] = dpic * one
    pic_ref[...] = picture
    grad_weight = grad_w[...]
    carried = grad_weight * weight
    later = jnp.sum(carried, axis=1, keepdims=True) - lane_cumsum(carried)
    grad_optical = grad_weight * passing * fading - later
    slope = jnp.where(pre >= 0.0, 1.0, small) / (1.0 + small)
    density[...] = grad_optical * visible * step * slope
    acc[...] = jnp.zeros_like(acc)
    zero = jnp.zeros((DROWS - PROWS, samples), F32)
    for k in range(rays):
        hot, bases = hots(k)
        grad = jnp.where(row == classes, density[k : k + 1, :], grads[k])
        moved = nt(jnp.concatenate([grad, zero], axis=0).astype(BF), hot)
        for t in range(tiles):
            acc[t, :, pl.ds(bases[t], WINDOW)] += moved[:, t * WINDOW : (t + 1) * WINDOW]
    for t in range(tiles):
        dp_ref[t] = acc[t, :, 0:CAP].astype(BF)


def composite(starts, pixels, owner, rank, view, heads, cot, layer, classes, follow=()):
    tiles, _, slots = heads.shape
    rays, samples = owner.shape
    outs = ((PROWS, rays), (tiles, DROWS, slots))
    return ordered(
        functools.partial(composite_kernel, classes, layer),
        (starts, pixels, owner, rank, view, heads, cot,),
        [sspec(), sspec()] + [whole(x.shape) for x in (owner, rank, view, heads, cot)],
        follow,
        grid=(1,),
        out_shape=(jax.ShapeDtypeStruct(outs[0], F32), jax.ShapeDtypeStruct(outs[1], BF)),
        out_specs=tuple(whole(s) for s in outs),
        scratch_shapes=[
            VMEM((tiles, 2 * PROWS, CAP + WINDOW), F32),
            VMEM((rays, PROWS, samples), F32),
            VMEM((rays, PROWS, samples), F32),
            VMEM((rays, samples), F32),
            VMEM((rays, samples), F32),
            VMEM((rays, samples), F32),
            VMEM((tiles, DROWS, CAP + WINDOW), F32),
        ],
        compiler_params=params(62.5),
        cost_estimate=cost(),
        name="composite",
    )


def add_kernel(parts, out_ref):
    total = parts[0].astype(F32)
    for n in range(1, parts.shape[0]):
        total = total + parts[n].astype(F32)
    total = total.astype(out_ref.dtype)
    for n in range(out_ref.shape[0]):
        out_ref[n] = total


def add_parts(parts, copies, follow=()):
    shape = (copies,) + parts.shape[1:]
    return ordered(
        add_kernel,
        (parts,),
        [whole(parts.shape)],
        follow,
        grid=(1,),
        out_shape=jax.ShapeDtypeStruct(shape, parts.dtype),
        out_specs=whole(shape),
        compiler_params=params(62.5),
        cost_estimate=cost(),
        name="add_parts",
    )


def hold_kernel(*refs):
    del refs


def hold(values, follow):
    return ordered(
        hold_kernel,
        values,
        [aspec()] * len(values),
        follow,
        out_shape=any_outs(*((x.shape, x.dtype) for x in values)),
        out_specs=(aspec(),) * len(values),
        input_output_aliases={n: n for n in range(len(values))},
        compiler_params=params(62.5),
        cost_estimate=cost(),
        name="hold",
    )


def all_to_all(value, axis):
    return lax.all_to_all(value, axis, split_axis=0, concat_axis=0, tiled=True)


def exchange(first, last):
    devices = lax.axis_size("tile")
    up = [(i, i + 1) for i in range(devices - 1)]
    down = [(i + 1, i) for i in range(devices - 1)]
    return lax.ppermute(last, "tile", up), lax.ppermute(first, "tile", down)


def norm_grads(y, grad, mean, inverse, gains, shifts):
    centred = (y - mean) * inverse
    normal = centred * gains + shifts
    sigma = 1.0 / (1.0 + jnp.exp(-normal))
    return grad * sigma * (1.0 + normal * (1.0 - sigma)), centred


def finish_back(sums, edges, ups, spare, out_sem):
    rows = edges.shape[1] - 16
    value = sums[...]
    high = value.astype(BF).astype(F32)
    middle = (value - high).astype(BF).astype(F32)
    low = value - high - middle
    tail = jnp.concatenate([high[0:2], middle[0:2], low[0:2], jnp.zeros((10,) + high.shape[1:], F32)], axis=0)
    tail = tail.astype(BF)
    edges[0, rows:, :] = tail
    edges[1, rows:, :] = tail
    spare[...] = tail
    first_ref, last_ref, far_ref = ups
    copies = [
        started(edges.at[0], first_ref, out_sem.at[0]),
        started(edges.at[1], last_ref, out_sem.at[1]),
        started(spare, far_ref, out_sem.at[2]),
    ]
    for copy in copies:
        copy.wait()


def norm_back_kernel(
    layer, count, cot, local, y, total_hbm, gain_hbm, shift_hbm, first_ref, last_ref, far_ref,
    cot_in, local_in, y_in, total, gain, shift, edges, sums, spare, in_sem, out_sem,
):
    planes, rows, _ = cot.shape
    small = [
        started(total_hbm, total, in_sem.at[3 * planes]),
        started(gain_hbm, gain, in_sem.at[3 * planes + 1]),
        started(shift_hbm, shift, in_sem.at[3 * planes + 2]),
    ]

    def in_copies(p):
        return [
            pltpu.make_async_copy(source.at[p], target.at[p], in_sem.at[3 * p + n])
            for n, (source, target) in enumerate(((cot, cot_in), (local, local_in), (y, y_in)))
        ]

    for p in range(planes):
        for copy in in_copies(p):
            copy.start()
    sums[...] = jnp.zeros_like(sums)
    for copy in small:
        copy.wait()
    mean, inverse = moments(total[...], count)
    gains, shifts = row_of(gain, layer), row_of(shift, layer)

    @pl.loop(0, planes)
    def _(p):
        for copy in in_copies(p):
            copy.wait()
        grad = cot_in[p].astype(F32) + local_in[p].astype(F32)
        inner, centred = norm_grads(y_in[p], grad, mean, inverse, gains, shifts)
        add_stats(sums, inner, inner * centred)
        for side, edge in ((0, 0), (1, planes - 1)):

            @pl.when(p == edge)
            def _():
                edges[side, 0:rows, :] = inner.astype(BF)

    finish_back(sums, edges, (first_ref, last_ref, far_ref), spare, out_sem)


def back_shapes(rows, channels):
    return ((rows + 16, channels), BF), ((rows + 16, channels), BF), ((16, channels), BF)


def back_scratch(rows, channels):
    return [VMEM((2, rows + 16, channels), BF), VMEM((8, channels), F32), VMEM((16, channels), BF)]


def norm_back(cot, local, y, total, gain, shift, layer, count, follow=()):
    planes, rows, channels = local.shape
    return ordered(
        functools.partial(norm_back_kernel, layer, count),
        (cot, local, y, total, gain, shift),
        [aspec()] * 6,
        follow,
        out_shape=any_outs(*back_shapes(rows, channels)),
        out_specs=(aspec(),) * 3,
        scratch_shapes=[VMEM(x.shape, x.dtype) for x in (cot, local, y, total, gain, shift)]
        + back_scratch(rows, channels)
        + sems(3 * planes + 3, 3),
        compiler_params=params(62.5),
        cost_estimate=cost(),
        name="norm_back",
    )


def share_back(sent):
    first, last, far = sent
    tiles = lax.axis_size("tile")

    def move(value, by):
        return lax.ppermute(value, "tile", [(i, (i + by) % tiles) for i in range(tiles)])

    return (move(last, 1), move(first, tiles - 1)) + tuple(move(far, n) for n in range(2, tiles - 1))


def turn_kernel(width, block, r_ref, out_ref, turned):
    planes, rows, channels = r_ref.shape
    chosen = out_ref.shape[1]
    pick = iota((chosen, channels), 1) == iota((chosen, channels), 0) + block[0] * chosen
    pick = pick.astype(F32).astype(BF)
    place = iota((chosen, rows), 1)
    on_y, on_z = lax.div(place, width), lax.rem(place, width)
    height = rows // width
    for p in range(planes):
        turned[...] = nt(pick, r_ref[p])
        for b in range(3):
            for c in range(3):
                shift = (b - 1) * width + (c - 1)
                value = turned[...]
                if shift:
                    value = pltpu.roll(value, (-shift) % rows, 1)
                y, z = on_y + (b - 1), on_z + (c - 1)
                inside = (y >= 0) & (y < height) & (z >= 0) & (z < width)
                value = jnp.where(inside, value, 0.0).astype(BF)
                for a in range(3):
                    target = p - a
                    if 0 <= target < planes - 2:
                        out_ref[9 * a + 3 * b + c, :, target * rows : (target + 1) * rows] = value


def turn(block, rounded, width, blocks, follow=()):
    planes, rows, channels = rounded.shape
    chosen = channels // blocks
    shape = (27, chosen, (planes - 2) * rows)
    return ordered(
        functools.partial(turn_kernel, width),
        (block, rounded,),
        [sspec(), whole(rounded.shape)],
        follow,
        grid=(1,),
        out_shape=jax.ShapeDtypeStruct(shape, BF),
        out_specs=whole(shape),
        scratch_shapes=[VMEM((chosen, rows), F32)],
        compiler_params=params(62.5),
        cost_estimate=cost(),
        name="turn",
    )


def weight_grad_kernel(layer, count, first, parts, tiles, spots, taps_hbm, *refs):
    grads, refs = refs[:parts], refs[parts:]
    if first:
        y, refs = refs[0], refs[1:]
        y_before, y_after = y.at[pl.ds(0, 1)], y.at[pl.ds(y.shape[0] - 1, 1)]
    else:
        y, y_before, y_after, refs = refs[0], refs[1], refs[2], refs[3:]
    own_far, others, refs = refs[0], refs[1:tiles], refs[tiles:]
    total_hbm, gain_hbm, shift_hbm, refs = *refs[:3], refs[3:]
    dy_ref, wg_ref, back_ref, refs = *refs[:3], refs[3:]
    grads_in, refs = refs[:parts], refs[parts:]
    (taps_in, y_in, y_halo, dn_halo, rest, back, total, gain, shift, dy_buf, dy_rows, wg_buf, in_sem,
     out_sem) = refs
    planes, rows, channels = grads[0].shape
    spare = (parts + 1) * planes
    lists = [
        (total_hbm.at[:, pl.ds(0, 8), :], total),
        (gain_hbm, gain),
        (shift_hbm, shift),
        (y_before, y_halo.at[pl.ds(0, 1)]),
        (y_after, y_halo.at[pl.ds(1, 1)]),
        (others[0], dn_halo.at[0]),
        (others[1], dn_halo.at[1]),
        (own_far, rest.at[0]),
    ] + [(other, rest.at[n + 1]) for n, other in enumerate(others[2:])]
    small = [
        started(source, target, in_sem.at[spare + n]) for n, (source, target) in enumerate(lists)
    ]

    def in_copies(p):
        copies = [pltpu.make_async_copy(y.at[p + first], y_in.at[p], in_sem.at[(parts + 1) * p])]
        for n in range(parts):
            copies.append(
                pltpu.make_async_copy(
                    grads[n].at[p], grads_in[n].at[p], in_sem.at[(parts + 1) * p + 1 + n]
                )
            )
        return copies

    for p in range(planes):
        for copy in in_copies(p):
            copy.start()
    heavy = started(taps_hbm, taps_in, in_sem.at[spare + len(lists)])
    for copy in small:
        copy.wait()
    tile = spots[2]
    tails = [rest[0], dn_halo[0, rows:, :], dn_halo[1, rows:, :]]
    tails += [rest[n] for n in range(1, rest.shape[0])]
    for by, tail in zip([0, 1, tiles - 1] + list(range(2, tiles - 1)), tails):
        value = tail.astype(F32)
        value = value[0:2] + value[2:4] + value[4:6]
        back[lax.rem(tile + tiles - by, tiles), 0:2, :] = value
    mean, inverse = moments(total[...], count)
    gains, shifts = row_of(gain, layer), row_of(shift, layer)
    scale = inverse * gains
    both = back[0, 0:2, :]
    for t in range(1, tiles):
        both = both + back[t, 0:2, :]
    back[0, 0:2, :] = both
    sums = both / count

    def finish(inner, centred):
        return scale * (inner - sums[0:1, :] - centred * sums[1:2, :])

    for side, place in ((0, 0), (1, planes + 1)):
        centred = (y_halo[side].astype(F32) - mean) * inverse
        value = finish(dn_halo[side, 0:rows, :].astype(F32), centred)
        dy_buf[place] = jnp.where(spots[side] > 0, value, 0.0).astype(BF)

    @pl.loop(0, planes)
    def _(p):
        for copy in in_copies(p):
            copy.wait()
        grad = grads_in[0][p].astype(F32)
        for n in range(1, parts):
            grad = grad + grads_in[n][p].astype(F32)
        value = finish(*norm_grads(y_in[p], grad, mean, inverse, gains, shifts)).astype(BF)
        dy_buf[p + 1] = value
        dy_rows[pl.ds(pl.multiple_of(p * rows, rows), rows), :] = value

    done = [
        started(dy_buf, dy_ref, out_sem.at[0]),
        started(back.at[0, pl.ds(0, 2), :], back_ref, out_sem.at[2]),
    ]
    heavy.wait()
    wg_buf[...] = nn(taps_in[...], dy_rows[...]).astype(BF)
    done.append(started(wg_buf, wg_ref, out_sem.at[1]))
    for copy in done:
        copy.wait()


def weight_grad(
    spots, taps_t, grads, y, y_halo, far, others, total, gain, shift, layer, count, follow=()
):
    planes, rows, channels = grads[0].shape
    wide = taps_t.shape[0]
    tiles = len(others) + 1
    ext = (planes + 2, rows, channels)
    own = (planes, rows, channels)
    operands = (taps_t,) + tuple(grads) + (y,) + tuple(y_halo) + (far,) + tuple(others)
    operands += (total, gain, shift)
    return ordered(
        functools.partial(weight_grad_kernel, layer, count, 0 if y_halo else 1, len(grads), tiles),
        (spots,) + operands,
        [sspec()] + [aspec()] * len(operands),
        follow,
        out_shape=any_outs((ext, BF), ((wide, channels), BF), ((2, channels), F32)),
        out_specs=(aspec(),) * 3,
        scratch_shapes=[VMEM(x.shape, x.dtype) for x in grads]
        + [
            VMEM(taps_t.shape, BF),
            VMEM(own, F32),
            VMEM((2, rows, channels), BF if y_halo else F32),
            VMEM((2, rows + 16, channels), BF),
            VMEM((tiles - 2, 16, channels), BF),
            VMEM((tiles, 8, channels), F32),
            VMEM((tiles, 8, channels), F32),
            VMEM(gain.shape, F32),
            VMEM(gain.shape, F32),
            VMEM(ext, BF),
            VMEM((planes * rows, channels), BF),
            VMEM((wide, channels), BF),
        ]
        + sems((len(grads) + 1) * planes + 8 + tiles, 3),
        compiler_params=params(62.5),
        cost_estimate=cost(),
        name="weight_grad",
    )


def conv_back_kernel(width, layer, count, parts, dy, w_hbm, *refs):
    more = count is not None
    grads, refs = refs[:parts], refs[parts:]
    if more:
        y, total_hbm, gain_hbm, shift_hbm, refs = *refs[:4], refs[4:]
    out_ref, refs = refs[0], refs[1:]
    if more:
        sent, refs = refs[:3], refs[3:]
    grads_in, refs = refs[:parts], refs[parts:]
    raw, xs, weight, out_buf, in_sem, w_sem, out_sem, refs = *refs[:7], refs[7:]
    ext_planes, rows, channels = dy.shape
    planes = ext_planes - 2
    group = planes // 2
    pairs = 2
    each = parts + 1
    body = started(dy, raw, in_sem.at[each * pairs])
    heavy = [
        started(
            w_hbm.at[layer, pl.ds((26 - o) * channels, channels), :],
            weight.at[:, pl.ds(o * channels, channels)],
            w_sem.at[o],
        )
        for o in range(27)
    ]
    small = []
    if more:
        y_in, total, gain, shift, edges, sums, spare, back_sem = refs
        small = [
            started(source, target, in_sem.at[each * pairs + 1 + n])
            for n, (source, target) in enumerate(
                ((total_hbm.at[:, pl.ds(0, 8), :], total), (gain_hbm, gain), (shift_hbm, shift))
            )
        ]
        sums[...] = jnp.zeros_like(sums)

    def in_copies(i):
        two = pl.ds(group * i, group)
        copies = [
            pltpu.make_async_copy(grads[n].at[two], grads_in[n].at[two], in_sem.at[each * i + n])
            for n in range(parts)
        ]
        if more:
            copies.append(
                pltpu.make_async_copy(
                    y.at[pl.ds(group * i + 1, group)], y_in.at[two], in_sem.at[each * i + parts]
                )
            )
        return copies

    def out_copy(i):
        two = pl.ds(group * i, group)
        return pltpu.make_async_copy(out_buf.at[two], out_ref.at[two], out_sem.at[i])

    for i in range(pairs):
        for copy in in_copies(i):
            copy.start()
    clear_edges(xs, width, rows)
    body.wait()

    @pl.loop(0, ext_planes)
    def _(p):
        put_plane(xs, p, raw[p].astype(F32), width)

    for copy in small + heavy:
        copy.wait()
    if more:
        mean, inverse = moments(total[...], count)
        gains, shifts = row_of(gain, layer - 1), row_of(shift, layer - 1)

    @pl.loop(0, pairs)
    def _(i):
        part = nt(tap_group(xs, group * i, group, width, rows), weight[...])
        for copy in in_copies(i):
            copy.wait()
        for n_plane in range(group):
            p = group * i + n_plane
            value = part[n_plane * rows : (n_plane + 1) * rows]
            for n in range(parts):
                value = value + grads_in[n][p].astype(F32)
            out_buf[p] = value
            if more:
                inner, centred = norm_grads(y_in[p], value, mean, inverse, gains, shifts)
                add_stats(sums, inner, inner * centred)

                for side, near in ((0, 0), (1, group - 1)):
                    if n_plane == near:

                        @pl.when(p == side * (planes - 1))
                        def _():
                            edges[side, 0:rows, :] = inner.astype(BF)

        out_copy(i).start()

    if more:
        finish_back(sums, edges, sent, spare, back_sem)
    for i in range(pairs):
        out_copy(i).wait()


def conv_back(dy, grads, weights, layer, width, norm=None, follow=()):
    ext_planes, rows, channels = dy.shape
    own = (ext_planes - 2, rows, channels)
    pairs = 2
    outs, extra, scratch = [(own, F32)], (), []
    if norm is not None:
        y, total, gain, shift, count = norm
        extra = (y, total, gain, shift)
        outs += list(back_shapes(rows, channels))
        scratch = [VMEM(own, F32), VMEM((total.shape[0], 8, channels), F32)]
        scratch += [VMEM(gain.shape, F32), VMEM(gain.shape, F32)]
        scratch += back_scratch(rows, channels) + sems(3)
    else:
        count = None
    return ordered(
        functools.partial(conv_back_kernel, width, layer, count, len(grads)),
        (dy, weights) + tuple(grads) + extra,
        [aspec()] * (2 + len(grads) + len(extra)),
        follow,
        out_shape=any_outs(*outs),
        out_specs=(aspec(),) * len(outs),
        scratch_shapes=[VMEM(x.shape, x.dtype) for x in grads]
        + [VMEM(dy.shape, BF)]
        + conv_scratch(ext_planes, rows, width, channels, True)
        + [VMEM(own, F32)]
        + sems(pairs * (len(grads) + 1) + 4, 27, pairs)
        + scratch,
        compiler_params=params(62.5),
        cost_estimate=cost(),
        name="conv_back",
    )


GROUP = 3


def gather_ray(slices):
    return lax.all_gather(slices.reshape(-1, slices.shape[-1]), "ray", axis=0)


def place_kernel(layer, blocks, source, *refs):
    out_ref, taken, out, in_sem, out_sem = refs[-5:]
    _, offsets, rows, _ = out_ref.shape
    chosen = rows // blocks
    steps = offsets // GROUP
    lines = GROUP * chosen

    def in_copy(n):
        some = pl.ds(n * lines, lines)
        return pltpu.make_async_copy(
            source.at[pl.ds(0, blocks), some], taken.at[:, some], in_sem.at[n]
        )

    for n in range(steps):
        in_copy(n).start()
    done = []
    for n in range(steps):
        in_copy(n).wait()
        for o in range(n * GROUP, (n + 1) * GROUP):
            for ray in range(blocks):
                out[o, ray * chosen : (ray + 1) * chosen, :] = taken[
                    ray, o * chosen : (o + 1) * chosen, :
                ].astype(F32)
        some = pl.ds(n * GROUP, GROUP)
        done.append(started(out.at[some], out_ref.at[layer, some], out_sem.at[n]))
    for copy in done:
        copy.wait()


def place(parts, layer, layers, blocks, kept, follow=()):
    _, lines, channels = parts.shape
    offsets = lines * blocks // channels
    return ordered(
        functools.partial(place_kernel, layer, blocks),
        (parts,) + kept,
        [aspec()] * (1 + len(kept)),
        follow,
        out_shape=jax.ShapeDtypeStruct((layers, offsets, channels, channels), F32),
        out_specs=aspec(),
        scratch_shapes=[VMEM((blocks, lines, channels), BF), VMEM((offsets, channels, channels), F32)]
        + sems(offsets // GROUP, offsets // GROUP),
        input_output_aliases={1: 0} if kept else {},
        compiler_params=params(62.5),
        cost_estimate=cost(),
        name="place",
    )


def per_device(
    volume,
    sample_cells,
    sample_fracs,
    view_mask,
    pixel_of_ray,
    conv_weight,
    norm_gain,
    norm_shift,
    hidden_weight,
    hidden_bias,
    density_weight,
    density_bias,
    semantic_weight,
    semantic_bias,
    render_cotangent,
    volume_cotangent,
):
    extent = volume.shape[:3]
    depth, height, width, channels = volume.shape
    rows = height * width
    voxels = depth * rows
    tiles = lax.axis_size("tile")
    ray_devices = lax.axis_size("ray")
    count = float(voxels * tiles)
    rays, samples = sample_cells.shape
    classes = semantic_weight.shape[2]
    layers = conv_weight.shape[0]
    blocks = min(BLOCKS, ray_devices)
    chosen = channels // blocks
    tile, ray = lax.axis_index("tile"), lax.axis_index("ray")
    block = lax.rem(ray, blocks).astype(jnp.int32).reshape(1)

    own = volume.reshape(depth, rows, channels)
    before, after = exchange(own[:2], own[-2:])
    flags = jnp.stack([tile > 0, tile < tiles - 1]).astype(jnp.int32)

    owner_of = lax.div(sample_cells, voxels)
    held = owner_of[None] == jnp.arange(tiles, dtype=jnp.int32)[:, None, None]
    earlier = jnp.arange(rays)[None, :] < jnp.arange(rays)[:, None]
    starts = jnp.sum(
        (held[:, None, :, :] & earlier[None, :, :, None]).astype(jnp.int32), axis=(2, 3)
    ).reshape(tiles * rays)
    pixels = pixel_of_ray[0]
    buffer, owner, rank = prepare(extent, starts, sample_cells, sample_fracs, tiles, channels)

    weights = conv_weight.reshape(layers, 27 * channels, channels)
    mlp = (
        hidden_weight,
        hidden_bias,
        semantic_weight,
        density_weight,
        semantic_bias,
        density_bias[None],
    )
    y_ext, v_ext, mixed = conv_first(before, own, after, buffer, weights, 0, width)
    total = received = all_to_all(mixed, "tile")
    taps_first = turn(block, v_ext, width, blocks)
    v_next, r_ext, y_next, stat, y_first, y_last = conv_next(
        flags, y_ext, v_ext, total, norm_gain, norm_shift, weights, 0, width, count,
        follow=(taps_first,),
    )
    total_next = all_to_all(stat, "tile")
    heads, feature, act, slope = sample(extent, received, (r_ext, 1), 0, mlp)
    heads_last, feature_last, act_last, slope_last, r_last = sample(
        extent, received, (y_next, v_next, total_next, norm_gain, norm_shift), 1, mlp, count,
        follow=(heads,),
    )

    def draw(heads, layer, follow):
        return composite(
            starts, pixels, owner, rank, view_mask, all_to_all(heads, "tile"), render_cotangent,
            layer, classes, follow=follow,
        )

    picture, grad_heads = draw(heads, 0, (heads_last,))
    picture_last, grad_heads_last = draw(heads_last, 1, (grad_heads,))
    shares = (ray_devices, voxels // ray_devices, channels)
    planes = (depth, rows, channels)
    local, pack = sample_back(
        extent, 0, received, all_to_all(grad_heads, "tile"), feature, act, slope, mlp, (),
        follow=(grad_heads_last,),
    )
    parts = all_to_all(local.reshape(shares), "ray")
    local_last, packed = sample_back(
        extent, 1, received, all_to_all(grad_heads_last, "tile"), feature_last, act_last,
        slope_last, mlp, (pack,), follow=(local,),
    )
    copies = add_parts(parts, ray_devices, follow=(local_last,))
    parts_last = all_to_all(local_last.reshape(shares), "ray")
    taps_next = turn(block, r_ext, width, blocks, follow=(copies,))
    copies_last = add_parts(parts_last, ray_devices, follow=(taps_next,))
    sums_last = all_to_all(copies_last, "ray").reshape(planes)
    y_edges = exchange(*hold((y_first, y_last), (copies_last,)))
    copies, packed = hold((copies, packed), (sums_last,) + y_edges)
    sums = all_to_all(copies, "ray").reshape(planes)
    packed = lax.psum_scatter(packed, "ray", scatter_dimension=0, tiled=True)

    cot = volume_cotangent.reshape(planes)
    wide_taps = (27 * chosen, voxels)
    spots = jnp.stack([tile > 0, tile < tiles - 1, tile]).astype(jnp.int32)
    sent = norm_back(
        cot, sums_last, y_next, total_next, norm_gain, norm_shift, 1, count,
        follow=y_edges + (copies,),
    )
    dy, part, back_last = weight_grad(
        spots, taps_next.reshape(wide_taps), (cot, sums_last), y_next, y_edges, sent[2],
        share_back(sent), total_next, norm_gain, norm_shift, 1, count,
    )
    share = (tiles, 27 * chosen // tiles, channels)
    (held,) = hold((part,), (sums,))
    parts = all_to_all(held.reshape(share), "tile")
    grad, *sent = conv_back(
        dy, (cot, sums_last, sums), weights, 1, width,
        (y_ext, total, norm_gain, norm_shift, count), follow=(held,),
    )
    others = share_back(sent)
    shards = add_parts(parts, tiles, follow=(sent[2],))
    shard = all_to_all(shards, "tile")

    dy, part, back = weight_grad(
        spots, taps_first.reshape(wide_taps), (grad,), y_ext, (), sent[2], others, total,
        norm_gain, norm_shift, 0, count, follow=(shards,),
    )
    (part,) = hold((part,), (shard,))
    parts = all_to_all(part.reshape(share), "tile")
    (shard,) = hold((shard,), (part,))
    copies = add_parts(parts, tiles, follow=(shard,))
    slices = all_to_all(copies, "tile")

    conv_grad = place(gather_ray(shard), 1, layers, blocks, (), follow=(slices,))
    packed = all_to_all(add_parts(packed[None], tiles, follow=(slices,)), "tile")
    (grad,) = conv_back(dy, (grad,), weights, 0, width, follow=(conv_grad,))
    packed = all_to_all(add_parts(packed, ray_devices, follow=(grad,)), "ray")
    packed = packed.reshape(layers, PACK, channels)[::-1]
    conv_grad = place(gather_ray(slices), 0, layers, blocks, (conv_grad,), follow=(grad,))

    at = channels + 16
    heads = packed[:, at : at + DROWS]
    head_bias = packed[:, at + DROWS, :DROWS]
    return (
        jnp.swapaxes(jnp.stack([picture, picture_last])[:, : classes + 1], 1, 2),
        r_last.reshape(volume.shape),
        grad.reshape(volume.shape),
        conv_grad,
        jnp.stack([back, back_last])[:, 1],
        jnp.stack([back, back_last])[:, 0],
        packed[:, :channels],
        packed[:, channels],
        heads[:, classes],
        head_bias[:, classes],
        jnp.swapaxes(heads[:, :classes], 1, 2),
        head_bias[:, :classes],
    )


def solution(mesh):
    in_specs = (
        P("tile", None, None, None),
        P(("ray", "tile"), None),
        P(None, ("ray", "tile"), None),
        P(("ray", "tile"), None),
        P(("ray", "tile"), None),
        P(),
        P(),
        P(),
        P(),
        P(),
        P(),
        P(),
        P(),
        P(),
        P(None, ("ray", "tile"), None),
        P("tile", None, None, None),
    )
    out_specs = (
        P(None, ("ray", "tile"), None),
        P("tile", None, None, None),
        P("tile", None, None, None),
        P(),
        P(),
        P(),
        P(),
        P(),
        P(),
        P(),
        P(),
        P(),
    )
    return jax.shard_map(
        per_device, mesh=mesh, in_specs=in_specs, out_specs=out_specs, check_vma=False
    )
```

```python
import functools

import jax
import jax.numpy as jnp
from jax import lax
from jax.experimental import pallas as pl
from jax.experimental.pallas import tpu as pltpu
from jax.sharding import PartitionSpec as P

CAP = 768
WINDOW = 256
LANES = 128
PROWS = 24
DROWS = 32
COORDS = 8
BLOCKS = 8
PACK = 320
epsilon = 1e-05
MIB = 1024 * 1024

BF = jnp.bfloat16
F32 = jnp.float32
VMEM = pltpu.VMEM
SMEM = pltpu.SMEM


def nn(left, right):
    return jnp.dot(left, right, preferred_element_type=F32)


def nt(left, right):
    return lax.dot_general(left, right, (((1,), (1,)), ((), ())), preferred_element_type=F32)


def iota(shape, dim):
    return lax.broadcasted_iota(jnp.int32, shape, dim)


def whole(shape):
    return pl.BlockSpec(shape, lambda *_: (0,) * len(shape))


def planes_of(step, shape, first=0):
    return pl.BlockSpec((step,) + shape[1:], lambda i: (i + first // step,) + (0,) * (len(shape) - 1))


def sspec():
    return pl.BlockSpec(memory_space=SMEM)


def aspec():
    return pl.BlockSpec(memory_space=pl.ANY)


def hspec():
    return pl.BlockSpec(memory_space=pltpu.HBM)


def ordered(kernel, operands, in_specs, follow, **options):
    count, skip = len(operands), len(follow)

    def body(*refs):
        kernel(*refs[:count], *refs[count + skip :])

    return pl.pallas_call(body, in_specs=list(in_specs) + [aspec()] * skip, **options)(
        *operands, *follow
    )


def params(mib):
    return pltpu.CompilerParams(vmem_limit_bytes=int(mib * MIB))


def cost():
    return pl.CostEstimate(flops=1, bytes_accessed=1, transcendentals=0)


def lane_cumsum(x):
    lane = iota(x.shape, 1)
    shift = 1
    while shift < x.shape[1]:
        x = x + jnp.where(lane >= shift, pltpu.roll(x, shift, 1), 0.0)
        shift *= 2
    return x


def window_onehots(starts, owner_row, rank_row, ray, rays, tiles):
    rows = iota((WINDOW, rank_row.shape[1]), 0)
    hots, bases = [], []
    for t in range(tiles):
        start = starts[t * rays + ray]
        base = (start // LANES) * LANES
        place = jnp.where(owner_row == t, rank_row + (start - base), -1)
        hots.append((rows == place).astype(F32).astype(BF))
        bases.append(pl.multiple_of(base, LANES))
    return jnp.concatenate(hots, axis=0), bases


def prep_kernel(extent, starts, cells_ref, fracs_ref, out_ref, owner_ref, rank_ref, vals, acc):
    depth, height, width = extent
    tiles = out_ref.shape[0]
    rays, samples = cells_ref.shape
    cells = cells_ref[...]
    voxels = depth * height * width
    owner = lax.div(cells, voxels)
    local = cells - owner * voxels
    base_x = lax.div(local, height * width)
    inner = local - base_x * (height * width)
    base_y = lax.div(inner, width)
    base_z = inner - base_y * width
    rank = jnp.zeros(cells.shape, F32)
    for t in range(tiles):
        mine = owner == t
        rank = jnp.where(mine, lane_cumsum(jnp.where(mine, 1.0, 0.0)) - 1.0, rank)
    owner_ref[...] = owner
    rank_ref[...] = rank.astype(jnp.int32)
    vals[...] = jnp.zeros_like(vals)
    rows = [(base_x + 1).astype(F32), base_y.astype(F32), base_z.astype(F32)]
    low = []
    for d in range(3):
        frac = fracs_ref[d]
        high = frac.astype(BF).astype(F32)
        rows.append(high)
        low.append(frac - high)
    rows += low
    for number, row in enumerate(rows):
        for k in range(rays):
            vals[number : number + 1, k * samples : (k + 1) * samples] = row[k : k + 1]
    acc[...] = jnp.zeros_like(acc)
    for k in range(rays):
        hot, bases = window_onehots(
            starts, owner_ref[k : k + 1, :], rank_ref[k : k + 1, :], k, rays, tiles
        )
        moved = nt(vals[:, k * samples : (k + 1) * samples].astype(BF), hot)
        for t in range(tiles):
            acc[t, :, pl.ds(bases[t], WINDOW)] += moved[:, t * WINDOW : (t + 1) * WINDOW]
    out_ref[...] = jnp.zeros_like(out_ref)
    wide = out_ref.shape[2]
    lines = CAP // wide
    for n in range(lines):
        part = slice(n * wide, (n + 1) * wide)
        for r in range(6):
            value = acc[:, r : r + 1, part]
            if r >= 3:
                value = value + acc[:, r + 3 : r + 4, part]
            out_ref[:, r * lines + n : r * lines + n + 1, :] = value


def prepare(extent, starts, cells, fracs, tiles, wide, follow=()):
    rays, samples = cells.shape
    outs = ((tiles, COORDS * CAP // wide, wide), (rays, samples), (rays, samples))
    return ordered(
        functools.partial(prep_kernel, extent),
        (starts, cells, fracs,),
        [sspec(), whole(cells.shape), whole(fracs.shape)],
        follow,
        grid=(1,),
        out_shape=(
            jax.ShapeDtypeStruct(outs[0], F32),
            jax.ShapeDtypeStruct(outs[1], jnp.int32),
            jax.ShapeDtypeStruct(outs[2], jnp.int32),
        ),
        out_specs=tuple(whole(s) for s in outs),
        scratch_shapes=[VMEM((16, rays * samples), F32), VMEM((tiles, 16, CAP + WINDOW), F32)],
        compiler_params=params(62.5),
        cost_estimate=cost(),
        name="prep",
    )


def started(source, target, sem):
    copy = pltpu.make_async_copy(source, target, sem)
    copy.start()
    return copy


def put_plane(xs, p, value, width):
    rows, channels = value.shape
    along = lax.rem(iota(value.shape, 0), width)
    left = jnp.where(along == 0, 0.0, pltpu.roll(value, 1, 0))
    right = jnp.where(along == width - 1, 0.0, pltpu.roll(value, rows - 1, 0))
    xs[p, width : width + rows, 0:channels] = left.astype(BF)
    xs[p, width : width + rows, channels : 2 * channels] = value.astype(BF)
    xs[p, width : width + rows, 2 * channels : 3 * channels] = right.astype(BF)


def clear_edges(xs, width, rows):
    planes, _, wide = xs.shape
    for p in range(planes):
        xs[p, 0:width, :] = jnp.zeros((width, wide), BF)
        xs[p, width + rows : 2 * width + rows, :] = jnp.zeros((width, wide), BF)


def taps(xs, p, width, rows):
    return jnp.concatenate(
        [xs[p + a, b * width : b * width + rows, :] for a in range(3) for b in range(3)], axis=1
    )


def tap_group(xs, first, count, width, rows):
    return jnp.concatenate([taps(xs, first + n, width, rows) for n in range(count)], axis=0)


def add_stats(sums, one, two):
    sums[0:1, :] += jnp.sum(one, axis=0, keepdims=True)
    sums[1:2, :] += jnp.sum(two, axis=0, keepdims=True)


def conv_scratch(planes, rows, width, channels, turned):
    shape = (channels, 27 * channels) if turned else (27 * channels, channels)
    return [VMEM((planes, rows + 2 * width, 3 * channels), BF), VMEM(shape, BF)]


def sems(*counts):
    return [pltpu.SemaphoreType.DMA((n,)) for n in counts]


def any_outs(*shapes):
    return tuple(jax.ShapeDtypeStruct(shape, dtype) for shape, dtype in shapes)


def conv_first_kernel(
    width, layer, before, own, after, coords, w_hbm, y_ref, v_ref, mix_ref,
    raw, xs, weight, y_buf, mix, in_sem, out_sem,
):
    planes, rows, channels = own.shape
    pairs = planes // 2 + 1
    body = [
        started(own.at[pl.ds(2 * i, 2)], raw.at[pl.ds(2 * i + 2, 2)], in_sem.at[i])
        for i in range(planes // 2)
    ]
    ends = [
        started(before, raw.at[pl.ds(0, 2)], in_sem.at[pairs]),
        started(after, raw.at[pl.ds(planes + 2, 2)], in_sem.at[pairs + 1]),
    ]
    heavy = started(w_hbm.at[layer], weight, in_sem.at[pairs + 2])
    light = started(coords, mix.at[:, pl.ds(8, coords.shape[1]), :], in_sem.at[pairs + 3])
    clear_edges(xs, width, rows)
    mix[:, 0:8, :] = jnp.zeros((mix.shape[0], 8, channels), F32)
    for copy in body + ends:
        copy.wait()

    @pl.loop(0, planes + 4)
    def _(p):
        put_plane(xs, p, raw[p].astype(F32), width)

    done = [started(raw.at[pl.ds(1, planes + 2)], v_ref, out_sem.at[pairs])]
    light.wait()
    heavy.wait()

    group = (planes + 2) // 2

    def out_copy(i):
        some = pl.ds(group * i, group)
        return pltpu.make_async_copy(y_buf.at[some], y_ref.at[some], out_sem.at[i])

    @pl.loop(0, 2)
    def _(i):
        p = group * i
        part = nn(tap_group(xs, p, group, width, rows), weight[...])
        for n in range(group):
            y_buf[p + n] = part[n * rows : (n + 1) * rows]
        out_copy(i).start()
        inner = part[rows : (group - 1) * rows]
        add_stats(mix.at[0], inner, inner * inner)
        edge = jnp.where(i == 0, part[(group - 1) * rows :], part[:rows])
        add_stats(mix.at[0], edge, edge * edge)

    for t in range(1, mix.shape[0]):
        mix[t, 0:8, :] = mix[0, 0:8, :]
    done.append(started(mix, mix_ref, out_sem.at[pairs + 1]))
    for copy in done:
        copy.wait()
    for i in range(2):
        out_copy(i).wait()


def conv_first(before, own, after, coords, weights, layer, width):
    planes, rows, channels = own.shape
    ext = (planes + 2, rows, channels)
    tiles, lines, _ = coords.shape
    pairs = planes // 2 + 1
    return ordered(
        functools.partial(conv_first_kernel, width, layer),
        (before, own, after, coords, weights),
        [aspec()] * 5,
        (),
        out_shape=any_outs((ext, F32), (ext, BF), ((tiles, 8 + lines, channels), F32)),
        out_specs=(aspec(),) * 3,
        scratch_shapes=[VMEM((planes + 4, rows, channels), BF)]
        + conv_scratch(planes + 4, rows, width, channels, False)
        + [VMEM(ext, F32), VMEM((tiles, 8 + lines, channels), F32)]
        + sems(pairs + 4, pairs + 2),
        compiler_params=params(62.5),
        cost_estimate=cost(),
        name="conv_first",
    )


def moments(total, count):
    both = jnp.sum(total, axis=0)
    mean = both[0:1, :] / count
    return mean, lax.rsqrt(both[1:2, :] / count - mean * mean + epsilon)


def row_of(ref, layer):
    return ref[layer : layer + 1, :]


def silu(value):
    return value * (1.0 / (1.0 + jnp.exp(-value)))


def conv_next_kernel(
    width, layer, count, flags, y_ext, v_ext, total_hbm, gain_hbm, shift_hbm, w_hbm,
    v_ref, r_ref, y_ref, stat_ref, first_ref, last_ref,
    y_in, v_in, total, gain, shift, xs, weight, v_buf, r_buf, y_buf, edges, stat, in_sem, out_sem,
):
    ext_planes, rows, channels = y_ext.shape
    pairs = ext_planes // 2
    small = [
        started(total_hbm.at[:, pl.ds(0, 8), :], total, in_sem.at[2 * pairs]),
        started(gain_hbm, gain, in_sem.at[2 * pairs + 1]),
        started(shift_hbm, shift, in_sem.at[2 * pairs + 2]),
    ]
    def in_copies(i):
        two = pl.ds(2 * i, 2)
        return (
            pltpu.make_async_copy(y_ext.at[two], y_in.at[two], in_sem.at[2 * i]),
            pltpu.make_async_copy(v_ext.at[two], v_in.at[two], in_sem.at[2 * i + 1]),
        )

    def mid_copies(i):
        two = pl.ds(2 * i, 2)
        return (
            pltpu.make_async_copy(v_buf.at[two], v_ref.at[two], out_sem.at[3 * i]),
            pltpu.make_async_copy(r_buf.at[two], r_ref.at[two], out_sem.at[3 * i + 1]),
        )

    def out_copy(i):
        two = pl.ds(2 * i - 2, 2)
        return pltpu.make_async_copy(y_buf.at[two], y_ref.at[two], out_sem.at[3 * i + 2])

    for i in range(pairs):
        for copy in in_copies(i):
            copy.start()
    heavy = started(w_hbm.at[layer + 1], weight, in_sem.at[2 * pairs + 3])
    clear_edges(xs, width, rows)
    stat[...] = jnp.zeros_like(stat)
    for copy in small:
        copy.wait()
    mean, inverse = moments(total[...], count)
    gains, shifts = row_of(gain, layer), row_of(shift, layer)

    @pl.loop(0, pairs)
    def _(i):
        for copy in in_copies(i):
            copy.wait()
        for side in range(2):
            p = 2 * i + side
            fresh = v_in[p].astype(F32) + silu((y_in[p] - mean) * inverse * gains + shifts)
            v_buf[p] = fresh
            outside = (p == side * (ext_planes - 1)) & (flags[side] == 0)
            rounded = jnp.where(outside, 0.0, fresh).astype(BF)
            r_buf[p] = rounded
            put_plane(xs, p, rounded.astype(F32), width)
        for copy in mid_copies(i):
            copy.start()

        @pl.when(i == 1)
        def _():
            heavy.wait()

        @pl.when(i > 0)
        def _():
            p = 2 * i - 2
            part = nn(tap_group(xs, p, 2, width, rows), weight[...])
            y_buf[p] = part[:rows]
            y_buf[p + 1] = part[rows:]
            add_stats(stat.at[0], part, part * part)
            out_copy(i).start()

    edges[0] = y_buf[0].astype(BF)
    edges[1] = y_buf[ext_planes - 3].astype(BF)
    for t in range(1, stat.shape[0]):
        stat[t] = stat[0]
    done = [
        started(stat, stat_ref, out_sem.at[2]),
        started(edges.at[pl.ds(0, 1)], first_ref, out_sem.at[3 * pairs]),
        started(edges.at[pl.ds(1, 1)], last_ref, out_sem.at[3 * pairs + 1]),
    ]
    for i in range(pairs):
        done += list(mid_copies(i)) + ([out_copy(i)] if i else [])
    for copy in done:
        copy.wait()


def conv_next(flags, y_ext, v_ext, total, gain, shift, weights, layer, width, count, follow=()):
    ext_planes, rows, channels = y_ext.shape
    ext = y_ext.shape
    inner = (ext_planes - 2, rows, channels)
    stat = (total.shape[0], 8, channels)
    pairs = ext_planes // 2
    edge = (1, rows, channels)
    return ordered(
        functools.partial(conv_next_kernel, width, layer, count),
        (flags, y_ext, v_ext, total, gain, shift, weights),
        [sspec()] + [aspec()] * 6,
        follow,
        out_shape=any_outs((ext, F32), (ext, BF), (inner, F32), (stat, F32), (edge, BF), (edge, BF)),
        out_specs=(aspec(),) * 6,
        scratch_shapes=[VMEM(ext, F32), VMEM(ext, BF), VMEM(stat, F32)]
        + [VMEM(gain.shape, F32)] * 2
        + conv_scratch(ext_planes, rows, width, channels, False)
        + [VMEM(ext, F32), VMEM(ext, BF), VMEM(inner, F32)]
        + [VMEM((2, rows, channels), BF), VMEM(stat, F32)]
        + sems(2 * pairs + 4, 3 * pairs + 2),
        compiler_params=params(62.5),
        cost_estimate=cost(),
        name="conv_next",
    )


def fill_weights(table, coords, extent):
    depth, height, width = extent
    samples = coords[0].shape[1]

    def along(base, frac, size):
        grid = iota((size, samples), 0).astype(F32)
        lower = jnp.where(grid == base, 1.0 - frac, 0.0)
        return lower + jnp.where(grid == base + 1.0, frac, 0.0)

    on_x = along(coords[0] - 1.0, coords[3], depth)
    on_y = along(coords[1], coords[4], height)
    on_z = along(coords[2], coords[5], width)
    for x in range(depth):
        on_xy = on_x[x : x + 1] * on_y
        for y in range(height):
            row = (x * height + y) * width
            table[row : row + width, :] = (on_xy[y : y + 1] * on_z).astype(BF)


def diagonal(rows, columns):
    return iota((rows, columns), 0) == iota((rows, columns), 1)


def identity(rows, columns):
    return diagonal(rows, columns).astype(F32).astype(BF)


def head_rows(semantic, density, rows):
    channels, classes = semantic.shape
    turned = nt(identity(rows, classes), semantic)
    return jnp.where(iota((rows, channels), 0) == classes, density.astype(F32), turned).astype(BF)


def column(row, rows):
    return jnp.sum(jnp.where(diagonal(rows, row.shape[1]), row, 0.0), axis=1, keepdims=True)


def coord_rows(block, slots):
    lines = slots // block.shape[1]
    return [
        jnp.concatenate(
            [block[8 + r * lines + n : 9 + r * lines + n, :] for n in range(lines)], axis=1
        )
        for r in range(6)
    ]


def sample_kernel(
    extent, layer, first, count, coords, *refs
):
    if count is None:
        r_hbm, refs = refs[0], refs[1:]
    else:
        y_hbm, v_hbm, total_hbm, gain, shift, refs = refs[0], refs[1], refs[2], refs[3], refs[4], refs[5:]
    hidden, hidden_b, semantic, density, semantic_b, density_b, refs = *refs[:6], refs[6:]
    p_ref, f_ref, g_ref, s_ref, refs = *refs[:4], refs[4:]
    if count is not None:
        r_out, refs = refs[0], refs[1:]
    turned, table, rounded, hidden_t, bias, head_t, head_b, sem, refs = *refs[:8], refs[8:]
    channels = turned.shape[0]
    depth = extent[0]
    classes = semantic.shape[2]
    slots = table.shape[1]
    rows = rounded.shape[1]
    step = pl.program_id(0)

    if count is not None:
        y_in, v_in, total, load_sem = refs

    def in_copies(p):
        return (
            pltpu.make_async_copy(y_hbm.at[p], y_in.at[p], load_sem.at[2 * p]),
            pltpu.make_async_copy(v_hbm.at[p + 1], v_in.at[p], load_sem.at[2 * p + 1]),
        )

    def out_copy(p):
        return pltpu.make_async_copy(rounded.at[p], r_out.at[p], sem.at[p])

    @pl.when(step == 0)
    def _():
        if count is None:
            copy = started(r_hbm.at[pl.ds(first, depth)], rounded, sem.at[0])
        else:
            light = started(total_hbm, total, load_sem.at[2 * depth])
            for p in range(depth):
                for copy in in_copies(p):
                    copy.start()
        same = identity(channels, channels)
        hidden_t[...] = nt(same, hidden[layer]).astype(BF)
        bias[...] = column(hidden_b[layer : layer + 1, :], channels)
        head_t[...] = head_rows(semantic[layer], density[layer : layer + 1, :], PROWS)
        last = jnp.sum(
            jnp.where(iota((1, density_b.shape[1]), 1) == layer, density_b[...], 0.0),
            axis=1,
            keepdims=True,
        )
        place = iota((PROWS, 1), 0) == classes
        head_b[...] = jnp.where(place, last, column(semantic_b[layer : layer + 1, :], PROWS))
        if count is None:
            copy.wait()
        else:
            light.wait()
            mean, inverse = moments(total[...], count)
            gains, shifts = row_of(gain, layer), row_of(shift, layer)

        @pl.loop(0, depth)
        def _(p):
            if count is not None:
                for copy in in_copies(p):
                    copy.wait()
                fresh = v_in[p] + silu((y_in[p] - mean) * inverse * gains + shifts)
                rounded[p] = fresh.astype(BF)
                out_copy(p).start()
            turned[:, pl.ds(pl.multiple_of(p * rows, rows), rows)] = nt(same, rounded[p]).astype(BF)

    fill_weights(table, coord_rows(coords[0], slots), extent)
    feature = nn(turned[...], table[...]).astype(BF)
    f_ref[0] = feature
    inner = nn(hidden_t[...], feature) + bias[...]
    small = jnp.exp(-jnp.abs(inner))
    act = (jnp.maximum(inner, 0.0) + jnp.log1p(small)).astype(BF)
    g_ref[0] = act
    s_ref[0] = jnp.where(inner >= 0.0, 1.0, small) / (1.0 + small)
    p_ref[0] = nn(head_t[...], act) + head_b[...]
    if count is not None:

        @pl.when(step == pl.num_programs(0) - 1)
        def _():
            for p in range(depth):
                out_copy(p).wait()


def per_tile(rows, lanes):
    return pl.BlockSpec((1, rows, lanes), lambda t: (t, 0, 0))


def sample(extent, received, source, layer, mlp, count=None, follow=()):
    tiles, lines, wide = received.shape
    slots = CAP
    rows, channels = extent[1] * extent[2], mlp[0].shape[1]
    depth = extent[0]
    voxels = depth * rows
    outs = [((tiles, PROWS, slots), F32)] + [((tiles, channels, slots), d) for d in (BF, BF, F32)]
    out_specs = [per_tile(n, slots) for n in (PROWS, channels, channels, channels)]
    scratch = [
        VMEM((channels, voxels), BF),
        VMEM((voxels, slots), BF),
        VMEM((depth, rows, channels), BF),
        VMEM((channels, channels), BF),
        VMEM((channels, 1), F32),
        VMEM((PROWS, channels), BF),
        VMEM((PROWS, 1), F32),
    ] + sems(depth)
    if count is None:
        first, given, specs = source[1], source[:1], [aspec()]
    else:
        first, given = 0, source
        specs = [aspec()] * 3 + [whole(x.shape) for x in source[3:]]
        outs.append(((depth, rows, channels), BF))
        out_specs.append(aspec())
        scratch += [VMEM((depth, rows, channels), F32)] * 2 + [VMEM(source[2].shape, F32)]
        scratch += sems(2 * depth + 1)
    return ordered(
        functools.partial(sample_kernel, extent, layer, first, count),
        (received,) + tuple(given) + mlp,
        [per_tile(lines, wide)] + specs + [whole(x.shape) for x in mlp],
        follow,
        grid=(tiles,),
        out_shape=any_outs(*outs),
        out_specs=tuple(out_specs),
        scratch_shapes=scratch,
        compiler_params=params(62.5),
        cost_estimate=cost(),
        name="sample",
    )


def sample_back_kernel(
    extent, layer, coords, dp_ref, f_ref, g_ref, s_ref, hidden, semantic, density, *refs
):
    du_ref, pack_ref, total, table, head = refs[-5:]
    step = pl.program_id(0)
    channels = hidden.shape[1]
    slots = table.shape[1]

    @pl.when(step == 0)
    def _():
        total[...] = jnp.zeros_like(total)
        pack_ref[0:PACK, :] = jnp.zeros((PACK, channels), F32)
        if len(refs) > 5:
            pack_ref[PACK : 2 * PACK, :] = refs[0][...]
        rows = head_rows(semantic[layer], density[layer : layer + 1, :], DROWS)
        head[...] = nt(identity(channels, channels), rows).astype(BF)

    fill_weights(table, coord_rows(coords[0], slots), extent)
    grad_heads = dp_ref[0]
    grad_inner = (nn(head[...], grad_heads) * s_ref[0]).astype(BF)
    ones = jnp.ones((16, slots), BF)
    pack_ref[0:channels, :] += nt(f_ref[0], grad_inner)
    pack_ref[channels : channels + 16, :] += nt(ones, grad_inner)
    at = channels + 16
    pack_ref[at : at + DROWS, :] += nt(grad_heads, g_ref[0])
    at += DROWS
    pack_ref[at : at + 16, 0:DROWS] += nt(ones, grad_heads)
    grad_features = nn(hidden[layer], grad_inner).astype(BF)
    total[...] += nt(table[...], grad_features)

    @pl.when(step == pl.num_programs(0) - 1)
    def _():
        du_ref[...] = total[...].astype(BF)


def sample_back(extent, layer, received, grad_heads, feature, act, slope, mlp, packs, follow=()):
    tiles, lines, wide = received.shape
    _, channels, slots = feature.shape
    voxels = extent[0] * extent[1] * extent[2]
    hidden, _, semantic, density = mlp[:4]
    outs = ((voxels, channels), (PACK * (1 + len(packs)), channels))
    return ordered(
        functools.partial(sample_back_kernel, extent, layer),
        (received, grad_heads, feature, act, slope, hidden, semantic, density) + packs,
        [per_tile(lines, wide)]
        + [per_tile(n, slots) for n in (DROWS, channels, channels, channels)]
        + [whole(x.shape) for x in (hidden, semantic, density) + packs],
        follow,
        grid=(tiles,),
        out_shape=any_outs((outs[0], BF), (outs[1], F32)),
        out_specs=tuple(whole(shape) for shape in outs),
        scratch_shapes=[
            VMEM((voxels, channels), F32),
            VMEM((voxels, slots), BF),
            VMEM((channels, DROWS), BF),
        ],
        compiler_params=params(62.5),
        cost_estimate=cost(),
        name="sample_back",
    )


def composite_kernel(
    classes, layer, starts, pixels, owner_ref, rank_ref, view, heads, cot,
    pic_ref, dp_ref, split, by_ray, grads, density, weights, grad_w, acc,
):
    tiles = heads.shape[0]
    rays, samples = owner_ref.shape
    step = 4.0 / samples
    split[...] = jnp.zeros_like(split)
    for t in range(tiles):
        value = heads[t]
        high = value.astype(BF)
        split[t, 0:PROWS, 0:CAP] = high.astype(F32)
        split[t, PROWS : 2 * PROWS, 0:CAP] = value - high.astype(F32)

    def hots(k):
        return window_onehots(
            starts, owner_ref[k : k + 1, :], rank_ref[k : k + 1, :], k, rays, tiles
        )

    for k in range(rays):
        hot, bases = hots(k)
        windows = jnp.concatenate(
            [split[t, :, pl.ds(bases[t], WINDOW)].astype(BF) for t in range(tiles)], axis=1
        )
        both = nn(windows, hot)
        one = both[:PROWS] + both[PROWS:]
        by_ray[k] = one
        density[k : k + 1, :] = one[classes : classes + 1]

    pre = density[...]
    visible = view[...].astype(F32)
    small = jnp.exp(-jnp.abs(pre))
    optical = visible * (jnp.maximum(pre, 0.0) + jnp.log1p(small)) * step
    passing = jnp.exp(-(lane_cumsum(optical) - optical))
    fading = jnp.exp(-optical)
    weight = passing * (1.0 - fading)
    weights[...] = weight
    row = iota((PROWS, samples), 0)
    lane = iota((PROWS, rays), 1)
    cotangent = nt(identity(PROWS, classes + 1), cot[layer])
    picture = jnp.zeros((PROWS, rays), F32)
    for k in range(rays):
        there = lane == pixels[k]
        dpic = jnp.sum(jnp.where(there, cotangent, 0.0), axis=1, keepdims=True)
        value = jnp.where(row < classes, by_ray[k], jnp.where(row == classes, 1.0, 0.0))
        one = weights[k : k + 1, :]
        colour = jnp.sum(value * one, axis=1, keepdims=True)
        picture = jnp.where(there, colour, picture)
        grad_w[k : k + 1, :] = jnp.sum(value * dpic, axis=0, keepdims=True)
        grads[k] = dpic * one
    pic_ref[...] = picture
    grad_weight = grad_w[...]
    carried = grad_weight * weight
    later = jnp.sum(carried, axis=1, keepdims=True) - lane_cumsum(carried)
    grad_optical = grad_weight * passing * fading - later
    slope = jnp.where(pre >= 0.0, 1.0, small) / (1.0 + small)
    density[...] = grad_optical * visible * step * slope
    acc[...] = jnp.zeros_like(acc)
    zero = jnp.zeros((DROWS - PROWS, samples), F32)
    for k in range(rays):
        hot, bases = hots(k)
        grad = jnp.where(row == classes, density[k : k + 1, :], grads[k])
        moved = nt(jnp.concatenate([grad, zero], axis=0).astype(BF), hot)
        for t in range(tiles):
            acc[t, :, pl.ds(bases[t], WINDOW)] += moved[:, t * WINDOW : (t + 1) * WINDOW]
    for t in range(tiles):
        dp_ref[t] = acc[t, :, 0:CAP].astype(BF)


def composite(starts, pixels, owner, rank, view, heads, cot, layer, classes, follow=()):
    tiles, _, slots = heads.shape
    rays, samples = owner.shape
    outs = ((PROWS, rays), (tiles, DROWS, slots))
    return ordered(
        functools.partial(composite_kernel, classes, layer),
        (starts, pixels, owner, rank, view, heads, cot,),
        [sspec(), sspec()] + [whole(x.shape) for x in (owner, rank, view, heads, cot)],
        follow,
        grid=(1,),
        out_shape=(jax.ShapeDtypeStruct(outs[0], F32), jax.ShapeDtypeStruct(outs[1], BF)),
        out_specs=tuple(whole(s) for s in outs),
        scratch_shapes=[
            VMEM((tiles, 2 * PROWS, CAP + WINDOW), F32),
            VMEM((rays, PROWS, samples), F32),
            VMEM((rays, PROWS, samples), F32),
            VMEM((rays, samples), F32),
            VMEM((rays, samples), F32),
            VMEM((rays, samples), F32),
            VMEM((tiles, DROWS, CAP + WINDOW), F32),
        ],
        compiler_params=params(62.5),
        cost_estimate=cost(),
        name="composite",
    )


def add_kernel(parts, out_ref):
    total = parts[0].astype(F32)
    for n in range(1, parts.shape[0]):
        total = total + parts[n].astype(F32)
    total = total.astype(out_ref.dtype)
    for n in range(out_ref.shape[0]):
        out_ref[n] = total


def add_parts(parts, copies, follow=()):
    shape = (copies,) + parts.shape[1:]
    return ordered(
        add_kernel,
        (parts,),
        [whole(parts.shape)],
        follow,
        grid=(1,),
        out_shape=jax.ShapeDtypeStruct(shape, parts.dtype),
        out_specs=whole(shape),
        compiler_params=params(62.5),
        cost_estimate=cost(),
        name="add_parts",
    )


def hold_kernel(*refs):
    del refs


def hold(values, follow):
    return ordered(
        hold_kernel,
        values,
        [aspec()] * len(values),
        follow,
        out_shape=any_outs(*((x.shape, x.dtype) for x in values)),
        out_specs=(aspec(),) * len(values),
        input_output_aliases={n: n for n in range(len(values))},
        compiler_params=params(62.5),
        cost_estimate=cost(),
        name="hold",
    )


def all_to_all(value, axis):
    return lax.all_to_all(value, axis, split_axis=0, concat_axis=0, tiled=True)


def exchange(first, last):
    devices = lax.axis_size("tile")
    up = [(i, i + 1) for i in range(devices - 1)]
    down = [(i + 1, i) for i in range(devices - 1)]
    return lax.ppermute(last, "tile", up), lax.ppermute(first, "tile", down)


def norm_grads(y, grad, mean, inverse, gains, shifts):
    centred = (y - mean) * inverse
    normal = centred * gains + shifts
    sigma = 1.0 / (1.0 + jnp.exp(-normal))
    return grad * sigma * (1.0 + normal * (1.0 - sigma)), centred


def finish_back(sums, edges, ups, spare, out_sem):
    rows = edges.shape[1] - 16
    value = sums[...]
    high = value.astype(BF).astype(F32)
    middle = (value - high).astype(BF).astype(F32)
    low = value - high - middle
    tail = jnp.concatenate([high[0:2], middle[0:2], low[0:2], jnp.zeros((10,) + high.shape[1:], F32)], axis=0)
    tail = tail.astype(BF)
    edges[0, rows:, :] = tail
    edges[1, rows:, :] = tail
    spare[...] = tail
    first_ref, last_ref, far_ref = ups
    copies = [
        started(edges.at[0], first_ref, out_sem.at[0]),
        started(edges.at[1], last_ref, out_sem.at[1]),
        started(spare, far_ref, out_sem.at[2]),
    ]
    for copy in copies:
        copy.wait()


def norm_back_kernel(
    layer, count, cot, local, y, total_hbm, gain_hbm, shift_hbm, first_ref, last_ref, far_ref,
    cot_in, local_in, y_in, total, gain, shift, edges, sums, spare, in_sem, out_sem,
):
    planes, rows, _ = cot.shape
    small = [
        started(total_hbm, total, in_sem.at[3 * planes]),
        started(gain_hbm, gain, in_sem.at[3 * planes + 1]),
        started(shift_hbm, shift, in_sem.at[3 * planes + 2]),
    ]

    def in_copies(p):
        return [
            pltpu.make_async_copy(source.at[p], target.at[p], in_sem.at[3 * p + n])
            for n, (source, target) in enumerate(((cot, cot_in), (local, local_in), (y, y_in)))
        ]

    for p in range(planes):
        for copy in in_copies(p):
            copy.start()
    sums[...] = jnp.zeros_like(sums)
    for copy in small:
        copy.wait()
    mean, inverse = moments(total[...], count)
    gains, shifts = row_of(gain, layer), row_of(shift, layer)

    @pl.loop(0, planes)
    def _(p):
        for copy in in_copies(p):
            copy.wait()
        grad = cot_in[p].astype(F32) + local_in[p].astype(F32)
        inner, centred = norm_grads(y_in[p], grad, mean, inverse, gains, shifts)
        add_stats(sums, inner, inner * centred)
        for side, edge in ((0, 0), (1, planes - 1)):

            @pl.when(p == edge)
            def _():
                edges[side, 0:rows, :] = inner.astype(BF)

    finish_back(sums, edges, (first_ref, last_ref, far_ref), spare, out_sem)


def back_shapes(rows, channels):
    return ((rows + 16, channels), BF), ((rows + 16, channels), BF), ((16, channels), BF)


def back_scratch(rows, channels):
    return [VMEM((2, rows + 16, channels), BF), VMEM((8, channels), F32), VMEM((16, channels), BF)]


def norm_back(cot, local, y, total, gain, shift, layer, count, follow=()):
    planes, rows, channels = local.shape
    return ordered(
        functools.partial(norm_back_kernel, layer, count),
        (cot, local, y, total, gain, shift),
        [aspec()] * 6,
        follow,
        out_shape=any_outs(*back_shapes(rows, channels)),
        out_specs=(aspec(),) * 3,
        scratch_shapes=[VMEM(x.shape, x.dtype) for x in (cot, local, y, total, gain, shift)]
        + back_scratch(rows, channels)
        + sems(3 * planes + 3, 3),
        compiler_params=params(62.5),
        cost_estimate=cost(),
        name="norm_back",
    )


def share_back(sent):
    first, last, far = sent
    tiles = lax.axis_size("tile")

    def move(value, by):
        return lax.ppermute(value, "tile", [(i, (i + by) % tiles) for i in range(tiles)])

    return (move(last, 1), move(first, tiles - 1)) + tuple(move(far, n) for n in range(2, tiles - 1))


def turn_kernel(width, block, r_ref, out_ref, turned):
    planes, rows, channels = r_ref.shape
    chosen = out_ref.shape[1]
    pick = iota((chosen, channels), 1) == iota((chosen, channels), 0) + block[0] * chosen
    pick = pick.astype(F32).astype(BF)
    place = iota((chosen, rows), 1)
    on_y, on_z = lax.div(place, width), lax.rem(place, width)
    height = rows // width
    for p in range(planes):
        turned[...] = nt(pick, r_ref[p])
        for b in range(3):
            for c in range(3):
                shift = (b - 1) * width + (c - 1)
                value = turned[...]
                if shift:
                    value = pltpu.roll(value, (-shift) % rows, 1)
                y, z = on_y + (b - 1), on_z + (c - 1)
                inside = (y >= 0) & (y < height) & (z >= 0) & (z < width)
                value = jnp.where(inside, value, 0.0).astype(BF)
                for a in range(3):
                    target = p - a
                    if 0 <= target < planes - 2:
                        out_ref[9 * a + 3 * b + c, :, target * rows : (target + 1) * rows] = value


def turn(block, rounded, width, blocks, follow=()):
    planes, rows, channels = rounded.shape
    chosen = channels // blocks
    shape = (27, chosen, (planes - 2) * rows)
    return ordered(
        functools.partial(turn_kernel, width),
        (block, rounded,),
        [sspec(), whole(rounded.shape)],
        follow,
        grid=(1,),
        out_shape=jax.ShapeDtypeStruct(shape, BF),
        out_specs=whole(shape),
        scratch_shapes=[VMEM((chosen, rows), F32)],
        compiler_params=params(62.5),
        cost_estimate=cost(),
        name="turn",
    )


def weight_grad_kernel(layer, count, first, parts, tiles, spots, taps_hbm, *refs):
    grads, refs = refs[:parts], refs[parts:]
    if first:
        y, refs = refs[0], refs[1:]
        y_before, y_after = y.at[pl.ds(0, 1)], y.at[pl.ds(y.shape[0] - 1, 1)]
    else:
        y, y_before, y_after, refs = refs[0], refs[1], refs[2], refs[3:]
    own_far, others, refs = refs[0], refs[1:tiles], refs[tiles:]
    total_hbm, gain_hbm, shift_hbm, refs = *refs[:3], refs[3:]
    dy_ref, wg_ref, back_ref, refs = *refs[:3], refs[3:]
    grads_in, refs = refs[:parts], refs[parts:]
    (taps_in, y_in, y_halo, dn_halo, rest, back, total, gain, shift, dy_buf, dy_rows, wg_buf, in_sem,
     out_sem) = refs
    planes, rows, channels = grads[0].shape
    spare = (parts + 1) * planes
    lists = [
        (total_hbm.at[:, pl.ds(0, 8), :], total),
        (gain_hbm, gain),
        (shift_hbm, shift),
        (y_before, y_halo.at[pl.ds(0, 1)]),
        (y_after, y_halo.at[pl.ds(1, 1)]),
        (others[0], dn_halo.at[0]),
        (others[1], dn_halo.at[1]),
        (own_far, rest.at[0]),
    ] + [(other, rest.at[n + 1]) for n, other in enumerate(others[2:])]
    small = [
        started(source, target, in_sem.at[spare + n]) for n, (source, target) in enumerate(lists)
    ]

    def in_copies(p):
        copies = [pltpu.make_async_copy(y.at[p + first], y_in.at[p], in_sem.at[(parts + 1) * p])]
        for n in range(parts):
            copies.append(
                pltpu.make_async_copy(
                    grads[n].at[p], grads_in[n].at[p], in_sem.at[(parts + 1) * p + 1 + n]
                )
            )
        return copies

    for p in range(planes):
        for copy in in_copies(p):
            copy.start()
    heavy = started(taps_hbm, taps_in, in_sem.at[spare + len(lists)])
    for copy in small:
        copy.wait()
    tile = spots[2]
    tails = [rest[0], dn_halo[0, rows:, :], dn_halo[1, rows:, :]]
    tails += [rest[n] for n in range(1, rest.shape[0])]
    for by, tail in zip([0, 1, tiles - 1] + list(range(2, tiles - 1)), tails):
        value = tail.astype(F32)
        value = value[0:2] + value[2:4] + value[4:6]
        back[lax.rem(tile + tiles - by, tiles), 0:2, :] = value
    mean, inverse = moments(total[...], count)
    gains, shifts = row_of(gain, layer), row_of(shift, layer)
    scale = inverse * gains
    both = back[0, 0:2, :]
    for t in range(1, tiles):
        both = both + back[t, 0:2, :]
    back[0, 0:2, :] = both
    sums = both / count

    def finish(inner, centred):
        return scale * (inner - sums[0:1, :] - centred * sums[1:2, :])

    for side, place in ((0, 0), (1, planes + 1)):
        centred = (y_halo[side].astype(F32) - mean) * inverse
        value = finish(dn_halo[side, 0:rows, :].astype(F32), centred)
        dy_buf[place] = jnp.where(spots[side] > 0, value, 0.0).astype(BF)

    @pl.loop(0, planes)
    def _(p):
        for copy in in_copies(p):
            copy.wait()
        grad = grads_in[0][p].astype(F32)
        for n in range(1, parts):
            grad = grad + grads_in[n][p].astype(F32)
        value = finish(*norm_grads(y_in[p], grad, mean, inverse, gains, shifts)).astype(BF)
        dy_buf[p + 1] = value
        dy_rows[pl.ds(pl.multiple_of(p * rows, rows), rows), :] = value

    done = [
        started(dy_buf, dy_ref, out_sem.at[0]),
        started(back.at[0, pl.ds(0, 2), :], back_ref, out_sem.at[2]),
    ]
    heavy.wait()
    wg_buf[...] = nn(taps_in[...], dy_rows[...]).astype(BF)
    done.append(started(wg_buf, wg_ref, out_sem.at[1]))
    for copy in done:
        copy.wait()


def weight_grad(
    spots, taps_t, grads, y, y_halo, far, others, total, gain, shift, layer, count, follow=()
):
    planes, rows, channels = grads[0].shape
    wide = taps_t.shape[0]
    tiles = len(others) + 1
    ext = (planes + 2, rows, channels)
    own = (planes, rows, channels)
    operands = (taps_t,) + tuple(grads) + (y,) + tuple(y_halo) + (far,) + tuple(others)
    operands += (total, gain, shift)
    return ordered(
        functools.partial(weight_grad_kernel, layer, count, 0 if y_halo else 1, len(grads), tiles),
        (spots,) + operands,
        [sspec()] + [aspec()] * len(operands),
        follow,
        out_shape=any_outs((ext, BF), ((wide, channels), BF), ((2, channels), F32)),
        out_specs=(aspec(),) * 3,
        scratch_shapes=[VMEM(x.shape, x.dtype) for x in grads]
        + [
            VMEM(taps_t.shape, BF),
            VMEM(own, F32),
            VMEM((2, rows, channels), BF if y_halo else F32),
            VMEM((2, rows + 16, channels), BF),
            VMEM((tiles - 2, 16, channels), BF),
            VMEM((tiles, 8, channels), F32),
            VMEM((tiles, 8, channels), F32),
            VMEM(gain.shape, F32),
            VMEM(gain.shape, F32),
            VMEM(ext, BF),
            VMEM((planes * rows, channels), BF),
            VMEM((wide, channels), BF),
        ]
        + sems((len(grads) + 1) * planes + 8 + tiles, 3),
        compiler_params=params(62.5),
        cost_estimate=cost(),
        name="weight_grad",
    )


def conv_back_kernel(width, layer, count, parts, dy, w_hbm, *refs):
    more = count is not None
    grads, refs = refs[:parts], refs[parts:]
    if more:
        y, total_hbm, gain_hbm, shift_hbm, refs = *refs[:4], refs[4:]
    out_ref, refs = refs[0], refs[1:]
    if more:
        sent, refs = refs[:3], refs[3:]
    grads_in, refs = refs[:parts], refs[parts:]
    raw, xs, weight, out_buf, in_sem, w_sem, out_sem, refs = *refs[:7], refs[7:]
    ext_planes, rows, channels = dy.shape
    planes = ext_planes - 2
    group = planes // 2
    pairs = 2
    each = parts + 1
    body = started(dy, raw, in_sem.at[each * pairs])
    heavy = [
        started(
            w_hbm.at[layer, pl.ds((26 - o) * channels, channels), :],
            weight.at[:, pl.ds(o * channels, channels)],
            w_sem.at[o],
        )
        for o in range(27)
    ]
    small = []
    if more:
        y_in, total, gain, shift, edges, sums, spare, back_sem = refs
        small = [
            started(source, target, in_sem.at[each * pairs + 1 + n])
            for n, (source, target) in enumerate(
                ((total_hbm.at[:, pl.ds(0, 8), :], total), (gain_hbm, gain), (shift_hbm, shift))
            )
        ]
        sums[...] = jnp.zeros_like(sums)

    def in_copies(i):
        two = pl.ds(group * i, group)
        copies = [
            pltpu.make_async_copy(grads[n].at[two], grads_in[n].at[two], in_sem.at[each * i + n])
            for n in range(parts)
        ]
        if more:
            copies.append(
                pltpu.make_async_copy(
                    y.at[pl.ds(group * i + 1, group)], y_in.at[two], in_sem.at[each * i + parts]
                )
            )
        return copies

    def out_copy(i):
        two = pl.ds(group * i, group)
        return pltpu.make_async_copy(out_buf.at[two], out_ref.at[two], out_sem.at[i])

    for i in range(pairs):
        for copy in in_copies(i):
            copy.start()
    clear_edges(xs, width, rows)
    body.wait()

    @pl.loop(0, ext_planes)
    def _(p):
        put_plane(xs, p, raw[p].astype(F32), width)

    for copy in small + heavy:
        copy.wait()
    if more:
        mean, inverse = moments(total[...], count)
        gains, shifts = row_of(gain, layer - 1), row_of(shift, layer - 1)

    @pl.loop(0, pairs)
    def _(i):
        part = nt(tap_group(xs, group * i, group, width, rows), weight[...])
        for copy in in_copies(i):
            copy.wait()
        for n_plane in range(group):
            p = group * i + n_plane
            value = part[n_plane * rows : (n_plane + 1) * rows]
            for n in range(parts):
                value = value + grads_in[n][p].astype(F32)
            out_buf[p] = value
            if more:
                inner, centred = norm_grads(y_in[p], value, mean, inverse, gains, shifts)
                add_stats(sums, inner, inner * centred)

                for side, near in ((0, 0), (1, group - 1)):
                    if n_plane == near:

                        @pl.when(p == side * (planes - 1))
                        def _():
                            edges[side, 0:rows, :] = inner.astype(BF)

        out_copy(i).start()

    if more:
        finish_back(sums, edges, sent, spare, back_sem)
    for i in range(pairs):
        out_copy(i).wait()


def conv_back(dy, grads, weights, layer, width, norm=None, follow=()):
    ext_planes, rows, channels = dy.shape
    own = (ext_planes - 2, rows, channels)
    pairs = 2
    outs, extra, scratch = [(own, F32)], (), []
    if norm is not None:
        y, total, gain, shift, count = norm
        extra = (y, total, gain, shift)
        outs += list(back_shapes(rows, channels))
        scratch = [VMEM(own, F32), VMEM((total.shape[0], 8, channels), F32)]
        scratch += [VMEM(gain.shape, F32), VMEM(gain.shape, F32)]
        scratch += back_scratch(rows, channels) + sems(3)
    else:
        count = None
    return ordered(
        functools.partial(conv_back_kernel, width, layer, count, len(grads)),
        (dy, weights) + tuple(grads) + extra,
        [aspec()] * (2 + len(grads) + len(extra)),
        follow,
        out_shape=any_outs(*outs),
        out_specs=(aspec(),) * len(outs),
        scratch_shapes=[VMEM(x.shape, x.dtype) for x in grads]
        + [VMEM(dy.shape, BF)]
        + conv_scratch(ext_planes, rows, width, channels, True)
        + [VMEM(own, F32)]
        + sems(pairs * (len(grads) + 1) + 4, 27, pairs)
        + scratch,
        compiler_params=params(62.5),
        cost_estimate=cost(),
        name="conv_back",
    )


GROUP = 3


def gather_ray(slices):
    return lax.all_gather(slices.reshape(-1, slices.shape[-1]), "ray", axis=0)


def place_kernel(layer, blocks, source, *refs):
    out_ref, taken, out, in_sem, out_sem = refs[-5:]
    _, offsets, rows, _ = out_ref.shape
    chosen = rows // blocks
    steps = offsets // GROUP
    lines = GROUP * chosen

    def in_copy(n):
        some = pl.ds(n * lines, lines)
        return pltpu.make_async_copy(
            source.at[pl.ds(0, blocks), some], taken.at[:, some], in_sem.at[n]
        )

    for n in range(steps):
        in_copy(n).start()
    done = []
    for n in range(steps):
        in_copy(n).wait()
        for o in range(n * GROUP, (n + 1) * GROUP):
            for ray in range(blocks):
                out[o, ray * chosen : (ray + 1) * chosen, :] = taken[
                    ray, o * chosen : (o + 1) * chosen, :
                ].astype(F32)
        some = pl.ds(n * GROUP, GROUP)
        done.append(started(out.at[some], out_ref.at[layer, some], out_sem.at[n]))
    for copy in done:
        copy.wait()


def place(parts, layer, layers, blocks, kept, follow=()):
    _, lines, channels = parts.shape
    offsets = lines * blocks // channels
    return ordered(
        functools.partial(place_kernel, layer, blocks),
        (parts,) + kept,
        [aspec()] * (1 + len(kept)),
        follow,
        out_shape=jax.ShapeDtypeStruct((layers, offsets, channels, channels), F32),
        out_specs=aspec(),
        scratch_shapes=[VMEM((blocks, lines, channels), BF), VMEM((offsets, channels, channels), F32)]
        + sems(offsets // GROUP, offsets // GROUP),
        input_output_aliases={1: 0} if kept else {},
        compiler_params=params(62.5),
        cost_estimate=cost(),
        name="place",
    )


def per_device(
    volume,
    sample_cells,
    sample_fracs,
    view_mask,
    pixel_of_ray,
    conv_weight,
    norm_gain,
    norm_shift,
    hidden_weight,
    hidden_bias,
    density_weight,
    density_bias,
    semantic_weight,
    semantic_bias,
    render_cotangent,
    volume_cotangent,
):
    extent = volume.shape[:3]
    depth, height, width, channels = volume.shape
    rows = height * width
    voxels = depth * rows
    tiles = lax.axis_size("tile")
    ray_devices = lax.axis_size("ray")
    count = float(voxels * tiles)
    rays, samples = sample_cells.shape
    classes = semantic_weight.shape[2]
    layers = conv_weight.shape[0]
    blocks = min(BLOCKS, ray_devices)
    chosen = channels // blocks
    tile, ray = lax.axis_index("tile"), lax.axis_index("ray")
    block = lax.rem(ray, blocks).astype(jnp.int32).reshape(1)

    own = volume.reshape(depth, rows, channels)
    before, after = exchange(own[:2], own[-2:])
    flags = jnp.stack([tile > 0, tile < tiles - 1]).astype(jnp.int32)

    owner_of = lax.div(sample_cells, voxels)
    held = owner_of[None] == jnp.arange(tiles, dtype=jnp.int32)[:, None, None]
    earlier = jnp.arange(rays)[None, :] < jnp.arange(rays)[:, None]
    starts = jnp.sum(
        (held[:, None, :, :] & earlier[None, :, :, None]).astype(jnp.int32), axis=(2, 3)
    ).reshape(tiles * rays)
    pixels = pixel_of_ray[0]
    buffer, owner, rank = prepare(extent, starts, sample_cells, sample_fracs, tiles, channels)

    weights = conv_weight.reshape(layers, 27 * channels, channels)
    mlp = (
        hidden_weight,
        hidden_bias,
        semantic_weight,
        density_weight,
        semantic_bias,
        density_bias[None],
    )
    y_ext, v_ext, mixed = conv_first(before, own, after, buffer, weights, 0, width)
    total = received = all_to_all(mixed, "tile")
    taps_first = turn(block, v_ext, width, blocks)
    v_next, r_ext, y_next, stat, y_first, y_last = conv_next(
        flags, y_ext, v_ext, total, norm_gain, norm_shift, weights, 0, width, count,
        follow=(taps_first,),
    )
    total_next = all_to_all(stat, "tile")
    heads, feature, act, slope = sample(extent, received, (r_ext, 1), 0, mlp)
    heads_last, feature_last, act_last, slope_last, r_last = sample(
        extent, received, (y_next, v_next, total_next, norm_gain, norm_shift), 1, mlp, count,
        follow=(heads,),
    )

    def draw(heads, layer, follow):
        return composite(
            starts, pixels, owner, rank, view_mask, all_to_all(heads, "tile"), render_cotangent,
            layer, classes, follow=follow,
        )

    picture, grad_heads = draw(heads, 0, (heads_last,))
    picture_last, grad_heads_last = draw(heads_last, 1, (grad_heads,))
    shares = (ray_devices, voxels // ray_devices, channels)
    planes = (depth, rows, channels)
    local, pack = sample_back(
        extent, 0, received, all_to_all(grad_heads, "tile"), feature, act, slope, mlp, (),
        follow=(grad_heads_last,),
    )
    parts = all_to_all(local.reshape(shares), "ray")
    local_last, packed = sample_back(
        extent, 1, received, all_to_all(grad_heads_last, "tile"), feature_last, act_last,
        slope_last, mlp, (pack,), follow=(local,),
    )
    copies = add_parts(parts, ray_devices, follow=(local_last,))
    parts_last = all_to_all(local_last.reshape(shares), "ray")
    taps_next = turn(block, r_ext, width, blocks, follow=(copies,))
    copies_last = add_parts(parts_last, ray_devices, follow=(taps_next,))
    sums_last = all_to_all(copies_last, "ray").reshape(planes)
    y_edges = exchange(*hold((y_first, y_last), (copies_last,)))
    copies, packed = hold((copies, packed), (sums_last,) + y_edges)
    sums = all_to_all(copies, "ray").reshape(planes)
    packed = lax.psum_scatter(packed, "ray", scatter_dimension=0, tiled=True)

    cot = volume_cotangent.reshape(planes)
    wide_taps = (27 * chosen, voxels)
    spots = jnp.stack([tile > 0, tile < tiles - 1, tile]).astype(jnp.int32)
    sent = norm_back(
        cot, sums_last, y_next, total_next, norm_gain, norm_shift, 1, count,
        follow=y_edges + (copies,),
    )
    dy, part, back_last = weight_grad(
        spots, taps_next.reshape(wide_taps), (cot, sums_last), y_next, y_edges, sent[2],
        share_back(sent), total_next, norm_gain, norm_shift, 1, count,
    )
    share = (tiles, 27 * chosen // tiles, channels)
    (held,) = hold((part,), (sums,))
    parts = all_to_all(held.reshape(share), "tile")
    grad, *sent = conv_back(
        dy, (cot, sums_last, sums), weights, 1, width,
        (y_ext, total, norm_gain, norm_shift, count), follow=(held,),
    )
    others = share_back(sent)
    shards = add_parts(parts, tiles, follow=others)
    shard = all_to_all(shards, "tile")

    dy, part, back = weight_grad(
        spots, taps_first.reshape(wide_taps), (grad,), y_ext, (), sent[2], others, total,
        norm_gain, norm_shift, 0, count, follow=(shards,),
    )
    (part,) = hold((part,), (shard,))
    parts = all_to_all(part.reshape(share), "tile")
    (shard,) = hold((shard,), (part,))
    copies = add_parts(parts, tiles, follow=(shard,))
    slices = all_to_all(copies, "tile")

    conv_grad = place(gather_ray(shard), 1, layers, blocks, (), follow=(slices,))
    packed = all_to_all(add_parts(packed[None], tiles, follow=(slices,)), "tile")
    packed = add_parts(packed, ray_devices, follow=(conv_grad,))
    (grad,) = conv_back(dy, (grad,), weights, 0, width, follow=(packed,))
    packed = all_to_all(packed, "ray")
    packed = packed.reshape(layers, PACK, channels)[::-1]
    conv_grad = place(gather_ray(slices), 0, layers, blocks, (conv_grad,), follow=(grad,))

    at = channels + 16
    heads = packed[:, at : at + DROWS]
    head_bias = packed[:, at + DROWS, :DROWS]
    return (
        jnp.swapaxes(jnp.stack([picture, picture_last])[:, : classes + 1], 1, 2),
        r_last.reshape(volume.shape),
        grad.reshape(volume.shape),
        conv_grad,
        jnp.stack([back, back_last])[:, 1],
        jnp.stack([back, back_last])[:, 0],
        packed[:, :channels],
        packed[:, channels],
        heads[:, classes],
        head_bias[:, classes],
        jnp.swapaxes(heads[:, :classes], 1, 2),
        head_bias[:, :classes],
    )


def solution(mesh):
    in_specs = (
        P("tile", None, None, None),
        P(("ray", "tile"), None),
        P(None, ("ray", "tile"), None),
        P(("ray", "tile"), None),
        P(("ray", "tile"), None),
        P(),
        P(),
        P(),
        P(),
        P(),
        P(),
        P(),
        P(),
        P(),
        P(None, ("ray", "tile"), None),
        P("tile", None, None, None),
    )
    out_specs = (
        P(None, ("ray", "tile"), None),
        P("tile", None, None, None),
        P("tile", None, None, None),
        P(),
        P(),
        P(),
        P(),
        P(),
        P(),
        P(),
        P(),
        P(),
    )
    return jax.shard_map(
        per_device, mesh=mesh, in_specs=in_specs, out_specs=out_specs, check_vma=False
    )
```

```python
import functools

import jax
import jax.numpy as jnp
from jax import lax
from jax.experimental import pallas as pl
from jax.experimental.pallas import tpu as pltpu
from jax.sharding import PartitionSpec as P

CAP = 768
WINDOW = 256
LANES = 128
PROWS = 24
DROWS = 32
COORDS = 8
BLOCKS = 8
PACK = 320
epsilon = 1e-05
MIB = 1024 * 1024

BF = jnp.bfloat16
F32 = jnp.float32
VMEM = pltpu.VMEM
SMEM = pltpu.SMEM


def nn(left, right):
    return jnp.dot(left, right, preferred_element_type=F32)


def nt(left, right):
    return lax.dot_general(left, right, (((1,), (1,)), ((), ())), preferred_element_type=F32)


def iota(shape, dim):
    return lax.broadcasted_iota(jnp.int32, shape, dim)


def whole(shape):
    return pl.BlockSpec(shape, lambda *_: (0,) * len(shape))


def planes_of(step, shape, first=0):
    return pl.BlockSpec((step,) + shape[1:], lambda i: (i + first // step,) + (0,) * (len(shape) - 1))


def sspec():
    return pl.BlockSpec(memory_space=SMEM)


def aspec():
    return pl.BlockSpec(memory_space=pl.ANY)


def hspec():
    return pl.BlockSpec(memory_space=pltpu.HBM)


def ordered(kernel, operands, in_specs, follow, **options):
    count, skip = len(operands), len(follow)

    def body(*refs):
        kernel(*refs[:count], *refs[count + skip :])

    return pl.pallas_call(body, in_specs=list(in_specs) + [aspec()] * skip, **options)(
        *operands, *follow
    )


def params(mib):
    return pltpu.CompilerParams(vmem_limit_bytes=int(mib * MIB))


def cost():
    return pl.CostEstimate(flops=1, bytes_accessed=1, transcendentals=0)


def lane_cumsum(x):
    lane = iota(x.shape, 1)
    shift = 1
    while shift < x.shape[1]:
        x = x + jnp.where(lane >= shift, pltpu.roll(x, shift, 1), 0.0)
        shift *= 2
    return x


def window_onehots(starts, owner_row, rank_row, ray, rays, tiles):
    rows = iota((WINDOW, rank_row.shape[1]), 0)
    hots, bases = [], []
    for t in range(tiles):
        start = starts[t * rays + ray]
        base = (start // LANES) * LANES
        place = jnp.where(owner_row == t, rank_row + (start - base), -1)
        hots.append((rows == place).astype(F32).astype(BF))
        bases.append(pl.multiple_of(base, LANES))
    return jnp.concatenate(hots, axis=0), bases


def prep_kernel(extent, starts, cells_ref, fracs_ref, out_ref, owner_ref, rank_ref, vals, acc):
    depth, height, width = extent
    tiles = out_ref.shape[0]
    rays, samples = cells_ref.shape
    cells = cells_ref[...]
    voxels = depth * height * width
    owner = lax.div(cells, voxels)
    local = cells - owner * voxels
    base_x = lax.div(local, height * width)
    inner = local - base_x * (height * width)
    base_y = lax.div(inner, width)
    base_z = inner - base_y * width
    rank = jnp.zeros(cells.shape, F32)
    for t in range(tiles):
        mine = owner == t
        rank = jnp.where(mine, lane_cumsum(jnp.where(mine, 1.0, 0.0)) - 1.0, rank)
    owner_ref[...] = owner
    rank_ref[...] = rank.astype(jnp.int32)
    vals[...] = jnp.zeros_like(vals)
    rows = [(base_x + 1).astype(F32), base_y.astype(F32), base_z.astype(F32)]
    low = []
    for d in range(3):
        frac = fracs_ref[d]
        high = frac.astype(BF).astype(F32)
        rows.append(high)
        low.append(frac - high)
    rows += low
    for number, row in enumerate(rows):
        for k in range(rays):
            vals[number : number + 1, k * samples : (k + 1) * samples] = row[k : k + 1]
    acc[...] = jnp.zeros_like(acc)
    for k in range(rays):
        hot, bases = window_onehots(
            starts, owner_ref[k : k + 1, :], rank_ref[k : k + 1, :], k, rays, tiles
        )
        moved = nt(vals[:, k * samples : (k + 1) * samples].astype(BF), hot)
        for t in range(tiles):
            acc[t, :, pl.ds(bases[t], WINDOW)] += moved[:, t * WINDOW : (t + 1) * WINDOW]
    out_ref[...] = jnp.zeros_like(out_ref)
    wide = out_ref.shape[2]
    lines = CAP // wide
    for n in range(lines):
        part = slice(n * wide, (n + 1) * wide)
        for r in range(6):
            value = acc[:, r : r + 1, part]
            if r >= 3:
                value = value + acc[:, r + 3 : r + 4, part]
            out_ref[:, r * lines + n : r * lines + n + 1, :] = value


def prepare(extent, starts, cells, fracs, tiles, wide, follow=()):
    rays, samples = cells.shape
    outs = ((tiles, COORDS * CAP // wide, wide), (rays, samples), (rays, samples))
    return ordered(
        functools.partial(prep_kernel, extent),
        (starts, cells, fracs,),
        [sspec(), whole(cells.shape), whole(fracs.shape)],
        follow,
        grid=(1,),
        out_shape=(
            jax.ShapeDtypeStruct(outs[0], F32),
            jax.ShapeDtypeStruct(outs[1], jnp.int32),
            jax.ShapeDtypeStruct(outs[2], jnp.int32),
        ),
        out_specs=tuple(whole(s) for s in outs),
        scratch_shapes=[VMEM((16, rays * samples), F32), VMEM((tiles, 16, CAP + WINDOW), F32)],
        compiler_params=params(62.5),
        cost_estimate=cost(),
        name="prep",
    )


def started(source, target, sem):
    copy = pltpu.make_async_copy(source, target, sem)
    copy.start()
    return copy


def put_plane(xs, p, value, width):
    rows, channels = value.shape
    along = lax.rem(iota(value.shape, 0), width)
    left = jnp.where(along == 0, 0.0, pltpu.roll(value, 1, 0))
    right = jnp.where(along == width - 1, 0.0, pltpu.roll(value, rows - 1, 0))
    xs[p, width : width + rows, 0:channels] = left.astype(BF)
    xs[p, width : width + rows, channels : 2 * channels] = value.astype(BF)
    xs[p, width : width + rows, 2 * channels : 3 * channels] = right.astype(BF)


def clear_edges(xs, width, rows):
    planes, _, wide = xs.shape
    for p in range(planes):
        xs[p, 0:width, :] = jnp.zeros((width, wide), BF)
        xs[p, width + rows : 2 * width + rows, :] = jnp.zeros((width, wide), BF)


def taps(xs, p, width, rows):
    return jnp.concatenate(
        [xs[p + a, b * width : b * width + rows, :] for a in range(3) for b in range(3)], axis=1
    )


def tap_group(xs, first, count, width, rows):
    return jnp.concatenate([taps(xs, first + n, width, rows) for n in range(count)], axis=0)


def add_stats(sums, one, two):
    sums[0:1, :] += jnp.sum(one, axis=0, keepdims=True)
    sums[1:2, :] += jnp.sum(two, axis=0, keepdims=True)


def conv_scratch(planes, rows, width, channels, turned):
    shape = (channels, 27 * channels) if turned else (27 * channels, channels)
    return [VMEM((planes, rows + 2 * width, 3 * channels), BF), VMEM(shape, BF)]


def sems(*counts):
    return [pltpu.SemaphoreType.DMA((n,)) for n in counts]


def any_outs(*shapes):
    return tuple(jax.ShapeDtypeStruct(shape, dtype) for shape, dtype in shapes)


def conv_first_kernel(
    width, layer, before, own, after, coords, w_hbm, y_ref, v_ref, mix_ref,
    raw, xs, weight, y_buf, mix, in_sem, out_sem,
):
    planes, rows, channels = own.shape
    pairs = planes // 2 + 1
    body = [
        started(own.at[pl.ds(2 * i, 2)], raw.at[pl.ds(2 * i + 2, 2)], in_sem.at[i])
        for i in range(planes // 2)
    ]
    ends = [
        started(before, raw.at[pl.ds(0, 2)], in_sem.at[pairs]),
        started(after, raw.at[pl.ds(planes + 2, 2)], in_sem.at[pairs + 1]),
    ]
    heavy = started(w_hbm.at[layer], weight, in_sem.at[pairs + 2])
    light = started(coords, mix.at[:, pl.ds(8, coords.shape[1]), :], in_sem.at[pairs + 3])
    clear_edges(xs, width, rows)
    mix[:, 0:8, :] = jnp.zeros((mix.shape[0], 8, channels), F32)
    for copy in body + ends:
        copy.wait()

    @pl.loop(0, planes + 4)
    def _(p):
        put_plane(xs, p, raw[p].astype(F32), width)

    done = [started(raw.at[pl.ds(1, planes + 2)], v_ref, out_sem.at[pairs])]
    light.wait()
    heavy.wait()

    group = (planes + 2) // 2

    def out_copy(i):
        some = pl.ds(group * i, group)
        return pltpu.make_async_copy(y_buf.at[some], y_ref.at[some], out_sem.at[i])

    @pl.loop(0, 2)
    def _(i):
        p = group * i
        part = nn(tap_group(xs, p, group, width, rows), weight[...])
        for n in range(group):
            y_buf[p + n] = part[n * rows : (n + 1) * rows]
        out_copy(i).start()
        inner = part[rows : (group - 1) * rows]
        add_stats(mix.at[0], inner, inner * inner)
        edge = jnp.where(i == 0, part[(group - 1) * rows :], part[:rows])
        add_stats(mix.at[0], edge, edge * edge)

    for t in range(1, mix.shape[0]):
        mix[t, 0:8, :] = mix[0, 0:8, :]
    done.append(started(mix, mix_ref, out_sem.at[pairs + 1]))
    for copy in done:
        copy.wait()
    for i in range(2):
        out_copy(i).wait()


def conv_first(before, own, after, coords, weights, layer, width):
    planes, rows, channels = own.shape
    ext = (planes + 2, rows, channels)
    tiles, lines, _ = coords.shape
    pairs = planes // 2 + 1
    return ordered(
        functools.partial(conv_first_kernel, width, layer),
        (before, own, after, coords, weights),
        [aspec()] * 5,
        (),
        out_shape=any_outs((ext, F32), (ext, BF), ((tiles, 8 + lines, channels), F32)),
        out_specs=(aspec(),) * 3,
        scratch_shapes=[VMEM((planes + 4, rows, channels), BF)]
        + conv_scratch(planes + 4, rows, width, channels, False)
        + [VMEM(ext, F32), VMEM((tiles, 8 + lines, channels), F32)]
        + sems(pairs + 4, pairs + 2),
        compiler_params=params(62.5),
        cost_estimate=cost(),
        name="conv_first",
    )


def moments(total, count):
    both = jnp.sum(total, axis=0)
    mean = both[0:1, :] / count
    return mean, lax.rsqrt(both[1:2, :] / count - mean * mean + epsilon)


def row_of(ref, layer):
    return ref[layer : layer + 1, :]


def silu(value):
    return value * (1.0 / (1.0 + jnp.exp(-value)))


def conv_next_kernel(
    width, layer, count, flags, y_ext, v_ext, total_hbm, gain_hbm, shift_hbm, w_hbm,
    v_ref, r_ref, y_ref, stat_ref, first_ref, last_ref,
    y_in, v_in, total, gain, shift, xs, weight, v_buf, r_buf, y_buf, edges, stat, in_sem, out_sem,
):
    ext_planes, rows, channels = y_ext.shape
    pairs = ext_planes // 2
    small = [
        started(total_hbm.at[:, pl.ds(0, 8), :], total, in_sem.at[2 * pairs]),
        started(gain_hbm, gain, in_sem.at[2 * pairs + 1]),
        started(shift_hbm, shift, in_sem.at[2 * pairs + 2]),
    ]
    def in_copies(i):
        two = pl.ds(2 * i, 2)
        return (
            pltpu.make_async_copy(y_ext.at[two], y_in.at[two], in_sem.at[2 * i]),
            pltpu.make_async_copy(v_ext.at[two], v_in.at[two], in_sem.at[2 * i + 1]),
        )

    def mid_copies(i):
        two = pl.ds(2 * i, 2)
        return (
            pltpu.make_async_copy(v_buf.at[two], v_ref.at[two], out_sem.at[3 * i]),
            pltpu.make_async_copy(r_buf.at[two], r_ref.at[two], out_sem.at[3 * i + 1]),
        )

    def out_copy(i):
        two = pl.ds(2 * i - 2, 2)
        return pltpu.make_async_copy(y_buf.at[two], y_ref.at[two], out_sem.at[3 * i + 2])

    for i in range(pairs):
        for copy in in_copies(i):
            copy.start()
    heavy = started(w_hbm.at[layer + 1], weight, in_sem.at[2 * pairs + 3])
    clear_edges(xs, width, rows)
    stat[...] = jnp.zeros_like(stat)
    for copy in small:
        copy.wait()
    mean, inverse = moments(total[...], count)
    gains, shifts = row_of(gain, layer), row_of(shift, layer)

    @pl.loop(0, pairs)
    def _(i):
        for copy in in_copies(i):
            copy.wait()
        for side in range(2):
            p = 2 * i + side
            fresh = v_in[p].astype(F32) + silu((y_in[p] - mean) * inverse * gains + shifts)
            v_buf[p] = fresh
            outside = (p == side * (ext_planes - 1)) & (flags[side] == 0)
            rounded = jnp.where(outside, 0.0, fresh).astype(BF)
            r_buf[p] = rounded
            put_plane(xs, p, rounded.astype(F32), width)
        for copy in mid_copies(i):
            copy.start()

        @pl.when(i == 1)
        def _():
            heavy.wait()

        @pl.when(i > 0)
        def _():
            p = 2 * i - 2
            part = nn(tap_group(xs, p, 2, width, rows), weight[...])
            y_buf[p] = part[:rows]
            y_buf[p + 1] = part[rows:]
            add_stats(stat.at[0], part, part * part)
            out_copy(i).start()

    edges[0] = y_buf[0].astype(BF)
    edges[1] = y_buf[ext_planes - 3].astype(BF)
    for t in range(1, stat.shape[0]):
        stat[t] = stat[0]
    done = [
        started(stat, stat_ref, out_sem.at[2]),
        started(edges.at[pl.ds(0, 1)], first_ref, out_sem.at[3 * pairs]),
        started(edges.at[pl.ds(1, 1)], last_ref, out_sem.at[3 * pairs + 1]),
    ]
    for i in range(pairs):
        done += list(mid_copies(i)) + ([out_copy(i)] if i else [])
    for copy in done:
        copy.wait()


def conv_next(flags, y_ext, v_ext, total, gain, shift, weights, layer, width, count, follow=()):
    ext_planes, rows, channels = y_ext.shape
    ext = y_ext.shape
    inner = (ext_planes - 2, rows, channels)
    stat = (total.shape[0], 8, channels)
    pairs = ext_planes // 2
    edge = (1, rows, channels)
    return ordered(
        functools.partial(conv_next_kernel, width, layer, count),
        (flags, y_ext, v_ext, total, gain, shift, weights),
        [sspec()] + [aspec()] * 6,
        follow,
        out_shape=any_outs((ext, F32), (ext, BF), (inner, F32), (stat, F32), (edge, BF), (edge, BF)),
        out_specs=(aspec(),) * 6,
        scratch_shapes=[VMEM(ext, F32), VMEM(ext, BF), VMEM(stat, F32)]
        + [VMEM(gain.shape, F32)] * 2
        + conv_scratch(ext_planes, rows, width, channels, False)
        + [VMEM(ext, F32), VMEM(ext, BF), VMEM(inner, F32)]
        + [VMEM((2, rows, channels), BF), VMEM(stat, F32)]
        + sems(2 * pairs + 4, 3 * pairs + 2),
        compiler_params=params(62.5),
        cost_estimate=cost(),
        name="conv_next",
    )


def fill_weights(table, coords, extent):
    depth, height, width = extent
    samples = coords[0].shape[1]

    def along(base, frac, size):
        grid = iota((size, samples), 0).astype(F32)
        lower = jnp.where(grid == base, 1.0 - frac, 0.0)
        return lower + jnp.where(grid == base + 1.0, frac, 0.0)

    on_x = along(coords[0] - 1.0, coords[3], depth)
    on_y = along(coords[1], coords[4], height)
    on_z = along(coords[2], coords[5], width)
    for x in range(depth):
        on_xy = on_x[x : x + 1] * on_y
        for y in range(height):
            row = (x * height + y) * width
            table[row : row + width, :] = (on_xy[y : y + 1] * on_z).astype(BF)


def diagonal(rows, columns):
    return iota((rows, columns), 0) == iota((rows, columns), 1)


def identity(rows, columns):
    return diagonal(rows, columns).astype(F32).astype(BF)


def head_rows(semantic, density, rows):
    channels, classes = semantic.shape
    turned = nt(identity(rows, classes), semantic)
    return jnp.where(iota((rows, channels), 0) == classes, density.astype(F32), turned).astype(BF)


def column(row, rows):
    return jnp.sum(jnp.where(diagonal(rows, row.shape[1]), row, 0.0), axis=1, keepdims=True)


def coord_rows(block, slots):
    lines = slots // block.shape[1]
    return [
        jnp.concatenate(
            [block[8 + r * lines + n : 9 + r * lines + n, :] for n in range(lines)], axis=1
        )
        for r in range(6)
    ]


def sample_kernel(
    extent, layer, first, count, coords, *refs
):
    if count is None:
        r_hbm, refs = refs[0], refs[1:]
    else:
        y_hbm, v_hbm, total_hbm, gain, shift, refs = refs[0], refs[1], refs[2], refs[3], refs[4], refs[5:]
    hidden, hidden_b, semantic, density, semantic_b, density_b, refs = *refs[:6], refs[6:]
    p_ref, f_ref, g_ref, s_ref, refs = *refs[:4], refs[4:]
    if count is not None:
        r_out, refs = refs[0], refs[1:]
    turned, table, rounded, hidden_t, bias, head_t, head_b, sem, refs = *refs[:8], refs[8:]
    channels = turned.shape[0]
    depth = extent[0]
    classes = semantic.shape[2]
    slots = table.shape[1]
    rows = rounded.shape[1]
    step = pl.program_id(0)

    if count is not None:
        y_in, v_in, total, load_sem = refs

    def in_copies(p):
        return (
            pltpu.make_async_copy(y_hbm.at[p], y_in.at[p], load_sem.at[2 * p]),
            pltpu.make_async_copy(v_hbm.at[p + 1], v_in.at[p], load_sem.at[2 * p + 1]),
        )

    def out_copy(p):
        return pltpu.make_async_copy(rounded.at[p], r_out.at[p], sem.at[p])

    @pl.when(step == 0)
    def _():
        if count is None:
            copy = started(r_hbm.at[pl.ds(first, depth)], rounded, sem.at[0])
        else:
            light = started(total_hbm, total, load_sem.at[2 * depth])
            for p in range(depth):
                for copy in in_copies(p):
                    copy.start()
        same = identity(channels, channels)
        hidden_t[...] = nt(same, hidden[layer]).astype(BF)
        bias[...] = column(hidden_b[layer : layer + 1, :], channels)
        head_t[...] = head_rows(semantic[layer], density[layer : layer + 1, :], PROWS)
        last = jnp.sum(
            jnp.where(iota((1, density_b.shape[1]), 1) == layer, density_b[...], 0.0),
            axis=1,
            keepdims=True,
        )
        place = iota((PROWS, 1), 0) == classes
        head_b[...] = jnp.where(place, last, column(semantic_b[layer : layer + 1, :], PROWS))
        if count is None:
            copy.wait()
        else:
            light.wait()
            mean, inverse = moments(total[...], count)
            gains, shifts = row_of(gain, layer), row_of(shift, layer)

        @pl.loop(0, depth)
        def _(p):
            if count is not None:
                for copy in in_copies(p):
                    copy.wait()
                fresh = v_in[p] + silu((y_in[p] - mean) * inverse * gains + shifts)
                rounded[p] = fresh.astype(BF)
                out_copy(p).start()
            turned[:, pl.ds(pl.multiple_of(p * rows, rows), rows)] = nt(same, rounded[p]).astype(BF)

    fill_weights(table, coord_rows(coords[0], slots), extent)
    feature = nn(turned[...], table[...]).astype(BF)
    f_ref[0] = feature
    inner = nn(hidden_t[...], feature) + bias[...]
    small = jnp.exp(-jnp.abs(inner))
    act = (jnp.maximum(inner, 0.0) + jnp.log1p(small)).astype(BF)
    g_ref[0] = act
    s_ref[0] = jnp.where(inner >= 0.0, 1.0, small) / (1.0 + small)
    p_ref[0] = nn(head_t[...], act) + head_b[...]
    if count is not None:

        @pl.when(step == pl.num_programs(0) - 1)
        def _():
            for p in range(depth):
                out_copy(p).wait()


def per_tile(rows, lanes):
    return pl.BlockSpec((1, rows, lanes), lambda t: (t, 0, 0))


def sample(extent, received, source, layer, mlp, count=None, follow=()):
    tiles, lines, wide = received.shape
    slots = CAP
    rows, channels = extent[1] * extent[2], mlp[0].shape[1]
    depth = extent[0]
    voxels = depth * rows
    outs = [((tiles, PROWS, slots), F32)] + [((tiles, channels, slots), d) for d in (BF, BF, F32)]
    out_specs = [per_tile(n, slots) for n in (PROWS, channels, channels, channels)]
    scratch = [
        VMEM((channels, voxels), BF),
        VMEM((voxels, slots), BF),
        VMEM((depth, rows, channels), BF),
        VMEM((channels, channels), BF),
        VMEM((channels, 1), F32),
        VMEM((PROWS, channels), BF),
        VMEM((PROWS, 1), F32),
    ] + sems(depth)
    if count is None:
        first, given, specs = source[1], source[:1], [aspec()]
    else:
        first, given = 0, source
        specs = [aspec()] * 3 + [whole(x.shape) for x in source[3:]]
        outs.append(((depth, rows, channels), BF))
        out_specs.append(aspec())
        scratch += [VMEM((depth, rows, channels), F32)] * 2 + [VMEM(source[2].shape, F32)]
        scratch += sems(2 * depth + 1)
    return ordered(
        functools.partial(sample_kernel, extent, layer, first, count),
        (received,) + tuple(given) + mlp,
        [per_tile(lines, wide)] + specs + [whole(x.shape) for x in mlp],
        follow,
        grid=(tiles,),
        out_shape=any_outs(*outs),
        out_specs=tuple(out_specs),
        scratch_shapes=scratch,
        compiler_params=params(62.5),
        cost_estimate=cost(),
        name="sample",
    )


def sample_back_kernel(
    extent, layer, coords, dp_ref, f_ref, g_ref, s_ref, hidden, semantic, density, *refs
):
    du_ref, pack_ref, total, table, head = refs[-5:]
    step = pl.program_id(0)
    channels = hidden.shape[1]
    slots = table.shape[1]

    @pl.when(step == 0)
    def _():
        total[...] = jnp.zeros_like(total)
        pack_ref[0:PACK, :] = jnp.zeros((PACK, channels), F32)
        if len(refs) > 5:
            pack_ref[PACK : 2 * PACK, :] = refs[0][...]
        rows = head_rows(semantic[layer], density[layer : layer + 1, :], DROWS)
        head[...] = nt(identity(channels, channels), rows).astype(BF)

    fill_weights(table, coord_rows(coords[0], slots), extent)
    grad_heads = dp_ref[0]
    grad_inner = (nn(head[...], grad_heads) * s_ref[0]).astype(BF)
    ones = jnp.ones((16, slots), BF)
    pack_ref[0:channels, :] += nt(f_ref[0], grad_inner)
    pack_ref[channels : channels + 16, :] += nt(ones, grad_inner)
    at = channels + 16
    pack_ref[at : at + DROWS, :] += nt(grad_heads, g_ref[0])
    at += DROWS
    pack_ref[at : at + 16, 0:DROWS] += nt(ones, grad_heads)
    grad_features = nn(hidden[layer], grad_inner).astype(BF)
    total[...] += nt(table[...], grad_features)

    @pl.when(step == pl.num_programs(0) - 1)
    def _():
        du_ref[...] = total[...].astype(BF)


def sample_back(extent, layer, received, grad_heads, feature, act, slope, mlp, packs, follow=()):
    tiles, lines, wide = received.shape
    _, channels, slots = feature.shape
    voxels = extent[0] * extent[1] * extent[2]
    hidden, _, semantic, density = mlp[:4]
    outs = ((voxels, channels), (PACK * (1 + len(packs)), channels))
    return ordered(
        functools.partial(sample_back_kernel, extent, layer),
        (received, grad_heads, feature, act, slope, hidden, semantic, density) + packs,
        [per_tile(lines, wide)]
        + [per_tile(n, slots) for n in (DROWS, channels, channels, channels)]
        + [whole(x.shape) for x in (hidden, semantic, density) + packs],
        follow,
        grid=(tiles,),
        out_shape=any_outs((outs[0], BF), (outs[1], F32)),
        out_specs=tuple(whole(shape) for shape in outs),
        scratch_shapes=[
            VMEM((voxels, channels), F32),
            VMEM((voxels, slots), BF),
            VMEM((channels, DROWS), BF),
        ],
        compiler_params=params(62.5),
        cost_estimate=cost(),
        name="sample_back",
    )


def composite_kernel(
    classes, layer, starts, pixels, owner_ref, rank_ref, view, heads, cot,
    pic_ref, dp_ref, split, by_ray, grads, density, weights, grad_w, acc,
):
    tiles = heads.shape[0]
    rays, samples = owner_ref.shape
    step = 4.0 / samples
    split[...] = jnp.zeros_like(split)
    for t in range(tiles):
        value = heads[t]
        high = value.astype(BF)
        split[t, 0:PROWS, 0:CAP] = high.astype(F32)
        split[t, PROWS : 2 * PROWS, 0:CAP] = value - high.astype(F32)

    def hots(k):
        return window_onehots(
            starts, owner_ref[k : k + 1, :], rank_ref[k : k + 1, :], k, rays, tiles
        )

    for k in range(rays):
        hot, bases = hots(k)
        windows = jnp.concatenate(
            [split[t, :, pl.ds(bases[t], WINDOW)].astype(BF) for t in range(tiles)], axis=1
        )
        both = nn(windows, hot)
        one = both[:PROWS] + both[PROWS:]
        by_ray[k] = one
        density[k : k + 1, :] = one[classes : classes + 1]

    pre = density[...]
    visible = view[...].astype(F32)
    small = jnp.exp(-jnp.abs(pre))
    optical = visible * (jnp.maximum(pre, 0.0) + jnp.log1p(small)) * step
    passing = jnp.exp(-(lane_cumsum(optical) - optical))
    fading = jnp.exp(-optical)
    weight = passing * (1.0 - fading)
    weights[...] = weight
    row = iota((PROWS, samples), 0)
    lane = iota((PROWS, rays), 1)
    cotangent = nt(identity(PROWS, classes + 1), cot[layer])
    picture = jnp.zeros((PROWS, rays), F32)
    for k in range(rays):
        there = lane == pixels[k]
        dpic = jnp.sum(jnp.where(there, cotangent, 0.0), axis=1, keepdims=True)
        value = jnp.where(row < classes, by_ray[k], jnp.where(row == classes, 1.0, 0.0))
        one = weights[k : k + 1, :]
        colour = jnp.sum(value * one, axis=1, keepdims=True)
        picture = jnp.where(there, colour, picture)
        grad_w[k : k + 1, :] = jnp.sum(value * dpic, axis=0, keepdims=True)
        grads[k] = dpic * one
    pic_ref[...] = picture
    grad_weight = grad_w[...]
    carried = grad_weight * weight
    later = jnp.sum(carried, axis=1, keepdims=True) - lane_cumsum(carried)
    grad_optical = grad_weight * passing * fading - later
    slope = jnp.where(pre >= 0.0, 1.0, small) / (1.0 + small)
    density[...] = grad_optical * visible * step * slope
    acc[...] = jnp.zeros_like(acc)
    zero = jnp.zeros((DROWS - PROWS, samples), F32)
    for k in range(rays):
        hot, bases = hots(k)
        grad = jnp.where(row == classes, density[k : k + 1, :], grads[k])
        moved = nt(jnp.concatenate([grad, zero], axis=0).astype(BF), hot)
        for t in range(tiles):
            acc[t, :, pl.ds(bases[t], WINDOW)] += moved[:, t * WINDOW : (t + 1) * WINDOW]
    for t in range(tiles):
        dp_ref[t] = acc[t, :, 0:CAP].astype(BF)


def composite(starts, pixels, owner, rank, view, heads, cot, layer, classes, follow=()):
    tiles, _, slots = heads.shape
    rays, samples = owner.shape
    outs = ((PROWS, rays), (tiles, DROWS, slots))
    return ordered(
        functools.partial(composite_kernel, classes, layer),
        (starts, pixels, owner, rank, view, heads, cot,),
        [sspec(), sspec()] + [whole(x.shape) for x in (owner, rank, view, heads, cot)],
        follow,
        grid=(1,),
        out_shape=(jax.ShapeDtypeStruct(outs[0], F32), jax.ShapeDtypeStruct(outs[1], BF)),
        out_specs=tuple(whole(s) for s in outs),
        scratch_shapes=[
            VMEM((tiles, 2 * PROWS, CAP + WINDOW), F32),
            VMEM((rays, PROWS, samples), F32),
            VMEM((rays, PROWS, samples), F32),
            VMEM((rays, samples), F32),
            VMEM((rays, samples), F32),
            VMEM((rays, samples), F32),
            VMEM((tiles, DROWS, CAP + WINDOW), F32),
        ],
        compiler_params=params(62.5),
        cost_estimate=cost(),
        name="composite",
    )


def add_kernel(parts, out_ref):
    total = parts[0].astype(F32)
    for n in range(1, parts.shape[0]):
        total = total + parts[n].astype(F32)
    total = total.astype(out_ref.dtype)
    for n in range(out_ref.shape[0]):
        out_ref[n] = total


def add_parts(parts, copies, follow=()):
    shape = (copies,) + parts.shape[1:]
    return ordered(
        add_kernel,
        (parts,),
        [whole(parts.shape)],
        follow,
        grid=(1,),
        out_shape=jax.ShapeDtypeStruct(shape, parts.dtype),
        out_specs=whole(shape),
        compiler_params=params(62.5),
        cost_estimate=cost(),
        name="add_parts",
    )


def hold_kernel(*refs):
    del refs


def hold(values, follow):
    return ordered(
        hold_kernel,
        values,
        [aspec()] * len(values),
        follow,
        out_shape=any_outs(*((x.shape, x.dtype) for x in values)),
        out_specs=(aspec(),) * len(values),
        input_output_aliases={n: n for n in range(len(values))},
        compiler_params=params(62.5),
        cost_estimate=cost(),
        name="hold",
    )


def all_to_all(value, axis):
    return lax.all_to_all(value, axis, split_axis=0, concat_axis=0, tiled=True)


def exchange(first, last):
    devices = lax.axis_size("tile")
    up = [(i, i + 1) for i in range(devices - 1)]
    down = [(i + 1, i) for i in range(devices - 1)]
    return lax.ppermute(last, "tile", up), lax.ppermute(first, "tile", down)


def norm_grads(y, grad, mean, inverse, gains, shifts):
    centred = (y - mean) * inverse
    normal = centred * gains + shifts
    sigma = 1.0 / (1.0 + jnp.exp(-normal))
    return grad * sigma * (1.0 + normal * (1.0 - sigma)), centred


def finish_back(sums, edges, ups, spare, out_sem):
    rows = edges.shape[1] - 16
    value = sums[...]
    high = value.astype(BF).astype(F32)
    middle = (value - high).astype(BF).astype(F32)
    low = value - high - middle
    tail = jnp.concatenate([high[0:2], middle[0:2], low[0:2], jnp.zeros((10,) + high.shape[1:], F32)], axis=0)
    tail = tail.astype(BF)
    edges[0, rows:, :] = tail
    edges[1, rows:, :] = tail
    spare[...] = tail
    first_ref, last_ref, far_ref = ups
    copies = [
        started(edges.at[0], first_ref, out_sem.at[0]),
        started(edges.at[1], last_ref, out_sem.at[1]),
        started(spare, far_ref, out_sem.at[2]),
    ]
    for copy in copies:
        copy.wait()


def norm_back_kernel(
    layer, count, cot, local, y, total_hbm, gain_hbm, shift_hbm, first_ref, last_ref, far_ref,
    cot_in, local_in, y_in, total, gain, shift, edges, sums, spare, in_sem, out_sem,
):
    planes, rows, _ = cot.shape
    small = [
        started(total_hbm, total, in_sem.at[3 * planes]),
        started(gain_hbm, gain, in_sem.at[3 * planes + 1]),
        started(shift_hbm, shift, in_sem.at[3 * planes + 2]),
    ]

    def in_copies(p):
        return [
            pltpu.make_async_copy(source.at[p], target.at[p], in_sem.at[3 * p + n])
            for n, (source, target) in enumerate(((cot, cot_in), (local, local_in), (y, y_in)))
        ]

    for p in range(planes):
        for copy in in_copies(p):
            copy.start()
    sums[...] = jnp.zeros_like(sums)
    for copy in small:
        copy.wait()
    mean, inverse = moments(total[...], count)
    gains, shifts = row_of(gain, layer), row_of(shift, layer)

    @pl.loop(0, planes)
    def _(p):
        for copy in in_copies(p):
            copy.wait()
        grad = cot_in[p].astype(F32) + local_in[p].astype(F32)
        inner, centred = norm_grads(y_in[p], grad, mean, inverse, gains, shifts)
        add_stats(sums, inner, inner * centred)
        for side, edge in ((0, 0), (1, planes - 1)):

            @pl.when(p == edge)
            def _():
                edges[side, 0:rows, :] = inner.astype(BF)

    finish_back(sums, edges, (first_ref, last_ref, far_ref), spare, out_sem)


def back_shapes(rows, channels):
    return ((rows + 16, channels), BF), ((rows + 16, channels), BF), ((16, channels), BF)


def back_scratch(rows, channels):
    return [VMEM((2, rows + 16, channels), BF), VMEM((8, channels), F32), VMEM((16, channels), BF)]


def norm_back(cot, local, y, total, gain, shift, layer, count, follow=()):
    planes, rows, channels = local.shape
    return ordered(
        functools.partial(norm_back_kernel, layer, count),
        (cot, local, y, total, gain, shift),
        [aspec()] * 6,
        follow,
        out_shape=any_outs(*back_shapes(rows, channels)),
        out_specs=(aspec(),) * 3,
        scratch_shapes=[VMEM(x.shape, x.dtype) for x in (cot, local, y, total, gain, shift)]
        + back_scratch(rows, channels)
        + sems(3 * planes + 3, 3),
        compiler_params=params(62.5),
        cost_estimate=cost(),
        name="norm_back",
    )


def share_back(sent):
    first, last, far = sent
    tiles = lax.axis_size("tile")

    def move(value, by):
        return lax.ppermute(value, "tile", [(i, (i + by) % tiles) for i in range(tiles)])

    return (move(last, 1), move(first, tiles - 1)) + tuple(move(far, n) for n in range(2, tiles - 1))


def turn_kernel(width, block, r_ref, out_ref, turned):
    planes, rows, channels = r_ref.shape
    chosen = out_ref.shape[1]
    pick = iota((chosen, channels), 1) == iota((chosen, channels), 0) + block[0] * chosen
    pick = pick.astype(F32).astype(BF)
    place = iota((chosen, rows), 1)
    on_y, on_z = lax.div(place, width), lax.rem(place, width)
    height = rows // width
    for p in range(planes):
        turned[...] = nt(pick, r_ref[p])
        for b in range(3):
            for c in range(3):
                shift = (b - 1) * width + (c - 1)
                value = turned[...]
                if shift:
                    value = pltpu.roll(value, (-shift) % rows, 1)
                y, z = on_y + (b - 1), on_z + (c - 1)
                inside = (y >= 0) & (y < height) & (z >= 0) & (z < width)
                value = jnp.where(inside, value, 0.0).astype(BF)
                for a in range(3):
                    target = p - a
                    if 0 <= target < planes - 2:
                        out_ref[9 * a + 3 * b + c, :, target * rows : (target + 1) * rows] = value


def turn(block, rounded, width, blocks, follow=()):
    planes, rows, channels = rounded.shape
    chosen = channels // blocks
    shape = (27, chosen, (planes - 2) * rows)
    return ordered(
        functools.partial(turn_kernel, width),
        (block, rounded,),
        [sspec(), whole(rounded.shape)],
        follow,
        grid=(1,),
        out_shape=jax.ShapeDtypeStruct(shape, BF),
        out_specs=whole(shape),
        scratch_shapes=[VMEM((chosen, rows), F32)],
        compiler_params=params(62.5),
        cost_estimate=cost(),
        name="turn",
    )


def weight_grad_kernel(layer, count, first, parts, tiles, spots, taps_hbm, *refs):
    grads, refs = refs[:parts], refs[parts:]
    if first:
        y, refs = refs[0], refs[1:]
        y_before, y_after = y.at[pl.ds(0, 1)], y.at[pl.ds(y.shape[0] - 1, 1)]
    else:
        y, y_before, y_after, refs = refs[0], refs[1], refs[2], refs[3:]
    own_far, others, refs = refs[0], refs[1:tiles], refs[tiles:]
    total_hbm, gain_hbm, shift_hbm, refs = *refs[:3], refs[3:]
    dy_ref, wg_ref, back_ref, refs = *refs[:3], refs[3:]
    grads_in, refs = refs[:parts], refs[parts:]
    (taps_in, y_in, y_halo, dn_halo, rest, back, total, gain, shift, dy_buf, dy_rows, wg_buf, in_sem,
     out_sem) = refs
    planes, rows, channels = grads[0].shape
    spare = (parts + 1) * planes
    lists = [
        (total_hbm.at[:, pl.ds(0, 8), :], total),
        (gain_hbm, gain),
        (shift_hbm, shift),
        (y_before, y_halo.at[pl.ds(0, 1)]),
        (y_after, y_halo.at[pl.ds(1, 1)]),
        (others[0], dn_halo.at[0]),
        (others[1], dn_halo.at[1]),
        (own_far, rest.at[0]),
    ] + [(other, rest.at[n + 1]) for n, other in enumerate(others[2:])]
    small = [
        started(source, target, in_sem.at[spare + n]) for n, (source, target) in enumerate(lists)
    ]

    def in_copies(p):
        copies = [pltpu.make_async_copy(y.at[p + first], y_in.at[p], in_sem.at[(parts + 1) * p])]
        for n in range(parts):
            copies.append(
                pltpu.make_async_copy(
                    grads[n].at[p], grads_in[n].at[p], in_sem.at[(parts + 1) * p + 1 + n]
                )
            )
        return copies

    for p in range(planes):
        for copy in in_copies(p):
            copy.start()
    heavy = started(taps_hbm, taps_in, in_sem.at[spare + len(lists)])
    for copy in small:
        copy.wait()
    tile = spots[2]
    tails = [rest[0], dn_halo[0, rows:, :], dn_halo[1, rows:, :]]
    tails += [rest[n] for n in range(1, rest.shape[0])]
    for by, tail in zip([0, 1, tiles - 1] + list(range(2, tiles - 1)), tails):
        value = tail.astype(F32)
        value = value[0:2] + value[2:4] + value[4:6]
        back[lax.rem(tile + tiles - by, tiles), 0:2, :] = value
    mean, inverse = moments(total[...], count)
    gains, shifts = row_of(gain, layer), row_of(shift, layer)
    scale = inverse * gains
    both = back[0, 0:2, :]
    for t in range(1, tiles):
        both = both + back[t, 0:2, :]
    back[0, 0:2, :] = both
    sums = both / count

    def finish(inner, centred):
        return scale * (inner - sums[0:1, :] - centred * sums[1:2, :])

    for side, place in ((0, 0), (1, planes + 1)):
        centred = (y_halo[side].astype(F32) - mean) * inverse
        value = finish(dn_halo[side, 0:rows, :].astype(F32), centred)
        dy_buf[place] = jnp.where(spots[side] > 0, value, 0.0).astype(BF)

    @pl.loop(0, planes)
    def _(p):
        for copy in in_copies(p):
            copy.wait()
        grad = grads_in[0][p].astype(F32)
        for n in range(1, parts):
            grad = grad + grads_in[n][p].astype(F32)
        value = finish(*norm_grads(y_in[p], grad, mean, inverse, gains, shifts)).astype(BF)
        dy_buf[p + 1] = value
        dy_rows[pl.ds(pl.multiple_of(p * rows, rows), rows), :] = value

    done = [
        started(dy_buf, dy_ref, out_sem.at[0]),
        started(back.at[0, pl.ds(0, 2), :], back_ref, out_sem.at[2]),
    ]
    heavy.wait()
    wg_buf[...] = nn(taps_in[...], dy_rows[...]).astype(BF)
    done.append(started(wg_buf, wg_ref, out_sem.at[1]))
    for copy in done:
        copy.wait()


def weight_grad(
    spots, taps_t, grads, y, y_halo, far, others, total, gain, shift, layer, count, follow=()
):
    planes, rows, channels = grads[0].shape
    wide = taps_t.shape[0]
    tiles = len(others) + 1
    ext = (planes + 2, rows, channels)
    own = (planes, rows, channels)
    operands = (taps_t,) + tuple(grads) + (y,) + tuple(y_halo) + (far,) + tuple(others)
    operands += (total, gain, shift)
    return ordered(
        functools.partial(weight_grad_kernel, layer, count, 0 if y_halo else 1, len(grads), tiles),
        (spots,) + operands,
        [sspec()] + [aspec()] * len(operands),
        follow,
        out_shape=any_outs((ext, BF), ((wide, channels), BF), ((2, channels), F32)),
        out_specs=(aspec(),) * 3,
        scratch_shapes=[VMEM(x.shape, x.dtype) for x in grads]
        + [
            VMEM(taps_t.shape, BF),
            VMEM(own, F32),
            VMEM((2, rows, channels), BF if y_halo else F32),
            VMEM((2, rows + 16, channels), BF),
            VMEM((tiles - 2, 16, channels), BF),
            VMEM((tiles, 8, channels), F32),
            VMEM((tiles, 8, channels), F32),
            VMEM(gain.shape, F32),
            VMEM(gain.shape, F32),
            VMEM(ext, BF),
            VMEM((planes * rows, channels), BF),
            VMEM((wide, channels), BF),
        ]
        + sems((len(grads) + 1) * planes + 8 + tiles, 3),
        compiler_params=params(62.5),
        cost_estimate=cost(),
        name="weight_grad",
    )


def conv_back_kernel(width, layer, count, parts, dy, w_hbm, *refs):
    more = count is not None
    grads, refs = refs[:parts], refs[parts:]
    if more:
        y, total_hbm, gain_hbm, shift_hbm, refs = *refs[:4], refs[4:]
    out_ref, refs = refs[0], refs[1:]
    if more:
        sent, refs = refs[:3], refs[3:]
    grads_in, refs = refs[:parts], refs[parts:]
    raw, xs, weight, out_buf, in_sem, w_sem, out_sem, refs = *refs[:7], refs[7:]
    ext_planes, rows, channels = dy.shape
    planes = ext_planes - 2
    group = planes // 2
    pairs = 2
    each = parts + 1
    body = started(dy, raw, in_sem.at[each * pairs])
    heavy = [
        started(
            w_hbm.at[layer, pl.ds((26 - o) * channels, channels), :],
            weight.at[:, pl.ds(o * channels, channels)],
            w_sem.at[o],
        )
        for o in range(27)
    ]
    small = []
    if more:
        y_in, total, gain, shift, edges, sums, spare, back_sem = refs
        small = [
            started(source, target, in_sem.at[each * pairs + 1 + n])
            for n, (source, target) in enumerate(
                ((total_hbm.at[:, pl.ds(0, 8), :], total), (gain_hbm, gain), (shift_hbm, shift))
            )
        ]
        sums[...] = jnp.zeros_like(sums)

    def in_copies(i):
        two = pl.ds(group * i, group)
        copies = [
            pltpu.make_async_copy(grads[n].at[two], grads_in[n].at[two], in_sem.at[each * i + n])
            for n in range(parts)
        ]
        if more:
            copies.append(
                pltpu.make_async_copy(
                    y.at[pl.ds(group * i + 1, group)], y_in.at[two], in_sem.at[each * i + parts]
                )
            )
        return copies

    def out_copy(i):
        two = pl.ds(group * i, group)
        return pltpu.make_async_copy(out_buf.at[two], out_ref.at[two], out_sem.at[i])

    for i in range(pairs):
        for copy in in_copies(i):
            copy.start()
    clear_edges(xs, width, rows)
    body.wait()

    @pl.loop(0, ext_planes)
    def _(p):
        put_plane(xs, p, raw[p].astype(F32), width)

    for copy in small + heavy:
        copy.wait()
    if more:
        mean, inverse = moments(total[...], count)
        gains, shifts = row_of(gain, layer - 1), row_of(shift, layer - 1)

    @pl.loop(0, pairs)
    def _(i):
        part = nt(tap_group(xs, group * i, group, width, rows), weight[...])
        for copy in in_copies(i):
            copy.wait()
        for n_plane in range(group):
            p = group * i + n_plane
            value = part[n_plane * rows : (n_plane + 1) * rows]
            for n in range(parts):
                value = value + grads_in[n][p].astype(F32)
            out_buf[p] = value
            if more:
                inner, centred = norm_grads(y_in[p], value, mean, inverse, gains, shifts)
                add_stats(sums, inner, inner * centred)

                for side, near in ((0, 0), (1, group - 1)):
                    if n_plane == near:

                        @pl.when(p == side * (planes - 1))
                        def _():
                            edges[side, 0:rows, :] = inner.astype(BF)

        out_copy(i).start()

    if more:
        finish_back(sums, edges, sent, spare, back_sem)
    for i in range(pairs):
        out_copy(i).wait()


def conv_back(dy, grads, weights, layer, width, norm=None, follow=()):
    ext_planes, rows, channels = dy.shape
    own = (ext_planes - 2, rows, channels)
    pairs = 2
    outs, extra, scratch = [(own, F32)], (), []
    if norm is not None:
        y, total, gain, shift, count = norm
        extra = (y, total, gain, shift)
        outs += list(back_shapes(rows, channels))
        scratch = [VMEM(own, F32), VMEM((total.shape[0], 8, channels), F32)]
        scratch += [VMEM(gain.shape, F32), VMEM(gain.shape, F32)]
        scratch += back_scratch(rows, channels) + sems(3)
    else:
        count = None
    return ordered(
        functools.partial(conv_back_kernel, width, layer, count, len(grads)),
        (dy, weights) + tuple(grads) + extra,
        [aspec()] * (2 + len(grads) + len(extra)),
        follow,
        out_shape=any_outs(*outs),
        out_specs=(aspec(),) * len(outs),
        scratch_shapes=[VMEM(x.shape, x.dtype) for x in grads]
        + [VMEM(dy.shape, BF)]
        + conv_scratch(ext_planes, rows, width, channels, True)
        + [VMEM(own, F32)]
        + sems(pairs * (len(grads) + 1) + 4, 27, pairs)
        + scratch,
        compiler_params=params(62.5),
        cost_estimate=cost(),
        name="conv_back",
    )


GROUP = 3


def order_kernel(spots, *refs):
    out_ref = refs[-1]
    tiles = out_ref.shape[0]
    for by in range(tiles):
        out_ref[lax.rem(spots[2] + tiles - by, tiles)] = refs[by][...]


def spread_tile(value, spots, follow):
    tiles = lax.axis_size("tile")
    parts = [value]
    for by in range(1, tiles):
        pairs = [(i, (i + by) % tiles) for i in range(tiles)]
        parts.append(lax.ppermute(value, "tile", pairs))
    shape = (tiles,) + value.shape
    return ordered(
        order_kernel,
        (spots,) + tuple(parts),
        [sspec()] + [whole(value.shape)] * tiles,
        follow,
        grid=(1,),
        out_shape=jax.ShapeDtypeStruct(shape, value.dtype),
        out_specs=whole(shape),
        compiler_params=params(62.5),
        cost_estimate=cost(),
        name="order_tiles",
    )


def gather_ray(slices):
    return lax.all_gather(slices.reshape(-1, slices.shape[-1]), "ray", axis=0)


def place_kernel(layer, blocks, source, *refs):
    out_ref, taken, out, in_sem, out_sem = refs[-5:]
    _, offsets, rows, _ = out_ref.shape
    chosen = rows // blocks
    steps = offsets // GROUP
    lines = GROUP * chosen

    def in_copy(n):
        some = pl.ds(n * lines, lines)
        return pltpu.make_async_copy(
            source.at[pl.ds(0, blocks), some], taken.at[:, some], in_sem.at[n]
        )

    for n in range(steps):
        in_copy(n).start()
    done = []
    for n in range(steps):
        in_copy(n).wait()
        for o in range(n * GROUP, (n + 1) * GROUP):
            for ray in range(blocks):
                out[o, ray * chosen : (ray + 1) * chosen, :] = taken[
                    ray, o * chosen : (o + 1) * chosen, :
                ].astype(F32)
        some = pl.ds(n * GROUP, GROUP)
        done.append(started(out.at[some], out_ref.at[layer, some], out_sem.at[n]))
    for copy in done:
        copy.wait()


def place(parts, layer, layers, blocks, kept, follow=()):
    _, lines, channels = parts.shape
    offsets = lines * blocks // channels
    return ordered(
        functools.partial(place_kernel, layer, blocks),
        (parts,) + kept,
        [aspec()] * (1 + len(kept)),
        follow,
        out_shape=jax.ShapeDtypeStruct((layers, offsets, channels, channels), F32),
        out_specs=aspec(),
        scratch_shapes=[VMEM((blocks, lines, channels), BF), VMEM((offsets, channels, channels), F32)]
        + sems(offsets // GROUP, offsets // GROUP),
        input_output_aliases={1: 0} if kept else {},
        compiler_params=params(62.5),
        cost_estimate=cost(),
        name="place",
    )


def per_device(
    volume,
    sample_cells,
    sample_fracs,
    view_mask,
    pixel_of_ray,
    conv_weight,
    norm_gain,
    norm_shift,
    hidden_weight,
    hidden_bias,
    density_weight,
    density_bias,
    semantic_weight,
    semantic_bias,
    render_cotangent,
    volume_cotangent,
):
    extent = volume.shape[:3]
    depth, height, width, channels = volume.shape
    rows = height * width
    voxels = depth * rows
    tiles = lax.axis_size("tile")
    ray_devices = lax.axis_size("ray")
    count = float(voxels * tiles)
    rays, samples = sample_cells.shape
    classes = semantic_weight.shape[2]
    layers = conv_weight.shape[0]
    blocks = min(BLOCKS, ray_devices)
    chosen = channels // blocks
    tile, ray = lax.axis_index("tile"), lax.axis_index("ray")
    block = lax.rem(ray, blocks).astype(jnp.int32).reshape(1)

    own = volume.reshape(depth, rows, channels)
    before, after = exchange(own[:2], own[-2:])
    flags = jnp.stack([tile > 0, tile < tiles - 1]).astype(jnp.int32)

    owner_of = lax.div(sample_cells, voxels)
    held = owner_of[None] == jnp.arange(tiles, dtype=jnp.int32)[:, None, None]
    earlier = jnp.arange(rays)[None, :] < jnp.arange(rays)[:, None]
    starts = jnp.sum(
        (held[:, None, :, :] & earlier[None, :, :, None]).astype(jnp.int32), axis=(2, 3)
    ).reshape(tiles * rays)
    pixels = pixel_of_ray[0]
    buffer, owner, rank = prepare(extent, starts, sample_cells, sample_fracs, tiles, channels)

    weights = conv_weight.reshape(layers, 27 * channels, channels)
    mlp = (
        hidden_weight,
        hidden_bias,
        semantic_weight,
        density_weight,
        semantic_bias,
        density_bias[None],
    )
    y_ext, v_ext, mixed = conv_first(before, own, after, buffer, weights, 0, width)
    total = received = all_to_all(mixed, "tile")
    taps_first = turn(block, v_ext, width, blocks)
    v_next, r_ext, y_next, stat, y_first, y_last = conv_next(
        flags, y_ext, v_ext, total, norm_gain, norm_shift, weights, 0, width, count,
        follow=(taps_first,),
    )
    total_next = all_to_all(stat, "tile")
    heads, feature, act, slope = sample(extent, received, (r_ext, 1), 0, mlp)
    heads_last, feature_last, act_last, slope_last, r_last = sample(
        extent, received, (y_next, v_next, total_next, norm_gain, norm_shift), 1, mlp, count,
        follow=(heads,),
    )

    def draw(heads, layer, follow):
        return composite(
            starts, pixels, owner, rank, view_mask, all_to_all(heads, "tile"), render_cotangent,
            layer, classes, follow=follow,
        )

    picture, grad_heads = draw(heads, 0, (heads_last,))
    picture_last, grad_heads_last = draw(heads_last, 1, (grad_heads,))
    shares = (ray_devices, voxels // ray_devices, channels)
    planes = (depth, rows, channels)
    local, pack = sample_back(
        extent, 0, received, all_to_all(grad_heads, "tile"), feature, act, slope, mlp, (),
        follow=(grad_heads_last,),
    )
    parts = all_to_all(local.reshape(shares), "ray")
    local_last, packed = sample_back(
        extent, 1, received, all_to_all(grad_heads_last, "tile"), feature_last, act_last,
        slope_last, mlp, (pack,), follow=(local,),
    )
    copies = add_parts(parts, ray_devices, follow=(local_last,))
    parts_last = all_to_all(local_last.reshape(shares), "ray")
    taps_next = turn(block, r_ext, width, blocks, follow=(copies,))
    copies_last = add_parts(parts_last, ray_devices, follow=(taps_next,))
    sums_last = all_to_all(copies_last, "ray").reshape(planes)
    y_edges = exchange(*hold((y_first, y_last), (copies_last,)))
    copies, packed = hold((copies, packed), (sums_last,) + y_edges)
    sums = all_to_all(copies, "ray").reshape(planes)
    packed = lax.psum_scatter(packed, "ray", scatter_dimension=0, tiled=True)

    cot = volume_cotangent.reshape(planes)
    wide_taps = (27 * chosen, voxels)
    spots = jnp.stack([tile > 0, tile < tiles - 1, tile]).astype(jnp.int32)
    sent = norm_back(
        cot, sums_last, y_next, total_next, norm_gain, norm_shift, 1, count,
        follow=y_edges + (copies,),
    )
    dy, part, back_last = weight_grad(
        spots, taps_next.reshape(wide_taps), (cot, sums_last), y_next, y_edges, sent[2],
        share_back(sent), total_next, norm_gain, norm_shift, 1, count,
    )
    share = (tiles, 27 * chosen // tiles, channels)
    (held,) = hold((part,), (sums,))
    parts = all_to_all(held.reshape(share), "tile")
    grad, *sent = conv_back(
        dy, (cot, sums_last, sums), weights, 1, width,
        (y_ext, total, norm_gain, norm_shift, count), follow=(held,),
    )
    others = share_back(sent)
    shard = add_parts(parts, 1, follow=others)[0]
    dy, part, back = weight_grad(
        spots, taps_first.reshape(wide_taps), (grad,), y_ext, (), sent[2], others, total,
        norm_gain, norm_shift, 0, count, follow=(shard,),
    )
    parts = all_to_all(part.reshape(share), "tile")
    shard = spread_tile(shard, spots, (part,)).reshape(27 * chosen, channels)
    copies = add_parts(parts, tiles, follow=(shard,))
    slices = all_to_all(copies, "tile")
    packed = all_to_all(add_parts(packed[None], tiles, follow=(slices,)), "tile")
    conv_grad = place(gather_ray(shard), 1, layers, blocks, (), follow=(slices,))
    packed = add_parts(packed, ray_devices, follow=(conv_grad,))
    (grad,) = conv_back(dy, (grad,), weights, 0, width, follow=(packed,))
    packed = all_to_all(packed.astype(BF), "ray").astype(F32)
    packed = packed.reshape(layers, PACK, channels)[::-1]
    conv_grad = place(gather_ray(slices), 0, layers, blocks, (conv_grad,), follow=(grad,))

    at = channels + 16
    heads = packed[:, at : at + DROWS]
    head_bias = packed[:, at + DROWS, :DROWS]
    return (
        jnp.swapaxes(jnp.stack([picture, picture_last])[:, : classes + 1], 1, 2),
        r_last.reshape(volume.shape),
        grad.reshape(volume.shape),
        conv_grad,
        jnp.stack([back, back_last])[:, 1],
        jnp.stack([back, back_last])[:, 0],
        packed[:, :channels],
        packed[:, channels],
        heads[:, classes],
        head_bias[:, classes],
        jnp.swapaxes(heads[:, :classes], 1, 2),
        head_bias[:, :classes],
    )


def solution(mesh):
    in_specs = (
        P("tile", None, None, None),
        P(("ray", "tile"), None),
        P(None, ("ray", "tile"), None),
        P(("ray", "tile"), None),
        P(("ray", "tile"), None),
        P(),
        P(),
        P(),
        P(),
        P(),
        P(),
        P(),
        P(),
        P(),
        P(None, ("ray", "tile"), None),
        P("tile", None, None, None),
    )
    out_specs = (
        P(None, ("ray", "tile"), None),
        P("tile", None, None, None),
        P("tile", None, None, None),
        P(),
        P(),
        P(),
        P(),
        P(),
        P(),
        P(),
        P(),
        P(),
    )
    return jax.shard_map(
        per_device, mesh=mesh, in_specs=in_specs, out_specs=out_specs, check_vma=False
    )
```

```python
import functools

import jax
import jax.numpy as jnp
from jax import lax
from jax.experimental import pallas as pl
from jax.experimental.pallas import tpu as pltpu
from jax.sharding import PartitionSpec as P

CAP = 768
WINDOW = 256
LANES = 128
PROWS = 24
DROWS = 32
COORDS = 8
BLOCKS = 8
PACK = 320
epsilon = 1e-05
MIB = 1024 * 1024

BF = jnp.bfloat16
F32 = jnp.float32
VMEM = pltpu.VMEM
SMEM = pltpu.SMEM


def nn(left, right):
    return jnp.dot(left, right, preferred_element_type=F32)


def nt(left, right):
    return lax.dot_general(left, right, (((1,), (1,)), ((), ())), preferred_element_type=F32)


def iota(shape, dim):
    return lax.broadcasted_iota(jnp.int32, shape, dim)


def whole(shape):
    return pl.BlockSpec(shape, lambda *_: (0,) * len(shape))


def planes_of(step, shape, first=0):
    return pl.BlockSpec((step,) + shape[1:], lambda i: (i + first // step,) + (0,) * (len(shape) - 1))


def sspec():
    return pl.BlockSpec(memory_space=SMEM)


def aspec():
    return pl.BlockSpec(memory_space=pl.ANY)


def hspec():
    return pl.BlockSpec(memory_space=pltpu.HBM)


def ordered(kernel, operands, in_specs, follow, **options):
    count, skip = len(operands), len(follow)

    def body(*refs):
        kernel(*refs[:count], *refs[count + skip :])

    return pl.pallas_call(body, in_specs=list(in_specs) + [aspec()] * skip, **options)(
        *operands, *follow
    )


def params(mib):
    return pltpu.CompilerParams(vmem_limit_bytes=int(mib * MIB))


def cost():
    return pl.CostEstimate(flops=1, bytes_accessed=1, transcendentals=0)


def lane_cumsum(x):
    lane = iota(x.shape, 1)
    shift = 1
    while shift < x.shape[1]:
        x = x + jnp.where(lane >= shift, pltpu.roll(x, shift, 1), 0.0)
        shift *= 2
    return x


def window_onehots(starts, owner_row, rank_row, ray, rays, tiles):
    rows = iota((WINDOW, rank_row.shape[1]), 0)
    hots, bases = [], []
    for t in range(tiles):
        start = starts[t * rays + ray]
        base = (start // LANES) * LANES
        place = jnp.where(owner_row == t, rank_row + (start - base), -1)
        hots.append((rows == place).astype(F32).astype(BF))
        bases.append(pl.multiple_of(base, LANES))
    return jnp.concatenate(hots, axis=0), bases


def prep_kernel(extent, starts, cells_ref, fracs_ref, out_ref, owner_ref, rank_ref, vals, acc):
    depth, height, width = extent
    tiles = out_ref.shape[0]
    rays, samples = cells_ref.shape
    cells = cells_ref[...]
    voxels = depth * height * width
    owner = lax.div(cells, voxels)
    local = cells - owner * voxels
    base_x = lax.div(local, height * width)
    inner = local - base_x * (height * width)
    base_y = lax.div(inner, width)
    base_z = inner - base_y * width
    rank = jnp.zeros(cells.shape, F32)
    for t in range(tiles):
        mine = owner == t
        rank = jnp.where(mine, lane_cumsum(jnp.where(mine, 1.0, 0.0)) - 1.0, rank)
    owner_ref[...] = owner
    rank_ref[...] = rank.astype(jnp.int32)
    vals[...] = jnp.zeros_like(vals)
    rows = [(base_x + 1).astype(F32), base_y.astype(F32), base_z.astype(F32)]
    low = []
    for d in range(3):
        frac = fracs_ref[d]
        high = frac.astype(BF).astype(F32)
        rows.append(high)
        low.append(frac - high)
    rows += low
    for number, row in enumerate(rows):
        for k in range(rays):
            vals[number : number + 1, k * samples : (k + 1) * samples] = row[k : k + 1]
    acc[...] = jnp.zeros_like(acc)
    for k in range(rays):
        hot, bases = window_onehots(
            starts, owner_ref[k : k + 1, :], rank_ref[k : k + 1, :], k, rays, tiles
        )
        moved = nt(vals[:, k * samples : (k + 1) * samples].astype(BF), hot)
        for t in range(tiles):
            acc[t, :, pl.ds(bases[t], WINDOW)] += moved[:, t * WINDOW : (t + 1) * WINDOW]
    out_ref[...] = jnp.zeros_like(out_ref)
    wide = out_ref.shape[2]
    lines = CAP // wide
    for n in range(lines):
        part = slice(n * wide, (n + 1) * wide)
        for r in range(6):
            value = acc[:, r : r + 1, part]
            if r >= 3:
                value = value + acc[:, r + 3 : r + 4, part]
            out_ref[:, r * lines + n : r * lines + n + 1, :] = value


def prepare(extent, starts, cells, fracs, tiles, wide, follow=()):
    rays, samples = cells.shape
    outs = ((tiles, COORDS * CAP // wide, wide), (rays, samples), (rays, samples))
    return ordered(
        functools.partial(prep_kernel, extent),
        (starts, cells, fracs,),
        [sspec(), whole(cells.shape), whole(fracs.shape)],
        follow,
        grid=(1,),
        out_shape=(
            jax.ShapeDtypeStruct(outs[0], F32),
            jax.ShapeDtypeStruct(outs[1], jnp.int32),
            jax.ShapeDtypeStruct(outs[2], jnp.int32),
        ),
        out_specs=tuple(whole(s) for s in outs),
        scratch_shapes=[VMEM((16, rays * samples), F32), VMEM((tiles, 16, CAP + WINDOW), F32)],
        compiler_params=params(62.5),
        cost_estimate=cost(),
        name="prep",
    )


def started(source, target, sem):
    copy = pltpu.make_async_copy(source, target, sem)
    copy.start()
    return copy


def put_plane(xs, p, value, width):
    rows, channels = value.shape
    along = lax.rem(iota(value.shape, 0), width)
    left = jnp.where(along == 0, 0.0, pltpu.roll(value, 1, 0))
    right = jnp.where(along == width - 1, 0.0, pltpu.roll(value, rows - 1, 0))
    xs[p, width : width + rows, 0:channels] = left.astype(BF)
    xs[p, width : width + rows, channels : 2 * channels] = value.astype(BF)
    xs[p, width : width + rows, 2 * channels : 3 * channels] = right.astype(BF)


def clear_edges(xs, width, rows):
    planes, _, wide = xs.shape
    for p in range(planes):
        xs[p, 0:width, :] = jnp.zeros((width, wide), BF)
        xs[p, width + rows : 2 * width + rows, :] = jnp.zeros((width, wide), BF)


def taps(xs, p, width, rows):
    return jnp.concatenate(
        [xs[p + a, b * width : b * width + rows, :] for a in range(3) for b in range(3)], axis=1
    )


def tap_group(xs, first, count, width, rows):
    return jnp.concatenate([taps(xs, first + n, width, rows) for n in range(count)], axis=0)


def add_stats(sums, one, two):
    sums[0:1, :] += jnp.sum(one, axis=0, keepdims=True)
    sums[1:2, :] += jnp.sum(two, axis=0, keepdims=True)


def conv_scratch(planes, rows, width, channels, turned):
    shape = (channels, 27 * channels) if turned else (27 * channels, channels)
    return [VMEM((planes, rows + 2 * width, 3 * channels), BF), VMEM(shape, BF)]


def sems(*counts):
    return [pltpu.SemaphoreType.DMA((n,)) for n in counts]


def any_outs(*shapes):
    return tuple(jax.ShapeDtypeStruct(shape, dtype) for shape, dtype in shapes)


def conv_first_kernel(
    width, layer, before, own, after, coords, w_hbm, y_ref, v_ref, mix_ref,
    raw, xs, weight, y_buf, mix, in_sem, out_sem,
):
    planes, rows, channels = own.shape
    pairs = planes // 2 + 1
    body = [
        started(own.at[pl.ds(2 * i, 2)], raw.at[pl.ds(2 * i + 2, 2)], in_sem.at[i])
        for i in range(planes // 2)
    ]
    ends = [
        started(before, raw.at[pl.ds(0, 2)], in_sem.at[pairs]),
        started(after, raw.at[pl.ds(planes + 2, 2)], in_sem.at[pairs + 1]),
    ]
    heavy = started(w_hbm.at[layer], weight, in_sem.at[pairs + 2])
    light = started(coords, mix.at[:, pl.ds(8, coords.shape[1]), :], in_sem.at[pairs + 3])
    clear_edges(xs, width, rows)
    mix[:, 0:8, :] = jnp.zeros((mix.shape[0], 8, channels), F32)
    for copy in body + ends:
        copy.wait()

    @pl.loop(0, planes + 4)
    def _(p):
        put_plane(xs, p, raw[p].astype(F32), width)

    done = [started(raw.at[pl.ds(1, planes + 2)], v_ref, out_sem.at[pairs])]
    light.wait()
    heavy.wait()

    group = (planes + 2) // 2

    def out_copy(i):
        some = pl.ds(group * i, group)
        return pltpu.make_async_copy(y_buf.at[some], y_ref.at[some], out_sem.at[i])

    @pl.loop(0, 2)
    def _(i):
        p = group * i
        part = nn(tap_group(xs, p, group, width, rows), weight[...])
        for n in range(group):
            y_buf[p + n] = part[n * rows : (n + 1) * rows]
        out_copy(i).start()
        inner = part[rows : (group - 1) * rows]
        add_stats(mix.at[0], inner, inner * inner)
        edge = jnp.where(i == 0, part[(group - 1) * rows :], part[:rows])
        add_stats(mix.at[0], edge, edge * edge)

    for t in range(1, mix.shape[0]):
        mix[t, 0:8, :] = mix[0, 0:8, :]
    done.append(started(mix, mix_ref, out_sem.at[pairs + 1]))
    for copy in done:
        copy.wait()
    for i in range(2):
        out_copy(i).wait()


def conv_first(before, own, after, coords, weights, layer, width):
    planes, rows, channels = own.shape
    ext = (planes + 2, rows, channels)
    tiles, lines, _ = coords.shape
    pairs = planes // 2 + 1
    return ordered(
        functools.partial(conv_first_kernel, width, layer),
        (before, own, after, coords, weights),
        [aspec()] * 5,
        (),
        out_shape=any_outs((ext, F32), (ext, BF), ((tiles, 8 + lines, channels), F32)),
        out_specs=(aspec(),) * 3,
        scratch_shapes=[VMEM((planes + 4, rows, channels), BF)]
        + conv_scratch(planes + 4, rows, width, channels, False)
        + [VMEM(ext, F32), VMEM((tiles, 8 + lines, channels), F32)]
        + sems(pairs + 4, pairs + 2),
        compiler_params=params(62.5),
        cost_estimate=cost(),
        name="conv_first",
    )


def moments(total, count):
    both = jnp.sum(total, axis=0)
    mean = both[0:1, :] / count
    return mean, lax.rsqrt(both[1:2, :] / count - mean * mean + epsilon)


def row_of(ref, layer):
    return ref[layer : layer + 1, :]


def silu(value):
    return value * (1.0 / (1.0 + jnp.exp(-value)))


def conv_next_kernel(
    width, layer, count, flags, y_ext, v_ext, total_hbm, gain_hbm, shift_hbm, w_hbm,
    v_ref, r_ref, y_ref, stat_ref, first_ref, last_ref,
    y_in, v_in, total, gain, shift, xs, weight, v_buf, r_buf, y_buf, edges, stat, in_sem, out_sem,
):
    ext_planes, rows, channels = y_ext.shape
    pairs = ext_planes // 2
    small = [
        started(total_hbm.at[:, pl.ds(0, 8), :], total, in_sem.at[2 * pairs]),
        started(gain_hbm, gain, in_sem.at[2 * pairs + 1]),
        started(shift_hbm, shift, in_sem.at[2 * pairs + 2]),
    ]
    def in_copies(i):
        two = pl.ds(2 * i, 2)
        return (
            pltpu.make_async_copy(y_ext.at[two], y_in.at[two], in_sem.at[2 * i]),
            pltpu.make_async_copy(v_ext.at[two], v_in.at[two], in_sem.at[2 * i + 1]),
        )

    def mid_copies(i):
        two = pl.ds(2 * i, 2)
        return (
            pltpu.make_async_copy(v_buf.at[two], v_ref.at[two], out_sem.at[3 * i]),
            pltpu.make_async_copy(r_buf.at[two], r_ref.at[two], out_sem.at[3 * i + 1]),
        )

    def out_copy(i):
        two = pl.ds(2 * i - 2, 2)
        return pltpu.make_async_copy(y_buf.at[two], y_ref.at[two], out_sem.at[3 * i + 2])

    for i in range(pairs):
        for copy in in_copies(i):
            copy.start()
    heavy = started(w_hbm.at[layer + 1], weight, in_sem.at[2 * pairs + 3])
    clear_edges(xs, width, rows)
    stat[...] = jnp.zeros_like(stat)
    for copy in small:
        copy.wait()
    mean, inverse = moments(total[...], count)
    gains, shifts = row_of(gain, layer), row_of(shift, layer)

    @pl.loop(0, pairs)
    def _(i):
        for copy in in_copies(i):
            copy.wait()
        for side in range(2):
            p = 2 * i + side
            fresh = v_in[p].astype(F32) + silu((y_in[p] - mean) * inverse * gains + shifts)
            v_buf[p] = fresh
            outside = (p == side * (ext_planes - 1)) & (flags[side] == 0)
            rounded = jnp.where(outside, 0.0, fresh).astype(BF)
            r_buf[p] = rounded
            put_plane(xs, p, rounded.astype(F32), width)
        for copy in mid_copies(i):
            copy.start()

        @pl.when(i == 1)
        def _():
            heavy.wait()

        @pl.when(i > 0)
        def _():
            p = 2 * i - 2
            part = nn(tap_group(xs, p, 2, width, rows), weight[...])
            y_buf[p] = part[:rows]
            y_buf[p + 1] = part[rows:]
            add_stats(stat.at[0], part, part * part)
            out_copy(i).start()

    edges[0] = y_buf[0].astype(BF)
    edges[1] = y_buf[ext_planes - 3].astype(BF)
    for t in range(1, stat.shape[0]):
        stat[t] = stat[0]
    done = [
        started(stat, stat_ref, out_sem.at[2]),
        started(edges.at[pl.ds(0, 1)], first_ref, out_sem.at[3 * pairs]),
        started(edges.at[pl.ds(1, 1)], last_ref, out_sem.at[3 * pairs + 1]),
    ]
    for i in range(pairs):
        done += list(mid_copies(i)) + ([out_copy(i)] if i else [])
    for copy in done:
        copy.wait()


def conv_next(flags, y_ext, v_ext, total, gain, shift, weights, layer, width, count, follow=()):
    ext_planes, rows, channels = y_ext.shape
    ext = y_ext.shape
    inner = (ext_planes - 2, rows, channels)
    stat = (total.shape[0], 8, channels)
    pairs = ext_planes // 2
    edge = (1, rows, channels)
    return ordered(
        functools.partial(conv_next_kernel, width, layer, count),
        (flags, y_ext, v_ext, total, gain, shift, weights),
        [sspec()] + [aspec()] * 6,
        follow,
        out_shape=any_outs((ext, F32), (ext, BF), (inner, F32), (stat, F32), (edge, BF), (edge, BF)),
        out_specs=(aspec(),) * 6,
        scratch_shapes=[VMEM(ext, F32), VMEM(ext, BF), VMEM(stat, F32)]
        + [VMEM(gain.shape, F32)] * 2
        + conv_scratch(ext_planes, rows, width, channels, False)
        + [VMEM(ext, F32), VMEM(ext, BF), VMEM(inner, F32)]
        + [VMEM((2, rows, channels), BF), VMEM(stat, F32)]
        + sems(2 * pairs + 4, 3 * pairs + 2),
        compiler_params=params(62.5),
        cost_estimate=cost(),
        name="conv_next",
    )


def fill_weights(table, coords, extent):
    depth, height, width = extent
    samples = coords[0].shape[1]

    def along(base, frac, size):
        grid = iota((size, samples), 0).astype(F32)
        lower = jnp.where(grid == base, 1.0 - frac, 0.0)
        return lower + jnp.where(grid == base + 1.0, frac, 0.0)

    on_x = along(coords[0] - 1.0, coords[3], depth)
    on_y = along(coords[1], coords[4], height)
    on_z = along(coords[2], coords[5], width)
    for x in range(depth):
        on_xy = on_x[x : x + 1] * on_y
        for y in range(height):
            row = (x * height + y) * width
            table[row : row + width, :] = (on_xy[y : y + 1] * on_z).astype(BF)


def diagonal(rows, columns):
    return iota((rows, columns), 0) == iota((rows, columns), 1)


def identity(rows, columns):
    return diagonal(rows, columns).astype(F32).astype(BF)


def head_rows(semantic, density, rows):
    channels, classes = semantic.shape
    turned = nt(identity(rows, classes), semantic)
    return jnp.where(iota((rows, channels), 0) == classes, density.astype(F32), turned).astype(BF)


def column(row, rows):
    return jnp.sum(jnp.where(diagonal(rows, row.shape[1]), row, 0.0), axis=1, keepdims=True)


def coord_rows(block, slots):
    lines = slots // block.shape[1]
    return [
        jnp.concatenate(
            [block[8 + r * lines + n : 9 + r * lines + n, :] for n in range(lines)], axis=1
        )
        for r in range(6)
    ]


def sample_kernel(
    extent, layer, first, count, coords, *refs
):
    if count is None:
        r_hbm, refs = refs[0], refs[1:]
    else:
        y_hbm, v_hbm, total_hbm, gain, shift, refs = refs[0], refs[1], refs[2], refs[3], refs[4], refs[5:]
    hidden, hidden_b, semantic, density, semantic_b, density_b, refs = *refs[:6], refs[6:]
    p_ref, f_ref, g_ref, s_ref, refs = *refs[:4], refs[4:]
    if count is not None:
        r_out, refs = refs[0], refs[1:]
    turned, table, rounded, hidden_t, bias, head_t, head_b, sem, refs = *refs[:8], refs[8:]
    channels = turned.shape[0]
    depth = extent[0]
    classes = semantic.shape[2]
    slots = table.shape[1]
    rows = rounded.shape[1]
    step = pl.program_id(0)

    if count is not None:
        y_in, v_in, total, load_sem = refs

    def in_copies(p):
        return (
            pltpu.make_async_copy(y_hbm.at[p], y_in.at[p], load_sem.at[2 * p]),
            pltpu.make_async_copy(v_hbm.at[p + 1], v_in.at[p], load_sem.at[2 * p + 1]),
        )

    def out_copy(p):
        return pltpu.make_async_copy(rounded.at[p], r_out.at[p], sem.at[p])

    @pl.when(step == 0)
    def _():
        if count is None:
            copy = started(r_hbm.at[pl.ds(first, depth)], rounded, sem.at[0])
        else:
            light = started(total_hbm, total, load_sem.at[2 * depth])
            for p in range(depth):
                for copy in in_copies(p):
                    copy.start()
        same = identity(channels, channels)
        hidden_t[...] = nt(same, hidden[layer]).astype(BF)
        bias[...] = column(hidden_b[layer : layer + 1, :], channels)
        head_t[...] = head_rows(semantic[layer], density[layer : layer + 1, :], PROWS)
        last = jnp.sum(
            jnp.where(iota((1, density_b.shape[1]), 1) == layer, density_b[...], 0.0),
            axis=1,
            keepdims=True,
        )
        place = iota((PROWS, 1), 0) == classes
        head_b[...] = jnp.where(place, last, column(semantic_b[layer : layer + 1, :], PROWS))
        if count is None:
            copy.wait()
        else:
            light.wait()
            mean, inverse = moments(total[...], count)
            gains, shifts = row_of(gain, layer), row_of(shift, layer)

        @pl.loop(0, depth)
        def _(p):
            if count is not None:
                for copy in in_copies(p):
                    copy.wait()
                fresh = v_in[p] + silu((y_in[p] - mean) * inverse * gains + shifts)
                rounded[p] = fresh.astype(BF)
                out_copy(p).start()
            turned[:, pl.ds(pl.multiple_of(p * rows, rows), rows)] = nt(same, rounded[p]).astype(BF)

    fill_weights(table, coord_rows(coords[0], slots), extent)
    feature = nn(turned[...], table[...]).astype(BF)
    f_ref[0] = feature
    inner = nn(hidden_t[...], feature) + bias[...]
    small = jnp.exp(-jnp.abs(inner))
    act = (jnp.maximum(inner, 0.0) + jnp.log1p(small)).astype(BF)
    g_ref[0] = act
    s_ref[0] = jnp.where(inner >= 0.0, 1.0, small) / (1.0 + small)
    p_ref[0] = nn(head_t[...], act) + head_b[...]
    if count is not None:

        @pl.when(step == pl.num_programs(0) - 1)
        def _():
            for p in range(depth):
                out_copy(p).wait()


def per_tile(rows, lanes):
    return pl.BlockSpec((1, rows, lanes), lambda t: (t, 0, 0))


def sample(extent, received, source, layer, mlp, count=None, follow=()):
    tiles, lines, wide = received.shape
    slots = CAP
    rows, channels = extent[1] * extent[2], mlp[0].shape[1]
    depth = extent[0]
    voxels = depth * rows
    outs = [((tiles, PROWS, slots), F32)] + [((tiles, channels, slots), d) for d in (BF, BF, F32)]
    out_specs = [per_tile(n, slots) for n in (PROWS, channels, channels, channels)]
    scratch = [
        VMEM((channels, voxels), BF),
        VMEM((voxels, slots), BF),
        VMEM((depth, rows, channels), BF),
        VMEM((channels, channels), BF),
        VMEM((channels, 1), F32),
        VMEM((PROWS, channels), BF),
        VMEM((PROWS, 1), F32),
    ] + sems(depth)
    if count is None:
        first, given, specs = source[1], source[:1], [aspec()]
    else:
        first, given = 0, source
        specs = [aspec()] * 3 + [whole(x.shape) for x in source[3:]]
        outs.append(((depth, rows, channels), BF))
        out_specs.append(aspec())
        scratch += [VMEM((depth, rows, channels), F32)] * 2 + [VMEM(source[2].shape, F32)]
        scratch += sems(2 * depth + 1)
    return ordered(
        functools.partial(sample_kernel, extent, layer, first, count),
        (received,) + tuple(given) + mlp,
        [per_tile(lines, wide)] + specs + [whole(x.shape) for x in mlp],
        follow,
        grid=(tiles,),
        out_shape=any_outs(*outs),
        out_specs=tuple(out_specs),
        scratch_shapes=scratch,
        compiler_params=params(62.5),
        cost_estimate=cost(),
        name="sample",
    )


def sample_back_kernel(
    extent, layer, coords, dp_ref, f_ref, g_ref, s_ref, hidden, semantic, density, *refs
):
    du_ref, pack_ref, total, table, head = refs[-5:]
    step = pl.program_id(0)
    channels = hidden.shape[1]
    slots = table.shape[1]

    @pl.when(step == 0)
    def _():
        total[...] = jnp.zeros_like(total)
        pack_ref[0:PACK, :] = jnp.zeros((PACK, channels), F32)
        if len(refs) > 5:
            pack_ref[PACK : 2 * PACK, :] = refs[0][...]
        rows = head_rows(semantic[layer], density[layer : layer + 1, :], DROWS)
        head[...] = nt(identity(channels, channels), rows).astype(BF)

    fill_weights(table, coord_rows(coords[0], slots), extent)
    grad_heads = dp_ref[0]
    grad_inner = (nn(head[...], grad_heads) * s_ref[0]).astype(BF)
    ones = jnp.ones((16, slots), BF)
    pack_ref[0:channels, :] += nt(f_ref[0], grad_inner)
    pack_ref[channels : channels + 16, :] += nt(ones, grad_inner)
    at = channels + 16
    pack_ref[at : at + DROWS, :] += nt(grad_heads, g_ref[0])
    at += DROWS
    pack_ref[at : at + 16, 0:DROWS] += nt(ones, grad_heads)
    grad_features = nn(hidden[layer], grad_inner).astype(BF)
    total[...] += nt(table[...], grad_features)

    @pl.when(step == pl.num_programs(0) - 1)
    def _():
        du_ref[...] = total[...].astype(BF)


def sample_back(extent, layer, received, grad_heads, feature, act, slope, mlp, packs, follow=()):
    tiles, lines, wide = received.shape
    _, channels, slots = feature.shape
    voxels = extent[0] * extent[1] * extent[2]
    hidden, _, semantic, density = mlp[:4]
    outs = ((voxels, channels), (PACK * (1 + len(packs)), channels))
    return ordered(
        functools.partial(sample_back_kernel, extent, layer),
        (received, grad_heads, feature, act, slope, hidden, semantic, density) + packs,
        [per_tile(lines, wide)]
        + [per_tile(n, slots) for n in (DROWS, channels, channels, channels)]
        + [whole(x.shape) for x in (hidden, semantic, density) + packs],
        follow,
        grid=(tiles,),
        out_shape=any_outs((outs[0], BF), (outs[1], F32)),
        out_specs=tuple(whole(shape) for shape in outs),
        scratch_shapes=[
            VMEM((voxels, channels), F32),
            VMEM((voxels, slots), BF),
            VMEM((channels, DROWS), BF),
        ],
        compiler_params=params(62.5),
        cost_estimate=cost(),
        name="sample_back",
    )


def composite_kernel(
    classes, layer, starts, pixels, owner_ref, rank_ref, view, heads, cot,
    pic_ref, dp_ref, split, by_ray, grads, density, weights, grad_w, acc,
):
    tiles = heads.shape[0]
    rays, samples = owner_ref.shape
    step = 4.0 / samples
    split[...] = jnp.zeros_like(split)
    for t in range(tiles):
        value = heads[t]
        high = value.astype(BF)
        split[t, 0:PROWS, 0:CAP] = high.astype(F32)
        split[t, PROWS : 2 * PROWS, 0:CAP] = value - high.astype(F32)

    def hots(k):
        return window_onehots(
            starts, owner_ref[k : k + 1, :], rank_ref[k : k + 1, :], k, rays, tiles
        )

    for k in range(rays):
        hot, bases = hots(k)
        windows = jnp.concatenate(
            [split[t, :, pl.ds(bases[t], WINDOW)].astype(BF) for t in range(tiles)], axis=1
        )
        both = nn(windows, hot)
        one = both[:PROWS] + both[PROWS:]
        by_ray[k] = one
        density[k : k + 1, :] = one[classes : classes + 1]

    pre = density[...]
    visible = view[...].astype(F32)
    small = jnp.exp(-jnp.abs(pre))
    optical = visible * (jnp.maximum(pre, 0.0) + jnp.log1p(small)) * step
    passing = jnp.exp(-(lane_cumsum(optical) - optical))
    fading = jnp.exp(-optical)
    weight = passing * (1.0 - fading)
    weights[...] = weight
    row = iota((PROWS, samples), 0)
    lane = iota((PROWS, rays), 1)
    cotangent = nt(identity(PROWS, classes + 1), cot[layer])
    picture = jnp.zeros((PROWS, rays), F32)
    for k in range(rays):
        there = lane == pixels[k]
        dpic = jnp.sum(jnp.where(there, cotangent, 0.0), axis=1, keepdims=True)
        value = jnp.where(row < classes, by_ray[k], jnp.where(row == classes, 1.0, 0.0))
        one = weights[k : k + 1, :]
        colour = jnp.sum(value * one, axis=1, keepdims=True)
        picture = jnp.where(there, colour, picture)
        grad_w[k : k + 1, :] = jnp.sum(value * dpic, axis=0, keepdims=True)
        grads[k] = dpic * one
    pic_ref[...] = picture
    grad_weight = grad_w[...]
    carried = grad_weight * weight
    later = jnp.sum(carried, axis=1, keepdims=True) - lane_cumsum(carried)
    grad_optical = grad_weight * passing * fading - later
    slope = jnp.where(pre >= 0.0, 1.0, small) / (1.0 + small)
    density[...] = grad_optical * visible * step * slope
    acc[...] = jnp.zeros_like(acc)
    zero = jnp.zeros((DROWS - PROWS, samples), F32)
    for k in range(rays):
        hot, bases = hots(k)
        grad = jnp.where(row == classes, density[k : k + 1, :], grads[k])
        moved = nt(jnp.concatenate([grad, zero], axis=0).astype(BF), hot)
        for t in range(tiles):
            acc[t, :, pl.ds(bases[t], WINDOW)] += moved[:, t * WINDOW : (t + 1) * WINDOW]
    for t in range(tiles):
        dp_ref[t] = acc[t, :, 0:CAP].astype(BF)


def composite(starts, pixels, owner, rank, view, heads, cot, layer, classes, follow=()):
    tiles, _, slots = heads.shape
    rays, samples = owner.shape
    outs = ((PROWS, rays), (tiles, DROWS, slots))
    return ordered(
        functools.partial(composite_kernel, classes, layer),
        (starts, pixels, owner, rank, view, heads, cot,),
        [sspec(), sspec()] + [whole(x.shape) for x in (owner, rank, view, heads, cot)],
        follow,
        grid=(1,),
        out_shape=(jax.ShapeDtypeStruct(outs[0], F32), jax.ShapeDtypeStruct(outs[1], BF)),
        out_specs=tuple(whole(s) for s in outs),
        scratch_shapes=[
            VMEM((tiles, 2 * PROWS, CAP + WINDOW), F32),
            VMEM((rays, PROWS, samples), F32),
            VMEM((rays, PROWS, samples), F32),
            VMEM((rays, samples), F32),
            VMEM((rays, samples), F32),
            VMEM((rays, samples), F32),
            VMEM((tiles, DROWS, CAP + WINDOW), F32),
        ],
        compiler_params=params(62.5),
        cost_estimate=cost(),
        name="composite",
    )


def add_kernel(parts, out_ref):
    total = parts[0].astype(F32)
    for n in range(1, parts.shape[0]):
        total = total + parts[n].astype(F32)
    total = total.astype(out_ref.dtype)
    for n in range(out_ref.shape[0]):
        out_ref[n] = total


def add_parts(parts, copies, follow=()):
    shape = (copies,) + parts.shape[1:]
    return ordered(
        add_kernel,
        (parts,),
        [whole(parts.shape)],
        follow,
        grid=(1,),
        out_shape=jax.ShapeDtypeStruct(shape, parts.dtype),
        out_specs=whole(shape),
        compiler_params=params(62.5),
        cost_estimate=cost(),
        name="add_parts",
    )


def add_arrays_kernel(*refs):
    total = refs[0][...].astype(F32)
    for ref in refs[1:-1]:
        total = total + ref[...].astype(F32)
    refs[-1][...] = total.astype(refs[-1].dtype)


def add_arrays(values, follow=()):
    return ordered(
        add_arrays_kernel,
        tuple(values),
        [whole(x.shape) for x in values],
        follow,
        grid=(1,),
        out_shape=jax.ShapeDtypeStruct(values[0].shape, values[0].dtype),
        out_specs=whole(values[0].shape),
        compiler_params=params(62.5),
        cost_estimate=cost(),
        name="add_arrays",
    )


def hold_kernel(*refs):
    del refs


def hold(values, follow):
    return ordered(
        hold_kernel,
        values,
        [aspec()] * len(values),
        follow,
        out_shape=any_outs(*((x.shape, x.dtype) for x in values)),
        out_specs=(aspec(),) * len(values),
        input_output_aliases={n: n for n in range(len(values))},
        compiler_params=params(62.5),
        cost_estimate=cost(),
        name="hold",
    )


def all_to_all(value, axis):
    return lax.all_to_all(value, axis, split_axis=0, concat_axis=0, tiled=True)


def exchange(first, last):
    devices = lax.axis_size("tile")
    up = [(i, i + 1) for i in range(devices - 1)]
    down = [(i + 1, i) for i in range(devices - 1)]
    return lax.ppermute(last, "tile", up), lax.ppermute(first, "tile", down)


def norm_grads(y, grad, mean, inverse, gains, shifts):
    centred = (y - mean) * inverse
    normal = centred * gains + shifts
    sigma = 1.0 / (1.0 + jnp.exp(-normal))
    return grad * sigma * (1.0 + normal * (1.0 - sigma)), centred


def finish_back(sums, edges, ups, spare, out_sem):
    rows = edges.shape[1] - 16
    value = sums[...]
    high = value.astype(BF).astype(F32)
    middle = (value - high).astype(BF).astype(F32)
    low = value - high - middle
    tail = jnp.concatenate([high[0:2], middle[0:2], low[0:2], jnp.zeros((10,) + high.shape[1:], F32)], axis=0)
    tail = tail.astype(BF)
    edges[0, rows:, :] = tail
    edges[1, rows:, :] = tail
    spare[...] = tail
    first_ref, last_ref, far_ref = ups
    copies = [
        started(edges.at[0], first_ref, out_sem.at[0]),
        started(edges.at[1], last_ref, out_sem.at[1]),
        started(spare, far_ref, out_sem.at[2]),
    ]
    for copy in copies:
        copy.wait()


def norm_back_kernel(
    layer, count, cot, local, y, total_hbm, gain_hbm, shift_hbm, first_ref, last_ref, far_ref,
    cot_in, local_in, y_in, total, gain, shift, edges, sums, spare, in_sem, out_sem,
):
    planes, rows, _ = cot.shape
    small = [
        started(total_hbm, total, in_sem.at[3 * planes]),
        started(gain_hbm, gain, in_sem.at[3 * planes + 1]),
        started(shift_hbm, shift, in_sem.at[3 * planes + 2]),
    ]

    def in_copies(p):
        return [
            pltpu.make_async_copy(source.at[p], target.at[p], in_sem.at[3 * p + n])
            for n, (source, target) in enumerate(((cot, cot_in), (local, local_in), (y, y_in)))
        ]

    for p in range(planes):
        for copy in in_copies(p):
            copy.start()
    sums[...] = jnp.zeros_like(sums)
    for copy in small:
        copy.wait()
    mean, inverse = moments(total[...], count)
    gains, shifts = row_of(gain, layer), row_of(shift, layer)

    @pl.loop(0, planes)
    def _(p):
        for copy in in_copies(p):
            copy.wait()
        grad = cot_in[p].astype(F32) + local_in[p].astype(F32)
        inner, centred = norm_grads(y_in[p], grad, mean, inverse, gains, shifts)
        add_stats(sums, inner, inner * centred)
        for side, edge in ((0, 0), (1, planes - 1)):

            @pl.when(p == edge)
            def _():
                edges[side, 0:rows, :] = inner.astype(BF)

    finish_back(sums, edges, (first_ref, last_ref, far_ref), spare, out_sem)


def back_shapes(rows, channels):
    return ((rows + 16, channels), BF), ((rows + 16, channels), BF), ((16, channels), BF)


def back_scratch(rows, channels):
    return [VMEM((2, rows + 16, channels), BF), VMEM((8, channels), F32), VMEM((16, channels), BF)]


def norm_back(cot, local, y, total, gain, shift, layer, count, follow=()):
    planes, rows, channels = local.shape
    return ordered(
        functools.partial(norm_back_kernel, layer, count),
        (cot, local, y, total, gain, shift),
        [aspec()] * 6,
        follow,
        out_shape=any_outs(*back_shapes(rows, channels)),
        out_specs=(aspec(),) * 3,
        scratch_shapes=[VMEM(x.shape, x.dtype) for x in (cot, local, y, total, gain, shift)]
        + back_scratch(rows, channels)
        + sems(3 * planes + 3, 3),
        compiler_params=params(62.5),
        cost_estimate=cost(),
        name="norm_back",
    )


def share_back(sent):
    first, last, far = sent
    tiles = lax.axis_size("tile")

    def move(value, by):
        return lax.ppermute(value, "tile", [(i, (i + by) % tiles) for i in range(tiles)])

    return (move(last, 1), move(first, tiles - 1)) + tuple(move(far, n) for n in range(2, tiles - 1))


def turn_kernel(width, block, r_ref, out_ref, turned):
    planes, rows, channels = r_ref.shape
    chosen = out_ref.shape[1]
    pick = iota((chosen, channels), 1) == iota((chosen, channels), 0) + block[0] * chosen
    pick = pick.astype(F32).astype(BF)
    place = iota((chosen, rows), 1)
    on_y, on_z = lax.div(place, width), lax.rem(place, width)
    height = rows // width
    for p in range(planes):
        turned[...] = nt(pick, r_ref[p])
        for b in range(3):
            for c in range(3):
                shift = (b - 1) * width + (c - 1)
                value = turned[...]
                if shift:
                    value = pltpu.roll(value, (-shift) % rows, 1)
                y, z = on_y + (b - 1), on_z + (c - 1)
                inside = (y >= 0) & (y < height) & (z >= 0) & (z < width)
                value = jnp.where(inside, value, 0.0).astype(BF)
                for a in range(3):
                    target = p - a
                    if 0 <= target < planes - 2:
                        out_ref[9 * a + 3 * b + c, :, target * rows : (target + 1) * rows] = value


def turn(block, rounded, width, blocks, follow=()):
    planes, rows, channels = rounded.shape
    chosen = channels // blocks
    shape = (27, chosen, (planes - 2) * rows)
    return ordered(
        functools.partial(turn_kernel, width),
        (block, rounded,),
        [sspec(), whole(rounded.shape)],
        follow,
        grid=(1,),
        out_shape=jax.ShapeDtypeStruct(shape, BF),
        out_specs=whole(shape),
        scratch_shapes=[VMEM((chosen, rows), F32)],
        compiler_params=params(62.5),
        cost_estimate=cost(),
        name="turn",
    )


def weight_grad_kernel(layer, count, first, parts, tiles, split, spots, taps_hbm, *refs):
    grads, refs = refs[:parts], refs[parts:]
    if first:
        y, refs = refs[0], refs[1:]
        y_before, y_after = y.at[pl.ds(0, 1)], y.at[pl.ds(y.shape[0] - 1, 1)]
    else:
        y, y_before, y_after, refs = refs[0], refs[1], refs[2], refs[3:]
    own_far, others, refs = refs[0], refs[1:tiles], refs[tiles:]
    total_hbm, gain_hbm, shift_hbm, refs = *refs[:3], refs[3:]
    shares = tiles if split else 1
    dy_ref, back_ref, wg_refs, refs = refs[0], refs[1], refs[2 : 2 + shares], refs[2 + shares :]
    grads_in, refs = refs[:parts], refs[parts:]
    (taps_in, y_in, y_halo, dn_halo, rest, back, total, gain, shift, dy_buf, dy_rows, wg_buf, in_sem,
     out_sem) = refs
    planes, rows, channels = grads[0].shape
    spare = (parts + 1) * planes
    lists = [
        (total_hbm.at[:, pl.ds(0, 8), :], total),
        (gain_hbm, gain),
        (shift_hbm, shift),
        (y_before, y_halo.at[pl.ds(0, 1)]),
        (y_after, y_halo.at[pl.ds(1, 1)]),
        (others[0], dn_halo.at[0]),
        (others[1], dn_halo.at[1]),
        (own_far, rest.at[0]),
    ] + [(other, rest.at[n + 1]) for n, other in enumerate(others[2:])]
    small = [
        started(source, target, in_sem.at[spare + n]) for n, (source, target) in enumerate(lists)
    ]

    def in_copies(p):
        copies = [pltpu.make_async_copy(y.at[p + first], y_in.at[p], in_sem.at[(parts + 1) * p])]
        for n in range(parts):
            copies.append(
                pltpu.make_async_copy(
                    grads[n].at[p], grads_in[n].at[p], in_sem.at[(parts + 1) * p + 1 + n]
                )
            )
        return copies

    for p in range(planes):
        for copy in in_copies(p):
            copy.start()
    heavy = started(taps_hbm, taps_in, in_sem.at[spare + len(lists)])
    for copy in small:
        copy.wait()
    tile = spots[2]
    tails = [rest[0], dn_halo[0, rows:, :], dn_halo[1, rows:, :]]
    tails += [rest[n] for n in range(1, rest.shape[0])]
    for by, tail in zip([0, 1, tiles - 1] + list(range(2, tiles - 1)), tails):
        value = tail.astype(F32)
        value = value[0:2] + value[2:4] + value[4:6]
        back[lax.rem(tile + tiles - by, tiles), 0:2, :] = value
    mean, inverse = moments(total[...], count)
    gains, shifts = row_of(gain, layer), row_of(shift, layer)
    scale = inverse * gains
    both = back[0, 0:2, :]
    for t in range(1, tiles):
        both = both + back[t, 0:2, :]
    back[0, 0:2, :] = both
    sums = both / count

    def finish(inner, centred):
        return scale * (inner - sums[0:1, :] - centred * sums[1:2, :])

    for side, place in ((0, 0), (1, planes + 1)):
        centred = (y_halo[side].astype(F32) - mean) * inverse
        value = finish(dn_halo[side, 0:rows, :].astype(F32), centred)
        dy_buf[place] = jnp.where(spots[side] > 0, value, 0.0).astype(BF)

    @pl.loop(0, planes)
    def _(p):
        for copy in in_copies(p):
            copy.wait()
        grad = grads_in[0][p].astype(F32)
        for n in range(1, parts):
            grad = grad + grads_in[n][p].astype(F32)
        value = finish(*norm_grads(y_in[p], grad, mean, inverse, gains, shifts)).astype(BF)
        dy_buf[p + 1] = value
        dy_rows[pl.ds(pl.multiple_of(p * rows, rows), rows), :] = value

    done = [
        started(dy_buf, dy_ref, out_sem.at[0]),
        started(back.at[0, pl.ds(0, 2), :], back_ref, out_sem.at[1]),
    ]
    heavy.wait()
    part = nn(taps_in[...], dy_rows[...])
    lines = wg_buf.shape[1]
    for t in range(tiles):
        wg_buf[t] = part[t * lines : (t + 1) * lines].astype(BF)
    if split:
        for by, wg_ref in enumerate(wg_refs):
            share = wg_buf.at[lax.rem(tile + by, tiles)]
            done.append(started(share, wg_ref, out_sem.at[2 + by]))
    else:
        done.append(started(wg_buf, wg_refs[0], out_sem.at[2]))
    for copy in done:
        copy.wait()


def weight_grad(
    spots, taps_t, grads, y, y_halo, far, others, total, gain, shift, layer, count, split,
    follow=(),
):
    planes, rows, channels = grads[0].shape
    wide = taps_t.shape[0]
    tiles = len(others) + 1
    ext = (planes + 2, rows, channels)
    own = (planes, rows, channels)
    operands = (taps_t,) + tuple(grads) + (y,) + tuple(y_halo) + (far,) + tuple(others)
    operands += (total, gain, shift)
    return ordered(
        functools.partial(
            weight_grad_kernel, layer, count, 0 if y_halo else 1, len(grads), tiles, split
        ),
        (spots,) + operands,
        [sspec()] + [aspec()] * len(operands),
        follow,
        out_shape=any_outs(
            (ext, BF),
            ((2, channels), F32),
            *(((wide // tiles, channels), BF),) * tiles
            if split
            else (((tiles, wide // tiles, channels), BF),),
        ),
        out_specs=(aspec(),) * (2 + (tiles if split else 1)),
        scratch_shapes=[VMEM(x.shape, x.dtype) for x in grads]
        + [
            VMEM(taps_t.shape, BF),
            VMEM(own, F32),
            VMEM((2, rows, channels), BF if y_halo else F32),
            VMEM((2, rows + 16, channels), BF),
            VMEM((tiles - 2, 16, channels), BF),
            VMEM((tiles, 8, channels), F32),
            VMEM((tiles, 8, channels), F32),
            VMEM(gain.shape, F32),
            VMEM(gain.shape, F32),
            VMEM(ext, BF),
            VMEM((planes * rows, channels), BF),
            VMEM((tiles, wide // tiles, channels), BF),
        ]
        + sems((len(grads) + 1) * planes + 8 + tiles, 2 + tiles),
        compiler_params=params(62.5),
        cost_estimate=cost(),
        name="weight_grad",
    )


def conv_back_kernel(width, layer, count, parts, dy, w_hbm, *refs):
    more = count is not None
    grads, refs = refs[:parts], refs[parts:]
    if more:
        y, total_hbm, gain_hbm, shift_hbm, refs = *refs[:4], refs[4:]
    out_ref, refs = refs[0], refs[1:]
    if more:
        sent, refs = refs[:3], refs[3:]
    grads_in, refs = refs[:parts], refs[parts:]
    raw, xs, weight, out_buf, in_sem, w_sem, out_sem, refs = *refs[:7], refs[7:]
    ext_planes, rows, channels = dy.shape
    planes = ext_planes - 2
    group = planes // 2
    pairs = 2
    each = parts + 1
    body = started(dy, raw, in_sem.at[each * pairs])
    heavy = [
        started(
            w_hbm.at[layer, pl.ds((26 - o) * channels, channels), :],
            weight.at[:, pl.ds(o * channels, channels)],
            w_sem.at[o],
        )
        for o in range(27)
    ]
    small = []
    if more:
        y_in, total, gain, shift, edges, sums, spare, back_sem = refs
        small = [
            started(source, target, in_sem.at[each * pairs + 1 + n])
            for n, (source, target) in enumerate(
                ((total_hbm.at[:, pl.ds(0, 8), :], total), (gain_hbm, gain), (shift_hbm, shift))
            )
        ]
        sums[...] = jnp.zeros_like(sums)

    def in_copies(i):
        two = pl.ds(group * i, group)
        copies = [
            pltpu.make_async_copy(grads[n].at[two], grads_in[n].at[two], in_sem.at[each * i + n])
            for n in range(parts)
        ]
        if more:
            copies.append(
                pltpu.make_async_copy(
                    y.at[pl.ds(group * i + 1, group)], y_in.at[two], in_sem.at[each * i + parts]
                )
            )
        return copies

    def out_copy(i):
        two = pl.ds(group * i, group)
        return pltpu.make_async_copy(out_buf.at[two], out_ref.at[two], out_sem.at[i])

    for i in range(pairs):
        for copy in in_copies(i):
            copy.start()
    clear_edges(xs, width, rows)
    body.wait()

    @pl.loop(0, ext_planes)
    def _(p):
        put_plane(xs, p, raw[p].astype(F32), width)

    for copy in small + heavy:
        copy.wait()
    if more:
        mean, inverse = moments(total[...], count)
        gains, shifts = row_of(gain, layer - 1), row_of(shift, layer - 1)

    @pl.loop(0, pairs)
    def _(i):
        part = nt(tap_group(xs, group * i, group, width, rows), weight[...])
        for copy in in_copies(i):
            copy.wait()
        for n_plane in range(group):
            p = group * i + n_plane
            value = part[n_plane * rows : (n_plane + 1) * rows]
            for n in range(parts):
                value = value + grads_in[n][p].astype(F32)
            out_buf[p] = value
            if more:
                inner, centred = norm_grads(y_in[p], value, mean, inverse, gains, shifts)
                add_stats(sums, inner, inner * centred)

                for side, near in ((0, 0), (1, group - 1)):
                    if n_plane == near:

                        @pl.when(p == side * (planes - 1))
                        def _():
                            edges[side, 0:rows, :] = inner.astype(BF)

        out_copy(i).start()

    if more:
        finish_back(sums, edges, sent, spare, back_sem)
    for i in range(pairs):
        out_copy(i).wait()


def conv_back(dy, grads, weights, layer, width, norm=None, follow=()):
    ext_planes, rows, channels = dy.shape
    own = (ext_planes - 2, rows, channels)
    pairs = 2
    outs, extra, scratch = [(own, F32)], (), []
    if norm is not None:
        y, total, gain, shift, count = norm
        extra = (y, total, gain, shift)
        outs += list(back_shapes(rows, channels))
        scratch = [VMEM(own, F32), VMEM((total.shape[0], 8, channels), F32)]
        scratch += [VMEM(gain.shape, F32), VMEM(gain.shape, F32)]
        scratch += back_scratch(rows, channels) + sems(3)
    else:
        count = None
    return ordered(
        functools.partial(conv_back_kernel, width, layer, count, len(grads)),
        (dy, weights) + tuple(grads) + extra,
        [aspec()] * (2 + len(grads) + len(extra)),
        follow,
        out_shape=any_outs(*outs),
        out_specs=(aspec(),) * len(outs),
        scratch_shapes=[VMEM(x.shape, x.dtype) for x in grads]
        + [VMEM(dy.shape, BF)]
        + conv_scratch(ext_planes, rows, width, channels, True)
        + [VMEM(own, F32)]
        + sems(pairs * (len(grads) + 1) + 4, 27, pairs)
        + scratch,
        compiler_params=params(62.5),
        cost_estimate=cost(),
        name="conv_back",
    )


GROUP = 3


def order_kernel(spots, *refs):
    out_ref = refs[-1]
    tiles = out_ref.shape[0]
    for by in range(tiles):
        out_ref[lax.rem(spots[2] + tiles - by, tiles)] = refs[by][...]


def spread_tile(value, spots, follow):
    tiles = lax.axis_size("tile")
    parts = [value]
    for by in range(1, tiles):
        pairs = [(i, (i + by) % tiles) for i in range(tiles)]
        parts.append(lax.ppermute(value, "tile", pairs))
    shape = (tiles,) + value.shape
    return ordered(
        order_kernel,
        (spots,) + tuple(parts),
        [sspec()] + [whole(value.shape)] * tiles,
        follow,
        grid=(1,),
        out_shape=jax.ShapeDtypeStruct(shape, value.dtype),
        out_specs=whole(shape),
        compiler_params=params(62.5),
        cost_estimate=cost(),
        name="order_tiles",
    )


def gather_ray(slices):
    return lax.all_gather(slices.reshape(-1, slices.shape[-1]), "ray", axis=0)


def place_kernel(layer, blocks, source, *refs):
    out_ref, taken, out, in_sem, out_sem = refs[-5:]
    _, offsets, rows, _ = out_ref.shape
    chosen = rows // blocks
    steps = offsets // GROUP
    lines = GROUP * chosen

    def in_copy(n):
        some = pl.ds(n * lines, lines)
        return pltpu.make_async_copy(
            source.at[pl.ds(0, blocks), some], taken.at[:, some], in_sem.at[n]
        )

    for n in range(steps):
        in_copy(n).start()
    done = []
    for n in range(steps):
        in_copy(n).wait()
        for o in range(n * GROUP, (n + 1) * GROUP):
            for ray in range(blocks):
                out[o, ray * chosen : (ray + 1) * chosen, :] = taken[
                    ray, o * chosen : (o + 1) * chosen, :
                ].astype(F32)
        some = pl.ds(n * GROUP, GROUP)
        done.append(started(out.at[some], out_ref.at[layer, some], out_sem.at[n]))
    for copy in done:
        copy.wait()


def place(parts, layer, layers, blocks, kept, follow=()):
    _, lines, channels = parts.shape
    offsets = lines * blocks // channels
    return ordered(
        functools.partial(place_kernel, layer, blocks),
        (parts,) + kept,
        [aspec()] * (1 + len(kept)),
        follow,
        out_shape=jax.ShapeDtypeStruct((layers, offsets, channels, channels), F32),
        out_specs=aspec(),
        scratch_shapes=[VMEM((blocks, lines, channels), BF), VMEM((offsets, channels, channels), F32)]
        + sems(offsets // GROUP, offsets // GROUP),
        input_output_aliases={1: 0} if kept else {},
        compiler_params=params(62.5),
        cost_estimate=cost(),
        name="place",
    )


def per_device(
    volume,
    sample_cells,
    sample_fracs,
    view_mask,
    pixel_of_ray,
    conv_weight,
    norm_gain,
    norm_shift,
    hidden_weight,
    hidden_bias,
    density_weight,
    density_bias,
    semantic_weight,
    semantic_bias,
    render_cotangent,
    volume_cotangent,
):
    extent = volume.shape[:3]
    depth, height, width, channels = volume.shape
    rows = height * width
    voxels = depth * rows
    tiles = lax.axis_size("tile")
    ray_devices = lax.axis_size("ray")
    count = float(voxels * tiles)
    rays, samples = sample_cells.shape
    classes = semantic_weight.shape[2]
    layers = conv_weight.shape[0]
    blocks = min(BLOCKS, ray_devices)
    chosen = channels // blocks
    tile, ray = lax.axis_index("tile"), lax.axis_index("ray")
    block = lax.rem(ray, blocks).astype(jnp.int32).reshape(1)

    own = volume.reshape(depth, rows, channels)
    before, after = exchange(own[:2], own[-2:])
    flags = jnp.stack([tile > 0, tile < tiles - 1]).astype(jnp.int32)

    owner_of = lax.div(sample_cells, voxels)
    held = owner_of[None] == jnp.arange(tiles, dtype=jnp.int32)[:, None, None]
    earlier = jnp.arange(rays)[None, :] < jnp.arange(rays)[:, None]
    starts = jnp.sum(
        (held[:, None, :, :] & earlier[None, :, :, None]).astype(jnp.int32), axis=(2, 3)
    ).reshape(tiles * rays)
    pixels = pixel_of_ray[0]
    buffer, owner, rank = prepare(extent, starts, sample_cells, sample_fracs, tiles, channels)

    weights = conv_weight.reshape(layers, 27 * channels, channels)
    mlp = (
        hidden_weight,
        hidden_bias,
        semantic_weight,
        density_weight,
        semantic_bias,
        density_bias[None],
    )
    y_ext, v_ext, mixed = conv_first(before, own, after, buffer, weights, 0, width)
    total = received = all_to_all(mixed, "tile")
    taps_first = turn(block, v_ext, width, blocks)
    v_next, r_ext, y_next, stat, y_first, y_last = conv_next(
        flags, y_ext, v_ext, total, norm_gain, norm_shift, weights, 0, width, count,
        follow=(taps_first,),
    )
    total_next = all_to_all(stat, "tile")
    heads, feature, act, slope = sample(extent, received, (r_ext, 1), 0, mlp)
    heads_last, feature_last, act_last, slope_last, r_last = sample(
        extent, received, (y_next, v_next, total_next, norm_gain, norm_shift), 1, mlp, count,
        follow=(heads,),
    )

    def draw(heads, layer, follow):
        return composite(
            starts, pixels, owner, rank, view_mask, all_to_all(heads, "tile"), render_cotangent,
            layer, classes, follow=follow,
        )

    picture, grad_heads = draw(heads, 0, (heads_last,))
    picture_last, grad_heads_last = draw(heads_last, 1, (grad_heads,))
    shares = (ray_devices, voxels // ray_devices, channels)
    planes = (depth, rows, channels)
    local, pack = sample_back(
        extent, 0, received, all_to_all(grad_heads, "tile"), feature, act, slope, mlp, (),
        follow=(grad_heads_last,),
    )
    parts = all_to_all(local.reshape(shares), "ray")
    local_last, packed = sample_back(
        extent, 1, received, all_to_all(grad_heads_last, "tile"), feature_last, act_last,
        slope_last, mlp, (pack,), follow=(local,),
    )
    copies = add_parts(parts, ray_devices, follow=(local_last,))
    parts_last = all_to_all(local_last.reshape(shares), "ray")
    taps_next = turn(block, r_ext, width, blocks, follow=(copies,))
    copies_last = add_parts(parts_last, ray_devices, follow=(taps_next,))
    sums_last = all_to_all(copies_last, "ray").reshape(planes)
    y_edges = exchange(*hold((y_first, y_last), (copies_last,)))
    copies, packed = hold((copies, packed), (sums_last,) + y_edges)
    sums = all_to_all(copies, "ray").reshape(planes)
    packed = lax.psum_scatter(packed, "ray", scatter_dimension=0, tiled=True)

    cot = volume_cotangent.reshape(planes)
    wide_taps = (27 * chosen, voxels)
    spots = jnp.stack([tile > 0, tile < tiles - 1, tile]).astype(jnp.int32)
    sent = norm_back(
        cot, sums_last, y_next, total_next, norm_gain, norm_shift, 1, count,
        follow=y_edges + (copies,),
    )
    dy, back_last, part = weight_grad(
        spots, taps_next.reshape(wide_taps), (cot, sums_last), y_next, y_edges, sent[2],
        share_back(sent), total_next, norm_gain, norm_shift, 1, count, False,
    )
    (held,) = hold((part,), (sums,))
    parts = all_to_all(held, "tile")
    grad, *sent = conv_back(
        dy, (cot, sums_last, sums), weights, 1, width,
        (y_ext, total, norm_gain, norm_shift, count), follow=(held,),
    )
    others = share_back(sent)
    shard = add_parts(parts, 1, follow=(sent[2],))[0]
    dy, back, *shares = weight_grad(
        spots, taps_first.reshape(wide_taps), (grad,), y_ext, (), sent[2], others, total,
        norm_gain, norm_shift, 0, count, True, follow=(shard,),
    )
    moved = [
        lax.ppermute(value, "tile", [(i, (i + by) % tiles) for i in range(tiles)])
        for by, value in enumerate(shares)
        if by
    ]
    shard = spread_tile(shard, spots, (shares[0],)).reshape(27 * chosen, channels)
    slices = spread_tile(add_arrays([shares[0]] + moved, (shard,)), spots, ())
    slices = slices.reshape(27 * chosen, channels)
    packed = all_to_all(add_parts(packed[None], tiles, follow=(slices,)), "tile")
    conv_grad = place(gather_ray(shard), 1, layers, blocks, (), follow=(slices,))
    packed = add_parts(packed, ray_devices, follow=(conv_grad,))
    (grad,) = conv_back(dy, (grad,), weights, 0, width, follow=(packed,))
    packed = all_to_all(packed.astype(BF), "ray").astype(F32)
    packed = packed.reshape(layers, PACK, channels)[::-1]
    conv_grad = place(gather_ray(slices), 0, layers, blocks, (conv_grad,), follow=(grad,))

    at = channels + 16
    heads = packed[:, at : at + DROWS]
    head_bias = packed[:, at + DROWS, :DROWS]
    return (
        jnp.swapaxes(jnp.stack([picture, picture_last])[:, : classes + 1], 1, 2),
        r_last.reshape(volume.shape),
        grad.reshape(volume.shape),
        conv_grad,
        jnp.stack([back, back_last])[:, 1],
        jnp.stack([back, back_last])[:, 0],
        packed[:, :channels],
        packed[:, channels],
        heads[:, classes],
        head_bias[:, classes],
        jnp.swapaxes(heads[:, :classes], 1, 2),
        head_bias[:, :classes],
    )


def solution(mesh):
    in_specs = (
        P("tile", None, None, None),
        P(("ray", "tile"), None),
        P(None, ("ray", "tile"), None),
        P(("ray", "tile"), None),
        P(("ray", "tile"), None),
        P(),
        P(),
        P(),
        P(),
        P(),
        P(),
        P(),
        P(),
        P(),
        P(None, ("ray", "tile"), None),
        P("tile", None, None, None),
    )
    out_specs = (
        P(None, ("ray", "tile"), None),
        P("tile", None, None, None),
        P("tile", None, None, None),
        P(),
        P(),
        P(),
        P(),
        P(),
        P(),
        P(),
        P(),
        P(),
    )
    return jax.shard_map(
        per_device, mesh=mesh, in_specs=in_specs, out_specs=out_specs, check_vma=False
    )
```

```python
import functools

import jax
import jax.numpy as jnp
from jax import lax
from jax.experimental import pallas as pl
from jax.experimental.pallas import tpu as pltpu
from jax.sharding import PartitionSpec as P

CAP = 768
WINDOW = 256
LANES = 128
PROWS = 24
DROWS = 32
COORDS = 8
BLOCKS = 8
PACK = 320
epsilon = 1e-05
MIB = 1024 * 1024

BF = jnp.bfloat16
F32 = jnp.float32
VMEM = pltpu.VMEM
SMEM = pltpu.SMEM


def nn(left, right):
    return jnp.dot(left, right, preferred_element_type=F32)


def nt(left, right):
    return lax.dot_general(left, right, (((1,), (1,)), ((), ())), preferred_element_type=F32)


def iota(shape, dim):
    return lax.broadcasted_iota(jnp.int32, shape, dim)


def whole(shape):
    return pl.BlockSpec(shape, lambda *_: (0,) * len(shape))


def planes_of(step, shape, first=0):
    return pl.BlockSpec((step,) + shape[1:], lambda i: (i + first // step,) + (0,) * (len(shape) - 1))


def sspec():
    return pl.BlockSpec(memory_space=SMEM)


def aspec():
    return pl.BlockSpec(memory_space=pl.ANY)


def hspec():
    return pl.BlockSpec(memory_space=pltpu.HBM)


def ordered(kernel, operands, in_specs, follow, **options):
    count, skip = len(operands), len(follow)

    def body(*refs):
        kernel(*refs[:count], *refs[count + skip :])

    return pl.pallas_call(body, in_specs=list(in_specs) + [aspec()] * skip, **options)(
        *operands, *follow
    )


def params(mib):
    return pltpu.CompilerParams(vmem_limit_bytes=int(mib * MIB))


def cost():
    return pl.CostEstimate(flops=1, bytes_accessed=1, transcendentals=0)


def lane_cumsum(x):
    lane = iota(x.shape, 1)
    shift = 1
    while shift < x.shape[1]:
        x = x + jnp.where(lane >= shift, pltpu.roll(x, shift, 1), 0.0)
        shift *= 2
    return x


def window_onehots(starts, owner_row, rank_row, ray, rays, tiles):
    rows = iota((WINDOW, rank_row.shape[1]), 0)
    hots, bases = [], []
    for t in range(tiles):
        start = starts[t * rays + ray]
        base = (start // LANES) * LANES
        place = jnp.where(owner_row == t, rank_row + (start - base), -1)
        hots.append((rows == place).astype(F32).astype(BF))
        bases.append(pl.multiple_of(base, LANES))
    return jnp.concatenate(hots, axis=0), bases


def prep_kernel(extent, starts, cells_ref, fracs_ref, out_ref, owner_ref, rank_ref, vals, acc):
    depth, height, width = extent
    tiles = out_ref.shape[0]
    rays, samples = cells_ref.shape
    cells = cells_ref[...]
    voxels = depth * height * width
    owner = lax.div(cells, voxels)
    local = cells - owner * voxels
    base_x = lax.div(local, height * width)
    inner = local - base_x * (height * width)
    base_y = lax.div(inner, width)
    base_z = inner - base_y * width
    rank = jnp.zeros(cells.shape, F32)
    for t in range(tiles):
        mine = owner == t
        rank = jnp.where(mine, lane_cumsum(jnp.where(mine, 1.0, 0.0)) - 1.0, rank)
    owner_ref[...] = owner
    rank_ref[...] = rank.astype(jnp.int32)
    vals[...] = jnp.zeros_like(vals)
    rows = [(base_x + 1).astype(F32), base_y.astype(F32), base_z.astype(F32)]
    low = []
    for d in range(3):
        frac = fracs_ref[d]
        high = frac.astype(BF).astype(F32)
        rows.append(high)
        low.append(frac - high)
    rows += low
    for number, row in enumerate(rows):
        for k in range(rays):
            vals[number : number + 1, k * samples : (k + 1) * samples] = row[k : k + 1]
    acc[...] = jnp.zeros_like(acc)
    for k in range(rays):
        hot, bases = window_onehots(
            starts, owner_ref[k : k + 1, :], rank_ref[k : k + 1, :], k, rays, tiles
        )
        moved = nt(vals[:, k * samples : (k + 1) * samples].astype(BF), hot)
        for t in range(tiles):
            acc[t, :, pl.ds(bases[t], WINDOW)] += moved[:, t * WINDOW : (t + 1) * WINDOW]
    out_ref[...] = jnp.zeros_like(out_ref)
    wide = out_ref.shape[2]
    lines = CAP // wide
    for n in range(lines):
        part = slice(n * wide, (n + 1) * wide)
        for r in range(6):
            value = acc[:, r : r + 1, part]
            if r >= 3:
                value = value + acc[:, r + 3 : r + 4, part]
            out_ref[:, r * lines + n : r * lines + n + 1, :] = value


def prepare(extent, starts, cells, fracs, tiles, wide, follow=()):
    rays, samples = cells.shape
    outs = ((tiles, COORDS * CAP // wide, wide), (rays, samples), (rays, samples))
    return ordered(
        functools.partial(prep_kernel, extent),
        (starts, cells, fracs,),
        [sspec(), whole(cells.shape), whole(fracs.shape)],
        follow,
        grid=(1,),
        out_shape=(
            jax.ShapeDtypeStruct(outs[0], F32),
            jax.ShapeDtypeStruct(outs[1], jnp.int32),
            jax.ShapeDtypeStruct(outs[2], jnp.int32),
        ),
        out_specs=tuple(whole(s) for s in outs),
        scratch_shapes=[VMEM((16, rays * samples), F32), VMEM((tiles, 16, CAP + WINDOW), F32)],
        compiler_params=params(62.5),
        cost_estimate=cost(),
        name="prep",
    )


def started(source, target, sem):
    copy = pltpu.make_async_copy(source, target, sem)
    copy.start()
    return copy


def put_plane(xs, p, value, width):
    rows, channels = value.shape
    along = lax.rem(iota(value.shape, 0), width)
    left = jnp.where(along == 0, 0.0, pltpu.roll(value, 1, 0))
    right = jnp.where(along == width - 1, 0.0, pltpu.roll(value, rows - 1, 0))
    xs[p, width : width + rows, 0:channels] = left.astype(BF)
    xs[p, width : width + rows, channels : 2 * channels] = value.astype(BF)
    xs[p, width : width + rows, 2 * channels : 3 * channels] = right.astype(BF)


def clear_edges(xs, width, rows):
    planes, _, wide = xs.shape
    for p in range(planes):
        xs[p, 0:width, :] = jnp.zeros((width, wide), BF)
        xs[p, width + rows : 2 * width + rows, :] = jnp.zeros((width, wide), BF)


def taps(xs, p, width, rows):
    return jnp.concatenate(
        [xs[p + a, b * width : b * width + rows, :] for a in range(3) for b in range(3)], axis=1
    )


def tap_group(xs, first, count, width, rows):
    return jnp.concatenate([taps(xs, first + n, width, rows) for n in range(count)], axis=0)


def add_stats(sums, one, two):
    sums[0:1, :] += jnp.sum(one, axis=0, keepdims=True)
    sums[1:2, :] += jnp.sum(two, axis=0, keepdims=True)


def conv_scratch(planes, rows, width, channels, turned):
    shape = (channels, 27 * channels) if turned else (27 * channels, channels)
    return [VMEM((planes, rows + 2 * width, 3 * channels), BF), VMEM(shape, BF)]


def sems(*counts):
    return [pltpu.SemaphoreType.DMA((n,)) for n in counts]


def any_outs(*shapes):
    return tuple(jax.ShapeDtypeStruct(shape, dtype) for shape, dtype in shapes)


def conv_first_kernel(
    width, layer, before, own, after, coords, w_hbm, y_ref, v_ref, mix_ref,
    raw, xs, weight, y_buf, mix, in_sem, out_sem,
):
    planes, rows, channels = own.shape
    pairs = planes // 2 + 1
    body = [
        started(own.at[pl.ds(2 * i, 2)], raw.at[pl.ds(2 * i + 2, 2)], in_sem.at[i])
        for i in range(planes // 2)
    ]
    ends = [
        started(before, raw.at[pl.ds(0, 2)], in_sem.at[pairs]),
        started(after, raw.at[pl.ds(planes + 2, 2)], in_sem.at[pairs + 1]),
    ]
    heavy = started(w_hbm.at[layer], weight, in_sem.at[pairs + 2])
    light = started(coords, mix.at[:, pl.ds(8, coords.shape[1]), :], in_sem.at[pairs + 3])
    clear_edges(xs, width, rows)
    mix[:, 0:8, :] = jnp.zeros((mix.shape[0], 8, channels), F32)
    for copy in body + ends:
        copy.wait()

    @pl.loop(0, planes + 4)
    def _(p):
        put_plane(xs, p, raw[p].astype(F32), width)

    done = [started(raw.at[pl.ds(1, planes + 2)], v_ref, out_sem.at[pairs])]
    light.wait()
    heavy.wait()

    group = (planes + 2) // 2

    def out_copy(i):
        some = pl.ds(group * i, group)
        return pltpu.make_async_copy(y_buf.at[some], y_ref.at[some], out_sem.at[i])

    @pl.loop(0, 2)
    def _(i):
        p = group * i
        part = nn(tap_group(xs, p, group, width, rows), weight[...])
        for n in range(group):
            y_buf[p + n] = part[n * rows : (n + 1) * rows]
        out_copy(i).start()
        inner = part[rows : (group - 1) * rows]
        add_stats(mix.at[0], inner, inner * inner)
        edge = jnp.where(i == 0, part[(group - 1) * rows :], part[:rows])
        add_stats(mix.at[0], edge, edge * edge)

    for t in range(1, mix.shape[0]):
        mix[t, 0:8, :] = mix[0, 0:8, :]
    done.append(started(mix, mix_ref, out_sem.at[pairs + 1]))
    for copy in done:
        copy.wait()
    for i in range(2):
        out_copy(i).wait()


def conv_first(before, own, after, coords, weights, layer, width):
    planes, rows, channels = own.shape
    ext = (planes + 2, rows, channels)
    tiles, lines, _ = coords.shape
    pairs = planes // 2 + 1
    return ordered(
        functools.partial(conv_first_kernel, width, layer),
        (before, own, after, coords, weights),
        [aspec()] * 5,
        (),
        out_shape=any_outs((ext, F32), (ext, BF), ((tiles, 8 + lines, channels), F32)),
        out_specs=(aspec(),) * 3,
        scratch_shapes=[VMEM((planes + 4, rows, channels), BF)]
        + conv_scratch(planes + 4, rows, width, channels, False)
        + [VMEM(ext, F32), VMEM((tiles, 8 + lines, channels), F32)]
        + sems(pairs + 4, pairs + 2),
        compiler_params=params(62.5),
        cost_estimate=cost(),
        name="conv_first",
    )


def moments(total, count):
    both = jnp.sum(total, axis=0)
    mean = both[0:1, :] / count
    return mean, lax.rsqrt(both[1:2, :] / count - mean * mean + epsilon)


def row_of(ref, layer):
    return ref[layer : layer + 1, :]


def silu(value):
    return value * (1.0 / (1.0 + jnp.exp(-value)))


def conv_next_kernel(
    width, layer, count, flags, y_ext, v_ext, total_hbm, gain_hbm, shift_hbm, w_hbm,
    v_ref, r_ref, y_ref, stat_ref, first_ref, last_ref,
    y_in, v_in, total, gain, shift, xs, weight, v_buf, r_buf, y_buf, edges, stat, in_sem, out_sem,
):
    ext_planes, rows, channels = y_ext.shape
    pairs = ext_planes // 2
    small = [
        started(total_hbm.at[:, pl.ds(0, 8), :], total, in_sem.at[2 * pairs]),
        started(gain_hbm, gain, in_sem.at[2 * pairs + 1]),
        started(shift_hbm, shift, in_sem.at[2 * pairs + 2]),
    ]
    def in_copies(i):
        two = pl.ds(2 * i, 2)
        return (
            pltpu.make_async_copy(y_ext.at[two], y_in.at[two], in_sem.at[2 * i]),
            pltpu.make_async_copy(v_ext.at[two], v_in.at[two], in_sem.at[2 * i + 1]),
        )

    def mid_copies(i):
        two = pl.ds(2 * i, 2)
        return (
            pltpu.make_async_copy(v_buf.at[two], v_ref.at[two], out_sem.at[3 * i]),
            pltpu.make_async_copy(r_buf.at[two], r_ref.at[two], out_sem.at[3 * i + 1]),
        )

    def out_copy(i):
        two = pl.ds(2 * i - 2, 2)
        return pltpu.make_async_copy(y_buf.at[two], y_ref.at[two], out_sem.at[3 * i + 2])

    for i in range(pairs):
        for copy in in_copies(i):
            copy.start()
    heavy = started(w_hbm.at[layer + 1], weight, in_sem.at[2 * pairs + 3])
    clear_edges(xs, width, rows)
    stat[...] = jnp.zeros_like(stat)
    for copy in small:
        copy.wait()
    mean, inverse = moments(total[...], count)
    gains, shifts = row_of(gain, layer), row_of(shift, layer)

    @pl.loop(0, pairs)
    def _(i):
        for copy in in_copies(i):
            copy.wait()
        for side in range(2):
            p = 2 * i + side
            fresh = v_in[p].astype(F32) + silu((y_in[p] - mean) * inverse * gains + shifts)
            v_buf[p] = fresh
            outside = (p == side * (ext_planes - 1)) & (flags[side] == 0)
            rounded = jnp.where(outside, 0.0, fresh).astype(BF)
            r_buf[p] = rounded
            put_plane(xs, p, rounded.astype(F32), width)
        for copy in mid_copies(i):
            copy.start()

        @pl.when(i == 1)
        def _():
            heavy.wait()

        @pl.when(i > 0)
        def _():
            p = 2 * i - 2
            part = nn(tap_group(xs, p, 2, width, rows), weight[...])
            y_buf[p] = part[:rows]
            y_buf[p + 1] = part[rows:]
            add_stats(stat.at[0], part, part * part)
            out_copy(i).start()

    edges[0] = y_buf[0].astype(BF)
    edges[1] = y_buf[ext_planes - 3].astype(BF)
    for t in range(1, stat.shape[0]):
        stat[t] = stat[0]
    done = [
        started(stat, stat_ref, out_sem.at[2]),
        started(edges.at[pl.ds(0, 1)], first_ref, out_sem.at[3 * pairs]),
        started(edges.at[pl.ds(1, 1)], last_ref, out_sem.at[3 * pairs + 1]),
    ]
    for i in range(pairs):
        done += list(mid_copies(i)) + ([out_copy(i)] if i else [])
    for copy in done:
        copy.wait()


def conv_next(flags, y_ext, v_ext, total, gain, shift, weights, layer, width, count, follow=()):
    ext_planes, rows, channels = y_ext.shape
    ext = y_ext.shape
    inner = (ext_planes - 2, rows, channels)
    stat = (total.shape[0], 8, channels)
    pairs = ext_planes // 2
    edge = (1, rows, channels)
    return ordered(
        functools.partial(conv_next_kernel, width, layer, count),
        (flags, y_ext, v_ext, total, gain, shift, weights),
        [sspec()] + [aspec()] * 6,
        follow,
        out_shape=any_outs((ext, F32), (ext, BF), (inner, F32), (stat, F32), (edge, BF), (edge, BF)),
        out_specs=(aspec(),) * 6,
        scratch_shapes=[VMEM(ext, F32), VMEM(ext, BF), VMEM(stat, F32)]
        + [VMEM(gain.shape, F32)] * 2
        + conv_scratch(ext_planes, rows, width, channels, False)
        + [VMEM(ext, F32), VMEM(ext, BF), VMEM(inner, F32)]
        + [VMEM((2, rows, channels), BF), VMEM(stat, F32)]
        + sems(2 * pairs + 4, 3 * pairs + 2),
        compiler_params=params(62.5),
        cost_estimate=cost(),
        name="conv_next",
    )


def fill_weights(table, coords, extent):
    depth, height, width = extent
    samples = coords[0].shape[1]

    def along(base, frac, size):
        grid = iota((size, samples), 0).astype(F32)
        lower = jnp.where(grid == base, 1.0 - frac, 0.0)
        return lower + jnp.where(grid == base + 1.0, frac, 0.0)

    on_x = along(coords[0] - 1.0, coords[3], depth)
    on_y = along(coords[1], coords[4], height)
    on_z = along(coords[2], coords[5], width)
    for x in range(depth):
        on_xy = on_x[x : x + 1] * on_y
        for y in range(height):
            row = (x * height + y) * width
            table[row : row + width, :] = (on_xy[y : y + 1] * on_z).astype(BF)


def diagonal(rows, columns):
    return iota((rows, columns), 0) == iota((rows, columns), 1)


def identity(rows, columns):
    return diagonal(rows, columns).astype(F32).astype(BF)


def head_rows(semantic, density, rows):
    channels, classes = semantic.shape
    turned = nt(identity(rows, classes), semantic)
    return jnp.where(iota((rows, channels), 0) == classes, density.astype(F32), turned).astype(BF)


def column(row, rows):
    return jnp.sum(jnp.where(diagonal(rows, row.shape[1]), row, 0.0), axis=1, keepdims=True)


def coord_rows(block, slots):
    lines = slots // block.shape[1]
    return [
        jnp.concatenate(
            [block[8 + r * lines + n : 9 + r * lines + n, :] for n in range(lines)], axis=1
        )
        for r in range(6)
    ]


def sample_kernel(
    extent, layer, first, count, coords, *refs
):
    if count is None:
        r_hbm, refs = refs[0], refs[1:]
    else:
        y_hbm, v_hbm, total_hbm, gain, shift, refs = refs[0], refs[1], refs[2], refs[3], refs[4], refs[5:]
    hidden, hidden_b, semantic, density, semantic_b, density_b, refs = *refs[:6], refs[6:]
    p_ref, f_ref, g_ref, s_ref, refs = *refs[:4], refs[4:]
    if count is not None:
        r_out, refs = refs[0], refs[1:]
    turned, table, rounded, hidden_t, bias, head_t, head_b, sem, refs = *refs[:8], refs[8:]
    channels = turned.shape[0]
    depth = extent[0]
    classes = semantic.shape[2]
    slots = table.shape[1]
    rows = rounded.shape[1]
    step = pl.program_id(0)

    if count is not None:
        y_in, v_in, total, load_sem = refs

    def in_copies(p):
        return (
            pltpu.make_async_copy(y_hbm.at[p], y_in.at[p], load_sem.at[2 * p]),
            pltpu.make_async_copy(v_hbm.at[p + 1], v_in.at[p], load_sem.at[2 * p + 1]),
        )

    def out_copy(p):
        return pltpu.make_async_copy(rounded.at[p], r_out.at[p], sem.at[p])

    @pl.when(step == 0)
    def _():
        if count is None:
            copy = started(r_hbm.at[pl.ds(first, depth)], rounded, sem.at[0])
        else:
            light = started(total_hbm, total, load_sem.at[2 * depth])
            for p in range(depth):
                for copy in in_copies(p):
                    copy.start()
        same = identity(channels, channels)
        hidden_t[...] = nt(same, hidden[layer]).astype(BF)
        bias[...] = column(hidden_b[layer : layer + 1, :], channels)
        head_t[...] = head_rows(semantic[layer], density[layer : layer + 1, :], PROWS)
        last = jnp.sum(
            jnp.where(iota((1, density_b.shape[1]), 1) == layer, density_b[...], 0.0),
            axis=1,
            keepdims=True,
        )
        place = iota((PROWS, 1), 0) == classes
        head_b[...] = jnp.where(place, last, column(semantic_b[layer : layer + 1, :], PROWS))
        if count is None:
            copy.wait()
        else:
            light.wait()
            mean, inverse = moments(total[...], count)
            gains, shifts = row_of(gain, layer), row_of(shift, layer)

        @pl.loop(0, depth)
        def _(p):
            if count is not None:
                for copy in in_copies(p):
                    copy.wait()
                fresh = v_in[p] + silu((y_in[p] - mean) * inverse * gains + shifts)
                rounded[p] = fresh.astype(BF)
                out_copy(p).start()
            turned[:, pl.ds(pl.multiple_of(p * rows, rows), rows)] = nt(same, rounded[p]).astype(BF)

    fill_weights(table, coord_rows(coords[0], slots), extent)
    feature = nn(turned[...], table[...]).astype(BF)
    f_ref[0] = feature
    inner = nn(hidden_t[...], feature) + bias[...]
    small = jnp.exp(-jnp.abs(inner))
    act = (jnp.maximum(inner, 0.0) + jnp.log1p(small)).astype(BF)
    g_ref[0] = act
    s_ref[0] = jnp.where(inner >= 0.0, 1.0, small) / (1.0 + small)
    p_ref[0] = nn(head_t[...], act) + head_b[...]
    if count is not None:

        @pl.when(step == pl.num_programs(0) - 1)
        def _():
            for p in range(depth):
                out_copy(p).wait()


def per_tile(rows, lanes):
    return pl.BlockSpec((1, rows, lanes), lambda t: (t, 0, 0))


def sample(extent, received, source, layer, mlp, count=None, follow=()):
    tiles, lines, wide = received.shape
    slots = CAP
    rows, channels = extent[1] * extent[2], mlp[0].shape[1]
    depth = extent[0]
    voxels = depth * rows
    outs = [((tiles, PROWS, slots), F32)] + [((tiles, channels, slots), d) for d in (BF, BF, F32)]
    out_specs = [per_tile(n, slots) for n in (PROWS, channels, channels, channels)]
    scratch = [
        VMEM((channels, voxels), BF),
        VMEM((voxels, slots), BF),
        VMEM((depth, rows, channels), BF),
        VMEM((channels, channels), BF),
        VMEM((channels, 1), F32),
        VMEM((PROWS, channels), BF),
        VMEM((PROWS, 1), F32),
    ] + sems(depth)
    if count is None:
        first, given, specs = source[1], source[:1], [aspec()]
    else:
        first, given = 0, source
        specs = [aspec()] * 3 + [whole(x.shape) for x in source[3:]]
        outs.append(((depth, rows, channels), BF))
        out_specs.append(aspec())
        scratch += [VMEM((depth, rows, channels), F32)] * 2 + [VMEM(source[2].shape, F32)]
        scratch += sems(2 * depth + 1)
    return ordered(
        functools.partial(sample_kernel, extent, layer, first, count),
        (received,) + tuple(given) + mlp,
        [per_tile(lines, wide)] + specs + [whole(x.shape) for x in mlp],
        follow,
        grid=(tiles,),
        out_shape=any_outs(*outs),
        out_specs=tuple(out_specs),
        scratch_shapes=scratch,
        compiler_params=params(62.5),
        cost_estimate=cost(),
        name="sample",
    )


def sample_back_kernel(
    extent, layer, coords, dp_ref, f_ref, g_ref, s_ref, hidden, semantic, density, *refs
):
    du_ref, pack_ref, total, table, head = refs[-5:]
    step = pl.program_id(0)
    channels = hidden.shape[1]
    slots = table.shape[1]

    @pl.when(step == 0)
    def _():
        total[...] = jnp.zeros_like(total)
        pack_ref[0:PACK, :] = jnp.zeros((PACK, channels), F32)
        if len(refs) > 5:
            pack_ref[PACK : 2 * PACK, :] = refs[0][...]
        rows = head_rows(semantic[layer], density[layer : layer + 1, :], DROWS)
        head[...] = nt(identity(channels, channels), rows).astype(BF)

    fill_weights(table, coord_rows(coords[0], slots), extent)
    grad_heads = dp_ref[0]
    grad_inner = (nn(head[...], grad_heads) * s_ref[0]).astype(BF)
    ones = jnp.ones((16, slots), BF)
    pack_ref[0:channels, :] += nt(f_ref[0], grad_inner)
    pack_ref[channels : channels + 16, :] += nt(ones, grad_inner)
    at = channels + 16
    pack_ref[at : at + DROWS, :] += nt(grad_heads, g_ref[0])
    at += DROWS
    pack_ref[at : at + 16, 0:DROWS] += nt(ones, grad_heads)
    grad_features = nn(hidden[layer], grad_inner).astype(BF)
    total[...] += nt(table[...], grad_features)

    @pl.when(step == pl.num_programs(0) - 1)
    def _():
        du_ref[...] = total[...].astype(BF)


def sample_back(extent, layer, received, grad_heads, feature, act, slope, mlp, packs, follow=()):
    tiles, lines, wide = received.shape
    _, channels, slots = feature.shape
    voxels = extent[0] * extent[1] * extent[2]
    hidden, _, semantic, density = mlp[:4]
    outs = ((voxels, channels), (PACK * (1 + len(packs)), channels))
    return ordered(
        functools.partial(sample_back_kernel, extent, layer),
        (received, grad_heads, feature, act, slope, hidden, semantic, density) + packs,
        [per_tile(lines, wide)]
        + [per_tile(n, slots) for n in (DROWS, channels, channels, channels)]
        + [whole(x.shape) for x in (hidden, semantic, density) + packs],
        follow,
        grid=(tiles,),
        out_shape=any_outs((outs[0], BF), (outs[1], F32)),
        out_specs=tuple(whole(shape) for shape in outs),
        scratch_shapes=[
            VMEM((voxels, channels), F32),
            VMEM((voxels, slots), BF),
            VMEM((channels, DROWS), BF),
        ],
        compiler_params=params(62.5),
        cost_estimate=cost(),
        name="sample_back",
    )


def composite_kernel(
    classes, layer, starts, pixels, owner_ref, rank_ref, view, heads, cot,
    pic_ref, dp_ref, split, by_ray, grads, density, weights, grad_w, acc,
):
    tiles = heads.shape[0]
    rays, samples = owner_ref.shape
    step = 4.0 / samples
    split[...] = jnp.zeros_like(split)
    for t in range(tiles):
        value = heads[t]
        high = value.astype(BF)
        split[t, 0:PROWS, 0:CAP] = high.astype(F32)
        split[t, PROWS : 2 * PROWS, 0:CAP] = value - high.astype(F32)

    def hots(k):
        return window_onehots(
            starts, owner_ref[k : k + 1, :], rank_ref[k : k + 1, :], k, rays, tiles
        )

    for k in range(rays):
        hot, bases = hots(k)
        windows = jnp.concatenate(
            [split[t, :, pl.ds(bases[t], WINDOW)].astype(BF) for t in range(tiles)], axis=1
        )
        both = nn(windows, hot)
        one = both[:PROWS] + both[PROWS:]
        by_ray[k] = one
        density[k : k + 1, :] = one[classes : classes + 1]

    pre = density[...]
    visible = view[...].astype(F32)
    small = jnp.exp(-jnp.abs(pre))
    optical = visible * (jnp.maximum(pre, 0.0) + jnp.log1p(small)) * step
    passing = jnp.exp(-(lane_cumsum(optical) - optical))
    fading = jnp.exp(-optical)
    weight = passing * (1.0 - fading)
    weights[...] = weight
    row = iota((PROWS, samples), 0)
    lane = iota((PROWS, rays), 1)
    cotangent = nt(identity(PROWS, classes + 1), cot[layer])
    picture = jnp.zeros((PROWS, rays), F32)
    for k in range(rays):
        there = lane == pixels[k]
        dpic = jnp.sum(jnp.where(there, cotangent, 0.0), axis=1, keepdims=True)
        value = jnp.where(row < classes, by_ray[k], jnp.where(row == classes, 1.0, 0.0))
        one = weights[k : k + 1, :]
        colour = jnp.sum(value * one, axis=1, keepdims=True)
        picture = jnp.where(there, colour, picture)
        grad_w[k : k + 1, :] = jnp.sum(value * dpic, axis=0, keepdims=True)
        grads[k] = dpic * one
    pic_ref[...] = picture
    grad_weight = grad_w[...]
    carried = grad_weight * weight
    later = jnp.sum(carried, axis=1, keepdims=True) - lane_cumsum(carried)
    grad_optical = grad_weight * passing * fading - later
    slope = jnp.where(pre >= 0.0, 1.0, small) / (1.0 + small)
    density[...] = grad_optical * visible * step * slope
    acc[...] = jnp.zeros_like(acc)
    zero = jnp.zeros((DROWS - PROWS, samples), F32)
    for k in range(rays):
        hot, bases = hots(k)
        grad = jnp.where(row == classes, density[k : k + 1, :], grads[k])
        moved = nt(jnp.concatenate([grad, zero], axis=0).astype(BF), hot)
        for t in range(tiles):
            acc[t, :, pl.ds(bases[t], WINDOW)] += moved[:, t * WINDOW : (t + 1) * WINDOW]
    for t in range(tiles):
        dp_ref[t] = acc[t, :, 0:CAP].astype(BF)


def composite(starts, pixels, owner, rank, view, heads, cot, layer, classes, follow=()):
    tiles, _, slots = heads.shape
    rays, samples = owner.shape
    outs = ((PROWS, rays), (tiles, DROWS, slots))
    return ordered(
        functools.partial(composite_kernel, classes, layer),
        (starts, pixels, owner, rank, view, heads, cot,),
        [sspec(), sspec()] + [whole(x.shape) for x in (owner, rank, view, heads, cot)],
        follow,
        grid=(1,),
        out_shape=(jax.ShapeDtypeStruct(outs[0], F32), jax.ShapeDtypeStruct(outs[1], BF)),
        out_specs=tuple(whole(s) for s in outs),
        scratch_shapes=[
            VMEM((tiles, 2 * PROWS, CAP + WINDOW), F32),
            VMEM((rays, PROWS, samples), F32),
            VMEM((rays, PROWS, samples), F32),
            VMEM((rays, samples), F32),
            VMEM((rays, samples), F32),
            VMEM((rays, samples), F32),
            VMEM((tiles, DROWS, CAP + WINDOW), F32),
        ],
        compiler_params=params(62.5),
        cost_estimate=cost(),
        name="composite",
    )


def add_kernel(parts, out_ref):
    total = parts[0].astype(F32)
    for n in range(1, parts.shape[0]):
        total = total + parts[n].astype(F32)
    total = total.astype(out_ref.dtype)
    for n in range(out_ref.shape[0]):
        out_ref[n] = total


def add_parts(parts, copies, follow=()):
    shape = (copies,) + parts.shape[1:]
    return ordered(
        add_kernel,
        (parts,),
        [whole(parts.shape)],
        follow,
        grid=(1,),
        out_shape=jax.ShapeDtypeStruct(shape, parts.dtype),
        out_specs=whole(shape),
        compiler_params=params(62.5),
        cost_estimate=cost(),
        name="add_parts",
    )


def add_arrays_kernel(*refs):
    total = refs[0][...].astype(F32)
    for ref in refs[1:-1]:
        total = total + ref[...].astype(F32)
    refs[-1][...] = total.astype(refs[-1].dtype)


def add_arrays(values, follow=()):
    return ordered(
        add_arrays_kernel,
        tuple(values),
        [whole(x.shape) for x in values],
        follow,
        grid=(1,),
        out_shape=jax.ShapeDtypeStruct(values[0].shape, values[0].dtype),
        out_specs=whole(values[0].shape),
        compiler_params=params(8),
        cost_estimate=cost(),
        name="add_arrays",
    )


def hold_kernel(*refs):
    del refs


def hold(values, follow):
    return ordered(
        hold_kernel,
        values,
        [aspec()] * len(values),
        follow,
        out_shape=any_outs(*((x.shape, x.dtype) for x in values)),
        out_specs=(aspec(),) * len(values),
        input_output_aliases={n: n for n in range(len(values))},
        compiler_params=params(62.5),
        cost_estimate=cost(),
        name="hold",
    )


def all_to_all(value, axis):
    return lax.all_to_all(value, axis, split_axis=0, concat_axis=0, tiled=True)


def exchange(first, last):
    devices = lax.axis_size("tile")
    up = [(i, i + 1) for i in range(devices - 1)]
    down = [(i + 1, i) for i in range(devices - 1)]
    return lax.ppermute(last, "tile", up), lax.ppermute(first, "tile", down)


def norm_grads(y, grad, mean, inverse, gains, shifts):
    centred = (y - mean) * inverse
    normal = centred * gains + shifts
    sigma = 1.0 / (1.0 + jnp.exp(-normal))
    return grad * sigma * (1.0 + normal * (1.0 - sigma)), centred


def finish_back(sums, edges, ups, spare, out_sem):
    rows = edges.shape[1] - 16
    value = sums[...]
    high = value.astype(BF).astype(F32)
    middle = (value - high).astype(BF).astype(F32)
    low = value - high - middle
    tail = jnp.concatenate([high[0:2], middle[0:2], low[0:2], jnp.zeros((10,) + high.shape[1:], F32)], axis=0)
    tail = tail.astype(BF)
    edges[0, rows:, :] = tail
    edges[1, rows:, :] = tail
    spare[...] = tail
    first_ref, last_ref, far_ref = ups
    copies = [
        started(edges.at[0], first_ref, out_sem.at[0]),
        started(edges.at[1], last_ref, out_sem.at[1]),
        started(spare, far_ref, out_sem.at[2]),
    ]
    for copy in copies:
        copy.wait()


def norm_back_kernel(
    layer, count, cot, local, y, total_hbm, gain_hbm, shift_hbm, first_ref, last_ref, far_ref,
    cot_in, local_in, y_in, total, gain, shift, edges, sums, spare, in_sem, out_sem,
):
    planes, rows, _ = cot.shape
    small = [
        started(total_hbm, total, in_sem.at[3 * planes]),
        started(gain_hbm, gain, in_sem.at[3 * planes + 1]),
        started(shift_hbm, shift, in_sem.at[3 * planes + 2]),
    ]

    def in_copies(p):
        return [
            pltpu.make_async_copy(source.at[p], target.at[p], in_sem.at[3 * p + n])
            for n, (source, target) in enumerate(((cot, cot_in), (local, local_in), (y, y_in)))
        ]

    for p in range(planes):
        for copy in in_copies(p):
            copy.start()
    sums[...] = jnp.zeros_like(sums)
    for copy in small:
        copy.wait()
    mean, inverse = moments(total[...], count)
    gains, shifts = row_of(gain, layer), row_of(shift, layer)

    @pl.loop(0, planes)
    def _(p):
        for copy in in_copies(p):
            copy.wait()
        grad = cot_in[p].astype(F32) + local_in[p].astype(F32)
        inner, centred = norm_grads(y_in[p], grad, mean, inverse, gains, shifts)
        add_stats(sums, inner, inner * centred)
        for side, edge in ((0, 0), (1, planes - 1)):

            @pl.when(p == edge)
            def _():
                edges[side, 0:rows, :] = inner.astype(BF)

    finish_back(sums, edges, (first_ref, last_ref, far_ref), spare, out_sem)


def back_shapes(rows, channels):
    return ((rows + 16, channels), BF), ((rows + 16, channels), BF), ((16, channels), BF)


def back_scratch(rows, channels):
    return [VMEM((2, rows + 16, channels), BF), VMEM((8, channels), F32), VMEM((16, channels), BF)]


def norm_back(cot, local, y, total, gain, shift, layer, count, follow=()):
    planes, rows, channels = local.shape
    return ordered(
        functools.partial(norm_back_kernel, layer, count),
        (cot, local, y, total, gain, shift),
        [aspec()] * 6,
        follow,
        out_shape=any_outs(*back_shapes(rows, channels)),
        out_specs=(aspec(),) * 3,
        scratch_shapes=[VMEM(x.shape, x.dtype) for x in (cot, local, y, total, gain, shift)]
        + back_scratch(rows, channels)
        + sems(3 * planes + 3, 3),
        compiler_params=params(62.5),
        cost_estimate=cost(),
        name="norm_back",
    )


def share_back(sent):
    first, last, far = sent
    tiles = lax.axis_size("tile")

    def move(value, by):
        return lax.ppermute(value, "tile", [(i, (i + by) % tiles) for i in range(tiles)])

    return (move(last, 1), move(first, tiles - 1)) + tuple(move(far, n) for n in range(2, tiles - 1))


def turn_kernel(width, block, r_ref, out_ref, turned):
    planes, rows, channels = r_ref.shape
    chosen = out_ref.shape[1]
    pick = iota((chosen, channels), 1) == iota((chosen, channels), 0) + block[0] * chosen
    pick = pick.astype(F32).astype(BF)
    place = iota((chosen, rows), 1)
    on_y, on_z = lax.div(place, width), lax.rem(place, width)
    height = rows // width
    for p in range(planes):
        turned[...] = nt(pick, r_ref[p])
        for b in range(3):
            for c in range(3):
                shift = (b - 1) * width + (c - 1)
                value = turned[...]
                if shift:
                    value = pltpu.roll(value, (-shift) % rows, 1)
                y, z = on_y + (b - 1), on_z + (c - 1)
                inside = (y >= 0) & (y < height) & (z >= 0) & (z < width)
                value = jnp.where(inside, value, 0.0).astype(BF)
                for a in range(3):
                    target = p - a
                    if 0 <= target < planes - 2:
                        out_ref[9 * a + 3 * b + c, :, target * rows : (target + 1) * rows] = value


def turn(block, rounded, width, blocks, follow=()):
    planes, rows, channels = rounded.shape
    chosen = channels // blocks
    shape = (27, chosen, (planes - 2) * rows)
    return ordered(
        functools.partial(turn_kernel, width),
        (block, rounded,),
        [sspec(), whole(rounded.shape)],
        follow,
        grid=(1,),
        out_shape=jax.ShapeDtypeStruct(shape, BF),
        out_specs=whole(shape),
        scratch_shapes=[VMEM((chosen, rows), F32)],
        compiler_params=params(62.5),
        cost_estimate=cost(),
        name="turn",
    )


def weight_grad_kernel(layer, count, first, parts, tiles, split, spots, taps_hbm, *refs):
    grads, refs = refs[:parts], refs[parts:]
    if first:
        y, refs = refs[0], refs[1:]
        y_before, y_after = y.at[pl.ds(0, 1)], y.at[pl.ds(y.shape[0] - 1, 1)]
    else:
        y, y_before, y_after, refs = refs[0], refs[1], refs[2], refs[3:]
    own_far, others, refs = refs[0], refs[1:tiles], refs[tiles:]
    total_hbm, gain_hbm, shift_hbm, refs = *refs[:3], refs[3:]
    shares = tiles if split else 1
    dy_ref, back_ref, wg_refs, refs = refs[0], refs[1], refs[2 : 2 + shares], refs[2 + shares :]
    grads_in, refs = refs[:parts], refs[parts:]
    (taps_in, y_in, y_halo, dn_halo, rest, back, total, gain, shift, dy_buf, dy_rows, wg_buf, in_sem,
     out_sem) = refs
    planes, rows, channels = grads[0].shape
    spare = (parts + 1) * planes
    lists = [
        (total_hbm.at[:, pl.ds(0, 8), :], total),
        (gain_hbm, gain),
        (shift_hbm, shift),
        (y_before, y_halo.at[pl.ds(0, 1)]),
        (y_after, y_halo.at[pl.ds(1, 1)]),
        (others[0], dn_halo.at[0]),
        (others[1], dn_halo.at[1]),
        (own_far, rest.at[0]),
    ] + [(other, rest.at[n + 1]) for n, other in enumerate(others[2:])]
    small = [
        started(source, target, in_sem.at[spare + n]) for n, (source, target) in enumerate(lists)
    ]

    def in_copies(p):
        copies = [pltpu.make_async_copy(y.at[p + first], y_in.at[p], in_sem.at[(parts + 1) * p])]
        for n in range(parts):
            copies.append(
                pltpu.make_async_copy(
                    grads[n].at[p], grads_in[n].at[p], in_sem.at[(parts + 1) * p + 1 + n]
                )
            )
        return copies

    for p in range(planes):
        for copy in in_copies(p):
            copy.start()
    heavy = started(taps_hbm, taps_in, in_sem.at[spare + len(lists)])
    for copy in small:
        copy.wait()
    tile = spots[2]
    tails = [rest[0], dn_halo[0, rows:, :], dn_halo[1, rows:, :]]
    tails += [rest[n] for n in range(1, rest.shape[0])]
    for by, tail in zip([0, 1, tiles - 1] + list(range(2, tiles - 1)), tails):
        value = tail.astype(F32)
        value = value[0:2] + value[2:4] + value[4:6]
        back[lax.rem(tile + tiles - by, tiles), 0:2, :] = value
    mean, inverse = moments(total[...], count)
    gains, shifts = row_of(gain, layer), row_of(shift, layer)
    scale = inverse * gains
    both = back[0, 0:2, :]
    for t in range(1, tiles):
        both = both + back[t, 0:2, :]
    back[0, 0:2, :] = both
    sums = both / count

    def finish(inner, centred):
        return scale * (inner - sums[0:1, :] - centred * sums[1:2, :])

    for side, place in ((0, 0), (1, planes + 1)):
        centred = (y_halo[side].astype(F32) - mean) * inverse
        value = finish(dn_halo[side, 0:rows, :].astype(F32), centred)
        dy_buf[place] = jnp.where(spots[side] > 0, value, 0.0).astype(BF)

    @pl.loop(0, planes)
    def _(p):
        for copy in in_copies(p):
            copy.wait()
        grad = grads_in[0][p].astype(F32)
        for n in range(1, parts):
            grad = grad + grads_in[n][p].astype(F32)
        value = finish(*norm_grads(y_in[p], grad, mean, inverse, gains, shifts)).astype(BF)
        dy_buf[p + 1] = value
        dy_rows[pl.ds(pl.multiple_of(p * rows, rows), rows), :] = value

    done = [
        started(dy_buf, dy_ref, out_sem.at[0]),
        started(back.at[0, pl.ds(0, 2), :], back_ref, out_sem.at[1]),
    ]
    heavy.wait()
    part = nn(taps_in[...], dy_rows[...])
    lines = wg_buf.shape[1]
    for t in range(tiles):
        wg_buf[t] = part[t * lines : (t + 1) * lines].astype(BF)
    if split:
        for by, wg_ref in enumerate(wg_refs):
            share = wg_buf.at[lax.rem(tile + by, tiles)]
            done.append(started(share, wg_ref, out_sem.at[2 + by]))
    else:
        done.append(started(wg_buf, wg_refs[0], out_sem.at[2]))
    for copy in done:
        copy.wait()


def weight_grad(
    spots, taps_t, grads, y, y_halo, far, others, total, gain, shift, layer, count, split,
    follow=(),
):
    planes, rows, channels = grads[0].shape
    wide = taps_t.shape[0]
    tiles = len(others) + 1
    ext = (planes + 2, rows, channels)
    own = (planes, rows, channels)
    operands = (taps_t,) + tuple(grads) + (y,) + tuple(y_halo) + (far,) + tuple(others)
    operands += (total, gain, shift)
    return ordered(
        functools.partial(
            weight_grad_kernel, layer, count, 0 if y_halo else 1, len(grads), tiles, split
        ),
        (spots,) + operands,
        [sspec()] + [aspec()] * len(operands),
        follow,
        out_shape=any_outs(
            (ext, BF),
            ((2, channels), F32),
            *(((wide // tiles, channels), BF),) * tiles
            if split
            else (((tiles, wide // tiles, channels), BF),),
        ),
        out_specs=(aspec(),) * (2 + (tiles if split else 1)),
        scratch_shapes=[VMEM(x.shape, x.dtype) for x in grads]
        + [
            VMEM(taps_t.shape, BF),
            VMEM(own, F32),
            VMEM((2, rows, channels), BF if y_halo else F32),
            VMEM((2, rows + 16, channels), BF),
            VMEM((tiles - 2, 16, channels), BF),
            VMEM((tiles, 8, channels), F32),
            VMEM((tiles, 8, channels), F32),
            VMEM(gain.shape, F32),
            VMEM(gain.shape, F32),
            VMEM(ext, BF),
            VMEM((planes * rows, channels), BF),
            VMEM((tiles, wide // tiles, channels), BF),
        ]
        + sems((len(grads) + 1) * planes + 8 + tiles, 2 + tiles),
        compiler_params=params(62.5),
        cost_estimate=cost(),
        name="weight_grad",
    )


def conv_back_kernel(width, layer, count, parts, dy, w_hbm, *refs):
    more = count is not None
    grads, refs = refs[:parts], refs[parts:]
    if more:
        y, total_hbm, gain_hbm, shift_hbm, refs = *refs[:4], refs[4:]
    out_ref, refs = refs[0], refs[1:]
    if more:
        sent, refs = refs[:3], refs[3:]
    grads_in, refs = refs[:parts], refs[parts:]
    raw, xs, weight, out_buf, in_sem, w_sem, out_sem, refs = *refs[:7], refs[7:]
    ext_planes, rows, channels = dy.shape
    planes = ext_planes - 2
    group = planes // 2
    pairs = 2
    each = parts + 1
    body = started(dy, raw, in_sem.at[each * pairs])
    heavy = [
        started(
            w_hbm.at[layer, pl.ds((26 - o) * channels, channels), :],
            weight.at[:, pl.ds(o * channels, channels)],
            w_sem.at[o],
        )
        for o in range(27)
    ]
    small = []
    if more:
        y_in, total, gain, shift, edges, sums, spare, back_sem = refs
        small = [
            started(source, target, in_sem.at[each * pairs + 1 + n])
            for n, (source, target) in enumerate(
                ((total_hbm.at[:, pl.ds(0, 8), :], total), (gain_hbm, gain), (shift_hbm, shift))
            )
        ]
        sums[...] = jnp.zeros_like(sums)

    def in_copies(i):
        two = pl.ds(group * i, group)
        copies = [
            pltpu.make_async_copy(grads[n].at[two], grads_in[n].at[two], in_sem.at[each * i + n])
            for n in range(parts)
        ]
        if more:
            copies.append(
                pltpu.make_async_copy(
                    y.at[pl.ds(group * i + 1, group)], y_in.at[two], in_sem.at[each * i + parts]
                )
            )
        return copies

    def out_copy(i):
        two = pl.ds(group * i, group)
        return pltpu.make_async_copy(out_buf.at[two], out_ref.at[two], out_sem.at[i])

    for i in range(pairs):
        for copy in in_copies(i):
            copy.start()
    clear_edges(xs, width, rows)
    body.wait()

    @pl.loop(0, ext_planes)
    def _(p):
        put_plane(xs, p, raw[p].astype(F32), width)

    for copy in small + heavy:
        copy.wait()
    if more:
        mean, inverse = moments(total[...], count)
        gains, shifts = row_of(gain, layer - 1), row_of(shift, layer - 1)

    @pl.loop(0, pairs)
    def _(i):
        part = nt(tap_group(xs, group * i, group, width, rows), weight[...])
        for copy in in_copies(i):
            copy.wait()
        for n_plane in range(group):
            p = group * i + n_plane
            value = part[n_plane * rows : (n_plane + 1) * rows]
            for n in range(parts):
                value = value + grads_in[n][p].astype(F32)
            out_buf[p] = value
            if more:
                inner, centred = norm_grads(y_in[p], value, mean, inverse, gains, shifts)
                add_stats(sums, inner, inner * centred)

                for side, near in ((0, 0), (1, group - 1)):
                    if n_plane == near:

                        @pl.when(p == side * (planes - 1))
                        def _():
                            edges[side, 0:rows, :] = inner.astype(BF)

        out_copy(i).start()

    if more:
        finish_back(sums, edges, sent, spare, back_sem)
    for i in range(pairs):
        out_copy(i).wait()


def conv_back(dy, grads, weights, layer, width, norm=None, follow=()):
    ext_planes, rows, channels = dy.shape
    own = (ext_planes - 2, rows, channels)
    pairs = 2
    outs, extra, scratch = [(own, F32)], (), []
    if norm is not None:
        y, total, gain, shift, count = norm
        extra = (y, total, gain, shift)
        outs += list(back_shapes(rows, channels))
        scratch = [VMEM(own, F32), VMEM((total.shape[0], 8, channels), F32)]
        scratch += [VMEM(gain.shape, F32), VMEM(gain.shape, F32)]
        scratch += back_scratch(rows, channels) + sems(3)
    else:
        count = None
    return ordered(
        functools.partial(conv_back_kernel, width, layer, count, len(grads)),
        (dy, weights) + tuple(grads) + extra,
        [aspec()] * (2 + len(grads) + len(extra)),
        follow,
        out_shape=any_outs(*outs),
        out_specs=(aspec(),) * len(outs),
        scratch_shapes=[VMEM(x.shape, x.dtype) for x in grads]
        + [VMEM(dy.shape, BF)]
        + conv_scratch(ext_planes, rows, width, channels, True)
        + [VMEM(own, F32)]
        + sems(pairs * (len(grads) + 1) + 4, 27, pairs)
        + scratch,
        compiler_params=params(62.5),
        cost_estimate=cost(),
        name="conv_back",
    )


GROUP = 3


def order_kernel(spots, *refs):
    out_ref = refs[-1]
    tiles = out_ref.shape[0]
    for by in range(tiles):
        out_ref[lax.rem(spots[2] + tiles - by, tiles)] = refs[by][...]


def spread_tile(value, spots, follow):
    tiles = lax.axis_size("tile")
    parts = [value]
    for by in range(1, tiles):
        pairs = [(i, (i + by) % tiles) for i in range(tiles)]
        parts.append(lax.ppermute(value, "tile", pairs))
    shape = (tiles,) + value.shape
    return ordered(
        order_kernel,
        (spots,) + tuple(parts),
        [sspec()] + [whole(value.shape)] * tiles,
        follow,
        grid=(1,),
        out_shape=jax.ShapeDtypeStruct(shape, value.dtype),
        out_specs=whole(shape),
        compiler_params=params(8),
        cost_estimate=cost(),
        name="order_tiles",
    )


def gather_ray(slices):
    return lax.all_gather(slices.reshape(-1, slices.shape[-1]), "ray", axis=0)


def place_kernel(layer, blocks, source, *refs):
    out_ref, taken, out, in_sem, out_sem = refs[-5:]
    _, offsets, rows, _ = out_ref.shape
    chosen = rows // blocks
    steps = offsets // GROUP
    lines = GROUP * chosen

    def in_copy(n):
        some = pl.ds(n * lines, lines)
        return pltpu.make_async_copy(
            source.at[pl.ds(0, blocks), some], taken.at[:, some], in_sem.at[n]
        )

    for n in range(steps):
        in_copy(n).start()
    done = []
    for n in range(steps):
        in_copy(n).wait()
        for o in range(n * GROUP, (n + 1) * GROUP):
            for ray in range(blocks):
                out[o, ray * chosen : (ray + 1) * chosen, :] = taken[
                    ray, o * chosen : (o + 1) * chosen, :
                ].astype(F32)
        some = pl.ds(n * GROUP, GROUP)
        done.append(started(out.at[some], out_ref.at[layer, some], out_sem.at[n]))
    for copy in done:
        copy.wait()


def place(parts, layer, layers, blocks, kept, follow=()):
    _, lines, channels = parts.shape
    offsets = lines * blocks // channels
    return ordered(
        functools.partial(place_kernel, layer, blocks),
        (parts,) + kept,
        [aspec()] * (1 + len(kept)),
        follow,
        out_shape=jax.ShapeDtypeStruct((layers, offsets, channels, channels), F32),
        out_specs=aspec(),
        scratch_shapes=[VMEM((blocks, lines, channels), BF), VMEM((offsets, channels, channels), F32)]
        + sems(offsets // GROUP, offsets // GROUP),
        input_output_aliases={1: 0} if kept else {},
        compiler_params=params(62.5),
        cost_estimate=cost(),
        name="place",
    )


def per_device(
    volume,
    sample_cells,
    sample_fracs,
    view_mask,
    pixel_of_ray,
    conv_weight,
    norm_gain,
    norm_shift,
    hidden_weight,
    hidden_bias,
    density_weight,
    density_bias,
    semantic_weight,
    semantic_bias,
    render_cotangent,
    volume_cotangent,
):
    extent = volume.shape[:3]
    depth, height, width, channels = volume.shape
    rows = height * width
    voxels = depth * rows
    tiles = lax.axis_size("tile")
    ray_devices = lax.axis_size("ray")
    count = float(voxels * tiles)
    rays, samples = sample_cells.shape
    classes = semantic_weight.shape[2]
    layers = conv_weight.shape[0]
    blocks = min(BLOCKS, ray_devices)
    chosen = channels // blocks
    tile, ray = lax.axis_index("tile"), lax.axis_index("ray")
    block = lax.rem(ray, blocks).astype(jnp.int32).reshape(1)

    own = volume.reshape(depth, rows, channels)
    before, after = exchange(own[:2], own[-2:])
    flags = jnp.stack([tile > 0, tile < tiles - 1]).astype(jnp.int32)

    owner_of = lax.div(sample_cells, voxels)
    held = owner_of[None] == jnp.arange(tiles, dtype=jnp.int32)[:, None, None]
    earlier = jnp.arange(rays)[None, :] < jnp.arange(rays)[:, None]
    starts = jnp.sum(
        (held[:, None, :, :] & earlier[None, :, :, None]).astype(jnp.int32), axis=(2, 3)
    ).reshape(tiles * rays)
    pixels = pixel_of_ray[0]
    buffer, owner, rank = prepare(extent, starts, sample_cells, sample_fracs, tiles, channels)

    weights = conv_weight.reshape(layers, 27 * channels, channels)
    mlp = (
        hidden_weight,
        hidden_bias,
        semantic_weight,
        density_weight,
        semantic_bias,
        density_bias[None],
    )
    y_ext, v_ext, mixed = conv_first(before, own, after, buffer, weights, 0, width)
    total = received = all_to_all(mixed, "tile")
    taps_first = turn(block, v_ext, width, blocks)
    v_next, r_ext, y_next, stat, y_first, y_last = conv_next(
        flags, y_ext, v_ext, total, norm_gain, norm_shift, weights, 0, width, count,
        follow=(taps_first,),
    )
    total_next = all_to_all(stat, "tile")
    heads, feature, act, slope = sample(extent, received, (r_ext, 1), 0, mlp)
    heads_last, feature_last, act_last, slope_last, r_last = sample(
        extent, received, (y_next, v_next, total_next, norm_gain, norm_shift), 1, mlp, count,
        follow=(heads,),
    )

    def draw(heads, layer, follow):
        return composite(
            starts, pixels, owner, rank, view_mask, all_to_all(heads, "tile"), render_cotangent,
            layer, classes, follow=follow,
        )

    picture, grad_heads = draw(heads, 0, (heads_last,))
    picture_last, grad_heads_last = draw(heads_last, 1, (grad_heads,))
    shares = (ray_devices, voxels // ray_devices, channels)
    planes = (depth, rows, channels)
    local, pack = sample_back(
        extent, 0, received, all_to_all(grad_heads, "tile"), feature, act, slope, mlp, (),
        follow=(grad_heads_last,),
    )
    parts = all_to_all(local.reshape(shares), "ray")
    local_last, packed = sample_back(
        extent, 1, received, all_to_all(grad_heads_last, "tile"), feature_last, act_last,
        slope_last, mlp, (pack,), follow=(local,),
    )
    copies = add_parts(parts, ray_devices, follow=(local_last,))
    parts_last = all_to_all(local_last.reshape(shares), "ray")
    taps_next = turn(block, r_ext, width, blocks, follow=(copies,))
    copies_last = add_parts(parts_last, ray_devices, follow=(taps_next,))
    sums_last = all_to_all(copies_last, "ray").reshape(planes)
    y_edges = exchange(*hold((y_first, y_last), (copies_last,)))
    copies, packed = hold((copies, packed), (sums_last,) + y_edges)
    sums = all_to_all(copies, "ray").reshape(planes)
    packed = lax.psum_scatter(packed, "ray", scatter_dimension=0, tiled=True)

    cot = volume_cotangent.reshape(planes)
    wide_taps = (27 * chosen, voxels)
    spots = jnp.stack([tile > 0, tile < tiles - 1, tile]).astype(jnp.int32)
    sent = norm_back(
        cot, sums_last, y_next, total_next, norm_gain, norm_shift, 1, count,
        follow=y_edges + (copies,),
    )
    dy, back_last, part = weight_grad(
        spots, taps_next.reshape(wide_taps), (cot, sums_last), y_next, y_edges, sent[2],
        share_back(sent), total_next, norm_gain, norm_shift, 1, count, False,
    )
    (held,) = hold((part,), (sums,))
    parts = all_to_all(held, "tile")
    grad, *sent = conv_back(
        dy, (cot, sums_last, sums), weights, 1, width,
        (y_ext, total, norm_gain, norm_shift, count), follow=(held,),
    )
    others = share_back(sent)
    shard = add_parts(parts, 1, follow=(sent[2],))[0]
    dy, back, *shares = weight_grad(
        spots, taps_first.reshape(wide_taps), (grad,), y_ext, (), sent[2], others, total,
        norm_gain, norm_shift, 0, count, True, follow=(shard,),
    )
    moved = [
        lax.ppermute(value, "tile", [(i, (i + by) % tiles) for i in range(tiles)])
        for by, value in enumerate(shares)
        if by
    ]
    shard = spread_tile(shard, spots, (shares[0],)).reshape(27 * chosen, channels)
    slices = spread_tile(add_arrays([shares[0]] + moved, (shard,)), spots, ())
    slices = slices.reshape(27 * chosen, channels)
    packed = all_to_all(add_parts(packed[None], tiles, follow=(slices,)), "tile")
    conv_grad = place(gather_ray(shard), 1, layers, blocks, (), follow=(slices,))
    packed = add_parts(packed, ray_devices, follow=(conv_grad,))
    (grad,) = conv_back(dy, (grad,), weights, 0, width, follow=(packed,))
    packed = all_to_all(packed.astype(BF), "ray").astype(F32)
    packed = packed.reshape(layers, PACK, channels)[::-1]
    at = channels + 16
    heads = packed[:, at : at + DROWS]
    head_bias = packed[:, at + DROWS, :DROWS]
    pictures = jnp.swapaxes(jnp.stack([picture, picture_last])[:, : classes + 1], 1, 2)
    norms = (jnp.stack([back, back_last])[:, 1], jnp.stack([back, back_last])[:, 0])
    rest = (
        packed[:, :channels],
        packed[:, channels],
        heads[:, classes],
        head_bias[:, classes],
        jnp.swapaxes(heads[:, :classes], 1, 2),
        head_bias[:, :classes],
    )
    conv_grad = place(
        gather_ray(slices), 0, layers, blocks, (conv_grad,), follow=(grad, pictures) + norms + rest
    )
    return (
        pictures,
        r_last.reshape(volume.shape),
        grad.reshape(volume.shape),
        conv_grad,
    ) + norms + rest


def solution(mesh):
    in_specs = (
        P("tile", None, None, None),
        P(("ray", "tile"), None),
        P(None, ("ray", "tile"), None),
        P(("ray", "tile"), None),
        P(("ray", "tile"), None),
        P(),
        P(),
        P(),
        P(),
        P(),
        P(),
        P(),
        P(),
        P(),
        P(None, ("ray", "tile"), None),
        P("tile", None, None, None),
    )
    out_specs = (
        P(None, ("ray", "tile"), None),
        P("tile", None, None, None),
        P("tile", None, None, None),
        P(),
        P(),
        P(),
        P(),
        P(),
        P(),
        P(),
        P(),
        P(),
    )
    return jax.shard_map(
        per_device, mesh=mesh, in_specs=in_specs, out_specs=out_specs, check_vma=False
    )
```

```python
import functools

import jax
import jax.numpy as jnp
from jax import lax
from jax.experimental import pallas as pl
from jax.experimental.pallas import tpu as pltpu
from jax.sharding import PartitionSpec as P

CAP = 768
WINDOW = 256
LANES = 128
PROWS = 24
DROWS = 32
COORDS = 8
BLOCKS = 8
PACK = 320
epsilon = 1e-05
MIB = 1024 * 1024

BF = jnp.bfloat16
F32 = jnp.float32
VMEM = pltpu.VMEM
SMEM = pltpu.SMEM


def nn(left, right):
    return jnp.dot(left, right, preferred_element_type=F32)


def nt(left, right):
    return lax.dot_general(left, right, (((1,), (1,)), ((), ())), preferred_element_type=F32)


def iota(shape, dim):
    return lax.broadcasted_iota(jnp.int32, shape, dim)


def whole(shape):
    return pl.BlockSpec(shape, lambda *_: (0,) * len(shape))


def planes_of(step, shape, first=0):
    return pl.BlockSpec((step,) + shape[1:], lambda i: (i + first // step,) + (0,) * (len(shape) - 1))


def sspec():
    return pl.BlockSpec(memory_space=SMEM)


def aspec():
    return pl.BlockSpec(memory_space=pl.ANY)


def hspec():
    return pl.BlockSpec(memory_space=pltpu.HBM)


def ordered(kernel, operands, in_specs, follow, **options):
    count, skip = len(operands), len(follow)

    def body(*refs):
        kernel(*refs[:count], *refs[count + skip :])

    return pl.pallas_call(body, in_specs=list(in_specs) + [aspec()] * skip, **options)(
        *operands, *follow
    )


def params(mib):
    return pltpu.CompilerParams(vmem_limit_bytes=int(mib * MIB))


def cost():
    return pl.CostEstimate(flops=1, bytes_accessed=1, transcendentals=0)


def lane_cumsum(x):
    lane = iota(x.shape, 1)
    shift = 1
    while shift < x.shape[1]:
        x = x + jnp.where(lane >= shift, pltpu.roll(x, shift, 1), 0.0)
        shift *= 2
    return x


def window_onehots(starts, owner_row, rank_row, ray, rays, tiles):
    rows = iota((WINDOW, rank_row.shape[1]), 0)
    hots, bases = [], []
    for t in range(tiles):
        start = starts[t * rays + ray]
        base = (start // LANES) * LANES
        place = jnp.where(owner_row == t, rank_row + (start - base), -1)
        hots.append((rows == place).astype(F32).astype(BF))
        bases.append(pl.multiple_of(base, LANES))
    return jnp.concatenate(hots, axis=0), bases


def prep_kernel(extent, starts, cells_ref, fracs_ref, out_ref, owner_ref, rank_ref, vals, acc):
    depth, height, width = extent
    tiles = out_ref.shape[0]
    rays, samples = cells_ref.shape
    cells = cells_ref[...]
    voxels = depth * height * width
    owner = lax.div(cells, voxels)
    local = cells - owner * voxels
    base_x = lax.div(local, height * width)
    inner = local - base_x * (height * width)
    base_y = lax.div(inner, width)
    base_z = inner - base_y * width
    rank = jnp.zeros(cells.shape, F32)
    for t in range(tiles):
        mine = owner == t
        rank = jnp.where(mine, lane_cumsum(jnp.where(mine, 1.0, 0.0)) - 1.0, rank)
    owner_ref[...] = owner
    rank_ref[...] = rank.astype(jnp.int32)
    vals[...] = jnp.zeros_like(vals)
    rows = [(base_x + 1).astype(F32), base_y.astype(F32), base_z.astype(F32)]
    low = []
    for d in range(3):
        frac = fracs_ref[d]
        high = frac.astype(BF).astype(F32)
        rows.append(high)
        low.append(frac - high)
    rows += low
    for number, row in enumerate(rows):
        for k in range(rays):
            vals[number : number + 1, k * samples : (k + 1) * samples] = row[k : k + 1]
    acc[...] = jnp.zeros_like(acc)
    for k in range(rays):
        hot, bases = window_onehots(
            starts, owner_ref[k : k + 1, :], rank_ref[k : k + 1, :], k, rays, tiles
        )
        moved = nt(vals[:, k * samples : (k + 1) * samples].astype(BF), hot)
        for t in range(tiles):
            acc[t, :, pl.ds(bases[t], WINDOW)] += moved[:, t * WINDOW : (t + 1) * WINDOW]
    out_ref[...] = jnp.zeros_like(out_ref)
    wide = out_ref.shape[2]
    lines = CAP // wide
    for n in range(lines):
        part = slice(n * wide, (n + 1) * wide)
        for r in range(6):
            value = acc[:, r : r + 1, part]
            if r >= 3:
                value = value + acc[:, r + 3 : r + 4, part]
            out_ref[:, r * lines + n : r * lines + n + 1, :] = value


def prepare(extent, starts, cells, fracs, tiles, wide, follow=()):
    rays, samples = cells.shape
    outs = ((tiles, COORDS * CAP // wide, wide), (rays, samples), (rays, samples))
    return ordered(
        functools.partial(prep_kernel, extent),
        (starts, cells, fracs,),
        [sspec(), whole(cells.shape), whole(fracs.shape)],
        follow,
        grid=(1,),
        out_shape=(
            jax.ShapeDtypeStruct(outs[0], F32),
            jax.ShapeDtypeStruct(outs[1], jnp.int32),
            jax.ShapeDtypeStruct(outs[2], jnp.int32),
        ),
        out_specs=tuple(whole(s) for s in outs),
        scratch_shapes=[VMEM((16, rays * samples), F32), VMEM((tiles, 16, CAP + WINDOW), F32)],
        compiler_params=params(62.5),
        cost_estimate=cost(),
        name="prep",
    )


def started(source, target, sem):
    copy = pltpu.make_async_copy(source, target, sem)
    copy.start()
    return copy


def put_plane(xs, p, value, width):
    rows, channels = value.shape
    along = lax.rem(iota(value.shape, 0), width)
    left = jnp.where(along == 0, 0.0, pltpu.roll(value, 1, 0))
    right = jnp.where(along == width - 1, 0.0, pltpu.roll(value, rows - 1, 0))
    xs[p, width : width + rows, 0:channels] = left.astype(BF)
    xs[p, width : width + rows, channels : 2 * channels] = value.astype(BF)
    xs[p, width : width + rows, 2 * channels : 3 * channels] = right.astype(BF)


def clear_edges(xs, width, rows):
    planes, _, wide = xs.shape
    for p in range(planes):
        xs[p, 0:width, :] = jnp.zeros((width, wide), BF)
        xs[p, width + rows : 2 * width + rows, :] = jnp.zeros((width, wide), BF)


def taps(xs, p, width, rows):
    return jnp.concatenate(
        [xs[p + a, b * width : b * width + rows, :] for a in range(3) for b in range(3)], axis=1
    )


def tap_group(xs, first, count, width, rows):
    return jnp.concatenate([taps(xs, first + n, width, rows) for n in range(count)], axis=0)


def add_stats(sums, one, two):
    sums[0:1, :] += jnp.sum(one, axis=0, keepdims=True)
    sums[1:2, :] += jnp.sum(two, axis=0, keepdims=True)


def conv_scratch(planes, rows, width, channels, turned):
    shape = (channels, 27 * channels) if turned else (27 * channels, channels)
    return [VMEM((planes, rows + 2 * width, 3 * channels), BF), VMEM(shape, BF)]


def sems(*counts):
    return [pltpu.SemaphoreType.DMA((n,)) for n in counts]


def any_outs(*shapes):
    return tuple(jax.ShapeDtypeStruct(shape, dtype) for shape, dtype in shapes)


def conv_first_kernel(
    width, layer, before, own, after, coords, w_hbm, y_ref, v_ref, mix_ref,
    raw, xs, weight, y_buf, mix, in_sem, out_sem,
):
    planes, rows, channels = own.shape
    pairs = planes // 2 + 1
    body = [
        started(own.at[pl.ds(2 * i, 2)], raw.at[pl.ds(2 * i + 2, 2)], in_sem.at[i])
        for i in range(planes // 2)
    ]
    ends = [
        started(before, raw.at[pl.ds(0, 2)], in_sem.at[pairs]),
        started(after, raw.at[pl.ds(planes + 2, 2)], in_sem.at[pairs + 1]),
    ]
    heavy = started(w_hbm.at[layer], weight, in_sem.at[pairs + 2])
    light = started(coords, mix.at[:, pl.ds(8, coords.shape[1]), :], in_sem.at[pairs + 3])
    clear_edges(xs, width, rows)
    mix[:, 0:8, :] = jnp.zeros((mix.shape[0], 8, channels), F32)
    for copy in body + ends:
        copy.wait()

    @pl.loop(0, planes + 4)
    def _(p):
        put_plane(xs, p, raw[p].astype(F32), width)

    done = [started(raw.at[pl.ds(1, planes + 2)], v_ref, out_sem.at[pairs])]
    light.wait()
    heavy.wait()

    group = (planes + 2) // 2

    def out_copy(i):
        some = pl.ds(group * i, group)
        return pltpu.make_async_copy(y_buf.at[some], y_ref.at[some], out_sem.at[i])

    @pl.loop(0, 2)
    def _(i):
        p = group * i
        part = nn(tap_group(xs, p, group, width, rows), weight[...])
        for n in range(group):
            y_buf[p + n] = part[n * rows : (n + 1) * rows]
        out_copy(i).start()
        inner = part[rows : (group - 1) * rows]
        add_stats(mix.at[0], inner, inner * inner)
        edge = jnp.where(i == 0, part[(group - 1) * rows :], part[:rows])
        add_stats(mix.at[0], edge, edge * edge)

    for t in range(1, mix.shape[0]):
        mix[t, 0:8, :] = mix[0, 0:8, :]
    done.append(started(mix, mix_ref, out_sem.at[pairs + 1]))
    for copy in done:
        copy.wait()
    for i in range(2):
        out_copy(i).wait()


def conv_first(before, own, after, coords, weights, layer, width):
    planes, rows, channels = own.shape
    ext = (planes + 2, rows, channels)
    tiles, lines, _ = coords.shape
    pairs = planes // 2 + 1
    return ordered(
        functools.partial(conv_first_kernel, width, layer),
        (before, own, after, coords, weights),
        [aspec()] * 5,
        (),
        out_shape=any_outs((ext, F32), (ext, BF), ((tiles, 8 + lines, channels), F32)),
        out_specs=(aspec(),) * 3,
        scratch_shapes=[VMEM((planes + 4, rows, channels), BF)]
        + conv_scratch(planes + 4, rows, width, channels, False)
        + [VMEM(ext, F32), VMEM((tiles, 8 + lines, channels), F32)]
        + sems(pairs + 4, pairs + 2),
        compiler_params=params(62.5),
        cost_estimate=cost(),
        name="conv_first",
    )


def moments(total, count):
    both = jnp.sum(total, axis=0)
    mean = both[0:1, :] / count
    return mean, lax.rsqrt(both[1:2, :] / count - mean * mean + epsilon)


def row_of(ref, layer):
    return ref[layer : layer + 1, :]


def silu(value):
    return value * (1.0 / (1.0 + jnp.exp(-value)))


def conv_next_kernel(
    width, layer, count, flags, y_ext, v_ext, total_hbm, gain_hbm, shift_hbm, w_hbm,
    v_ref, r_ref, y_ref, stat_ref, first_ref, last_ref,
    y_in, v_in, total, gain, shift, xs, weight, v_buf, r_buf, y_buf, edges, stat, in_sem, out_sem,
):
    ext_planes, rows, channels = y_ext.shape
    pairs = ext_planes // 2
    small = [
        started(total_hbm.at[:, pl.ds(0, 8), :], total, in_sem.at[2 * pairs]),
        started(gain_hbm, gain, in_sem.at[2 * pairs + 1]),
        started(shift_hbm, shift, in_sem.at[2 * pairs + 2]),
    ]
    def in_copies(i):
        two = pl.ds(2 * i, 2)
        return (
            pltpu.make_async_copy(y_ext.at[two], y_in.at[two], in_sem.at[2 * i]),
            pltpu.make_async_copy(v_ext.at[two], v_in.at[two], in_sem.at[2 * i + 1]),
        )

    def mid_copies(i):
        two = pl.ds(2 * i, 2)
        return (
            pltpu.make_async_copy(v_buf.at[two], v_ref.at[two], out_sem.at[3 * i]),
            pltpu.make_async_copy(r_buf.at[two], r_ref.at[two], out_sem.at[3 * i + 1]),
        )

    def out_copy(i):
        two = pl.ds(2 * i - 2, 2)
        return pltpu.make_async_copy(y_buf.at[two], y_ref.at[two], out_sem.at[3 * i + 2])

    for i in range(pairs):
        for copy in in_copies(i):
            copy.start()
    heavy = started(w_hbm.at[layer + 1], weight, in_sem.at[2 * pairs + 3])
    clear_edges(xs, width, rows)
    stat[...] = jnp.zeros_like(stat)
    for copy in small:
        copy.wait()
    mean, inverse = moments(total[...], count)
    gains, shifts = row_of(gain, layer), row_of(shift, layer)

    @pl.loop(0, pairs)
    def _(i):
        for copy in in_copies(i):
            copy.wait()
        for side in range(2):
            p = 2 * i + side
            fresh = v_in[p].astype(F32) + silu((y_in[p] - mean) * inverse * gains + shifts)
            v_buf[p] = fresh
            outside = (p == side * (ext_planes - 1)) & (flags[side] == 0)
            rounded = jnp.where(outside, 0.0, fresh).astype(BF)
            r_buf[p] = rounded
            put_plane(xs, p, rounded.astype(F32), width)
        for copy in mid_copies(i):
            copy.start()

        @pl.when(i == 1)
        def _():
            heavy.wait()

        @pl.when(i > 0)
        def _():
            p = 2 * i - 2
            part = nn(tap_group(xs, p, 2, width, rows), weight[...])
            y_buf[p] = part[:rows]
            y_buf[p + 1] = part[rows:]
            add_stats(stat.at[0], part, part * part)
            out_copy(i).start()

    edges[0] = y_buf[0].astype(BF)
    edges[1] = y_buf[ext_planes - 3].astype(BF)
    for t in range(1, stat.shape[0]):
        stat[t] = stat[0]
    done = [
        started(stat, stat_ref, out_sem.at[2]),
        started(edges.at[pl.ds(0, 1)], first_ref, out_sem.at[3 * pairs]),
        started(edges.at[pl.ds(1, 1)], last_ref, out_sem.at[3 * pairs + 1]),
    ]
    for i in range(pairs):
        done += list(mid_copies(i)) + ([out_copy(i)] if i else [])
    for copy in done:
        copy.wait()


def conv_next(flags, y_ext, v_ext, total, gain, shift, weights, layer, width, count, follow=()):
    ext_planes, rows, channels = y_ext.shape
    ext = y_ext.shape
    inner = (ext_planes - 2, rows, channels)
    stat = (total.shape[0], 8, channels)
    pairs = ext_planes // 2
    edge = (1, rows, channels)
    return ordered(
        functools.partial(conv_next_kernel, width, layer, count),
        (flags, y_ext, v_ext, total, gain, shift, weights),
        [sspec()] + [aspec()] * 6,
        follow,
        out_shape=any_outs((ext, F32), (ext, BF), (inner, F32), (stat, F32), (edge, BF), (edge, BF)),
        out_specs=(aspec(),) * 6,
        scratch_shapes=[VMEM(ext, F32), VMEM(ext, BF), VMEM(stat, F32)]
        + [VMEM(gain.shape, F32)] * 2
        + conv_scratch(ext_planes, rows, width, channels, False)
        + [VMEM(ext, F32), VMEM(ext, BF), VMEM(inner, F32)]
        + [VMEM((2, rows, channels), BF), VMEM(stat, F32)]
        + sems(2 * pairs + 4, 3 * pairs + 2),
        compiler_params=params(62.5),
        cost_estimate=cost(),
        name="conv_next",
    )


def fill_weights(table, coords, extent):
    depth, height, width = extent
    samples = coords[0].shape[1]

    def along(base, frac, size):
        grid = iota((size, samples), 0).astype(F32)
        lower = jnp.where(grid == base, 1.0 - frac, 0.0)
        return lower + jnp.where(grid == base + 1.0, frac, 0.0)

    on_x = along(coords[0] - 1.0, coords[3], depth)
    on_y = along(coords[1], coords[4], height)
    on_z = along(coords[2], coords[5], width)
    for x in range(depth):
        on_xy = on_x[x : x + 1] * on_y
        for y in range(height):
            row = (x * height + y) * width
            table[row : row + width, :] = (on_xy[y : y + 1] * on_z).astype(BF)


def diagonal(rows, columns):
    return iota((rows, columns), 0) == iota((rows, columns), 1)


def identity(rows, columns):
    return diagonal(rows, columns).astype(F32).astype(BF)


def head_rows(semantic, density, rows):
    channels, classes = semantic.shape
    turned = nt(identity(rows, classes), semantic)
    return jnp.where(iota((rows, channels), 0) == classes, density.astype(F32), turned).astype(BF)


def column(row, rows):
    return jnp.sum(jnp.where(diagonal(rows, row.shape[1]), row, 0.0), axis=1, keepdims=True)


def coord_rows(block, slots):
    lines = slots // block.shape[1]
    return [
        jnp.concatenate(
            [block[8 + r * lines + n : 9 + r * lines + n, :] for n in range(lines)], axis=1
        )
        for r in range(6)
    ]


def sample_kernel(
    extent, layer, first, count, coords, *refs
):
    if count is None:
        r_hbm, refs = refs[0], refs[1:]
    else:
        y_hbm, v_hbm, total_hbm, gain, shift, refs = refs[0], refs[1], refs[2], refs[3], refs[4], refs[5:]
    hidden, hidden_b, semantic, density, semantic_b, density_b, refs = *refs[:6], refs[6:]
    p_ref, f_ref, g_ref, s_ref, refs = *refs[:4], refs[4:]
    if count is not None:
        r_out, refs = refs[0], refs[1:]
    turned, table, rounded, hidden_t, bias, head_t, head_b, sem, refs = *refs[:8], refs[8:]
    channels = turned.shape[0]
    depth = extent[0]
    classes = semantic.shape[2]
    slots = table.shape[1]
    rows = rounded.shape[1]
    step = pl.program_id(0)

    if count is not None:
        y_in, v_in, total, load_sem = refs

    def in_copies(p):
        return (
            pltpu.make_async_copy(y_hbm.at[p], y_in.at[p], load_sem.at[2 * p]),
            pltpu.make_async_copy(v_hbm.at[p + 1], v_in.at[p], load_sem.at[2 * p + 1]),
        )

    def out_copy(p):
        return pltpu.make_async_copy(rounded.at[p], r_out.at[p], sem.at[p])

    @pl.when(step == 0)
    def _():
        if count is None:
            copy = started(r_hbm.at[pl.ds(first, depth)], rounded, sem.at[0])
        else:
            light = started(total_hbm, total, load_sem.at[2 * depth])
            for p in range(depth):
                for copy in in_copies(p):
                    copy.start()
        same = identity(channels, channels)
        hidden_t[...] = nt(same, hidden[layer]).astype(BF)
        bias[...] = column(hidden_b[layer : layer + 1, :], channels)
        head_t[...] = head_rows(semantic[layer], density[layer : layer + 1, :], PROWS)
        last = jnp.sum(
            jnp.where(iota((1, density_b.shape[1]), 1) == layer, density_b[...], 0.0),
            axis=1,
            keepdims=True,
        )
        place = iota((PROWS, 1), 0) == classes
        head_b[...] = jnp.where(place, last, column(semantic_b[layer : layer + 1, :], PROWS))
        if count is None:
            copy.wait()
        else:
            light.wait()
            mean, inverse = moments(total[...], count)
            gains, shifts = row_of(gain, layer), row_of(shift, layer)

        @pl.loop(0, depth)
        def _(p):
            if count is not None:
                for copy in in_copies(p):
                    copy.wait()
                fresh = v_in[p] + silu((y_in[p] - mean) * inverse * gains + shifts)
                rounded[p] = fresh.astype(BF)
                out_copy(p).start()
            turned[:, pl.ds(pl.multiple_of(p * rows, rows), rows)] = nt(same, rounded[p]).astype(BF)

    fill_weights(table, coord_rows(coords[0], slots), extent)
    feature = nn(turned[...], table[...]).astype(BF)
    f_ref[0] = feature
    inner = nn(hidden_t[...], feature) + bias[...]
    small = jnp.exp(-jnp.abs(inner))
    act = (jnp.maximum(inner, 0.0) + jnp.log1p(small)).astype(BF)
    g_ref[0] = act
    s_ref[0] = jnp.where(inner >= 0.0, 1.0, small) / (1.0 + small)
    p_ref[0] = nn(head_t[...], act) + head_b[...]
    if count is not None:

        @pl.when(step == pl.num_programs(0) - 1)
        def _():
            for p in range(depth):
                out_copy(p).wait()


def per_tile(rows, lanes):
    return pl.BlockSpec((1, rows, lanes), lambda t: (t, 0, 0))


def sample(extent, received, source, layer, mlp, count=None, follow=()):
    tiles, lines, wide = received.shape
    slots = CAP
    rows, channels = extent[1] * extent[2], mlp[0].shape[1]
    depth = extent[0]
    voxels = depth * rows
    outs = [((tiles, PROWS, slots), F32)] + [((tiles, channels, slots), d) for d in (BF, BF, F32)]
    out_specs = [per_tile(n, slots) for n in (PROWS, channels, channels, channels)]
    scratch = [
        VMEM((channels, voxels), BF),
        VMEM((voxels, slots), BF),
        VMEM((depth, rows, channels), BF),
        VMEM((channels, channels), BF),
        VMEM((channels, 1), F32),
        VMEM((PROWS, channels), BF),
        VMEM((PROWS, 1), F32),
    ] + sems(depth)
    if count is None:
        first, given, specs = source[1], source[:1], [aspec()]
    else:
        first, given = 0, source
        specs = [aspec()] * 3 + [whole(x.shape) for x in source[3:]]
        outs.append(((depth, rows, channels), BF))
        out_specs.append(aspec())
        scratch += [VMEM((depth, rows, channels), F32)] * 2 + [VMEM(source[2].shape, F32)]
        scratch += sems(2 * depth + 1)
    return ordered(
        functools.partial(sample_kernel, extent, layer, first, count),
        (received,) + tuple(given) + mlp,
        [per_tile(lines, wide)] + specs + [whole(x.shape) for x in mlp],
        follow,
        grid=(tiles,),
        out_shape=any_outs(*outs),
        out_specs=tuple(out_specs),
        scratch_shapes=scratch,
        compiler_params=params(62.5),
        cost_estimate=cost(),
        name="sample",
    )


def sample_back_kernel(
    extent, layer, coords, dp_ref, f_ref, g_ref, s_ref, hidden, semantic, density, *refs
):
    du_ref, pack_ref, total, table, head = refs[-5:]
    step = pl.program_id(0)
    channels = hidden.shape[1]
    slots = table.shape[1]

    @pl.when(step == 0)
    def _():
        total[...] = jnp.zeros_like(total)
        pack_ref[0:PACK, :] = jnp.zeros((PACK, channels), F32)
        if len(refs) > 5:
            pack_ref[PACK : 2 * PACK, :] = refs[0][...]
        rows = head_rows(semantic[layer], density[layer : layer + 1, :], DROWS)
        head[...] = nt(identity(channels, channels), rows).astype(BF)

    fill_weights(table, coord_rows(coords[0], slots), extent)
    grad_heads = dp_ref[0]
    grad_inner = (nn(head[...], grad_heads) * s_ref[0]).astype(BF)
    ones = jnp.ones((16, slots), BF)
    pack_ref[0:channels, :] += nt(f_ref[0], grad_inner)
    pack_ref[channels : channels + 16, :] += nt(ones, grad_inner)
    at = channels + 16
    pack_ref[at : at + DROWS, :] += nt(grad_heads, g_ref[0])
    at += DROWS
    pack_ref[at : at + 16, 0:DROWS] += nt(ones, grad_heads)
    grad_features = nn(hidden[layer], grad_inner).astype(BF)
    total[...] += nt(table[...], grad_features)

    @pl.when(step == pl.num_programs(0) - 1)
    def _():
        du_ref[...] = total[...].astype(BF)


def sample_back(extent, layer, received, grad_heads, feature, act, slope, mlp, packs, follow=()):
    tiles, lines, wide = received.shape
    _, channels, slots = feature.shape
    voxels = extent[0] * extent[1] * extent[2]
    hidden, _, semantic, density = mlp[:4]
    outs = ((voxels, channels), (PACK * (1 + len(packs)), channels))
    return ordered(
        functools.partial(sample_back_kernel, extent, layer),
        (received, grad_heads, feature, act, slope, hidden, semantic, density) + packs,
        [per_tile(lines, wide)]
        + [per_tile(n, slots) for n in (DROWS, channels, channels, channels)]
        + [whole(x.shape) for x in (hidden, semantic, density) + packs],
        follow,
        grid=(tiles,),
        out_shape=any_outs((outs[0], BF), (outs[1], F32)),
        out_specs=tuple(whole(shape) for shape in outs),
        scratch_shapes=[
            VMEM((voxels, channels), F32),
            VMEM((voxels, slots), BF),
            VMEM((channels, DROWS), BF),
        ],
        compiler_params=params(62.5),
        cost_estimate=cost(),
        name="sample_back",
    )


def composite_kernel(
    classes, layer, starts, pixels, owner_ref, rank_ref, view, heads, cot,
    pic_ref, dp_ref, split, by_ray, grads, density, weights, grad_w, acc,
):
    tiles = heads.shape[0]
    rays, samples = owner_ref.shape
    step = 4.0 / samples
    split[...] = jnp.zeros_like(split)
    for t in range(tiles):
        value = heads[t]
        high = value.astype(BF)
        split[t, 0:PROWS, 0:CAP] = high.astype(F32)
        split[t, PROWS : 2 * PROWS, 0:CAP] = value - high.astype(F32)

    def hots(k):
        return window_onehots(
            starts, owner_ref[k : k + 1, :], rank_ref[k : k + 1, :], k, rays, tiles
        )

    for k in range(rays):
        hot, bases = hots(k)
        windows = jnp.concatenate(
            [split[t, :, pl.ds(bases[t], WINDOW)].astype(BF) for t in range(tiles)], axis=1
        )
        both = nn(windows, hot)
        one = both[:PROWS] + both[PROWS:]
        by_ray[k] = one
        density[k : k + 1, :] = one[classes : classes + 1]

    pre = density[...]
    visible = view[...].astype(F32)
    small = jnp.exp(-jnp.abs(pre))
    optical = visible * (jnp.maximum(pre, 0.0) + jnp.log1p(small)) * step
    passing = jnp.exp(-(lane_cumsum(optical) - optical))
    fading = jnp.exp(-optical)
    weight = passing * (1.0 - fading)
    weights[...] = weight
    row = iota((PROWS, samples), 0)
    lane = iota((PROWS, rays), 1)
    cotangent = nt(identity(PROWS, classes + 1), cot[layer])
    picture = jnp.zeros((PROWS, rays), F32)
    for k in range(rays):
        there = lane == pixels[k]
        dpic = jnp.sum(jnp.where(there, cotangent, 0.0), axis=1, keepdims=True)
        value = jnp.where(row < classes, by_ray[k], jnp.where(row == classes, 1.0, 0.0))
        one = weights[k : k + 1, :]
        colour = jnp.sum(value * one, axis=1, keepdims=True)
        picture = jnp.where(there, colour, picture)
        grad_w[k : k + 1, :] = jnp.sum(value * dpic, axis=0, keepdims=True)
        grads[k] = dpic * one
    pic_ref[...] = picture
    grad_weight = grad_w[...]
    carried = grad_weight * weight
    later = jnp.sum(carried, axis=1, keepdims=True) - lane_cumsum(carried)
    grad_optical = grad_weight * passing * fading - later
    slope = jnp.where(pre >= 0.0, 1.0, small) / (1.0 + small)
    density[...] = grad_optical * visible * step * slope
    acc[...] = jnp.zeros_like(acc)
    zero = jnp.zeros((DROWS - PROWS, samples), F32)
    for k in range(rays):
        hot, bases = hots(k)
        grad = jnp.where(row == classes, density[k : k + 1, :], grads[k])
        moved = nt(jnp.concatenate([grad, zero], axis=0).astype(BF), hot)
        for t in range(tiles):
            acc[t, :, pl.ds(bases[t], WINDOW)] += moved[:, t * WINDOW : (t + 1) * WINDOW]
    for t in range(tiles):
        dp_ref[t] = acc[t, :, 0:CAP].astype(BF)


def composite(starts, pixels, owner, rank, view, heads, cot, layer, classes, follow=()):
    tiles, _, slots = heads.shape
    rays, samples = owner.shape
    outs = ((PROWS, rays), (tiles, DROWS, slots))
    return ordered(
        functools.partial(composite_kernel, classes, layer),
        (starts, pixels, owner, rank, view, heads, cot,),
        [sspec(), sspec()] + [whole(x.shape) for x in (owner, rank, view, heads, cot)],
        follow,
        grid=(1,),
        out_shape=(jax.ShapeDtypeStruct(outs[0], F32), jax.ShapeDtypeStruct(outs[1], BF)),
        out_specs=tuple(whole(s) for s in outs),
        scratch_shapes=[
            VMEM((tiles, 2 * PROWS, CAP + WINDOW), F32),
            VMEM((rays, PROWS, samples), F32),
            VMEM((rays, PROWS, samples), F32),
            VMEM((rays, samples), F32),
            VMEM((rays, samples), F32),
            VMEM((rays, samples), F32),
            VMEM((tiles, DROWS, CAP + WINDOW), F32),
        ],
        compiler_params=params(62.5),
        cost_estimate=cost(),
        name="composite",
    )


def add_kernel(parts, out_ref):
    total = parts[0].astype(F32)
    for n in range(1, parts.shape[0]):
        total = total + parts[n].astype(F32)
    total = total.astype(out_ref.dtype)
    for n in range(out_ref.shape[0]):
        out_ref[n] = total


def add_parts(parts, copies, follow=()):
    shape = (copies,) + parts.shape[1:]
    return ordered(
        add_kernel,
        (parts,),
        [whole(parts.shape)],
        follow,
        grid=(1,),
        out_shape=jax.ShapeDtypeStruct(shape, parts.dtype),
        out_specs=whole(shape),
        compiler_params=params(62.5),
        cost_estimate=cost(),
        name="add_parts",
    )


def add_arrays_kernel(*refs):
    total = refs[0][...].astype(F32)
    for ref in refs[1:-1]:
        total = total + ref[...].astype(F32)
    refs[-1][...] = total.astype(refs[-1].dtype)


def add_arrays(values, follow=()):
    return ordered(
        add_arrays_kernel,
        tuple(values),
        [whole(x.shape) for x in values],
        follow,
        grid=(1,),
        out_shape=jax.ShapeDtypeStruct(values[0].shape, values[0].dtype),
        out_specs=whole(values[0].shape),
        compiler_params=params(8),
        cost_estimate=cost(),
        name="add_arrays",
    )


def hold_kernel(*refs):
    del refs


def hold(values, follow):
    return ordered(
        hold_kernel,
        values,
        [aspec()] * len(values),
        follow,
        out_shape=any_outs(*((x.shape, x.dtype) for x in values)),
        out_specs=(aspec(),) * len(values),
        input_output_aliases={n: n for n in range(len(values))},
        compiler_params=params(62.5),
        cost_estimate=cost(),
        name="hold",
    )


def all_to_all(value, axis):
    return lax.all_to_all(value, axis, split_axis=0, concat_axis=0, tiled=True)


def exchange(first, last):
    devices = lax.axis_size("tile")
    up = [(i, i + 1) for i in range(devices - 1)]
    down = [(i + 1, i) for i in range(devices - 1)]
    return lax.ppermute(last, "tile", up), lax.ppermute(first, "tile", down)


def norm_grads(y, grad, mean, inverse, gains, shifts):
    centred = (y - mean) * inverse
    normal = centred * gains + shifts
    sigma = 1.0 / (1.0 + jnp.exp(-normal))
    return grad * sigma * (1.0 + normal * (1.0 - sigma)), centred


def finish_back(sums, edges, ups, spare, out_sem):
    rows = edges.shape[1] - 16
    value = sums[...]
    high = value.astype(BF).astype(F32)
    middle = (value - high).astype(BF).astype(F32)
    low = value - high - middle
    tail = jnp.concatenate([high[0:2], middle[0:2], low[0:2], jnp.zeros((10,) + high.shape[1:], F32)], axis=0)
    tail = tail.astype(BF)
    edges[0, rows:, :] = tail
    edges[1, rows:, :] = tail
    spare[...] = tail
    first_ref, last_ref, far_ref = ups
    copies = [
        started(edges.at[0], first_ref, out_sem.at[0]),
        started(edges.at[1], last_ref, out_sem.at[1]),
        started(spare, far_ref, out_sem.at[2]),
    ]
    for copy in copies:
        copy.wait()


def norm_back_kernel(
    layer, count, cot, local, y, total_hbm, gain_hbm, shift_hbm, first_ref, last_ref, far_ref,
    cot_in, local_in, y_in, total, gain, shift, edges, sums, spare, in_sem, out_sem,
):
    planes, rows, _ = cot.shape
    small = [
        started(total_hbm, total, in_sem.at[3 * planes]),
        started(gain_hbm, gain, in_sem.at[3 * planes + 1]),
        started(shift_hbm, shift, in_sem.at[3 * planes + 2]),
    ]

    def in_copies(p):
        return [
            pltpu.make_async_copy(source.at[p], target.at[p], in_sem.at[3 * p + n])
            for n, (source, target) in enumerate(((cot, cot_in), (local, local_in), (y, y_in)))
        ]

    for p in range(planes):
        for copy in in_copies(p):
            copy.start()
    sums[...] = jnp.zeros_like(sums)
    for copy in small:
        copy.wait()
    mean, inverse = moments(total[...], count)
    gains, shifts = row_of(gain, layer), row_of(shift, layer)

    @pl.loop(0, planes)
    def _(p):
        for copy in in_copies(p):
            copy.wait()
        grad = cot_in[p].astype(F32) + local_in[p].astype(F32)
        inner, centred = norm_grads(y_in[p], grad, mean, inverse, gains, shifts)
        add_stats(sums, inner, inner * centred)
        for side, edge in ((0, 0), (1, planes - 1)):

            @pl.when(p == edge)
            def _():
                edges[side, 0:rows, :] = inner.astype(BF)

    finish_back(sums, edges, (first_ref, last_ref, far_ref), spare, out_sem)


def back_shapes(rows, channels):
    return ((rows + 16, channels), BF), ((rows + 16, channels), BF), ((16, channels), BF)


def back_scratch(rows, channels):
    return [VMEM((2, rows + 16, channels), BF), VMEM((8, channels), F32), VMEM((16, channels), BF)]


def norm_back(cot, local, y, total, gain, shift, layer, count, follow=()):
    planes, rows, channels = local.shape
    return ordered(
        functools.partial(norm_back_kernel, layer, count),
        (cot, local, y, total, gain, shift),
        [aspec()] * 6,
        follow,
        out_shape=any_outs(*back_shapes(rows, channels)),
        out_specs=(aspec(),) * 3,
        scratch_shapes=[VMEM(x.shape, x.dtype) for x in (cot, local, y, total, gain, shift)]
        + back_scratch(rows, channels)
        + sems(3 * planes + 3, 3),
        compiler_params=params(62.5),
        cost_estimate=cost(),
        name="norm_back",
    )


def share_back(sent):
    first, last, far = sent
    tiles = lax.axis_size("tile")

    def move(value, by):
        return lax.ppermute(value, "tile", [(i, (i + by) % tiles) for i in range(tiles)])

    return (move(last, 1), move(first, tiles - 1)) + tuple(move(far, n) for n in range(2, tiles - 1))


def turn_kernel(width, block, r_ref, out_ref, turned):
    planes, rows, channels = r_ref.shape
    chosen = out_ref.shape[1]
    pick = iota((chosen, channels), 1) == iota((chosen, channels), 0) + block[0] * chosen
    pick = pick.astype(F32).astype(BF)
    place = iota((chosen, rows), 1)
    on_y, on_z = lax.div(place, width), lax.rem(place, width)
    height = rows // width
    for p in range(planes):
        turned[...] = nt(pick, r_ref[p])
        for b in range(3):
            for c in range(3):
                shift = (b - 1) * width + (c - 1)
                value = turned[...]
                if shift:
                    value = pltpu.roll(value, (-shift) % rows, 1)
                y, z = on_y + (b - 1), on_z + (c - 1)
                inside = (y >= 0) & (y < height) & (z >= 0) & (z < width)
                value = jnp.where(inside, value, 0.0).astype(BF)
                for a in range(3):
                    target = p - a
                    if 0 <= target < planes - 2:
                        out_ref[9 * a + 3 * b + c, :, target * rows : (target + 1) * rows] = value


def turn(block, rounded, width, blocks, follow=()):
    planes, rows, channels = rounded.shape
    chosen = channels // blocks
    shape = (27, chosen, (planes - 2) * rows)
    return ordered(
        functools.partial(turn_kernel, width),
        (block, rounded,),
        [sspec(), whole(rounded.shape)],
        follow,
        grid=(1,),
        out_shape=jax.ShapeDtypeStruct(shape, BF),
        out_specs=whole(shape),
        scratch_shapes=[VMEM((chosen, rows), F32)],
        compiler_params=params(62.5),
        cost_estimate=cost(),
        name="turn",
    )


def weight_grad_kernel(layer, count, first, parts, tiles, split, spots, taps_hbm, *refs):
    grads, refs = refs[:parts], refs[parts:]
    if first:
        y, refs = refs[0], refs[1:]
        y_before, y_after = y.at[pl.ds(0, 1)], y.at[pl.ds(y.shape[0] - 1, 1)]
    else:
        y, y_before, y_after, refs = refs[0], refs[1], refs[2], refs[3:]
    own_far, others, refs = refs[0], refs[1:tiles], refs[tiles:]
    total_hbm, gain_hbm, shift_hbm, refs = *refs[:3], refs[3:]
    shares = tiles if split else 1
    dy_ref, back_ref, wg_refs, refs = refs[0], refs[1], refs[2 : 2 + shares], refs[2 + shares :]
    grads_in, refs = refs[:parts], refs[parts:]
    (taps_in, y_in, y_halo, dn_halo, rest, back, total, gain, shift, dy_buf, dy_rows, wg_buf, in_sem,
     out_sem) = refs
    planes, rows, channels = grads[0].shape
    spare = (parts + 1) * planes
    lists = [
        (total_hbm.at[:, pl.ds(0, 8), :], total),
        (gain_hbm, gain),
        (shift_hbm, shift),
        (y_before, y_halo.at[pl.ds(0, 1)]),
        (y_after, y_halo.at[pl.ds(1, 1)]),
        (others[0], dn_halo.at[0]),
        (others[1], dn_halo.at[1]),
        (own_far, rest.at[0]),
    ] + [(other, rest.at[n + 1]) for n, other in enumerate(others[2:])]
    small = [
        started(source, target, in_sem.at[spare + n]) for n, (source, target) in enumerate(lists)
    ]

    def in_copies(p):
        copies = [pltpu.make_async_copy(y.at[p + first], y_in.at[p], in_sem.at[(parts + 1) * p])]
        for n in range(parts):
            copies.append(
                pltpu.make_async_copy(
                    grads[n].at[p], grads_in[n].at[p], in_sem.at[(parts + 1) * p + 1 + n]
                )
            )
        return copies

    for p in range(planes):
        for copy in in_copies(p):
            copy.start()
    heavy = started(taps_hbm, taps_in, in_sem.at[spare + len(lists)])
    for copy in small:
        copy.wait()
    tile = spots[2]
    tails = [rest[0], dn_halo[0, rows:, :], dn_halo[1, rows:, :]]
    tails += [rest[n] for n in range(1, rest.shape[0])]
    for by, tail in zip([0, 1, tiles - 1] + list(range(2, tiles - 1)), tails):
        value = tail.astype(F32)
        value = value[0:2] + value[2:4] + value[4:6]
        back[lax.rem(tile + tiles - by, tiles), 0:2, :] = value
    mean, inverse = moments(total[...], count)
    gains, shifts = row_of(gain, layer), row_of(shift, layer)
    scale = inverse * gains
    both = back[0, 0:2, :]
    for t in range(1, tiles):
        both = both + back[t, 0:2, :]
    back[0, 0:2, :] = both
    sums = both / count

    def finish(inner, centred):
        return scale * (inner - sums[0:1, :] - centred * sums[1:2, :])

    for side, place in ((0, 0), (1, planes + 1)):
        centred = (y_halo[side].astype(F32) - mean) * inverse
        value = finish(dn_halo[side, 0:rows, :].astype(F32), centred)
        dy_buf[place] = jnp.where(spots[side] > 0, value, 0.0).astype(BF)

    @pl.loop(0, planes)
    def _(p):
        for copy in in_copies(p):
            copy.wait()
        grad = grads_in[0][p].astype(F32)
        for n in range(1, parts):
            grad = grad + grads_in[n][p].astype(F32)
        value = finish(*norm_grads(y_in[p], grad, mean, inverse, gains, shifts)).astype(BF)
        dy_buf[p + 1] = value
        dy_rows[pl.ds(pl.multiple_of(p * rows, rows), rows), :] = value

    done = [
        started(dy_buf, dy_ref, out_sem.at[0]),
        started(back.at[0, pl.ds(0, 2), :], back_ref, out_sem.at[1]),
    ]
    heavy.wait()
    part = nn(taps_in[...], dy_rows[...])
    lines = wg_buf.shape[1]
    for t in range(tiles):
        wg_buf[t] = part[t * lines : (t + 1) * lines].astype(BF)
    if split:
        for by, wg_ref in enumerate(wg_refs):
            share = wg_buf.at[lax.rem(tile + by, tiles)]
            done.append(started(share, wg_ref, out_sem.at[2 + by]))
    else:
        done.append(started(wg_buf, wg_refs[0], out_sem.at[2]))
    for copy in done:
        copy.wait()


def weight_grad(
    spots, taps_t, grads, y, y_halo, far, others, total, gain, shift, layer, count, split,
    follow=(),
):
    planes, rows, channels = grads[0].shape
    wide = taps_t.shape[0]
    tiles = len(others) + 1
    ext = (planes + 2, rows, channels)
    own = (planes, rows, channels)
    operands = (taps_t,) + tuple(grads) + (y,) + tuple(y_halo) + (far,) + tuple(others)
    operands += (total, gain, shift)
    return ordered(
        functools.partial(
            weight_grad_kernel, layer, count, 0 if y_halo else 1, len(grads), tiles, split
        ),
        (spots,) + operands,
        [sspec()] + [aspec()] * len(operands),
        follow,
        out_shape=any_outs(
            (ext, BF),
            ((2, channels), F32),
            *(((wide // tiles, channels), BF),) * tiles
            if split
            else (((tiles, wide // tiles, channels), BF),),
        ),
        out_specs=(aspec(),) * (2 + (tiles if split else 1)),
        scratch_shapes=[VMEM(x.shape, x.dtype) for x in grads]
        + [
            VMEM(taps_t.shape, BF),
            VMEM(own, F32),
            VMEM((2, rows, channels), BF if y_halo else F32),
            VMEM((2, rows + 16, channels), BF),
            VMEM((tiles - 2, 16, channels), BF),
            VMEM((tiles, 8, channels), F32),
            VMEM((tiles, 8, channels), F32),
            VMEM(gain.shape, F32),
            VMEM(gain.shape, F32),
            VMEM(ext, BF),
            VMEM((planes * rows, channels), BF),
            VMEM((tiles, wide // tiles, channels), BF),
        ]
        + sems((len(grads) + 1) * planes + 8 + tiles, 2 + tiles),
        compiler_params=params(62.5),
        cost_estimate=cost(),
        name="weight_grad",
    )


def conv_back_kernel(width, layer, count, parts, dy, w_hbm, *refs):
    more = count is not None
    grads, refs = refs[:parts], refs[parts:]
    if more:
        y, total_hbm, gain_hbm, shift_hbm, refs = *refs[:4], refs[4:]
    out_ref, refs = refs[0], refs[1:]
    if more:
        sent, refs = refs[:3], refs[3:]
    grads_in, refs = refs[:parts], refs[parts:]
    raw, xs, weight, out_buf, in_sem, w_sem, out_sem, refs = *refs[:7], refs[7:]
    ext_planes, rows, channels = dy.shape
    planes = ext_planes - 2
    group = planes // 2
    pairs = 2
    each = parts + 1
    body = started(dy, raw, in_sem.at[each * pairs])
    heavy = [
        started(
            w_hbm.at[layer, pl.ds((26 - o) * channels, channels), :],
            weight.at[:, pl.ds(o * channels, channels)],
            w_sem.at[o],
        )
        for o in range(27)
    ]
    small = []
    if more:
        y_in, total, gain, shift, edges, sums, spare, back_sem = refs
        small = [
            started(source, target, in_sem.at[each * pairs + 1 + n])
            for n, (source, target) in enumerate(
                ((total_hbm.at[:, pl.ds(0, 8), :], total), (gain_hbm, gain), (shift_hbm, shift))
            )
        ]
        sums[...] = jnp.zeros_like(sums)

    def in_copies(i):
        two = pl.ds(group * i, group)
        copies = [
            pltpu.make_async_copy(grads[n].at[two], grads_in[n].at[two], in_sem.at[each * i + n])
            for n in range(parts)
        ]
        if more:
            copies.append(
                pltpu.make_async_copy(
                    y.at[pl.ds(group * i + 1, group)], y_in.at[two], in_sem.at[each * i + parts]
                )
            )
        return copies

    def out_copy(i):
        two = pl.ds(group * i, group)
        return pltpu.make_async_copy(out_buf.at[two], out_ref.at[two], out_sem.at[i])

    for i in range(pairs):
        for copy in in_copies(i):
            copy.start()
    clear_edges(xs, width, rows)
    body.wait()

    @pl.loop(0, ext_planes)
    def _(p):
        put_plane(xs, p, raw[p].astype(F32), width)

    for copy in small + heavy:
        copy.wait()
    if more:
        mean, inverse = moments(total[...], count)
        gains, shifts = row_of(gain, layer - 1), row_of(shift, layer - 1)

    @pl.loop(0, pairs)
    def _(i):
        part = nt(tap_group(xs, group * i, group, width, rows), weight[...])
        for copy in in_copies(i):
            copy.wait()
        for n_plane in range(group):
            p = group * i + n_plane
            value = part[n_plane * rows : (n_plane + 1) * rows]
            for n in range(parts):
                value = value + grads_in[n][p].astype(F32)
            out_buf[p] = value
            if more:
                inner, centred = norm_grads(y_in[p], value, mean, inverse, gains, shifts)
                add_stats(sums, inner, inner * centred)

                for side, near in ((0, 0), (1, group - 1)):
                    if n_plane == near:

                        @pl.when(p == side * (planes - 1))
                        def _():
                            edges[side, 0:rows, :] = inner.astype(BF)

        out_copy(i).start()

    if more:
        finish_back(sums, edges, sent, spare, back_sem)
    for i in range(pairs):
        out_copy(i).wait()


def conv_back(dy, grads, weights, layer, width, norm=None, follow=()):
    ext_planes, rows, channels = dy.shape
    own = (ext_planes - 2, rows, channels)
    pairs = 2
    outs, extra, scratch = [(own, F32)], (), []
    if norm is not None:
        y, total, gain, shift, count = norm
        extra = (y, total, gain, shift)
        outs += list(back_shapes(rows, channels))
        scratch = [VMEM(own, F32), VMEM((total.shape[0], 8, channels), F32)]
        scratch += [VMEM(gain.shape, F32), VMEM(gain.shape, F32)]
        scratch += back_scratch(rows, channels) + sems(3)
    else:
        count = None
    return ordered(
        functools.partial(conv_back_kernel, width, layer, count, len(grads)),
        (dy, weights) + tuple(grads) + extra,
        [aspec()] * (2 + len(grads) + len(extra)),
        follow,
        out_shape=any_outs(*outs),
        out_specs=(aspec(),) * len(outs),
        scratch_shapes=[VMEM(x.shape, x.dtype) for x in grads]
        + [VMEM(dy.shape, BF)]
        + conv_scratch(ext_planes, rows, width, channels, True)
        + [VMEM(own, F32)]
        + sems(pairs * (len(grads) + 1) + 4, 27, pairs)
        + scratch,
        compiler_params=params(62.5),
        cost_estimate=cost(),
        name="conv_back",
    )


GROUP = 3


def ray_grid():
    chips = lax.axis_size("ray") // 2
    wide = max(n for n in range(1, chips + 1) if chips % n == 0 and n * n <= chips)
    return chips // wide, wide


def from_ray(value, down, right, core):
    tall, wide = ray_grid()
    pairs = []
    for y in range(tall):
        for x in range(wide):
            for c in range(2):
                source = ((y + down) % tall * wide + (x + right) % wide) * 2 + (c + core) % 2
                pairs.append((source, (y * wide + x) * 2 + c))
    return lax.ppermute(value, "ray", pairs)


def spread_ray(value):
    tall, wide = ray_grid()
    found = [(value, (0, 0, 0))]
    found += [(from_ray(value, 0, x, 0), (0, x, 0)) for x in range(1, wide)]
    found += [
        (from_ray(v, y, 0, 0), (y, d[1], 0)) for y in range(1, tall) for v, d in tuple(found[:wide])
    ]
    found += [(from_ray(v, 0, 0, 1), (d[0], d[1], 1)) for v, d in tuple(found)]
    return found


def order_kernel(spots, *refs):
    tiles = refs[-1].shape[0]
    outs = refs[tiles:]
    wide = outs[0].shape[-1]
    for by in range(tiles):
        place = lax.rem(spots[2] + tiles - by, tiles)
        for n, out_ref in enumerate(outs):
            out_ref[place] = refs[by][:, n * wide : (n + 1) * wide]


def spread_tile(value, spots, follow, pieces):
    tiles = lax.axis_size("tile")
    parts = [value]
    for by in range(1, tiles):
        pairs = [(i, (i + by) % tiles) for i in range(tiles)]
        parts.append(lax.ppermute(value, "tile", pairs))
    shape = (tiles, value.shape[0], value.shape[1] // pieces)
    found = ordered(
        order_kernel,
        (spots,) + tuple(parts),
        [sspec()] + [whole(value.shape)] * tiles,
        follow,
        grid=(1,),
        out_shape=any_outs(*[(shape, value.dtype)] * pieces),
        out_specs=(whole(shape),) * pieces,
        compiler_params=params(8),
        cost_estimate=cost(),
        name="order_tiles",
    )
    return [x.reshape(-1, shape[2]) for x in found]


def place_mixed_kernel(layer, blocks, distances, grid, spots, source, *refs):
    near, refs = refs[: len(distances)], refs[-6:]
    out_ref, left, right, out, in_sem, out_sem = refs
    tall, wide = grid
    _, offsets, rows, _ = out_ref.shape
    chosen = rows // blocks
    half = left.shape[2]
    count = len(distances)
    far = started(source.at[pl.ds(0, blocks)], left, in_sem.at[count])
    copies = [started(ref, right.at[n], in_sem.at[n]) for n, ref in enumerate(near)]
    far.wait()
    for copy in copies:
        copy.wait()

    @pl.loop(0, offsets)
    def _(o):
        some = pl.ds(pl.multiple_of(o * chosen, chosen), chosen)
        for ray in range(blocks):
            out[o, ray * chosen : (ray + 1) * chosen, 0:half] = left[ray, some, :].astype(F32)
        for n, (down, across, core) in enumerate(distances):
            y, x = lax.rem(spots[3] + down, tall), lax.rem(spots[4] + across, wide)
            ray = (y * wide + x) * 2 + lax.rem(spots[5] + core, 2)
            row = pl.multiple_of(lax.rem(ray, blocks) * chosen, chosen)
            out[o, pl.ds(row, chosen), half : 2 * half] = right[n, some, :].astype(F32)

    done = started(out, out_ref.at[layer], out_sem.at[0])
    done.wait()


def place_mixed(spots, gathered, found, layer, layers, blocks, follow=()):
    _, lines, half = gathered.shape
    channels = 2 * half
    offsets = lines * blocks // channels
    return ordered(
        functools.partial(
            place_mixed_kernel, layer, blocks, tuple(d for _, d in found), ray_grid()
        ),
        (spots, gathered) + tuple(v for v, _ in found),
        [sspec()] + [aspec()] * (1 + len(found)),
        follow,
        out_shape=jax.ShapeDtypeStruct((layers, offsets, channels, channels), F32),
        out_specs=aspec(),
        scratch_shapes=[
            VMEM((blocks, lines, half), BF),
            VMEM((len(found), lines, half), BF),
            VMEM((offsets, channels, channels), F32),
        ]
        + sems(len(found) + 1, 1),
        compiler_params=params(62.5),
        cost_estimate=cost(),
        name="place_mixed",
    )


def gather_ray(slices):
    return lax.all_gather(slices.reshape(-1, slices.shape[-1]), "ray", axis=0)


def place_kernel(layer, blocks, source, *refs):
    out_ref, taken, out, in_sem, out_sem = refs[-5:]
    _, offsets, rows, _ = out_ref.shape
    chosen = rows // blocks
    steps = offsets // GROUP
    lines = GROUP * chosen

    def in_copy(n):
        some = pl.ds(n * lines, lines)
        return pltpu.make_async_copy(
            source.at[pl.ds(0, blocks), some], taken.at[:, some], in_sem.at[n]
        )

    for n in range(steps):
        in_copy(n).start()
    done = []
    for n in range(steps):
        in_copy(n).wait()
        for o in range(n * GROUP, (n + 1) * GROUP):
            for ray in range(blocks):
                out[o, ray * chosen : (ray + 1) * chosen, :] = taken[
                    ray, o * chosen : (o + 1) * chosen, :
                ].astype(F32)
        some = pl.ds(n * GROUP, GROUP)
        done.append(started(out.at[some], out_ref.at[layer, some], out_sem.at[n]))
    for copy in done:
        copy.wait()


def place(parts, layer, layers, blocks, kept, follow=()):
    _, lines, channels = parts.shape
    offsets = lines * blocks // channels
    return ordered(
        functools.partial(place_kernel, layer, blocks),
        (parts,) + kept,
        [aspec()] * (1 + len(kept)),
        follow,
        out_shape=jax.ShapeDtypeStruct((layers, offsets, channels, channels), F32),
        out_specs=aspec(),
        scratch_shapes=[VMEM((blocks, lines, channels), BF), VMEM((offsets, channels, channels), F32)]
        + sems(offsets // GROUP, offsets // GROUP),
        input_output_aliases={1: 0} if kept else {},
        compiler_params=params(62.5),
        cost_estimate=cost(),
        name="place",
    )


def per_device(
    volume,
    sample_cells,
    sample_fracs,
    view_mask,
    pixel_of_ray,
    conv_weight,
    norm_gain,
    norm_shift,
    hidden_weight,
    hidden_bias,
    density_weight,
    density_bias,
    semantic_weight,
    semantic_bias,
    render_cotangent,
    volume_cotangent,
):
    extent = volume.shape[:3]
    depth, height, width, channels = volume.shape
    rows = height * width
    voxels = depth * rows
    tiles = lax.axis_size("tile")
    ray_devices = lax.axis_size("ray")
    count = float(voxels * tiles)
    rays, samples = sample_cells.shape
    classes = semantic_weight.shape[2]
    layers = conv_weight.shape[0]
    blocks = min(BLOCKS, ray_devices)
    chosen = channels // blocks
    tile, ray = lax.axis_index("tile"), lax.axis_index("ray")
    block = lax.rem(ray, blocks).astype(jnp.int32).reshape(1)

    own = volume.reshape(depth, rows, channels)
    before, after = exchange(own[:2], own[-2:])
    flags = jnp.stack([tile > 0, tile < tiles - 1]).astype(jnp.int32)

    owner_of = lax.div(sample_cells, voxels)
    held = owner_of[None] == jnp.arange(tiles, dtype=jnp.int32)[:, None, None]
    earlier = jnp.arange(rays)[None, :] < jnp.arange(rays)[:, None]
    starts = jnp.sum(
        (held[:, None, :, :] & earlier[None, :, :, None]).astype(jnp.int32), axis=(2, 3)
    ).reshape(tiles * rays)
    pixels = pixel_of_ray[0]
    buffer, owner, rank = prepare(extent, starts, sample_cells, sample_fracs, tiles, channels)

    weights = conv_weight.reshape(layers, 27 * channels, channels)
    mlp = (
        hidden_weight,
        hidden_bias,
        semantic_weight,
        density_weight,
        semantic_bias,
        density_bias[None],
    )
    y_ext, v_ext, mixed = conv_first(before, own, after, buffer, weights, 0, width)
    total = received = all_to_all(mixed, "tile")
    taps_first = turn(block, v_ext, width, blocks)
    v_next, r_ext, y_next, stat, y_first, y_last = conv_next(
        flags, y_ext, v_ext, total, norm_gain, norm_shift, weights, 0, width, count,
        follow=(taps_first,),
    )
    total_next = all_to_all(stat, "tile")
    heads, feature, act, slope = sample(extent, received, (r_ext, 1), 0, mlp)
    heads_last, feature_last, act_last, slope_last, r_last = sample(
        extent, received, (y_next, v_next, total_next, norm_gain, norm_shift), 1, mlp, count,
        follow=(heads,),
    )

    def draw(heads, layer, follow):
        return composite(
            starts, pixels, owner, rank, view_mask, all_to_all(heads, "tile"), render_cotangent,
            layer, classes, follow=follow,
        )

    picture, grad_heads = draw(heads, 0, (heads_last,))
    picture_last, grad_heads_last = draw(heads_last, 1, (grad_heads,))
    shares = (ray_devices, voxels // ray_devices, channels)
    planes = (depth, rows, channels)
    local, pack = sample_back(
        extent, 0, received, all_to_all(grad_heads, "tile"), feature, act, slope, mlp, (),
        follow=(grad_heads_last,),
    )
    parts = all_to_all(local.reshape(shares), "ray")
    local_last, packed = sample_back(
        extent, 1, received, all_to_all(grad_heads_last, "tile"), feature_last, act_last,
        slope_last, mlp, (pack,), follow=(local,),
    )
    copies = add_parts(parts, ray_devices, follow=(local_last,))
    parts_last = all_to_all(local_last.reshape(shares), "ray")
    taps_next = turn(block, r_ext, width, blocks, follow=(copies,))
    copies_last = add_parts(parts_last, ray_devices, follow=(taps_next,))
    sums_last = all_to_all(copies_last, "ray").reshape(planes)
    y_edges = exchange(*hold((y_first, y_last), (copies_last,)))
    copies, packed = hold((copies, packed), (sums_last,) + y_edges)
    sums = all_to_all(copies, "ray").reshape(planes)
    packed = lax.psum_scatter(packed, "ray", scatter_dimension=0, tiled=True)

    cot = volume_cotangent.reshape(planes)
    wide_taps = (27 * chosen, voxels)
    _, across = ray_grid()
    spots = jnp.stack(
        [tile > 0, tile < tiles - 1, tile, ray // (2 * across), ray // 2 % across, ray % 2]
    ).astype(jnp.int32)
    sent = norm_back(
        cot, sums_last, y_next, total_next, norm_gain, norm_shift, 1, count,
        follow=y_edges + (copies,),
    )
    dy, back_last, part = weight_grad(
        spots, taps_next.reshape(wide_taps), (cot, sums_last), y_next, y_edges, sent[2],
        share_back(sent), total_next, norm_gain, norm_shift, 1, count, False,
    )
    (held,) = hold((part,), (sums,))
    parts = all_to_all(held, "tile")
    grad, *sent = conv_back(
        dy, (cot, sums_last, sums), weights, 1, width,
        (y_ext, total, norm_gain, norm_shift, count), follow=(held,),
    )
    others = share_back(sent)
    shard = add_parts(parts, 1, follow=(sent[2],))[0]
    dy, back, *shares = weight_grad(
        spots, taps_first.reshape(wide_taps), (grad,), y_ext, (), sent[2], others, total,
        norm_gain, norm_shift, 0, count, True, follow=(shard,),
    )
    moved = [
        lax.ppermute(value, "tile", [(i, (i + by) % tiles) for i in range(tiles)])
        for by, value in enumerate(shares)
        if by
    ]
    left, right = spread_tile(shard, spots, (shares[0],), 2)
    added = add_arrays([shares[0]] + moved, (left,))
    near = spread_ray(*hold((right,), (added,)))
    (slices,) = spread_tile(added, spots, tuple(v for v, _ in near[1 : ray_grid()[1]]), 1)
    packed = all_to_all(add_parts(packed[None], tiles, follow=(slices,)), "tile")
    conv_grad = place_mixed(spots, gather_ray(left), near, 1, layers, blocks, follow=(slices,))
    packed = add_parts(packed, ray_devices, follow=(conv_grad,))
    (grad,) = conv_back(dy, (grad,), weights, 0, width, follow=(packed,))
    packed = all_to_all(packed.astype(BF), "ray").astype(F32)
    packed = packed.reshape(layers, PACK, channels)[::-1]
    at = channels + 16
    heads = packed[:, at : at + DROWS]
    head_bias = packed[:, at + DROWS, :DROWS]
    pictures = jnp.swapaxes(jnp.stack([picture, picture_last])[:, : classes + 1], 1, 2)
    norms = (jnp.stack([back, back_last])[:, 1], jnp.stack([back, back_last])[:, 0])
    rest = (
        packed[:, :channels],
        packed[:, channels],
        heads[:, classes],
        head_bias[:, classes],
        jnp.swapaxes(heads[:, :classes], 1, 2),
        head_bias[:, :classes],
    )
    conv_grad = place(
        gather_ray(slices), 0, layers, blocks, (conv_grad,), follow=(grad, pictures) + norms + rest
    )
    return (
        pictures,
        r_last.reshape(volume.shape),
        grad.reshape(volume.shape),
        conv_grad,
    ) + norms + rest


def solution(mesh):
    in_specs = (
        P("tile", None, None, None),
        P(("ray", "tile"), None),
        P(None, ("ray", "tile"), None),
        P(("ray", "tile"), None),
        P(("ray", "tile"), None),
        P(),
        P(),
        P(),
        P(),
        P(),
        P(),
        P(),
        P(),
        P(),
        P(None, ("ray", "tile"), None),
        P("tile", None, None, None),
    )
    out_specs = (
        P(None, ("ray", "tile"), None),
        P("tile", None, None, None),
        P("tile", None, None, None),
        P(),
        P(),
        P(),
        P(),
        P(),
        P(),
        P(),
        P(),
        P(),
    )
    return jax.shard_map(
        per_device, mesh=mesh, in_specs=in_specs, out_specs=out_specs, check_vma=False
    )
```
